256 devices in a mesh: tm: 64 (over z, y, core), chan: 4 (over x).
Axes of the slice: x: 4, y: 4, z: 8, core: 2. Of those that a mesh axis runs over, the one named last changes fastest.
Arguments:
- tokens: bfloat16 [65536, 1024], P('tm', 'chan'), may hold values from -180 to 180
- norm_gain: float32 [1024], replicated, may hold values from 0.25 to 1.75
- w_value: bfloat16 [1024, 1024], P(None, 'chan'), may hold values from -0.1875 to 0.1875
- w_gate: bfloat16 [1024, 1024], P(None, 'chan'), may hold values from -0.1875 to 0.1875
- phi_taps: float32 [32, 512], replicated, may hold values from -0.0625 to 0.0625
- tap_coeff: float32 [32, 1024], P(None, 'chan'), may hold values from -6 to 6
- skip_gain: float32 [1024], P('chan'), may hold values from -6 to 6
- basis_up: float32 [16, 256], replicated, may hold values from -0.375 to 0.375
- basis_down: float32 [16, 256], replicated, may hold values from -1.5 to 1.5
- lift_maps: float32 [6, 2, 16, 16], replicated, may hold values from -1 to 1
- spread_maps: float32 [6, 2, 16, 16], replicated, may hold values from -1.5 to 1.5
- couplings: float32 [7, 2, 16, 16, 1024], P(None, None, None, None, 'chan'), may hold values from -1 to 1
Outputs:
- filtered: bfloat16 [65536, 1024], P('tm', 'chan')
The draws below stay inside these ranges and needn't reach their ends.
All inputs are finite; a program needn't handle non-finite values.
Results may differ from the reference program's by a relative error of at most 0.007.
Values may be sent and summed in bfloat16 or wider, within the bound.
A program may use at most 128 MiB of HBM per device.

```python
import math
import jax
import jax.numpy as jnp
from jax import lax

C = 1024
L = 256
R = 16
Q = 32
LEVELS = 7
FRAMES = 65536


def draw_tokens(key, part):
    key = jax.random.fold_in(key, 7)
    noise_key, row_key, col_key = jax.random.split(key, 3)
    noise = jax.random.truncated_normal(noise_key, -6.0, 6.0, (FRAMES, C), jnp.float32)
    row_scale = jnp.exp(jax.random.uniform(row_key, (FRAMES, 1), jnp.float32, 0.0, math.log(10.0)))
    ramp = 1.0 + 2.0 * jnp.arange(C, dtype=jnp.float32)[None, :] / (C - 1)
    col_scale = jnp.exp(jax.random.uniform(col_key, (1, C), jnp.float32, 0.0, math.log(10.0))) * ramp
    return (0.1 * noise * row_scale * col_scale).astype(jnp.bfloat16)


def block_scale(own_key, shape, pieces, low, high):
    def one(axis_at, blocks):
        steps = jax.random.uniform(jax.random.fold_in(jax.random.fold_in(own_key, 6), axis_at), (blocks,), jnp.float32, low / len(pieces), high / len(pieces))
        return jnp.repeat(jnp.exp(steps), shape[axis_at] // blocks).reshape((-1,) + (1,) * (len(shape) - axis_at - 1))

    factor_of = one(*pieces[0])
    for cut in pieces[1:]:
        factor_of = factor_of * one(*cut)
    return factor_of


def gaussian(rng, dims, deviation, limit, pieces=(), kind=jnp.bfloat16):
    values = jax.random.normal(rng, dims, jnp.float32) * deviation
    if len(pieces) > 0:
        values = block_scale(rng, dims, pieces, -0.22, 0.18) * values
    return jnp.clip(values, min=-limit, max=limit).astype(kind)


def setup_inputs(seed: int = 0) -> dict:
    arg_keys = jax.random.split(jax.random.key(seed), 13)
    return {
        "tokens": draw_tokens(jax.random.fold_in(arg_keys[12], 71), 0),
        "norm_gain": jnp.clip(1.0 + 0.15 * jax.random.normal(arg_keys[1], (C,), jnp.float32), 0.25, 1.75),
        "w_value": gaussian(arg_keys[2], (C, C), C ** -0.5, 0.1875, ((1, 4),)),
        "w_gate": gaussian(arg_keys[3], (C, C), C ** -0.5, 0.1875, ((1, 4),)),
        "phi_taps": gaussian(arg_keys[4], (Q, 2 * L), (L * Q) ** -0.5, 0.0625, (), jnp.float32),
        "tap_coeff": gaussian(arg_keys[5], (Q, C), 1.0, 6.0, ((1, 4),), jnp.float32),
        "skip_gain": gaussian(arg_keys[6], (C,), 1.0, 6.0, ((0, 4),), jnp.float32),
        "basis_up": gaussian(arg_keys[7], (R, L), L ** -0.5, 0.375, (), jnp.float32),
        "basis_down": gaussian(arg_keys[8], (R, L), R ** -0.5, 1.5, (), jnp.float32),
        "lift_maps": gaussian(arg_keys[9], (LEVELS - 1, 2, R, R), (2 * R) ** -0.5, 1.0, (), jnp.float32),
        "spread_maps": gaussian(arg_keys[10], (LEVELS - 1, 2, R, R), R ** -0.5, 1.5, (), jnp.float32),
        "couplings": gaussian(arg_keys[11], (LEVELS, 2, R, R, C), (2 * R) ** -0.5, 1.0, ((4, 4),), jnp.float32),
    }


def couple_apply(matrix, moments):
    return jnp.einsum('prc,brc->bpc', matrix, moments, precision=lax.Precision.HIGHEST)

def lift_apply(matrix, moments):
    return jnp.einsum('rs,bsc->brc', matrix, moments, precision=lax.Precision.HIGHEST)

def earlier(source_arr, blocks):
    padding = jnp.zeros((blocks,) + source_arr.shape[1:], source_arr.dtype)
    return jnp.concatenate([padding, source_arr[:-blocks]], 0)

def reference(tokens, norm_gain, w_value, w_gate, phi_taps, tap_coeff, skip_gain, basis_up, basis_down, lift_maps, spread_maps, couplings):
    as_float = tokens.astype(jnp.float32)
    squares = lax.optimization_barrier(jnp.sum(as_float * as_float, axis=1))
    inverse = lax.rsqrt(squares / C + 1e-06)
    scaled = (as_float * norm_gain[None, :]).astype(jnp.bfloat16)
    value_rows = (jnp.dot(scaled, w_value, preferred_element_type=jnp.float32) * inverse[:, None]).astype(jnp.bfloat16)
    gate_rows = jax.nn.sigmoid(jnp.dot(scaled, w_gate, preferred_element_type=jnp.float32) * inverse[:, None])
    lag_grid = jnp.arange(L, dtype=jnp.int32)[:, None] + L - jnp.arange(2 * L, dtype=jnp.int32)[None, :]
    tap_table = jnp.where(lag_grid[None] >= 0, phi_taps[:, jnp.clip(lag_grid, 0, 2 * L - 1)], 0.0).astype(jnp.bfloat16)
    leaf_count = FRAMES // L
    leaves = value_rows.reshape(leaf_count, L, C)
    stacked = jnp.concatenate([jnp.zeros((1, L, C), jnp.bfloat16), leaves], 0)
    window = jnp.concatenate([stacked[:-1], stacked[1:]], 1).astype(jnp.float32)

    def near_step(running, inputs):
        tab_rows, weights = inputs
        product = jnp.einsum('ts,bsc->btc', tab_rows.astype(jnp.float32), window, precision=lax.Precision.HIGHEST)
        return (running + product * weights[None, None, :], None)
    near_field, ignored = lax.scan(near_step, jnp.zeros((leaf_count, L, C), jnp.float32), (tap_table, tap_coeff))
    level_count = couplings.shape[0]
    moments = [jnp.einsum('rt,btc->brc', basis_up, leaves.astype(jnp.float32), precision=lax.Precision.HIGHEST)]
    for level_id in range(level_count - 1):
        finer = moments[level_id]
        moments.append(lift_apply(lift_maps[level_id, 0], finer[0::2]) + lift_apply(lift_maps[level_id, 1], finer[1::2]))
    far_terms = []
    odd_masks = []
    for level_id in range(level_count):
        finer = moments[level_id]
        odd_mask = (jnp.arange(finer.shape[0], dtype=jnp.int32) % 2).astype(jnp.float32)[:, None, None]
        odd_masks.append(odd_mask)
        far_terms.append(couple_apply(couplings[level_id, 0], earlier(finer, 2)) + odd_mask * couple_apply(couplings[level_id, 1], earlier(finer, 3)))
    expansion = far_terms[-1]
    for level_id in range(level_count - 2, -1, -1):
        parents = jnp.repeat(expansion, 2, axis=0)
        even_part = lift_apply(spread_maps[level_id, 0], parents)
        odd_part = lift_apply(spread_maps[level_id, 1], parents)
        expansion = far_terms[level_id] + jnp.where(odd_masks[level_id] > 0.5, odd_part, even_part)
    far_field = jnp.einsum('rt,brc->btc', basis_down, expansion, precision=lax.Precision.HIGHEST)
    combined = near_field + far_field + skip_gain[None, None, :] * leaves.astype(jnp.float32)
    return (gate_rows.reshape(leaf_count, L, C) * combined).reshape(FRAMES, C).astype(jnp.bfloat16)
```

```python
import jax
import jax.numpy as jnp
import ml_dtypes
import numpy as np
from jax import lax
from jax.experimental import pallas as pl
from jax.experimental.pallas import tpu as pltpu
from jax.sharding import PartitionSpec as P

MESH = pl.DeviceIdType.MESH
F32 = jnp.float32
BF16 = jnp.bfloat16
HIGHEST = lax.Precision.HIGHEST

LEAF = 256
LEAVES = 4
WIDTH = 256
RANK = 16
PLANES = 8
PLANE = 8
ORDER = (3, 2, 1, 0)


def transform_tables():
    odd = np.arange(LEAF)[:, None] + 0.5
    angle = 2 * np.pi * odd * np.arange(LEAF)[None, :] / (2 * LEAF)
    forward = np.concatenate([np.cos(angle), -np.sin(angle)], 0)

    def split(table):
        high = table.astype(ml_dtypes.bfloat16)
        low = (table - high.astype(np.float64)).astype(ml_dtypes.bfloat16)
        return np.concatenate([high, low], 1)

    return split(forward), split(forward.T / LEAF)


def exact_dot(left, right):
    return jnp.dot(left, right, precision=HIGHEST, preferred_element_type=F32)


def dot(left, right):
    return jnp.dot(left, right, preferred_element_type=F32)


def halves(value):
    high = value.astype(BF16)
    return high, (value - high.astype(F32)).astype(BF16)


def selector(lanes, period, shift, limit):
    row = lax.broadcasted_iota(jnp.int32, (RANK, lanes), 0)
    lane = lax.broadcasted_iota(jnp.int32, (RANK, lanes), 1)
    return ((lax.rem(lane, period) == row + shift) & (lane < limit)).astype(F32)


def body(
    tok, gain, w_value, w_gate, phi, coeff, skip, up, down, lift, spread, coup, fwd, inv,
    out,
    g, w, gain_v, phi_v, coeff_v, skip_v, up_v, down_v, lift_v, spread_v, coup_v, fwd_v, inv_v,
    vals, halo, gate, near, spec, khat, mom_m, lift_m, six_m, far_m, red_m, moms,
    m2, m2_prev, ctx_out, ctx_in, pack_out, pack_in, m5_in, far0, far1, out_v,
    local_sem, dsend, drecv, rsend, rrecv, hsem, csem, s1, r1, s1p, r1p, s2, r2, s5, r5, osem,
):
    t = lax.axis_index("tm")
    x = lax.axis_index("chan")
    core = lax.rem(t, 2)
    y = lax.rem(lax.div(t, 2), 4)
    z = lax.div(t, PLANE)
    own = lax.rem(t, PLANE)
    right, left = lax.rem(x + 1, 4), lax.rem(x + 3, 4)

    m2_prev[...] = jnp.zeros_like(m2_prev)
    ctx_in[...] = jnp.zeros_like(ctx_in)
    pack_in[...] = jnp.zeros_like(pack_in)
    m5_in[...] = jnp.zeros_like(m5_in)
    halo[...] = jnp.zeros_like(halo)

    barrier = pltpu.get_barrier_semaphore()

    def greet(frames, chans):
        pl.semaphore_signal(barrier, inc=1, device_id=(frames, chans), device_id_type=MESH)

    greet(t, right)
    greet(t, left)
    for k in range(1, PLANE):
        greet(z * PLANE + lax.rem(own + k, PLANE), x)
    for k in range(1, PLANES):

        @pl.when(z >= k)
        def _():
            greet(t - k * PLANE, x)

    @pl.when((y == 0) & (z > 0))
    def _():
        greet((z - 1) * PLANE + 6, x)
        greet((z - 1) * PLANE + 7, x)

    copies = {}

    def local(name, source, target):
        copies[name] = pltpu.make_async_copy(source, target, local_sem.at[len(copies)])
        copies[name].start()

    local("tok", tok, g.at[0])
    owners = [x, left, right, lax.rem(x + 2, 4)]
    for slot in range(4):
        rows = pl.ds(pl.multiple_of(owners[slot] * WIDTH, WIDTH), WIDTH)
        local(("v", slot), w_value.at[rows], w.at[slot, :, pl.ds(0, WIDTH)])
        local(("g", slot), w_gate.at[rows], w.at[slot, :, pl.ds(WIDTH, WIDTH)])
    for name, source, target in (
        ("gain", gain, gain_v),
        ("phi", phi, phi_v),
        ("coeff", coeff, coeff_v),
        ("fwd", fwd, fwd_v),
        ("skip", skip, skip_v),
        ("up", up, up_v),
        ("down", down, down_v),
        ("lift", lift, lift_v),
        ("spread", spread, spread_v),
        ("inv", inv, inv_v),
        ("coup", coup, coup_v),
    ):
        local(name, source, target)

    pl.semaphore_wait(barrier, 2 + 7 + (7 - z) + jnp.where((y == 3) & (z < 7), 2, 0))

    def direct(leaf, way):
        rows = pl.ds(leaf * LEAF, LEAF)
        return pltpu.make_async_remote_copy(
            src_ref=tok.at[rows],
            dst_ref=g.at[1 + way, rows],
            send_sem=dsend.at[way, leaf],
            recv_sem=drecv.at[way, leaf],
            device_id=(t, left if way else right),
            device_id_type=MESH,
        )

    def relay(leaf, way):
        rows = pl.ds(leaf * LEAF + way * (LEAF // 2), LEAF // 2)
        return pltpu.make_async_remote_copy(
            src_ref=g.at[1 + way, rows],
            dst_ref=g.at[3, rows],
            send_sem=rsend.at[way, leaf],
            recv_sem=rrecv.at[way, leaf],
            device_id=(t, left if way else right),
            device_id_type=MESH,
        )

    def send_direct(place):
        for way in range(2):
            direct(ORDER[place], way).start()

    def pass_on(place):
        for way in range(2):
            direct(ORDER[place], way).wait_recv()
            relay(ORDER[place], way).start()

    def wait_relayed(place):
        for way in range(2):
            relay(ORDER[place], way).wait_recv()

    def tables_near():
        for name in ("phi", "coeff", "fwd"):
            copies[name].wait()
        taps = phi_v[...].astype(BF16).astype(F32)
        kernel_taps = lax.dot_general(
            taps, coeff_v[...], (((0,), (0,)), ((), ())), precision=HIGHEST, preferred_element_type=F32
        )
        both = jnp.concatenate([kernel_taps[:LEAF], kernel_taps[LEAF:]], 1)
        high, low = halves(both)
        hat = dot(fwd_v[...], jnp.concatenate([high, high], 0)) + dot(fwd_v[:, :LEAF], low)
        a_re, a_im = hat[:LEAF, :WIDTH], hat[LEAF:, :WIDTH]
        b_re, b_im = hat[:LEAF, WIDTH:], hat[LEAF:, WIDTH:]
        row = lax.broadcasted_iota(jnp.int32, (LEAF, WIDTH), 0)
        sign = (1 - 2 * lax.rem(row, 2)).astype(F32)
        khat[0] = a_re
        khat[1] = a_im
        khat[2] = b_re - sign * a_im
        khat[3] = b_im + sign * a_re

    def tables_moments():
        copies["up"].wait()
        copies["lift"].wait()
        base = up_v[...]
        first = [exact_dot(lift_v[0, k], base) for k in range(2)]
        for leaf in range(LEAVES):
            second = exact_dot(lift_v[1, leaf // 2], first[leaf % 2])
            high, low = halves(jnp.concatenate([base, first[leaf % 2], second], 0))
            mom_m[leaf] = jnp.concatenate([high, low], 1)

    def tables_lift():
        def pair(level):
            return exact_dot(lift_v[level, 0], selector(128, 32, 0, 128)) + exact_dot(
                lift_v[level, 1], selector(128, 32, 16, 128)
            )

        def blocks(level, copies_of):
            rows = jnp.concatenate([pair(level)] * copies_of, 0)
            row = lax.broadcasted_iota(jnp.int32, rows.shape, 0)
            lane = lax.broadcasted_iota(jnp.int32, rows.shape, 1)
            return jnp.where(lax.div(row, RANK) == lax.div(lane, 2 * RANK), rows, 0.0)

        three = blocks(2, 8)
        four = exact_dot(blocks(3, 2), three)
        five = exact_dot(blocks(4, 1), jnp.concatenate([four, jnp.zeros((96, 128), F32)], 0))
        whole = jnp.concatenate([four, three[32:64], five, three[:32]], 0)
        high, low = halves(whole)
        lift_m[...] = jnp.concatenate([high, low], 1)
        six = exact_dot(lift_v[5, 0], selector(128, 32, 0, 64)) + exact_dot(
            lift_v[5, 1], selector(128, 32, 16, 64)
        )
        high = six.astype(BF16).astype(F32)
        lane = lax.broadcasted_iota(jnp.int32, six.shape, 1)
        six_m[...] = jnp.where(lane < 32, high, six - high).astype(BF16)

    def tables_far():
        copies["spread"].wait()
        copies["down"].wait()
        row = lax.broadcasted_iota(jnp.int32, (RANK, LEAF), 0)
        lane = lax.broadcasted_iota(jnp.int32, (RANK, LEAF), 1)
        summing = (lax.div(lane, RANK) == row).astype(F32)
        chain = None
        for k in range(5):
            if k > 0:
                step = spread_v[1 + k, lax.rem(lax.div(t, 2 ** (k - 1)), 2)]
                chain = step if k == 1 else exact_dot(chain, step)
            high, low = halves(summing if k == 0 else exact_dot(chain, summing))
            red_m[k] = jnp.concatenate([high, low], 0)
        for leaf in range(LEAVES):
            near_step = spread_v[0, leaf % 2]
            both_steps = exact_dot(near_step, spread_v[1, leaf // 2])
            mix = (
                selector(LEAF, 48, 0, 144)
                + exact_dot(near_step, selector(LEAF, 48, 16, 144))
                + exact_dot(both_steps, selector(LEAF, 48, 32, 144))
            )
            whole = lax.dot_general(
                down_v[...], mix, (((0,), (0,)), ((), ())), precision=HIGHEST, preferred_element_type=F32
            )
            high = whole.astype(BF16).astype(F32)
            lane_at = lax.broadcasted_iota(jnp.int32, whole.shape, 1)
            far_m[leaf] = jnp.where(lane_at < 96, high, whole - high).astype(BF16)

    def project(leaf):
        rows = pl.ds(leaf * LEAF, LEAF)
        squares = jnp.zeros((LEAF, WIDTH), F32)
        parts = []
        for slot in range(4):
            tokens = g[slot, rows, :].astype(F32)
            squares = squares + tokens * tokens
            scale = gain_v[:, pl.ds(pl.multiple_of(owners[slot] * WIDTH, WIDTH), WIDTH)]
            parts.append((tokens * scale).astype(BF16))
        inverse = lax.rsqrt(jnp.sum(squares, axis=1, keepdims=True) / 1024 + 1e-06)
        sums = dot(jnp.concatenate(parts, 1), w[...].reshape(4 * WIDTH, 2 * WIDTH))
        value = (sums[:, :WIDTH] * inverse).astype(BF16)
        vals[rows, :] = value
        gate[rows, :] = jax.nn.sigmoid(sums[:, WIDTH:] * inverse)
        twice = jnp.concatenate([value, value], 0)
        moms[leaf] = dot(mom_m[leaf], twice)
        spec[leaf] = dot(fwd_v[...], twice)

    def near_rows(leaf):
        rows = pl.ds(leaf * LEAF, LEAF)
        before = leaf - 1 if leaf > 0 else LEAVES
        a_re, a_im = spec[leaf, :LEAF, :], spec[leaf, LEAF:, :]
        b_re, b_im = spec[before, :LEAF, :], spec[before, LEAF:, :]
        out_re = khat[0] * a_re - khat[1] * a_im + khat[2] * b_re - khat[3] * b_im
        out_im = khat[0] * a_im + khat[1] * a_re + khat[2] * b_im + khat[3] * b_re
        high, low = halves(jnp.concatenate([out_re, out_im], 0))
        total = dot(inv_v[...], jnp.concatenate([high, high], 0)) + dot(inv_v[:, : 2 * LEAF], low)
        near[rows, :] = total + skip_v[...] * vals[rows, :].astype(F32)

    def coupled(level, source_two, source_three):
        product = coup_v[level, 0] * source_two[None]
        if source_three is not None:
            product = product + coup_v[level, 1] * source_three[None]
        return halves(product.reshape(RANK * RANK, WIDTH))

    send_direct(0)
    send_direct(1)
    tables_near()
    pass_on(0)
    send_direct(2)
    tables_moments()
    pass_on(1)
    send_direct(3)
    for slot in range(4):
        copies["v", slot].wait()
        copies["g", slot].wait()
    copies["tok"].wait()
    copies["gain"].wait()
    copies["skip"].wait()
    copies["inv"].wait()
    wait_relayed(0)
    project(3)

    halo_copy = pltpu.make_async_remote_copy(
        src_ref=vals.at[pl.ds(3 * LEAF, LEAF)],
        dst_ref=halo,
        send_sem=hsem.at[0],
        recv_sem=hsem.at[1],
        device_id=(t + 1, x),
        device_id_type=MESH,
    )

    @pl.when(t < PLANES * PLANE - 1)
    def _():
        halo_copy.start()

    tables_lift()
    pass_on(2)
    wait_relayed(1)
    project(2)
    near_rows(3)
    pass_on(3)
    tables_far()
    wait_relayed(2)
    project(1)
    near_rows(2)
    wait_relayed(3)
    project(0)

    total = moms[0, 32:48, :] + moms[1, 32:48, :] + moms[2, 32:48, :] + moms[3, 32:48, :]
    m2[own] = total.astype(BF16)

    def plane_copy(k):
        return pltpu.make_async_remote_copy(
            src_ref=m2.at[own],
            dst_ref=m2.at[own],
            send_sem=s1.at[k - 1],
            recv_sem=r1.at[k - 1],
            device_id=(z * PLANE + lax.rem(own + k, PLANE), x),
            device_id_type=MESH,
        )

    def plane_arrival(k):
        return pltpu.make_async_remote_copy(
            src_ref=m2.at[own],
            dst_ref=m2.at[lax.rem(own + PLANE - k, PLANE)],
            send_sem=s1.at[k - 1],
            recv_sem=r1.at[k - 1],
            device_id=(z * PLANE + lax.rem(own + k, PLANE), x),
            device_id_type=MESH,
        )

    for k in range(1, PLANE):
        plane_copy(k).start()

    def next_plane_copy(target, source):
        return pltpu.make_async_remote_copy(
            src_ref=m2.at[own],
            dst_ref=m2_prev.at[source],
            send_sem=s1p.at[target],
            recv_sem=r1p.at[source],
            device_id=((z + 1) * PLANE + target, x),
            device_id_type=MESH,
        )

    @pl.when((y == 3) & (z < PLANES - 1))
    def _():
        for target in range(2):
            next_plane_copy(target, core).start()

    ctx_out[...] = jnp.concatenate(
        [
            moms[2, 0:16, :],
            moms[3, 0:16, :],
            moms[0, 16:32, :] + moms[1, 16:32, :],
            moms[2, 16:32, :] + moms[3, 16:32, :],
        ],
        0,
    ).astype(BF16)
    ctx_copy = pltpu.make_async_remote_copy(
        src_ref=ctx_out,
        dst_ref=ctx_in,
        send_sem=csem.at[0],
        recv_sem=csem.at[1],
        device_id=(t + 1, x),
        device_id_type=MESH,
    )

    @pl.when(t < PLANES * PLANE - 1)
    def _():
        ctx_copy.start()

    near_rows(1)

    for k in range(1, PLANE):
        plane_arrival(k).wait_recv()
    stack = m2[...].reshape(PLANE * RANK, WIDTH)
    lifted = dot(lift_m[...], jnp.concatenate([stack, stack], 0))
    pack_out[...] = lifted[:80].astype(BF16)

    def pack_copy(rows):
        return pltpu.make_async_remote_copy(
            src_ref=pack_out.at[pl.ds(0, rows)],
            dst_ref=pack_in.at[pl.ds(0, rows)],
            send_sem=s2,
            recv_sem=r2,
            device_id=(t + PLANE, x),
            device_id_type=MESH,
        )

    def five_copy(k):
        return pltpu.make_async_remote_copy(
            src_ref=pack_out.at[pl.ds(64, RANK)],
            dst_ref=m5_in.at[k],
            send_sem=s5.at[k],
            recv_sem=r5.at[k],
            device_id=(t + k * PLANE, x),
            device_id_type=MESH,
        )

    @pl.when((z < PLANES - 1) & (y < 2))
    def _():
        pack_copy(64).start()

    @pl.when((z < PLANES - 1) & (y >= 2))
    def _():
        pack_copy(32).start()

    for k in range(2, PLANES):

        @pl.when(z + k < PLANES)
        def _():
            five_copy(k).start()

    @pl.when(t > 0)
    def _():
        halo_copy.wait_recv()

    before = halo[...]
    spec[LEAVES] = dot(fwd_v[...], jnp.concatenate([before, before], 0))
    near_rows(0)

    copies["coup"].wait()
    summing = red_m[0, :RANK, :]

    def gathered(level, source_two, source_three=None):
        high, low = coupled(level, source_two, source_three)
        return dot(summing, high) + dot(summing, low)

    @pl.when(t > 0)
    def _():
        ctx_copy.wait_recv()

    prev = ctx_in[...].astype(F32)
    own0 = [moms[leaf, 0:16, :] for leaf in range(2)]
    far0[0] = gathered(0, prev[0:16])
    far0[1] = gathered(0, prev[16:32], prev[0:16])
    far0[2] = gathered(0, own0[0])
    far0[3] = gathered(0, own0[1], own0[0])
    far1[0] = gathered(1, prev[32:48])
    far1[1] = gathered(1, prev[48:64], prev[32:48])

    @pl.when((y == 0) & (z > 0))
    def _():
        for source in range(2):
            next_plane_copy(source, source).wait_recv()

    def reduced(k, source_two, source_three):
        high, low = coupled(2 + k, source_two, source_three)
        both = dot(red_m[k], high)
        return both[:RANK] + both[RANK:] + dot(red_m[k, :RANK, :], low)

    at = 2 * jnp.maximum(y - 1, 0)
    inside = y > 0
    two = jnp.where(inside, m2[at + core], m2_prev[core]).astype(F32)
    three = jnp.where(inside, m2[at], m2_prev[0]).astype(F32) * core.astype(F32)
    expansion = reduced(0, two, three)

    @pl.when((z > 0) & (y < 2))
    def _():
        pack_copy(64).wait_recv()

    @pl.when((z > 0) & (y >= 2))
    def _():
        pack_copy(32).wait_recv()

    odd = lax.rem(y, 2)
    lower = y < 2
    here = jnp.where(odd == 1, lifted[96:112], lifted[80:96])
    coming = pack_in[pl.ds(pl.multiple_of(32 + odd * RANK, RANK), RANK), :].astype(F32)
    two = jnp.where(lower, coming, here)
    three = jnp.where(lower, pack_in[32:48, :].astype(F32), lifted[80:96]) * odd.astype(F32)
    expansion = expansion + reduced(1, two, three)
    odd = lax.div(y, 2)
    two = pack_in[pl.ds(pl.multiple_of(odd * RANK, RANK), RANK), :].astype(F32)
    three = pack_in[0:16, :].astype(F32) * odd.astype(F32)
    expansion = expansion + reduced(2, two, three)

    for k in range(2, PLANES):

        @pl.when(z >= k)
        def _():
            five_copy(k).wait_recv()

    odd = lax.rem(z, 2)
    expansion = expansion + reduced(
        3, m5_in[2].astype(F32), m5_in[3].astype(F32) * odd.astype(F32)
    )
    pad = jnp.zeros((64, WIDTH), BF16)

    def sixth(base):
        pair = [m5_in[base], m5_in[base - 1]]
        return dot(six_m[...], jnp.concatenate(pair + pair + [pad], 0))

    odd_six = lax.rem(lax.div(z, 2), 2)
    expansion = expansion + reduced(
        4, sixth(4 + odd), sixth(6 + odd) * odd_six.astype(F32)
    )

    def out_copy(leaf):
        rows = pl.ds(leaf * LEAF, LEAF)
        return pltpu.make_async_copy(out_v.at[rows], out.at[rows], osem.at[leaf])

    for leaf in range(LEAVES):
        rows = pl.ds(leaf * LEAF, LEAF)
        high, low = halves(jnp.concatenate([far0[leaf], far1[leaf // 2], expansion], 0))
        whole = jnp.concatenate([high, low, high, jnp.zeros((112, WIDTH), BF16)], 0)
        combined = near[rows, :] + dot(far_m[leaf], whole)
        out_v[rows, :] = (gate[rows, :] * combined).astype(BF16)
        out_copy(leaf).start()

    for way in range(2):
        for leaf in range(LEAVES):
            direct(leaf, way).wait_send()
            relay(leaf, way).wait_send()
    for k in range(1, PLANE):
        plane_copy(k).wait_send()

    @pl.when((y == 3) & (z < PLANES - 1))
    def _():
        for target in range(2):
            next_plane_copy(target, core).wait_send()

    @pl.when(t < PLANES * PLANE - 1)
    def _():
        halo_copy.wait_send()
        ctx_copy.wait_send()

    @pl.when((z < PLANES - 1) & (y < 2))
    def _():
        pack_copy(64).wait_send()

    @pl.when((z < PLANES - 1) & (y >= 2))
    def _():
        pack_copy(32).wait_send()

    for k in range(2, PLANES):

        @pl.when(z + k < PLANES)
        def _():
            five_copy(k).wait_send()

    for leaf in range(LEAVES):
        out_copy(leaf).wait()


def per_device(
    tokens,
    norm_gain,
    w_value,
    w_gate,
    phi_taps,
    tap_coeff,
    skip_gain,
    basis_up,
    basis_down,
    lift_maps,
    spread_maps,
    couplings,
):
    forward, inverse = transform_tables()
    any_space = pl.BlockSpec(memory_space=pl.ANY)
    frames = LEAF * LEAVES
    vmem = pltpu.VMEM
    dma = pltpu.SemaphoreType.DMA
    scratch = [
        vmem((4, frames, WIDTH), BF16),
        vmem((4, WIDTH, 2 * WIDTH), BF16),
        vmem((1, 4 * WIDTH), F32),
        vmem(phi_taps.shape, F32),
        vmem(tap_coeff.shape, F32),
        vmem((1, WIDTH), F32),
        vmem(basis_up.shape, F32),
        vmem(basis_down.shape, F32),
        vmem(lift_maps.shape, F32),
        vmem(spread_maps.shape, F32),
        vmem(couplings.shape, F32),
        vmem(forward.shape, BF16),
        vmem(inverse.shape, BF16),
        vmem((frames, WIDTH), BF16),
        vmem((LEAF, WIDTH), BF16),
        vmem((frames, WIDTH), F32),
        vmem((frames, WIDTH), F32),
        vmem((LEAVES + 1, 2 * LEAF, WIDTH), F32),
        vmem((4, LEAF, WIDTH), F32),
        vmem((LEAVES, 48, 2 * LEAF), BF16),
        vmem((112, 256), BF16),
        vmem((RANK, 128), BF16),
        vmem((LEAVES, LEAF, LEAF), BF16),
        vmem((5, 2 * RANK, LEAF), BF16),
        vmem((LEAVES, 48, WIDTH), F32),
        vmem((PLANE, RANK, WIDTH), BF16),
        vmem((2, RANK, WIDTH), BF16),
        vmem((64, WIDTH), BF16),
        vmem((64, WIDTH), BF16),
        vmem((80, WIDTH), BF16),
        vmem((64, WIDTH), BF16),
        vmem((PLANES, RANK, WIDTH), BF16),
        vmem((LEAVES, RANK, WIDTH), F32),
        vmem((2, RANK, WIDTH), F32),
        vmem((frames, WIDTH), BF16),
        dma((20,)),
        dma((2, LEAVES)),
        dma((2, LEAVES)),
        dma((2, LEAVES)),
        dma((2, LEAVES)),
        dma((2,)),
        dma((2,)),
        dma((PLANE - 1,)),
        dma((PLANE - 1,)),
        dma((2,)),
        dma((2,)),
        dma(()),
        dma(()),
        dma((PLANES,)),
        dma((PLANES,)),
        dma((LEAVES,)),
    ]
    return pl.pallas_call(
        body,
        out_shape=jax.ShapeDtypeStruct(tokens.shape, BF16),
        in_specs=[any_space] * 14,
        out_specs=any_space,
        scratch_shapes=scratch,
        compiler_params=pltpu.CompilerParams(
            collective_id=0, has_side_effects=True, vmem_limit_bytes=48 * 1024 * 1024
        ),
        cost_estimate=pl.CostEstimate(flops=4 * 10**9, bytes_accessed=8 * 10**6, transcendentals=10**6),
    )(
        tokens,
        norm_gain.reshape(1, -1),
        w_value,
        w_gate,
        phi_taps,
        tap_coeff,
        skip_gain.reshape(1, -1),
        basis_up,
        basis_down,
        lift_maps,
        spread_maps,
        couplings,
        jnp.asarray(forward),
        jnp.asarray(inverse),
    )


def solution(mesh):
    placed = (
        P("tm", "chan"),
        P(),
        P(None, "chan"),
        P(None, "chan"),
        P(),
        P(None, "chan"),
        P("chan"),
        P(),
        P(),
        P(),
        P(),
        P(None, None, None, None, "chan"),
    )
    return jax.shard_map(
        per_device, mesh=mesh, in_specs=placed, out_specs=P("tm", "chan"), check_vma=False
    )
```

```python
import jax
import jax.numpy as jnp
import numpy as np
from jax import lax
from jax.experimental import pallas as pl
from jax.experimental.pallas import tpu as pltpu
from jax.sharding import PartitionSpec as P

MESH = pl.DeviceIdType.MESH
F32 = jnp.float32
BF16 = jnp.bfloat16
HIGHEST = lax.Precision.HIGHEST

LEAF = 256
LEAVES = 4
WIDTH = 256
RANK = 16
PLANES = 8
PLANE = 8
ORDER = (3, 2, 1, 0)


def transform_tables():
    odd = np.arange(LEAF)[:, None] + 0.5
    angle = 2 * np.pi * odd * np.arange(LEAF)[None, :] / (2 * LEAF)
    forward = np.concatenate([np.cos(angle), -np.sin(angle)], 0)
    return forward.astype(np.float32), (forward.T / LEAF).astype(np.float32)


def exact_dot(left, right):
    return jnp.dot(left, right, precision=HIGHEST, preferred_element_type=F32)


def dot(left, right):
    return jnp.dot(left, right, preferred_element_type=F32)


def halves(value):
    high = value.astype(BF16)
    return high, (value - high.astype(F32)).astype(BF16)


def selector(lanes, period, shift, limit):
    row = lax.broadcasted_iota(jnp.int32, (RANK, lanes), 0)
    lane = lax.broadcasted_iota(jnp.int32, (RANK, lanes), 1)
    return ((lax.rem(lane, period) == row + shift) & (lane < limit)).astype(F32)


def body(
    tok, gain, w_value, w_gate, phi, coeff, skip, up, down, lift, spread, coup, fwd, inv,
    out,
    g, w, gain_v, phi_v, coeff_v, skip_v, up_v, down_v, lift_v, spread_v, coup_v, fwd_f, inv_f, fwd_v, inv_v,
    vals, halo, gate, near, spec, khat, mom_m, lift_m, six_m, far_m, red_m, moms,
    m2, m2_prev, ctx_out, ctx_in, pack_out, pack_in, m5_in, far0, far1,
    local_sem, dsend, drecv, rsend, rrecv, hsem, csem, s1, r1, s1p, r1p, s2, r2, s5, r5,
):
    t = lax.axis_index("tm")
    x = lax.axis_index("chan")
    core = lax.rem(t, 2)
    y = lax.rem(lax.div(t, 2), 4)
    z = lax.div(t, PLANE)
    own = lax.rem(t, PLANE)
    right, left = lax.rem(x + 1, 4), lax.rem(x + 3, 4)

    m2_prev[...] = jnp.zeros_like(m2_prev)
    ctx_in[...] = jnp.zeros_like(ctx_in)
    pack_in[...] = jnp.zeros_like(pack_in)
    m5_in[...] = jnp.zeros_like(m5_in)
    halo[...] = jnp.zeros_like(halo)

    barrier = pltpu.get_barrier_semaphore()

    def greet(frames, chans):
        pl.semaphore_signal(barrier, inc=1, device_id=(frames, chans), device_id_type=MESH)

    greet(t, right)
    greet(t, left)
    for k in range(1, PLANE):
        greet(z * PLANE + lax.rem(own + k, PLANE), x)
    for k in range(1, PLANES):

        @pl.when(z >= k)
        def _():
            greet(t - k * PLANE, x)

    @pl.when((y == 0) & (z > 0))
    def _():
        greet((z - 1) * PLANE + 6, x)
        greet((z - 1) * PLANE + 7, x)

    copies = {}

    def local(name, source, target):
        copies[name] = pltpu.make_async_copy(source, target, local_sem.at[len(copies)])
        copies[name].start()

    local("tok", tok, g.at[0])
    owners = [x, left, right, lax.rem(x + 2, 4)]
    for slot in range(4):
        rows = pl.ds(pl.multiple_of(owners[slot] * WIDTH, WIDTH), WIDTH)
        local(("v", slot), w_value.at[rows], w.at[slot, :, pl.ds(0, WIDTH)])
        local(("g", slot), w_gate.at[rows], w.at[slot, :, pl.ds(WIDTH, WIDTH)])
    for name, source, target in (
        ("gain", gain, gain_v),
        ("phi", phi, phi_v),
        ("coeff", coeff, coeff_v),
        ("fwd", fwd, fwd_f),
        ("skip", skip, skip_v),
        ("up", up, up_v),
        ("down", down, down_v),
        ("lift", lift, lift_v),
        ("spread", spread, spread_v),
        ("inv", inv, inv_f),
        ("coup", coup, coup_v),
    ):
        local(name, source, target)

    pl.semaphore_wait(barrier, 2 + 7 + (7 - z) + jnp.where((y == 3) & (z < 7), 2, 0))

    def direct(leaf, way):
        rows = pl.ds(leaf * LEAF, LEAF)
        return pltpu.make_async_remote_copy(
            src_ref=tok.at[rows],
            dst_ref=g.at[1 + way, rows],
            send_sem=dsend.at[way, leaf],
            recv_sem=drecv.at[way, leaf],
            device_id=(t, left if way else right),
            device_id_type=MESH,
        )

    def relay(leaf, way):
        rows = pl.ds(leaf * LEAF + way * (LEAF // 2), LEAF // 2)
        return pltpu.make_async_remote_copy(
            src_ref=g.at[1 + way, rows],
            dst_ref=g.at[3, rows],
            send_sem=rsend.at[way, leaf],
            recv_sem=rrecv.at[way, leaf],
            device_id=(t, left if way else right),
            device_id_type=MESH,
        )

    def send_direct(place):
        for way in range(2):
            direct(ORDER[place], way).start()

    def pass_on(place):
        for way in range(2):
            direct(ORDER[place], way).wait_recv()
            relay(ORDER[place], way).start()

    def wait_relayed(place):
        for way in range(2):
            relay(ORDER[place], way).wait_recv()

    def tables_near():
        for name in ("phi", "coeff", "fwd"):
            copies[name].wait()
        fwd_v[...] = jnp.concatenate(halves(fwd_f[...]), 1)
        taps = phi_v[...].astype(BF16).astype(F32)
        kernel_taps = lax.dot_general(
            taps, coeff_v[...], (((0,), (0,)), ((), ())), precision=HIGHEST, preferred_element_type=F32
        )
        both = jnp.concatenate([kernel_taps[:LEAF], kernel_taps[LEAF:]], 1)
        high, low = halves(both)
        hat = dot(fwd_v[...], jnp.concatenate([high, high], 0)) + dot(fwd_v[:, :LEAF], low)
        a_re, a_im = hat[:LEAF, :WIDTH], hat[LEAF:, :WIDTH]
        b_re, b_im = hat[:LEAF, WIDTH:], hat[LEAF:, WIDTH:]
        row = lax.broadcasted_iota(jnp.int32, (LEAF, WIDTH), 0)
        sign = (1 - 2 * lax.rem(row, 2)).astype(F32)
        khat[0] = a_re
        khat[1] = a_im
        khat[2] = b_re - sign * a_im
        khat[3] = b_im + sign * a_re

    def tables_moments():
        copies["up"].wait()
        copies["lift"].wait()
        base = up_v[...]
        first = [exact_dot(lift_v[0, k], base) for k in range(2)]
        for leaf in range(LEAVES):
            second = exact_dot(lift_v[1, leaf // 2], first[leaf % 2])
            high, low = halves(jnp.concatenate([base, first[leaf % 2], second], 0))
            mom_m[leaf] = jnp.concatenate([high, low], 1)

    def tables_lift():
        def pair(level):
            return exact_dot(lift_v[level, 0], selector(128, 32, 0, 128)) + exact_dot(
                lift_v[level, 1], selector(128, 32, 16, 128)
            )

        def blocks(level, copies_of):
            rows = jnp.concatenate([pair(level)] * copies_of, 0)
            row = lax.broadcasted_iota(jnp.int32, rows.shape, 0)
            lane = lax.broadcasted_iota(jnp.int32, rows.shape, 1)
            return jnp.where(lax.div(row, RANK) == lax.div(lane, 2 * RANK), rows, 0.0)

        three = blocks(2, 8)
        four = exact_dot(blocks(3, 2), three)
        five = exact_dot(blocks(4, 1), jnp.concatenate([four, jnp.zeros((96, 128), F32)], 0))
        whole = jnp.concatenate([four, three[32:64], five, three[:32]], 0)
        high, low = halves(whole)
        lift_m[...] = jnp.concatenate([high, low], 1)
        six = exact_dot(lift_v[5, 0], selector(128, 32, 0, 64)) + exact_dot(
            lift_v[5, 1], selector(128, 32, 16, 64)
        )
        high = six.astype(BF16).astype(F32)
        lane = lax.broadcasted_iota(jnp.int32, six.shape, 1)
        six_m[...] = jnp.where(lane < 32, high, six - high).astype(BF16)

    def tables_far():
        copies["spread"].wait()
        copies["down"].wait()
        row = lax.broadcasted_iota(jnp.int32, (RANK, LEAF), 0)
        lane = lax.broadcasted_iota(jnp.int32, (RANK, LEAF), 1)
        summing = (lax.div(lane, RANK) == row).astype(F32)
        chain = None
        for k in range(5):
            if k > 0:
                step = spread_v[1 + k, lax.rem(lax.div(t, 2 ** (k - 1)), 2)]
                chain = step if k == 1 else exact_dot(chain, step)
            high, low = halves(summing if k == 0 else exact_dot(chain, summing))
            red_m[k] = jnp.concatenate([high, low], 0)
        for leaf in range(LEAVES):
            near_step = spread_v[0, leaf % 2]
            both_steps = exact_dot(near_step, spread_v[1, leaf // 2])
            mix = (
                selector(LEAF, 48, 0, 144)
                + exact_dot(near_step, selector(LEAF, 48, 16, 144))
                + exact_dot(both_steps, selector(LEAF, 48, 32, 144))
            )
            whole = lax.dot_general(
                down_v[...], mix, (((0,), (0,)), ((), ())), precision=HIGHEST, preferred_element_type=F32
            )
            high = whole.astype(BF16).astype(F32)
            lane_at = lax.broadcasted_iota(jnp.int32, whole.shape, 1)
            far_m[leaf] = jnp.where(lane_at < 96, high, whole - high).astype(BF16)

    def project(leaf):
        rows = pl.ds(leaf * LEAF, LEAF)
        squares = jnp.zeros((LEAF, WIDTH), F32)
        parts = []
        for slot in range(4):
            tokens = g[slot, rows, :].astype(F32)
            squares = squares + tokens * tokens
            scale = gain_v[:, pl.ds(pl.multiple_of(owners[slot] * WIDTH, WIDTH), WIDTH)]
            parts.append((tokens * scale).astype(BF16))
        inverse = lax.rsqrt(jnp.sum(squares, axis=1, keepdims=True) / 1024 + 1e-06)
        sums = dot(jnp.concatenate(parts, 1), w[...].reshape(4 * WIDTH, 2 * WIDTH))
        value = (sums[:, :WIDTH] * inverse).astype(BF16)
        vals[rows, :] = value
        gate[rows, :] = jax.nn.sigmoid(sums[:, WIDTH:] * inverse)
        twice = jnp.concatenate([value, value], 0)
        moms[leaf] = dot(mom_m[leaf], twice)
        spec[leaf] = dot(fwd_v[...], twice)

    def near_rows(leaf):
        rows = pl.ds(leaf * LEAF, LEAF)
        before = leaf - 1 if leaf > 0 else LEAVES
        a_re, a_im = spec[leaf, :LEAF, :], spec[leaf, LEAF:, :]
        b_re, b_im = spec[before, :LEAF, :], spec[before, LEAF:, :]
        out_re = khat[0] * a_re - khat[1] * a_im + khat[2] * b_re - khat[3] * b_im
        out_im = khat[0] * a_im + khat[1] * a_re + khat[2] * b_im + khat[3] * b_re
        high, low = halves(jnp.concatenate([out_re, out_im], 0))
        total = dot(inv_v[...], jnp.concatenate([high, high], 0)) + dot(inv_v[:, : 2 * LEAF], low)
        near[rows, :] = total + skip_v[...] * vals[rows, :].astype(F32)

    def coupled(level, source_two, source_three):
        product = coup_v[level, 0] * source_two[None]
        if source_three is not None:
            product = product + coup_v[level, 1] * source_three[None]
        return halves(product.reshape(RANK * RANK, WIDTH))

    send_direct(0)
    send_direct(1)
    tables_near()
    pass_on(0)
    send_direct(2)
    tables_moments()
    pass_on(1)
    send_direct(3)
    for slot in range(4):
        copies["v", slot].wait()
        copies["g", slot].wait()
    copies["tok"].wait()
    copies["gain"].wait()
    copies["skip"].wait()
    copies["inv"].wait()
    inv_v[...] = jnp.concatenate(halves(inv_f[...]), 1)
    wait_relayed(0)
    project(3)

    halo_copy = pltpu.make_async_remote_copy(
        src_ref=vals.at[pl.ds(3 * LEAF, LEAF)],
        dst_ref=halo,
        send_sem=hsem.at[0],
        recv_sem=hsem.at[1],
        device_id=(t + 1, x),
        device_id_type=MESH,
    )

    @pl.when(t < PLANES * PLANE - 1)
    def _():
        halo_copy.start()

    tables_lift()
    pass_on(2)
    wait_relayed(1)
    project(2)
    near_rows(3)
    pass_on(3)
    tables_far()
    wait_relayed(2)
    project(1)
    near_rows(2)
    wait_relayed(3)
    project(0)

    total = moms[0, 32:48, :] + moms[1, 32:48, :] + moms[2, 32:48, :] + moms[3, 32:48, :]
    m2[own] = total.astype(BF16)

    def plane_copy(k):
        return pltpu.make_async_remote_copy(
            src_ref=m2.at[own],
            dst_ref=m2.at[own],
            send_sem=s1.at[k - 1],
            recv_sem=r1.at[k - 1],
            device_id=(z * PLANE + lax.rem(own + k, PLANE), x),
            device_id_type=MESH,
        )

    def plane_arrival(k):
        return pltpu.make_async_remote_copy(
            src_ref=m2.at[own],
            dst_ref=m2.at[lax.rem(own + PLANE - k, PLANE)],
            send_sem=s1.at[k - 1],
            recv_sem=r1.at[k - 1],
            device_id=(z * PLANE + lax.rem(own + k, PLANE), x),
            device_id_type=MESH,
        )

    for k in range(1, PLANE):
        plane_copy(k).start()

    def next_plane_copy(target, source):
        return pltpu.make_async_remote_copy(
            src_ref=m2.at[own],
            dst_ref=m2_prev.at[source],
            send_sem=s1p.at[target],
            recv_sem=r1p.at[source],
            device_id=((z + 1) * PLANE + target, x),
            device_id_type=MESH,
        )

    @pl.when((y == 3) & (z < PLANES - 1))
    def _():
        for target in range(2):
            next_plane_copy(target, core).start()

    ctx_out[...] = jnp.concatenate(
        [
            moms[2, 0:16, :],
            moms[3, 0:16, :],
            moms[0, 16:32, :] + moms[1, 16:32, :],
            moms[2, 16:32, :] + moms[3, 16:32, :],
        ],
        0,
    ).astype(BF16)
    ctx_copy = pltpu.make_async_remote_copy(
        src_ref=ctx_out,
        dst_ref=ctx_in,
        send_sem=csem.at[0],
        recv_sem=csem.at[1],
        device_id=(t + 1, x),
        device_id_type=MESH,
    )

    @pl.when(t < PLANES * PLANE - 1)
    def _():
        ctx_copy.start()

    near_rows(1)

    for k in range(1, PLANE):
        plane_arrival(k).wait_recv()
    stack = m2[...].reshape(PLANE * RANK, WIDTH)
    lifted = dot(lift_m[...], jnp.concatenate([stack, stack], 0))
    pack_out[...] = lifted[:80].astype(BF16)

    def pack_copy(rows):
        return pltpu.make_async_remote_copy(
            src_ref=pack_out.at[pl.ds(0, rows)],
            dst_ref=pack_in.at[pl.ds(0, rows)],
            send_sem=s2,
            recv_sem=r2,
            device_id=(t + PLANE, x),
            device_id_type=MESH,
        )

    def five_copy(k):
        return pltpu.make_async_remote_copy(
            src_ref=pack_out.at[pl.ds(64, RANK)],
            dst_ref=m5_in.at[k],
            send_sem=s5.at[k],
            recv_sem=r5.at[k],
            device_id=(t + k * PLANE, x),
            device_id_type=MESH,
        )

    @pl.when((z < PLANES - 1) & (y < 2))
    def _():
        pack_copy(64).start()

    @pl.when((z < PLANES - 1) & (y >= 2))
    def _():
        pack_copy(32).start()

    for k in range(2, PLANES):

        @pl.when(z + k < PLANES)
        def _():
            five_copy(k).start()

    @pl.when(t > 0)
    def _():
        halo_copy.wait_recv()

    before = halo[...]
    spec[LEAVES] = dot(fwd_v[...], jnp.concatenate([before, before], 0))
    near_rows(0)

    copies["coup"].wait()
    summing = red_m[0, :RANK, :]

    def gathered(level, source_two, source_three=None):
        high, low = coupled(level, source_two, source_three)
        return dot(summing, high) + dot(summing, low)

    @pl.when(t > 0)
    def _():
        ctx_copy.wait_recv()

    prev = ctx_in[...].astype(F32)
    own0 = [moms[leaf, 0:16, :] for leaf in range(2)]
    far0[0] = gathered(0, prev[0:16])
    far0[1] = gathered(0, prev[16:32], prev[0:16])
    far0[2] = gathered(0, own0[0])
    far0[3] = gathered(0, own0[1], own0[0])
    far1[0] = gathered(1, prev[32:48])
    far1[1] = gathered(1, prev[48:64], prev[32:48])

    @pl.when((y == 0) & (z > 0))
    def _():
        for source in range(2):
            next_plane_copy(source, source).wait_recv()

    def reduced(k, source_two, source_three):
        high, low = coupled(2 + k, source_two, source_three)
        both = dot(red_m[k], high)
        return both[:RANK] + both[RANK:] + dot(red_m[k, :RANK, :], low)

    at = 2 * jnp.maximum(y - 1, 0)
    inside = y > 0
    two = jnp.where(inside, m2[at + core], m2_prev[core]).astype(F32)
    three = jnp.where(inside, m2[at], m2_prev[0]).astype(F32) * core.astype(F32)
    expansion = reduced(0, two, three)

    @pl.when((z > 0) & (y < 2))
    def _():
        pack_copy(64).wait_recv()

    @pl.when((z > 0) & (y >= 2))
    def _():
        pack_copy(32).wait_recv()

    odd = lax.rem(y, 2)
    lower = y < 2
    here = jnp.where(odd == 1, lifted[96:112], lifted[80:96])
    coming = pack_in[pl.ds(pl.multiple_of(32 + odd * RANK, RANK), RANK), :].astype(F32)
    two = jnp.where(lower, coming, here)
    three = jnp.where(lower, pack_in[32:48, :].astype(F32), lifted[80:96]) * odd.astype(F32)
    expansion = expansion + reduced(1, two, three)
    odd = lax.div(y, 2)
    two = pack_in[pl.ds(pl.multiple_of(odd * RANK, RANK), RANK), :].astype(F32)
    three = pack_in[0:16, :].astype(F32) * odd.astype(F32)
    expansion = expansion + reduced(2, two, three)

    for k in range(2, PLANES):

        @pl.when(z >= k)
        def _():
            five_copy(k).wait_recv()

    odd = lax.rem(z, 2)
    expansion = expansion + reduced(
        3, m5_in[2].astype(F32), m5_in[3].astype(F32) * odd.astype(F32)
    )
    pad = jnp.zeros((64, WIDTH), BF16)

    def sixth(base):
        pair = [m5_in[base], m5_in[base - 1]]
        return dot(six_m[...], jnp.concatenate(pair + pair + [pad], 0))

    odd_six = lax.rem(lax.div(z, 2), 2)
    expansion = expansion + reduced(
        4, sixth(4 + odd), sixth(6 + odd) * odd_six.astype(F32)
    )

    for leaf in range(LEAVES):
        rows = pl.ds(leaf * LEAF, LEAF)
        high, low = halves(jnp.concatenate([far0[leaf], far1[leaf // 2], expansion], 0))
        whole = jnp.concatenate([high, low, high, jnp.zeros((112, WIDTH), BF16)], 0)
        combined = near[rows, :] + dot(far_m[leaf], whole)
        out[rows, :] = (gate[rows, :] * combined).astype(BF16)

    for way in range(2):
        for leaf in range(LEAVES):
            direct(leaf, way).wait_send()
            relay(leaf, way).wait_send()
    for k in range(1, PLANE):
        plane_copy(k).wait_send()

    @pl.when((y == 3) & (z < PLANES - 1))
    def _():
        for target in range(2):
            next_plane_copy(target, core).wait_send()

    @pl.when(t < PLANES * PLANE - 1)
    def _():
        halo_copy.wait_send()
        ctx_copy.wait_send()

    @pl.when((z < PLANES - 1) & (y < 2))
    def _():
        pack_copy(64).wait_send()

    @pl.when((z < PLANES - 1) & (y >= 2))
    def _():
        pack_copy(32).wait_send()

    for k in range(2, PLANES):

        @pl.when(z + k < PLANES)
        def _():
            five_copy(k).wait_send()


def per_device(
    tokens,
    norm_gain,
    w_value,
    w_gate,
    phi_taps,
    tap_coeff,
    skip_gain,
    basis_up,
    basis_down,
    lift_maps,
    spread_maps,
    couplings,
):
    forward, inverse = transform_tables()
    in_hbm = pl.BlockSpec(memory_space=pltpu.HBM)
    frames = LEAF * LEAVES
    vmem = pltpu.VMEM
    dma = pltpu.SemaphoreType.DMA
    scratch = [
        vmem((4, frames, WIDTH), BF16),
        vmem((4, WIDTH, 2 * WIDTH), BF16),
        vmem((1, 4 * WIDTH), F32),
        vmem(phi_taps.shape, F32),
        vmem(tap_coeff.shape, F32),
        vmem((1, WIDTH), F32),
        vmem(basis_up.shape, F32),
        vmem(basis_down.shape, F32),
        vmem(lift_maps.shape, F32),
        vmem(spread_maps.shape, F32),
        vmem(couplings.shape, F32),
        vmem(forward.shape, F32),
        vmem(inverse.shape, F32),
        vmem((2 * LEAF, 2 * LEAF), BF16),
        vmem((LEAF, 4 * LEAF), BF16),
        vmem((frames, WIDTH), BF16),
        vmem((LEAF, WIDTH), BF16),
        vmem((frames, WIDTH), F32),
        vmem((frames, WIDTH), F32),
        vmem((LEAVES + 1, 2 * LEAF, WIDTH), F32),
        vmem((4, LEAF, WIDTH), F32),
        vmem((LEAVES, 48, 2 * LEAF), BF16),
        vmem((112, 256), BF16),
        vmem((RANK, 128), BF16),
        vmem((LEAVES, LEAF, LEAF), BF16),
        vmem((5, 2 * RANK, LEAF), BF16),
        vmem((LEAVES, 48, WIDTH), F32),
        vmem((PLANE, RANK, WIDTH), BF16),
        vmem((2, RANK, WIDTH), BF16),
        vmem((64, WIDTH), BF16),
        vmem((64, WIDTH), BF16),
        vmem((80, WIDTH), BF16),
        vmem((64, WIDTH), BF16),
        vmem((PLANES, RANK, WIDTH), BF16),
        vmem((LEAVES, RANK, WIDTH), F32),
        vmem((2, RANK, WIDTH), F32),
        dma((20,)),
        dma((2, LEAVES)),
        dma((2, LEAVES)),
        dma((2, LEAVES)),
        dma((2, LEAVES)),
        dma((2,)),
        dma((2,)),
        dma((PLANE - 1,)),
        dma((PLANE - 1,)),
        dma((2,)),
        dma((2,)),
        dma(()),
        dma(()),
        dma((PLANES,)),
        dma((PLANES,)),
    ]
    return pl.pallas_call(
        body,
        out_shape=jax.ShapeDtypeStruct(tokens.shape, BF16),
        in_specs=[in_hbm] * 14,
        out_specs=pl.BlockSpec(memory_space=pltpu.VMEM),
        scratch_shapes=scratch,
        compiler_params=pltpu.CompilerParams(
            collective_id=0, has_side_effects=True, vmem_limit_bytes=60 * 1024 * 1024
        ),
        cost_estimate=pl.CostEstimate(flops=4 * 10**9, bytes_accessed=8 * 10**6, transcendentals=10**6),
    )(
        tokens,
        norm_gain.reshape(1, -1),
        w_value,
        w_gate,
        phi_taps,
        tap_coeff,
        skip_gain.reshape(1, -1),
        basis_up,
        basis_down,
        lift_maps,
        spread_maps,
        couplings,
        jnp.asarray(forward),
        jnp.asarray(inverse),
    )


def solution(mesh):
    placed = (
        P("tm", "chan"),
        P(),
        P(None, "chan"),
        P(None, "chan"),
        P(),
        P(None, "chan"),
        P("chan"),
        P(),
        P(),
        P(),
        P(),
        P(None, None, None, None, "chan"),
    )
    return jax.shard_map(
        per_device, mesh=mesh, in_specs=placed, out_specs=P("tm", "chan"), check_vma=False
    )
```

```python
import jax
import jax.numpy as jnp
import numpy as np
from jax import lax
from jax.experimental import pallas as pl
from jax.experimental.pallas import tpu as pltpu
from jax.sharding import PartitionSpec as P

MESH = pl.DeviceIdType.MESH
F32 = jnp.float32
BF16 = jnp.bfloat16
HIGHEST = lax.Precision.HIGHEST

LEAF = 256
LEAVES = 4
WIDTH = 256
RANK = 16
PLANES = 8
PLANE = 8


def transform_tables():
    odd = np.arange(LEAF)[:, None] + 0.5
    angle = 2 * np.pi * odd * np.arange(LEAF)[None, :] / (2 * LEAF)
    forward = np.concatenate([np.cos(angle), -np.sin(angle)], 0)
    return forward.astype(np.float32), (forward.T / LEAF).astype(np.float32)


def exact_dot(left, right):
    return jnp.dot(left, right, precision=HIGHEST, preferred_element_type=F32)


def dot(left, right):
    return jnp.dot(left, right, preferred_element_type=F32)


def halves(value):
    high = value.astype(BF16)
    return high, (value - high.astype(F32)).astype(BF16)


def selector(lanes, period, shift, limit):
    row = lax.broadcasted_iota(jnp.int32, (RANK, lanes), 0)
    lane = lax.broadcasted_iota(jnp.int32, (RANK, lanes), 1)
    return ((lax.rem(lane, period) == row + shift) & (lane < limit)).astype(F32)


def body(
    tok, gain, w_value, w_gate, phi, coeff, skip, up, down, lift, spread, coup, fwd, inv,
    out,
    g, w, gain_v, phi_v, coeff_v, skip_v, up_v, down_v, lift_v, spread_v, coup_v, fwd_f, inv_f, fwd_v, inv_v,
    vals, halo, gate, near, spec, khat, mom_m, lift_m, six_m, far_m, red_m, moms,
    m2, m2_prev, ctx_out, ctx_in, pack_out, pack_in, m5_in, far0, far1,
    local_sem, dsend, drecv, rsend, rrecv, hsem, csem, s1, r1, s1p, r1p, s2, r2, s5, r5, ready_plane, ready_later,
):
    t = lax.axis_index("tm")
    x = lax.axis_index("chan")
    core = lax.rem(t, 2)
    y = lax.rem(lax.div(t, 2), 4)
    z = lax.div(t, PLANE)
    own = lax.rem(t, PLANE)
    right, left = lax.rem(x + 1, 4), lax.rem(x + 3, 4)

    m2_prev[...] = jnp.zeros_like(m2_prev)
    ctx_in[...] = jnp.zeros_like(ctx_in)
    pack_in[...] = jnp.zeros_like(pack_in)
    m5_in[...] = jnp.zeros_like(m5_in)
    halo[...] = jnp.zeros_like(halo)

    barrier = pltpu.get_barrier_semaphore()

    def signal(semaphore, frames, chans):
        pl.semaphore_signal(semaphore, inc=1, device_id=(frames, chans), device_id_type=MESH)

    signal(barrier, t, right)
    signal(barrier, t, left)
    for k in range(1, PLANE):

        @pl.when(own + k < PLANE)
        def _():
            signal(barrier, t + k, x)

    for k in range(1, PLANES):

        @pl.when(z + k < PLANES)
        def _():
            signal(barrier, t + k * PLANE, x)

    @pl.when((y == 3) & (z < PLANES - 1))
    def _():
        signal(barrier, (z + 1) * PLANE, x)
        signal(barrier, (z + 1) * PLANE + 1, x)

    copies = {}

    def local(name, source, target):
        copies[name] = pltpu.make_async_copy(source, target, local_sem.at[len(copies)])
        copies[name].start()

    local("tok", tok, g.at[0])
    owners = [x, left, right, lax.rem(x + 2, 4)]
    for slot in range(4):
        rows = pl.ds(pl.multiple_of(owners[slot] * WIDTH, WIDTH), WIDTH)
        local(("v", slot), w_value.at[rows], w.at[slot, :, pl.ds(0, WIDTH)])
        local(("g", slot), w_gate.at[rows], w.at[slot, :, pl.ds(WIDTH, WIDTH)])
    for name, source, target in (
        ("gain", gain, gain_v),
        ("phi", phi, phi_v),
        ("coeff", coeff, coeff_v),
        ("fwd", fwd, fwd_f),
        ("skip", skip, skip_v),
        ("up", up, up_v),
        ("down", down, down_v),
        ("lift", lift, lift_v),
        ("spread", spread, spread_v),
        ("inv", inv, inv_f),
        ("coup", coup, coup_v),
    ):
        local(name, source, target)

    pl.semaphore_wait(barrier, 2 + own + z + jnp.where((y == 0) & (z > 0), 2, 0))

    def leaf_rows(leaf):
        return pl.ds(leaf * LEAF if isinstance(leaf, int) else pl.multiple_of(leaf * LEAF, LEAF), LEAF)

    def direct(leaf, way):
        rows = leaf_rows(leaf)
        return pltpu.make_async_remote_copy(
            src_ref=tok.at[rows],
            dst_ref=g.at[1 + way, rows],
            send_sem=dsend.at[way, leaf],
            recv_sem=drecv.at[way, leaf],
            device_id=(t, left if way else right),
            device_id_type=MESH,
        )

    def relay(leaf, way):
        start = leaf * LEAF + way * (LEAF // 2)
        rows = pl.ds(start if isinstance(leaf, int) else pl.multiple_of(start, LEAF // 2), LEAF // 2)
        return pltpu.make_async_remote_copy(
            src_ref=g.at[1 + way, rows],
            dst_ref=g.at[3, rows],
            send_sem=rsend.at[way, leaf],
            recv_sem=rrecv.at[way, leaf],
            device_id=(t, left if way else right),
            device_id_type=MESH,
        )

    def send_direct(place):
        for way in range(2):
            direct(3 - place, way).start()

    def pass_on(place):
        for way in range(2):
            direct(3 - place, way).wait_recv()
            relay(3 - place, way).start()

    def wait_relayed(place):
        for way in range(2):
            relay(3 - place, way).wait_recv()

    def tables_near():
        for name in ("phi", "coeff", "fwd"):
            copies[name].wait()
        fwd_v[...] = jnp.concatenate(halves(fwd_f[...]), 1)
        taps = phi_v[...].astype(BF16).astype(F32)
        kernel_taps = lax.dot_general(
            taps, coeff_v[...], (((0,), (0,)), ((), ())), precision=HIGHEST, preferred_element_type=F32
        )
        both = jnp.concatenate([kernel_taps[:LEAF], kernel_taps[LEAF:]], 1)
        high, low = halves(both)
        hat = dot(fwd_v[...], jnp.concatenate([high, high], 0)) + dot(fwd_v[:, :LEAF], low)
        a_re, a_im = hat[:LEAF, :WIDTH], hat[LEAF:, :WIDTH]
        b_re, b_im = hat[:LEAF, WIDTH:], hat[LEAF:, WIDTH:]
        row = lax.broadcasted_iota(jnp.int32, (LEAF, WIDTH), 0)
        sign = (1 - 2 * lax.rem(row, 2)).astype(F32)
        khat[0] = a_re
        khat[1] = a_im
        khat[2] = b_re - sign * a_im
        khat[3] = b_im + sign * a_re

    def tables_moments():
        copies["up"].wait()
        copies["lift"].wait()
        base = up_v[...]
        first = [exact_dot(lift_v[0, k], base) for k in range(2)]
        for leaf in range(LEAVES):
            second = exact_dot(lift_v[1, leaf // 2], first[leaf % 2])
            high, low = halves(jnp.concatenate([base, first[leaf % 2], second], 0))
            mom_m[leaf] = jnp.concatenate([high, low], 1)

    def tables_lift():
        def pair(level):
            return exact_dot(lift_v[level, 0], selector(128, 32, 0, 128)) + exact_dot(
                lift_v[level, 1], selector(128, 32, 16, 128)
            )

        def blocks(level, copies_of):
            rows = jnp.concatenate([pair(level)] * copies_of, 0)
            row = lax.broadcasted_iota(jnp.int32, rows.shape, 0)
            lane = lax.broadcasted_iota(jnp.int32, rows.shape, 1)
            return jnp.where(lax.div(row, RANK) == lax.div(lane, 2 * RANK), rows, 0.0)

        three = blocks(2, 8)
        four = exact_dot(blocks(3, 2), three)
        five = exact_dot(blocks(4, 1), jnp.concatenate([four, jnp.zeros((96, 128), F32)], 0))
        whole = jnp.concatenate([four, three[32:64], five, three[:32]], 0)
        high, low = halves(whole)
        lift_m[...] = jnp.concatenate([high, low], 1)
        six = exact_dot(lift_v[5, 0], selector(128, 32, 0, 64)) + exact_dot(
            lift_v[5, 1], selector(128, 32, 16, 64)
        )
        high = six.astype(BF16).astype(F32)
        lane = lax.broadcasted_iota(jnp.int32, six.shape, 1)
        six_m[...] = jnp.where(lane < 32, high, six - high).astype(BF16)

    def tables_far():
        copies["spread"].wait()
        copies["down"].wait()
        row = lax.broadcasted_iota(jnp.int32, (RANK, LEAF), 0)
        lane = lax.broadcasted_iota(jnp.int32, (RANK, LEAF), 1)
        summing = (lax.div(lane, RANK) == row).astype(F32)
        chain = None
        for k in range(5):
            if k > 0:
                step = spread_v[1 + k, lax.rem(lax.div(t, 2 ** (k - 1)), 2)]
                chain = step if k == 1 else exact_dot(chain, step)
            high, low = halves(summing if k == 0 else exact_dot(chain, summing))
            red_m[k] = jnp.concatenate([high, low], 0)
        for leaf in range(LEAVES):
            near_step = spread_v[0, leaf % 2]
            both_steps = exact_dot(near_step, spread_v[1, leaf // 2])
            mix = (
                selector(LEAF, 48, 0, 144)
                + exact_dot(near_step, selector(LEAF, 48, 16, 144))
                + exact_dot(both_steps, selector(LEAF, 48, 32, 144))
            )
            whole = lax.dot_general(
                down_v[...], mix, (((0,), (0,)), ((), ())), precision=HIGHEST, preferred_element_type=F32
            )
            high = whole.astype(BF16).astype(F32)
            lane_at = lax.broadcasted_iota(jnp.int32, whole.shape, 1)
            far_m[leaf] = jnp.where(lane_at < 96, high, whole - high).astype(BF16)

    def scaled_rows(leaf):
        rows = leaf_rows(leaf)
        squares = jnp.zeros((LEAF, WIDTH), F32)
        parts = []
        for slot in range(4):
            tokens = g[slot, rows, :].astype(F32)
            squares = squares + tokens * tokens
            scale = gain_v[:, pl.ds(pl.multiple_of(owners[slot] * WIDTH, WIDTH), WIDTH)]
            parts.append((tokens * scale).astype(BF16))
        inverse = lax.rsqrt(jnp.sum(squares, axis=1, keepdims=True) / 1024 + 1e-06)
        return jnp.concatenate(parts, 1), inverse

    def weights(which):
        return w[:, :, which * WIDTH : (which + 1) * WIDTH].reshape(4 * WIDTH, WIDTH)

    def values_of(leaf, scaled, inverse):
        value = (dot(scaled, weights(0)) * inverse).astype(BF16)
        vals[leaf_rows(leaf), :] = value
        twice = jnp.concatenate([value, value], 0)
        moms[leaf] = dot(mom_m[leaf], twice)
        return twice

    def gates_of(leaf, scaled, inverse):
        gate[leaf_rows(leaf), :] = jax.nn.sigmoid(dot(scaled, weights(1)) * inverse)

    def project(leaf):
        scaled, inverse = scaled_rows(leaf)
        twice = values_of(leaf, scaled, inverse)
        gates_of(leaf, scaled, inverse)
        spec[leaf] = dot(fwd_v[...], twice)

    def near_rows(leaf):
        rows = leaf_rows(leaf)
        before = (leaf - 1 if leaf > 0 else LEAVES) if isinstance(leaf, int) else leaf - 1
        a_re, a_im = spec[leaf, :LEAF, :], spec[leaf, LEAF:, :]
        b_re, b_im = spec[before, :LEAF, :], spec[before, LEAF:, :]
        out_re = khat[0] * a_re - khat[1] * a_im + khat[2] * b_re - khat[3] * b_im
        out_im = khat[0] * a_im + khat[1] * a_re + khat[2] * b_im + khat[3] * b_re
        high, low = halves(jnp.concatenate([out_re, out_im], 0))
        total = dot(inv_v[...], jnp.concatenate([high, high], 0)) + dot(inv_v[:, : 2 * LEAF], low)
        near[rows, :] = total + skip_v[...] * vals[rows, :].astype(F32)

    def coupled(level, source_two, source_three):
        product = coup_v[level, 0] * source_two[None]
        if source_three is not None:
            product = product + coup_v[level, 1] * source_three[None]
        return product.reshape(RANK * RANK, WIDTH).astype(BF16)

    send_direct(0)
    send_direct(1)

    for k in range(1, PLANE):

        @pl.when(own >= k)
        def _():
            signal(ready_plane, t - k, x)

    @pl.when((y == 0) & (z > 0))
    def _():
        signal(ready_plane, (z - 1) * PLANE + 6, x)
        signal(ready_plane, (z - 1) * PLANE + 7, x)

    for k in range(1, PLANES):

        @pl.when(z >= k)
        def _():
            signal(ready_later, t - k * PLANE, x)

    tables_near()
    pass_on(0)
    send_direct(2)
    tables_moments()
    tables_lift()
    pass_on(1)
    send_direct(3)
    tables_far()
    copies["inv"].wait()
    inv_v[...] = jnp.concatenate(halves(inv_f[...]), 1)
    for slot in range(4):
        copies["v", slot].wait()
        copies["g", slot].wait()
    for name in ("tok", "gain", "skip", "coup"):
        copies[name].wait()

    answers = 7 - own + jnp.where((y == 3) & (z < PLANES - 1), 2, 0)

    @pl.when(answers > 0)
    def _():
        pl.semaphore_wait(ready_plane, answers)

    halo_copy = pltpu.make_async_remote_copy(
        src_ref=vals.at[pl.ds(3 * LEAF, LEAF)],
        dst_ref=halo,
        send_sem=hsem.at[0],
        recv_sem=hsem.at[1],
        device_id=(t + 1, x),
        device_id_type=MESH,
    )

    def step(i, carry):
        wait_relayed(i)
        project(3 - i)

        @pl.when((i == 0) & (t < PLANES * PLANE - 1))
        def _():
            halo_copy.start()

        @pl.when(i < 2)
        def _():
            pass_on(i + 2)

        @pl.when(i > 0)
        def _():
            near_rows(4 - i)

        return carry

    lax.fori_loop(0, 3, step, 0)

    wait_relayed(3)
    scaled, inverse = scaled_rows(0)
    twice = values_of(0, scaled, inverse)

    total = moms[0, 32:48, :] + moms[1, 32:48, :] + moms[2, 32:48, :] + moms[3, 32:48, :]
    m2[own] = total.astype(BF16)

    def plane_copy(k):
        return pltpu.make_async_remote_copy(
            src_ref=m2.at[own],
            dst_ref=m2.at[own],
            send_sem=s1.at[k - 1],
            recv_sem=r1.at[k - 1],
            device_id=(z * PLANE + lax.rem(own + k, PLANE), x),
            device_id_type=MESH,
        )

    def plane_arrival(k):
        return pltpu.make_async_remote_copy(
            src_ref=m2.at[own],
            dst_ref=m2.at[lax.rem(own + PLANE - k, PLANE)],
            send_sem=s1.at[k - 1],
            recv_sem=r1.at[k - 1],
            device_id=(z * PLANE + lax.rem(own + k, PLANE), x),
            device_id_type=MESH,
        )

    for k in range(1, PLANE):
        plane_copy(k).start()

    def next_plane_copy(target, source):
        return pltpu.make_async_remote_copy(
            src_ref=m2.at[own],
            dst_ref=m2_prev.at[source],
            send_sem=s1p.at[target],
            recv_sem=r1p.at[source],
            device_id=((z + 1) * PLANE + target, x),
            device_id_type=MESH,
        )

    @pl.when((y == 3) & (z < PLANES - 1))
    def _():
        for target in range(2):
            next_plane_copy(target, core).start()

    ctx_out[...] = jnp.concatenate(
        [
            moms[2, 0:16, :],
            moms[3, 0:16, :],
            moms[0, 16:32, :] + moms[1, 16:32, :],
            moms[2, 16:32, :] + moms[3, 16:32, :],
        ],
        0,
    ).astype(BF16)
    ctx_copy = pltpu.make_async_remote_copy(
        src_ref=ctx_out,
        dst_ref=ctx_in,
        send_sem=csem.at[0],
        recv_sem=csem.at[1],
        device_id=(t + 1, x),
        device_id_type=MESH,
    )

    @pl.when(t < PLANES * PLANE - 1)
    def _():
        ctx_copy.start()

    gates_of(0, scaled, inverse)
    spec[0] = dot(fwd_v[...], twice)
    near_rows(1)

    for k in range(1, PLANE):
        plane_arrival(k).wait_recv()
    stack = m2[...].reshape(PLANE * RANK, WIDTH)
    lifted = dot(lift_m[...], jnp.concatenate([stack, stack], 0))
    pack_out[...] = lifted[:80].astype(BF16)

    @pl.when(z < PLANES - 1)
    def _():
        pl.semaphore_wait(ready_later, 7 - z)

    def pack_copy(rows):
        return pltpu.make_async_remote_copy(
            src_ref=pack_out.at[pl.ds(0, rows)],
            dst_ref=pack_in.at[pl.ds(0, rows)],
            send_sem=s2,
            recv_sem=r2,
            device_id=(t + PLANE, x),
            device_id_type=MESH,
        )

    def five_copy(k):
        return pltpu.make_async_remote_copy(
            src_ref=pack_out.at[pl.ds(64, RANK)],
            dst_ref=m5_in.at[k],
            send_sem=s5.at[k],
            recv_sem=r5.at[k],
            device_id=(t + k * PLANE, x),
            device_id_type=MESH,
        )

    @pl.when((z < PLANES - 1) & (y < 2))
    def _():
        pack_copy(64).start()

    @pl.when((z < PLANES - 1) & (y >= 2))
    def _():
        pack_copy(32).start()

    for k in range(2, PLANES):

        @pl.when(z + k < PLANES)
        def _():
            five_copy(k).start()

    @pl.when(t > 0)
    def _():
        halo_copy.wait_recv()

    before = halo[...]
    spec[LEAVES] = dot(fwd_v[...], jnp.concatenate([before, before], 0))
    near_rows(0)

    summing = red_m[0, :RANK, :]

    def gathered(level, source_two, source_three=None):
        return dot(summing, coupled(level, source_two, source_three))

    @pl.when(t > 0)
    def _():
        ctx_copy.wait_recv()

    prev = ctx_in[...].astype(F32)
    own0 = [moms[leaf, 0:16, :] for leaf in range(2)]
    far0[0] = gathered(0, prev[0:16])
    far0[1] = gathered(0, prev[16:32], prev[0:16])
    far0[2] = gathered(0, own0[0])
    far0[3] = gathered(0, own0[1], own0[0])
    far1[0] = gathered(1, prev[32:48])
    far1[1] = gathered(1, prev[48:64], prev[32:48])

    @pl.when((y == 0) & (z > 0))
    def _():
        for source in range(2):
            next_plane_copy(source, source).wait_recv()

    def reduced(k, source_two, source_three):
        return dot(red_m[k], coupled(2 + k, source_two, source_three))

    at = 2 * jnp.maximum(y - 1, 0)
    inside = y > 0
    two = jnp.where(inside, m2[at + core], m2_prev[core]).astype(F32)
    three = jnp.where(inside, m2[at], m2_prev[0]).astype(F32) * core.astype(F32)
    expansion = reduced(0, two, three)

    @pl.when((z > 0) & (y < 2))
    def _():
        pack_copy(64).wait_recv()

    @pl.when((z > 0) & (y >= 2))
    def _():
        pack_copy(32).wait_recv()

    odd = lax.rem(y, 2)
    lower = y < 2
    here = jnp.where(odd == 1, lifted[96:112], lifted[80:96])
    coming = pack_in[pl.ds(pl.multiple_of(32 + odd * RANK, RANK), RANK), :].astype(F32)
    two = jnp.where(lower, coming, here)
    three = jnp.where(lower, pack_in[32:48, :].astype(F32), lifted[80:96]) * odd.astype(F32)
    expansion = expansion + reduced(1, two, three)
    odd = lax.div(y, 2)
    two = pack_in[pl.ds(pl.multiple_of(odd * RANK, RANK), RANK), :].astype(F32)
    three = pack_in[0:16, :].astype(F32) * odd.astype(F32)
    expansion = expansion + reduced(2, two, three)

    for k in range(2, PLANES):

        @pl.when(z >= k)
        def _():
            five_copy(k).wait_recv()

    odd = lax.rem(z, 2)
    expansion = expansion + reduced(
        3, m5_in[2].astype(F32), m5_in[3].astype(F32) * odd.astype(F32)
    )
    pad = jnp.zeros((64, WIDTH), BF16)

    def sixth(base):
        pair = [m5_in[base], m5_in[base - 1]]
        return dot(six_m[...], jnp.concatenate(pair + pair + [pad], 0))

    odd_six = lax.rem(lax.div(z, 2), 2)
    expansion = expansion + reduced(
        4, sixth(4 + odd), sixth(6 + odd) * odd_six.astype(F32)
    )

    expansion = expansion[:RANK] + expansion[RANK:]

    def finish(leaf, carry):
        rows = leaf_rows(leaf)
        high, low = halves(jnp.concatenate([far0[leaf], far1[lax.div(leaf, 2)], expansion], 0))
        whole = jnp.concatenate([high, low, high, jnp.zeros((112, WIDTH), BF16)], 0)
        combined = near[rows, :] + dot(far_m[leaf], whole)
        out[rows, :] = (gate[rows, :] * combined).astype(BF16)
        return carry

    lax.fori_loop(0, LEAVES, finish, 0)

    for way in range(2):
        for leaf in range(LEAVES):
            direct(leaf, way).wait_send()
            relay(leaf, way).wait_send()
    for k in range(1, PLANE):
        plane_copy(k).wait_send()

    @pl.when((y == 3) & (z < PLANES - 1))
    def _():
        for target in range(2):
            next_plane_copy(target, core).wait_send()

    @pl.when(t < PLANES * PLANE - 1)
    def _():
        halo_copy.wait_send()
        ctx_copy.wait_send()

    @pl.when((z < PLANES - 1) & (y < 2))
    def _():
        pack_copy(64).wait_send()

    @pl.when((z < PLANES - 1) & (y >= 2))
    def _():
        pack_copy(32).wait_send()

    for k in range(2, PLANES):

        @pl.when(z + k < PLANES)
        def _():
            five_copy(k).wait_send()


def per_device(
    tokens,
    norm_gain,
    w_value,
    w_gate,
    phi_taps,
    tap_coeff,
    skip_gain,
    basis_up,
    basis_down,
    lift_maps,
    spread_maps,
    couplings,
):
    forward, inverse = transform_tables()
    in_hbm = pl.BlockSpec(memory_space=pltpu.HBM)
    frames = LEAF * LEAVES
    vmem = pltpu.VMEM
    dma = pltpu.SemaphoreType.DMA
    scratch = [
        vmem((4, frames, WIDTH), BF16),
        vmem((4, WIDTH, 2 * WIDTH), BF16),
        vmem((1, 4 * WIDTH), F32),
        vmem(phi_taps.shape, F32),
        vmem(tap_coeff.shape, F32),
        vmem((1, WIDTH), F32),
        vmem(basis_up.shape, F32),
        vmem(basis_down.shape, F32),
        vmem(lift_maps.shape, F32),
        vmem(spread_maps.shape, F32),
        vmem(couplings.shape, F32),
        vmem(forward.shape, F32),
        vmem(inverse.shape, F32),
        vmem((2 * LEAF, 2 * LEAF), BF16),
        vmem((LEAF, 4 * LEAF), BF16),
        vmem((frames, WIDTH), BF16),
        vmem((LEAF, WIDTH), BF16),
        vmem((frames, WIDTH), F32),
        vmem((frames, WIDTH), F32),
        vmem((LEAVES + 1, 2 * LEAF, WIDTH), F32),
        vmem((4, LEAF, WIDTH), F32),
        vmem((LEAVES, 48, 2 * LEAF), BF16),
        vmem((112, 256), BF16),
        vmem((RANK, 128), BF16),
        vmem((LEAVES, LEAF, LEAF), BF16),
        vmem((5, 2 * RANK, LEAF), BF16),
        vmem((LEAVES, 48, WIDTH), F32),
        vmem((PLANE, RANK, WIDTH), BF16),
        vmem((2, RANK, WIDTH), BF16),
        vmem((64, WIDTH), BF16),
        vmem((64, WIDTH), BF16),
        vmem((80, WIDTH), BF16),
        vmem((64, WIDTH), BF16),
        vmem((PLANES, RANK, WIDTH), BF16),
        vmem((LEAVES, RANK, WIDTH), F32),
        vmem((2, RANK, WIDTH), F32),
        dma((20,)),
        dma((2, LEAVES)),
        dma((2, LEAVES)),
        dma((2, LEAVES)),
        dma((2, LEAVES)),
        dma((2,)),
        dma((2,)),
        dma((PLANE - 1,)),
        dma((PLANE - 1,)),
        dma((2,)),
        dma((2,)),
        dma(()),
        dma(()),
        dma((PLANES,)),
        dma((PLANES,)),
        pltpu.SemaphoreType.REGULAR,
        pltpu.SemaphoreType.REGULAR,
    ]
    return pl.pallas_call(
        body,
        out_shape=jax.ShapeDtypeStruct(tokens.shape, BF16),
        in_specs=[in_hbm] * 14,
        out_specs=pl.BlockSpec(memory_space=pltpu.VMEM),
        scratch_shapes=scratch,
        compiler_params=pltpu.CompilerParams(
            collective_id=0, has_side_effects=True, vmem_limit_bytes=60 * 1024 * 1024
        ),
        cost_estimate=pl.CostEstimate(flops=4 * 10**9, bytes_accessed=8 * 10**6, transcendentals=10**6),
    )(
        tokens,
        norm_gain.reshape(1, -1),
        w_value,
        w_gate,
        phi_taps,
        tap_coeff,
        skip_gain.reshape(1, -1),
        basis_up,
        basis_down,
        lift_maps,
        spread_maps,
        couplings,
        jnp.asarray(forward),
        jnp.asarray(inverse),
    )


def solution(mesh):
    placed = (
        P("tm", "chan"),
        P(),
        P(None, "chan"),
        P(None, "chan"),
        P(),
        P(None, "chan"),
        P("chan"),
        P(),
        P(),
        P(),
        P(),
        P(None, None, None, None, "chan"),
    )
    return jax.shard_map(
        per_device, mesh=mesh, in_specs=placed, out_specs=P("tm", "chan"), check_vma=False
    )
```

```python
import jax
import jax.numpy as jnp
import numpy as np
from jax import lax
from jax.experimental import pallas as pl
from jax.experimental.pallas import tpu as pltpu
from jax.sharding import PartitionSpec as P

MESH = pl.DeviceIdType.MESH
F32 = jnp.float32
BF16 = jnp.bfloat16
HIGHEST = lax.Precision.HIGHEST

LEAF = 256
LEAVES = 4
WIDTH = 256
RANK = 16
PLANES = 8
PLANE = 8


def transform_tables():
    odd = np.arange(LEAF)[:, None] + 0.5
    angle = 2 * np.pi * odd * np.arange(LEAF)[None, :] / (2 * LEAF)
    forward = np.concatenate([np.cos(angle), -np.sin(angle)], 0)
    return forward.astype(np.float32), (forward.T / LEAF).astype(np.float32)


def exact_dot(left, right):
    return jnp.dot(left, right, precision=HIGHEST, preferred_element_type=F32)


def dot(left, right):
    return jnp.dot(left, right, preferred_element_type=F32)


def halves(value):
    high = value.astype(BF16)
    return high, (value - high.astype(F32)).astype(BF16)


def selector(lanes, period, shift, limit):
    row = lax.broadcasted_iota(jnp.int32, (RANK, lanes), 0)
    lane = lax.broadcasted_iota(jnp.int32, (RANK, lanes), 1)
    return ((lax.rem(lane, period) == row + shift) & (lane < limit)).astype(F32)


def body(
    tok, gain, w_value, w_gate, phi, coeff, skip, up, down, lift, spread, coup, fwd, inv,
    out,
    g, w, gain_v, phi_v, coeff_v, skip_v, up_v, down_v, lift_v, spread_v, coup_v, fwd_f, inv_f, fwd_v, inv_v,
    vals, halo, gate, near, spec, khat, mom_m, lift_m, six_m, far_m, red_m, moms,
    m2, m2_prev, ctx_out, ctx_in, pack_out, pack_in, m5_in, far0, far1, out_v,
    local_sem, dsend, drecv, rsend, rrecv, hsem, csem, s1, r1, s1p, r1p, s2, r2, s5, r5, ready_plane, ready_later, osem,
):
    t = lax.axis_index("tm")
    x = lax.axis_index("chan")
    core = lax.rem(t, 2)
    y = lax.rem(lax.div(t, 2), 4)
    z = lax.div(t, PLANE)
    own = lax.rem(t, PLANE)
    right, left = lax.rem(x + 1, 4), lax.rem(x + 3, 4)

    barrier = pltpu.get_barrier_semaphore()

    def signal(semaphore, frames, chans):
        pl.semaphore_signal(semaphore, inc=1, device_id=(frames, chans), device_id_type=MESH)

    signal(barrier, t, right)
    signal(barrier, t, left)

    m2_prev[...] = jnp.zeros_like(m2_prev)
    ctx_in[...] = jnp.zeros_like(ctx_in)
    pack_in[...] = jnp.zeros_like(pack_in)
    m5_in[...] = jnp.zeros_like(m5_in)
    halo[...] = jnp.zeros_like(halo)
    for k in range(1, PLANE):

        @pl.when(own + k < PLANE)
        def _():
            signal(barrier, t + k, x)

    for k in range(1, PLANES):

        @pl.when(z + k < PLANES)
        def _():
            signal(barrier, t + k * PLANE, x)

    @pl.when((y == 3) & (z < PLANES - 1))
    def _():
        signal(barrier, (z + 1) * PLANE, x)
        signal(barrier, (z + 1) * PLANE + 1, x)

    pl.semaphore_wait(barrier, 2 + own + z + jnp.where((y == 0) & (z > 0), 2, 0))

    owners = [x, left, right, lax.rem(x + 2, 4)]

    def leaf_at(place):
        return (place + 3) % LEAVES if isinstance(place, int) else lax.rem(place + 3, LEAVES)

    def leaf_rows(leaf):
        return pl.ds(leaf * LEAF if isinstance(leaf, int) else pl.multiple_of(leaf * LEAF, LEAF), LEAF)

    def direct(leaf, way):
        rows = leaf_rows(leaf)
        return pltpu.make_async_remote_copy(
            src_ref=tok.at[rows],
            dst_ref=g.at[1 + way, rows],
            send_sem=dsend.at[way, leaf],
            recv_sem=drecv.at[way, leaf],
            device_id=(t, left if way else right),
            device_id_type=MESH,
        )

    def relay(leaf, way):
        start = leaf * LEAF + way * (LEAF // 2)
        rows = pl.ds(start if isinstance(leaf, int) else pl.multiple_of(start, LEAF // 2), LEAF // 2)
        return pltpu.make_async_remote_copy(
            src_ref=g.at[1 + way, rows],
            dst_ref=g.at[3, rows],
            send_sem=rsend.at[way, leaf],
            recv_sem=rrecv.at[way, leaf],
            device_id=(t, left if way else right),
            device_id_type=MESH,
        )

    def send_direct(place):
        for way in range(2):
            direct(leaf_at(place), way).start()

    def pass_on(place):
        for way in range(2):
            direct(leaf_at(place), way).wait_recv()
            relay(leaf_at(place), way).start()

    def wait_relayed(place):
        for way in range(2):
            relay(leaf_at(place), way).wait_recv()

    def tables_near():
        for name in ("phi", "coeff", "fwd"):
            copies[name].wait()
        fwd_v[...] = jnp.concatenate(halves(fwd_f[...]), 1)
        taps = phi_v[...].astype(BF16).astype(F32)
        kernel_taps = lax.dot_general(
            taps, coeff_v[...], (((0,), (0,)), ((), ())), precision=HIGHEST, preferred_element_type=F32
        )
        both = jnp.concatenate([kernel_taps[:LEAF], kernel_taps[LEAF:]], 1)
        high, low = halves(both)
        hat = dot(fwd_v[...], jnp.concatenate([high, high], 0)) + dot(fwd_v[:, :LEAF], low)
        a_re, a_im = hat[:LEAF, :WIDTH], hat[LEAF:, :WIDTH]
        b_re, b_im = hat[:LEAF, WIDTH:], hat[LEAF:, WIDTH:]
        row = lax.broadcasted_iota(jnp.int32, (LEAF, WIDTH), 0)
        sign = (1 - 2 * lax.rem(row, 2)).astype(F32)
        khat[0] = a_re
        khat[1] = a_im
        khat[2] = b_re - sign * a_im
        khat[3] = b_im + sign * a_re

    def tables_moments():
        copies["up"].wait()
        copies["lift"].wait()
        base = up_v[...]
        first = [exact_dot(lift_v[0, k], base) for k in range(2)]
        for leaf in range(LEAVES):
            second = exact_dot(lift_v[1, leaf // 2], first[leaf % 2])
            high, low = halves(jnp.concatenate([base, first[leaf % 2], second], 0))
            mom_m[leaf] = jnp.concatenate([high, low], 1)

    def tables_lift():
        def pair(level):
            return exact_dot(lift_v[level, 0], selector(128, 32, 0, 128)) + exact_dot(
                lift_v[level, 1], selector(128, 32, 16, 128)
            )

        def blocks(level, copies_of):
            rows = jnp.concatenate([pair(level)] * copies_of, 0)
            row = lax.broadcasted_iota(jnp.int32, rows.shape, 0)
            lane = lax.broadcasted_iota(jnp.int32, rows.shape, 1)
            return jnp.where(lax.div(row, RANK) == lax.div(lane, 2 * RANK), rows, 0.0)

        three = blocks(2, 8)
        four = exact_dot(blocks(3, 2), three)
        five = exact_dot(blocks(4, 1), jnp.concatenate([four, jnp.zeros((96, 128), F32)], 0))
        whole = jnp.concatenate([four, three[32:64], five, three[:32]], 0)
        high, low = halves(whole)
        lift_m[...] = jnp.concatenate([high, low], 1)
        six = exact_dot(lift_v[5, 0], selector(128, 32, 0, 64)) + exact_dot(
            lift_v[5, 1], selector(128, 32, 16, 64)
        )
        high = six.astype(BF16).astype(F32)
        lane = lax.broadcasted_iota(jnp.int32, six.shape, 1)
        six_m[...] = jnp.where(lane < 32, high, six - high).astype(BF16)

    def tables_far():
        copies["spread"].wait()
        copies["down"].wait()
        row = lax.broadcasted_iota(jnp.int32, (RANK, LEAF), 0)
        lane = lax.broadcasted_iota(jnp.int32, (RANK, LEAF), 1)
        summing = (lax.div(lane, RANK) == row).astype(F32)
        chain = None
        for k in range(5):
            if k > 0:
                step = spread_v[1 + k, lax.rem(lax.div(t, 2 ** (k - 1)), 2)]
                chain = step if k == 1 else exact_dot(chain, step)
            high, low = halves(summing if k == 0 else exact_dot(chain, summing))
            red_m[k] = jnp.concatenate([high, low], 0)
        for leaf in range(LEAVES):
            near_step = spread_v[0, leaf % 2]
            both_steps = exact_dot(near_step, spread_v[1, leaf // 2])
            mix = (
                selector(LEAF, 48, 0, 144)
                + exact_dot(near_step, selector(LEAF, 48, 16, 144))
                + exact_dot(both_steps, selector(LEAF, 48, 32, 144))
            )
            whole = lax.dot_general(
                down_v[...], mix, (((0,), (0,)), ((), ())), precision=HIGHEST, preferred_element_type=F32
            )
            high = whole.astype(BF16).astype(F32)
            lane_at = lax.broadcasted_iota(jnp.int32, whole.shape, 1)
            far_m[leaf] = jnp.where(lane_at < 96, high, whole - high).astype(BF16)

    def scaled_rows(leaf, slots):
        rows = leaf_rows(leaf)
        squares = jnp.zeros((LEAF, WIDTH), F32)
        parts = []
        for slot in slots:
            tokens = g[slot, rows, :].astype(F32)
            squares = squares + tokens * tokens
            scale = gain_v[:, pl.ds(pl.multiple_of(owners[slot] * WIDTH, WIDTH), WIDTH)]
            parts.append((tokens * scale).astype(BF16))
        return jnp.concatenate(parts, 1), squares

    def inverse_of(squares):
        return lax.rsqrt(jnp.sum(squares, axis=1, keepdims=True) / 1024 + 1e-06)

    def weights(which, slots):
        return w[:slots, :, which * WIDTH : (which + 1) * WIDTH].reshape(slots * WIDTH, WIDTH)

    def values_of(leaf, sums, inverse):
        value = (sums * inverse).astype(BF16)
        vals[leaf_rows(leaf), :] = value
        twice = jnp.concatenate([value, value], 0)
        moms[leaf] = dot(mom_m[leaf], twice)
        return twice

    def gates_of(leaf, sums, inverse):
        gate[leaf_rows(leaf), :] = jax.nn.sigmoid(sums * inverse)

    def project(leaf):
        scaled, squares = scaled_rows(leaf, range(4))
        inverse = inverse_of(squares)
        twice = values_of(leaf, dot(scaled, weights(0, 4)), inverse)
        gates_of(leaf, dot(scaled, weights(1, 4)), inverse)
        spec[leaf] = dot(fwd_v[...], twice)

    def near_rows(leaf):
        rows = leaf_rows(leaf)
        before = (leaf - 1 if leaf > 0 else LEAVES) if isinstance(leaf, int) else leaf - 1
        a_re, a_im = spec[leaf, :LEAF, :], spec[leaf, LEAF:, :]
        b_re, b_im = spec[before, :LEAF, :], spec[before, LEAF:, :]
        out_re = khat[0] * a_re - khat[1] * a_im + khat[2] * b_re - khat[3] * b_im
        out_im = khat[0] * a_im + khat[1] * a_re + khat[2] * b_im + khat[3] * b_re
        high, low = halves(jnp.concatenate([out_re, out_im], 0))
        total = dot(inv_v[...], jnp.concatenate([high, high], 0)) + dot(inv_v[:, : 2 * LEAF], low)
        near[rows, :] = total + skip_v[...] * vals[rows, :].astype(F32)

    def coupled(level, source_two, source_three):
        product = coup_v[level, 0] * source_two[None]
        if source_three is not None:
            product = product + coup_v[level, 1] * source_three[None]
        return product.reshape(RANK * RANK, WIDTH).astype(BF16)

    send_direct(0)
    send_direct(1)

    copies = {}

    def local(name, source, target):
        copies[name] = pltpu.make_async_copy(source, target, local_sem.at[len(copies)])
        copies[name].start()

    local("tok", tok, g.at[0])
    for slot in range(4):
        rows = pl.ds(pl.multiple_of(owners[slot] * WIDTH, WIDTH), WIDTH)
        local(("v", slot), w_value.at[rows], w.at[slot, :, pl.ds(0, WIDTH)])
        local(("g", slot), w_gate.at[rows], w.at[slot, :, pl.ds(WIDTH, WIDTH)])
    for name, source, target in (
        ("gain", gain, gain_v),
        ("phi", phi, phi_v),
        ("coeff", coeff, coeff_v),
        ("fwd", fwd, fwd_f),
        ("skip", skip, skip_v),
        ("up", up, up_v),
        ("down", down, down_v),
        ("lift", lift, lift_v),
        ("spread", spread, spread_v),
        ("inv", inv, inv_f),
        ("coup", coup, coup_v),
    ):
        local(name, source, target)

    for k in range(1, PLANE):

        @pl.when(own >= k)
        def _():
            signal(ready_plane, t - k, x)

    @pl.when((y == 0) & (z > 0))
    def _():
        signal(ready_plane, (z - 1) * PLANE + 6, x)
        signal(ready_plane, (z - 1) * PLANE + 7, x)

    for k in range(1, PLANES):

        @pl.when(z >= k)
        def _():
            signal(ready_later, t - k * PLANE, x)

    tables_near()
    pass_on(0)
    send_direct(2)
    tables_moments()
    tables_lift()
    pass_on(1)
    send_direct(3)
    tables_far()
    copies["inv"].wait()
    inv_v[...] = jnp.concatenate(halves(inv_f[...]), 1)
    for slot in range(4):
        copies["v", slot].wait()
        copies["g", slot].wait()
    for name in ("tok", "gain", "skip", "coup"):
        copies[name].wait()

    answers = 7 - own + jnp.where((y == 3) & (z < PLANES - 1), 2, 0)

    @pl.when(answers > 0)
    def _():
        pl.semaphore_wait(ready_plane, answers)

    halo_copy = pltpu.make_async_remote_copy(
        src_ref=vals.at[pl.ds(3 * LEAF, LEAF)],
        dst_ref=halo,
        send_sem=hsem.at[0],
        recv_sem=hsem.at[1],
        device_id=(t + 1, x),
        device_id_type=MESH,
    )

    def ctx_copy(part):
        return pltpu.make_async_remote_copy(
            src_ref=ctx_out.at[pl.ds(part * 32, 32)],
            dst_ref=ctx_in.at[pl.ds(part * 32, 32)],
            send_sem=csem.at[0, part],
            recv_sem=csem.at[1, part],
            device_id=(t + 1, x),
            device_id_type=MESH,
        )

    def step(i, carry):
        wait_relayed(i)
        project(leaf_at(i))

        @pl.when((i == 0) & (t < PLANES * PLANE - 1))
        def _():
            halo_copy.start()

        @pl.when(i < 2)
        def _():
            pass_on(i + 2)

        return carry

    lax.fori_loop(0, 3, step, 0)

    ctx_out[:32] = jnp.concatenate([moms[3, 0:16, :], moms[0, 16:32, :] + moms[1, 16:32, :]], 0).astype(BF16)

    @pl.when(t < PLANES * PLANE - 1)
    def _():
        ctx_copy(0).start()

    summing = red_m[0, :RANK, :]

    def gathered(level, source_two, source_three=None):
        return dot(summing, coupled(level, source_two, source_three))

    far0[2] = gathered(0, moms[0, 0:16, :])
    far0[3] = gathered(0, moms[1, 0:16, :], moms[0, 0:16, :])
    near_rows(1)

    @pl.when(t > 0)
    def _():
        halo_copy.wait_recv()

    before = halo[...]
    spec[LEAVES] = dot(fwd_v[...], jnp.concatenate([before, before], 0))
    near_rows(0)

    scaled, squares = scaled_rows(2, (0, 1, 2))
    first_value = dot(scaled, weights(0, 3))
    first_gate = dot(scaled, weights(1, 3))
    wait_relayed(3)
    scaled, more_squares = scaled_rows(2, (3,))
    inverse = inverse_of(squares + more_squares)
    twice = values_of(2, first_value + dot(scaled, w[3, :, :WIDTH]), inverse)

    total = moms[0, 32:48, :] + moms[1, 32:48, :] + moms[2, 32:48, :] + moms[3, 32:48, :]
    m2[own] = total.astype(BF16)

    def plane_copy(k):
        return pltpu.make_async_remote_copy(
            src_ref=m2.at[own],
            dst_ref=m2.at[own],
            send_sem=s1.at[k - 1],
            recv_sem=r1.at[k - 1],
            device_id=(z * PLANE + lax.rem(own + k, PLANE), x),
            device_id_type=MESH,
        )

    def plane_arrival(k):
        return pltpu.make_async_remote_copy(
            src_ref=m2.at[own],
            dst_ref=m2.at[lax.rem(own + PLANE - k, PLANE)],
            send_sem=s1.at[k - 1],
            recv_sem=r1.at[k - 1],
            device_id=(z * PLANE + lax.rem(own + k, PLANE), x),
            device_id_type=MESH,
        )

    for k in range(1, PLANE):
        plane_copy(k).start()

    def next_plane_copy(target, source):
        return pltpu.make_async_remote_copy(
            src_ref=m2.at[own],
            dst_ref=m2_prev.at[source],
            send_sem=s1p.at[target],
            recv_sem=r1p.at[source],
            device_id=((z + 1) * PLANE + target, x),
            device_id_type=MESH,
        )

    @pl.when((y == 3) & (z < PLANES - 1))
    def _():
        for target in range(2):
            next_plane_copy(target, core).start()

    ctx_out[32:] = jnp.concatenate([moms[2, 0:16, :], moms[2, 16:32, :] + moms[3, 16:32, :]], 0).astype(BF16)

    @pl.when(t < PLANES * PLANE - 1)
    def _():
        ctx_copy(1).start()

    gates_of(2, first_gate + dot(scaled, w[3, :, WIDTH:]), inverse)
    spec[2] = dot(fwd_v[...], twice)
    near_rows(2)

    @pl.when(t > 0)
    def _():
        ctx_copy(0).wait_recv()

    far1[0] = gathered(1, ctx_in[16:32, :].astype(F32))

    for way in range(2):
        for leaf in range(LEAVES):
            direct(leaf, way).wait_send()
            relay(leaf, way).wait_send()

    for k in range(1, PLANE):
        plane_arrival(k).wait_recv()
    stack = m2[...].reshape(PLANE * RANK, WIDTH)
    lifted = dot(lift_m[...], jnp.concatenate([stack, stack], 0))
    pack_out[...] = lifted[:80].astype(BF16)

    @pl.when(z < PLANES - 1)
    def _():
        pl.semaphore_wait(ready_later, 7 - z)

    def pack_copy(rows):
        return pltpu.make_async_remote_copy(
            src_ref=pack_out.at[pl.ds(0, rows)],
            dst_ref=pack_in.at[pl.ds(0, rows)],
            send_sem=s2,
            recv_sem=r2,
            device_id=(t + PLANE, x),
            device_id_type=MESH,
        )

    def five_copy(k):
        return pltpu.make_async_remote_copy(
            src_ref=pack_out.at[pl.ds(64, RANK)],
            dst_ref=m5_in.at[k],
            send_sem=s5.at[k],
            recv_sem=r5.at[k],
            device_id=(t + k * PLANE, x),
            device_id_type=MESH,
        )

    @pl.when((z < PLANES - 1) & (y < 2))
    def _():
        pack_copy(64).start()

    @pl.when((z < PLANES - 1) & (y >= 2))
    def _():
        pack_copy(32).start()

    for k in range(2, PLANES):

        @pl.when(z + k < PLANES)
        def _():
            five_copy(k).start()

    near_rows(3)

    @pl.when(t > 0)
    def _():
        ctx_copy(1).wait_recv()

    prev = ctx_in[...].astype(F32)
    far0[0] = gathered(0, prev[32:48])
    far0[1] = gathered(0, prev[0:16], prev[32:48])
    far1[1] = gathered(1, prev[48:64], prev[16:32])

    for k in range(1, PLANE):
        plane_copy(k).wait_send()

    @pl.when(t < PLANES * PLANE - 1)
    def _():
        halo_copy.wait_send()
        ctx_copy(0).wait_send()
        ctx_copy(1).wait_send()

    @pl.when((y == 3) & (z < PLANES - 1))
    def _():
        for target in range(2):
            next_plane_copy(target, core).wait_send()

    @pl.when((y == 0) & (z > 0))
    def _():
        for source in range(2):
            next_plane_copy(source, source).wait_recv()

    def reduced(k, source_two, source_three):
        return dot(red_m[k], coupled(2 + k, source_two, source_three))

    at = 2 * jnp.maximum(y - 1, 0)
    inside = y > 0
    two = jnp.where(inside, m2[at + core], m2_prev[core]).astype(F32)
    three = jnp.where(inside, m2[at], m2_prev[0]).astype(F32) * core.astype(F32)
    expansion = reduced(0, two, three)

    @pl.when((z > 0) & (y < 2))
    def _():
        pack_copy(64).wait_recv()

    @pl.when((z > 0) & (y >= 2))
    def _():
        pack_copy(32).wait_recv()

    odd = lax.rem(y, 2)
    lower = y < 2
    here = jnp.where(odd == 1, lifted[96:112], lifted[80:96])
    coming = pack_in[pl.ds(pl.multiple_of(32 + odd * RANK, RANK), RANK), :].astype(F32)
    two = jnp.where(lower, coming, here)
    three = jnp.where(lower, pack_in[32:48, :].astype(F32), lifted[80:96]) * odd.astype(F32)
    expansion = expansion + reduced(1, two, three)
    odd = lax.div(y, 2)
    two = pack_in[pl.ds(pl.multiple_of(odd * RANK, RANK), RANK), :].astype(F32)
    three = pack_in[0:16, :].astype(F32) * odd.astype(F32)
    expansion = expansion + reduced(2, two, three)

    for k in range(2, PLANES):

        @pl.when(z >= k)
        def _():
            five_copy(k).wait_recv()

    odd = lax.rem(z, 2)
    expansion = expansion + reduced(
        3, m5_in[2].astype(F32), m5_in[3].astype(F32) * odd.astype(F32)
    )
    pad = jnp.zeros((64, WIDTH), BF16)

    def sixth(base):
        pair = [m5_in[base], m5_in[base - 1]]
        return dot(six_m[...], jnp.concatenate(pair + pair + [pad], 0))

    odd_six = lax.rem(lax.div(z, 2), 2)
    expansion = expansion + reduced(
        4, sixth(4 + odd), sixth(6 + odd) * odd_six.astype(F32)
    )

    expansion = expansion[:RANK] + expansion[RANK:]

    def out_copy(leaf):
        rows = leaf_rows(leaf)
        return pltpu.make_async_copy(out_v.at[rows], out.at[rows], osem.at[leaf])

    for leaf in range(LEAVES):
        rows = leaf_rows(leaf)
        high, low = halves(jnp.concatenate([far0[leaf], far1[leaf // 2], expansion], 0))
        whole = jnp.concatenate([high, low, high, jnp.zeros((112, WIDTH), BF16)], 0)
        combined = near[rows, :] + dot(far_m[leaf], whole)
        out_v[rows, :] = (gate[rows, :] * combined).astype(BF16)
        out_copy(leaf).start()

    @pl.when((z < PLANES - 1) & (y < 2))
    def _():
        pack_copy(64).wait_send()

    @pl.when((z < PLANES - 1) & (y >= 2))
    def _():
        pack_copy(32).wait_send()

    for k in range(2, PLANES):

        @pl.when(z + k < PLANES)
        def _():
            five_copy(k).wait_send()

    for leaf in range(LEAVES):
        out_copy(leaf).wait()


def hand_over(source, target, sems):
    copies = []
    for part in range(LEAVES):
        rows = pl.ds(part * LEAF, LEAF)
        copies.append(pltpu.make_async_copy(source.at[rows], target.at[rows], sems.at[part]))
        copies[part].start()
    for copy in copies:
        copy.wait()


def per_device(
    tokens,
    norm_gain,
    w_value,
    w_gate,
    phi_taps,
    tap_coeff,
    skip_gain,
    basis_up,
    basis_down,
    lift_maps,
    spread_maps,
    couplings,
):
    forward, inverse = transform_tables()
    in_hbm = pl.BlockSpec(memory_space=pltpu.HBM)
    frames = LEAF * LEAVES
    vmem = pltpu.VMEM
    dma = pltpu.SemaphoreType.DMA
    scratch = [
        vmem((4, frames, WIDTH), BF16),
        vmem((4, WIDTH, 2 * WIDTH), BF16),
        vmem((1, 4 * WIDTH), F32),
        vmem(phi_taps.shape, F32),
        vmem(tap_coeff.shape, F32),
        vmem((1, WIDTH), F32),
        vmem(basis_up.shape, F32),
        vmem(basis_down.shape, F32),
        vmem(lift_maps.shape, F32),
        vmem(spread_maps.shape, F32),
        vmem(couplings.shape, F32),
        vmem(forward.shape, F32),
        vmem(inverse.shape, F32),
        vmem((2 * LEAF, 2 * LEAF), BF16),
        vmem((LEAF, 4 * LEAF), BF16),
        vmem((frames, WIDTH), BF16),
        vmem((LEAF, WIDTH), BF16),
        vmem((frames, WIDTH), F32),
        vmem((frames, WIDTH), F32),
        vmem((LEAVES + 1, 2 * LEAF, WIDTH), F32),
        vmem((4, LEAF, WIDTH), F32),
        vmem((LEAVES, 48, 2 * LEAF), BF16),
        vmem((112, 256), BF16),
        vmem((RANK, 128), BF16),
        vmem((LEAVES, LEAF, LEAF), BF16),
        vmem((5, 2 * RANK, LEAF), BF16),
        vmem((LEAVES, 48, WIDTH), F32),
        vmem((PLANE, RANK, WIDTH), BF16),
        vmem((2, RANK, WIDTH), BF16),
        vmem((64, WIDTH), BF16),
        vmem((64, WIDTH), BF16),
        vmem((80, WIDTH), BF16),
        vmem((64, WIDTH), BF16),
        vmem((PLANES, RANK, WIDTH), BF16),
        vmem((LEAVES, RANK, WIDTH), F32),
        vmem((2, RANK, WIDTH), F32),
        vmem((frames, WIDTH), BF16),
        dma((20,)),
        dma((2, LEAVES)),
        dma((2, LEAVES)),
        dma((2, LEAVES)),
        dma((2, LEAVES)),
        dma((2,)),
        dma((2, 2)),
        dma((PLANE - 1,)),
        dma((PLANE - 1,)),
        dma((2,)),
        dma((2,)),
        dma(()),
        dma(()),
        dma((PLANES,)),
        dma((PLANES,)),
        pltpu.SemaphoreType.REGULAR,
        pltpu.SemaphoreType.REGULAR,
        dma((LEAVES,)),
    ]
    result = pl.pallas_call(
        body,
        out_shape=jax.ShapeDtypeStruct(tokens.shape, BF16),
        in_specs=[in_hbm] * 14,
        out_specs=in_hbm,
        scratch_shapes=scratch,
        compiler_params=pltpu.CompilerParams(
            collective_id=0, has_side_effects=True, vmem_limit_bytes=60 * 1024 * 1024
        ),
        cost_estimate=pl.CostEstimate(flops=4 * 10**9, bytes_accessed=8 * 10**6, transcendentals=10**6),
    )(
        tokens,
        norm_gain.reshape(1, -1),
        w_value,
        w_gate,
        phi_taps,
        tap_coeff,
        skip_gain.reshape(1, -1),
        basis_up,
        basis_down,
        lift_maps,
        spread_maps,
        couplings,
        jnp.asarray(forward),
        jnp.asarray(inverse),
    )
    return pl.pallas_call(
        hand_over,
        out_shape=jax.ShapeDtypeStruct(tokens.shape, BF16),
        in_specs=[in_hbm],
        out_specs=in_hbm,
        scratch_shapes=[dma((LEAVES,))],
        compiler_params=pltpu.CompilerParams(vmem_limit_bytes=60 * 1024 * 1024),
    )(result)


def solution(mesh):
    placed = (
        P("tm", "chan"),
        P(),
        P(None, "chan"),
        P(None, "chan"),
        P(),
        P(None, "chan"),
        P("chan"),
        P(),
        P(),
        P(),
        P(),
        P(None, None, None, None, "chan"),
    )
    return jax.shard_map(
        per_device, mesh=mesh, in_specs=placed, out_specs=P("tm", "chan"), check_vma=False
    )
```

```python
import jax
import jax.numpy as jnp
import numpy as np
from jax import lax
from jax.experimental import pallas as pl
from jax.experimental.pallas import tpu as pltpu
from jax.sharding import PartitionSpec as P

MESH = pl.DeviceIdType.MESH
F32 = jnp.float32
BF16 = jnp.bfloat16
HIGHEST = lax.Precision.HIGHEST

LEAF = 256
LEAVES = 4
WIDTH = 256
RANK = 16
PLANES = 8
PLANE = 8


def transform_tables():
    odd = np.arange(LEAF)[:, None] + 0.5
    angle = 2 * np.pi * odd * np.arange(LEAF)[None, :] / (2 * LEAF)
    forward = np.concatenate([np.cos(angle), -np.sin(angle)], 0)
    return forward.astype(np.float32), (forward.T / LEAF).astype(np.float32)


def exact_dot(left, right):
    return jnp.dot(left, right, precision=HIGHEST, preferred_element_type=F32)


def dot(left, right):
    return jnp.dot(left, right, preferred_element_type=F32)


def halves(value):
    high = value.astype(BF16)
    return high, (value - high.astype(F32)).astype(BF16)


def selector(lanes, period, shift, limit):
    row = lax.broadcasted_iota(jnp.int32, (RANK, lanes), 0)
    lane = lax.broadcasted_iota(jnp.int32, (RANK, lanes), 1)
    return ((lax.rem(lane, period) == row + shift) & (lane < limit)).astype(F32)


def body(
    tok, gain, w_value, w_gate, phi, coeff, skip, up, down, lift, spread, coup, fwd, inv,
    out,
    g, w, gain_v, phi_v, coeff_v, skip_v, up_v, down_v, lift_v, spread_v, coup_v, fwd_f, inv_f, fwd_v, inv_v,
    vals, halo, gate, near, spec, khat, mom_m, lift_m, six_m, far_m, red_m, moms,
    m2, m2_prev, ctx_out, ctx_in, pack_out, pack_in, m5_in, far0, far1, out_v,
    local_sem, dsend, drecv, rsend, rrecv, hsem, csem, s1, r1, s1p, r1p, s2, r2, s5, r5, ready_plane, ready_next, ready_edge, ready_later, osem,
):
    t = lax.axis_index("tm")
    x = lax.axis_index("chan")
    core = lax.rem(t, 2)
    y = lax.rem(lax.div(t, 2), 4)
    z = lax.div(t, PLANE)
    own = lax.rem(t, PLANE)
    right, left = lax.rem(x + 1, 4), lax.rem(x + 3, 4)

    barrier = pltpu.get_barrier_semaphore()

    def signal(semaphore, frames, chans):
        pl.semaphore_signal(semaphore, inc=1, device_id=(frames, chans), device_id_type=MESH)

    signal(barrier, t, right)
    signal(barrier, t, left)

    @pl.when(z < PLANES - 1)
    def _():
        signal(barrier, t + PLANE, x)

    for k in range(1, PLANE):

        @pl.when(own + k < PLANE)
        def _():
            signal(barrier, t + k, x)

    m2_prev[...] = jnp.zeros_like(m2_prev)
    ctx_in[...] = jnp.zeros_like(ctx_in)
    pack_in[...] = jnp.zeros_like(pack_in)
    m5_in[...] = jnp.zeros_like(m5_in)
    halo[...] = jnp.zeros_like(halo)

    pl.semaphore_wait(barrier, 2 + own + jnp.where(z > 0, 1, 0))

    owners = [x, left, right, lax.rem(x + 2, 4)]

    def leaf_at(place):
        return (place + 3) % LEAVES if isinstance(place, int) else lax.rem(place + 3, LEAVES)

    def leaf_rows(leaf):
        return pl.ds(leaf * LEAF if isinstance(leaf, int) else pl.multiple_of(leaf * LEAF, LEAF), LEAF)

    def direct(leaf, way):
        rows = leaf_rows(leaf)
        return pltpu.make_async_remote_copy(
            src_ref=tok.at[rows],
            dst_ref=g.at[1 + way, rows],
            send_sem=dsend.at[way, leaf],
            recv_sem=drecv.at[way, leaf],
            device_id=(t, left if way else right),
            device_id_type=MESH,
        )

    def relay(leaf, way):
        start = leaf * LEAF + way * (LEAF // 2)
        rows = pl.ds(start if isinstance(leaf, int) else pl.multiple_of(start, LEAF // 2), LEAF // 2)
        return pltpu.make_async_remote_copy(
            src_ref=g.at[1 + way, rows],
            dst_ref=g.at[3, rows],
            send_sem=rsend.at[way, leaf],
            recv_sem=rrecv.at[way, leaf],
            device_id=(t, left if way else right),
            device_id_type=MESH,
        )

    def send_direct(place):
        for way in range(2):
            direct(leaf_at(place), way).start()

    def pass_on(place):
        for way in range(2):
            direct(leaf_at(place), way).wait_recv()
            relay(leaf_at(place), way).start()

    def wait_relayed(place):
        for way in range(2):
            relay(leaf_at(place), way).wait_recv()

    def tables_near():
        for name in ("phi", "coeff", "fwd"):
            copies[name].wait()
        fwd_v[...] = jnp.concatenate(halves(fwd_f[...]), 1)
        taps = phi_v[...].astype(BF16).astype(F32)
        kernel_taps = lax.dot_general(
            taps, coeff_v[...], (((0,), (0,)), ((), ())), precision=HIGHEST, preferred_element_type=F32
        )
        both = jnp.concatenate([kernel_taps[:LEAF], kernel_taps[LEAF:]], 1)
        high, low = halves(both)
        hat = dot(fwd_v[...], jnp.concatenate([high, high], 0)) + dot(fwd_v[:, :LEAF], low)
        a_re, a_im = hat[:LEAF, :WIDTH], hat[LEAF:, :WIDTH]
        b_re, b_im = hat[:LEAF, WIDTH:], hat[LEAF:, WIDTH:]
        row = lax.broadcasted_iota(jnp.int32, (LEAF, WIDTH), 0)
        sign = (1 - 2 * lax.rem(row, 2)).astype(F32)
        khat[0] = a_re
        khat[1] = a_im
        khat[2] = b_re - sign * a_im
        khat[3] = b_im + sign * a_re

    def tables_moments():
        copies["up"].wait()
        copies["lift"].wait()
        base = up_v[...]
        first = [exact_dot(lift_v[0, k], base) for k in range(2)]
        for leaf in range(LEAVES):
            second = exact_dot(lift_v[1, leaf // 2], first[leaf % 2])
            high, low = halves(jnp.concatenate([base, first[leaf % 2], second], 0))
            mom_m[leaf] = jnp.concatenate([high, low], 1)

    def tables_lift():
        def pair(level):
            return exact_dot(lift_v[level, 0], selector(128, 32, 0, 128)) + exact_dot(
                lift_v[level, 1], selector(128, 32, 16, 128)
            )

        def blocks(level, copies_of):
            rows = jnp.concatenate([pair(level)] * copies_of, 0)
            row = lax.broadcasted_iota(jnp.int32, rows.shape, 0)
            lane = lax.broadcasted_iota(jnp.int32, rows.shape, 1)
            return jnp.where(lax.div(row, RANK) == lax.div(lane, 2 * RANK), rows, 0.0)

        three = blocks(2, 8)
        four = exact_dot(blocks(3, 2), three)
        five = exact_dot(blocks(4, 1), jnp.concatenate([four, jnp.zeros((96, 128), F32)], 0))
        whole = jnp.concatenate([four, three[32:64], five, three[:32]], 0)
        high, low = halves(whole)
        lift_m[...] = jnp.concatenate([high, low], 1)
        six = exact_dot(lift_v[5, 0], selector(128, 32, 0, 64)) + exact_dot(
            lift_v[5, 1], selector(128, 32, 16, 64)
        )
        high = six.astype(BF16).astype(F32)
        lane = lax.broadcasted_iota(jnp.int32, six.shape, 1)
        six_m[...] = jnp.where(lane < 32, high, six - high).astype(BF16)

    def tables_far():
        copies["spread"].wait()
        copies["down"].wait()
        row = lax.broadcasted_iota(jnp.int32, (RANK, LEAF), 0)
        lane = lax.broadcasted_iota(jnp.int32, (RANK, LEAF), 1)
        summing = (lax.div(lane, RANK) == row).astype(F32)
        chain = None
        for k in range(5):
            if k > 0:
                step = spread_v[1 + k, lax.rem(lax.div(t, 2 ** (k - 1)), 2)]
                chain = step if k == 1 else exact_dot(chain, step)
            high, low = halves(summing if k == 0 else exact_dot(chain, summing))
            red_m[k] = jnp.concatenate([high, low], 0)
        for leaf in range(LEAVES):
            near_step = spread_v[0, leaf % 2]
            both_steps = exact_dot(near_step, spread_v[1, leaf // 2])
            mix = (
                selector(LEAF, 48, 0, 144)
                + exact_dot(near_step, selector(LEAF, 48, 16, 144))
                + exact_dot(both_steps, selector(LEAF, 48, 32, 144))
            )
            whole = lax.dot_general(
                down_v[...], mix, (((0,), (0,)), ((), ())), precision=HIGHEST, preferred_element_type=F32
            )
            high = whole.astype(BF16).astype(F32)
            lane_at = lax.broadcasted_iota(jnp.int32, whole.shape, 1)
            far_m[leaf] = jnp.where(lane_at < 96, high, whole - high).astype(BF16)

    def scaled_rows(leaf, slots):
        rows = leaf_rows(leaf)
        squares = jnp.zeros((LEAF, WIDTH), F32)
        parts = []
        for slot in slots:
            tokens = g[slot, rows, :].astype(F32)
            squares = squares + tokens * tokens
            scale = gain_v[:, pl.ds(pl.multiple_of(owners[slot] * WIDTH, WIDTH), WIDTH)]
            parts.append((tokens * scale).astype(BF16))
        return jnp.concatenate(parts, 1), squares

    def inverse_of(squares):
        return lax.rsqrt(jnp.sum(squares, axis=1, keepdims=True) / 1024 + 1e-06)

    def weights(which, slots):
        return w[:slots, :, which * WIDTH : (which + 1) * WIDTH].reshape(slots * WIDTH, WIDTH)

    def values_of(leaf, sums, inverse):
        value = (sums * inverse).astype(BF16)
        vals[leaf_rows(leaf), :] = value
        twice = jnp.concatenate([value, value], 0)
        moms[leaf] = dot(mom_m[leaf], twice)
        return twice

    def gates_of(leaf, sums, inverse):
        gate[leaf_rows(leaf), :] = jax.nn.sigmoid(sums * inverse)

    def project(leaf):
        scaled, squares = scaled_rows(leaf, range(4))
        inverse = inverse_of(squares)
        twice = values_of(leaf, dot(scaled, weights(0, 4)), inverse)
        gates_of(leaf, dot(scaled, weights(1, 4)), inverse)
        spec[leaf] = dot(fwd_v[...], twice)

    def near_rows(leaf):
        rows = leaf_rows(leaf)
        before = (leaf - 1 if leaf > 0 else LEAVES) if isinstance(leaf, int) else leaf - 1
        a_re, a_im = spec[leaf, :LEAF, :], spec[leaf, LEAF:, :]
        b_re, b_im = spec[before, :LEAF, :], spec[before, LEAF:, :]
        out_re = khat[0] * a_re - khat[1] * a_im + khat[2] * b_re - khat[3] * b_im
        out_im = khat[0] * a_im + khat[1] * a_re + khat[2] * b_im + khat[3] * b_re
        high, low = halves(jnp.concatenate([out_re, out_im], 0))
        total = dot(inv_v[...], jnp.concatenate([high, high], 0)) + dot(inv_v[:, : 2 * LEAF], low)
        near[rows, :] = total + skip_v[...] * vals[rows, :].astype(F32)

    def coupled(level, source_two, source_three):
        product = coup_v[level, 0] * source_two[None]
        if source_three is not None:
            product = product + coup_v[level, 1] * source_three[None]
        return product.reshape(RANK * RANK, WIDTH).astype(BF16)

    send_direct(0)
    send_direct(1)

    copies = {}

    def local(name, source, target):
        copies[name] = pltpu.make_async_copy(source, target, local_sem.at[len(copies)])
        copies[name].start()

    local("tok", tok, g.at[0])
    for slot in range(4):
        rows = pl.ds(pl.multiple_of(owners[slot] * WIDTH, WIDTH), WIDTH)
        local(("v", slot), w_value.at[rows], w.at[slot, :, pl.ds(0, WIDTH)])
        local(("g", slot), w_gate.at[rows], w.at[slot, :, pl.ds(WIDTH, WIDTH)])
    for name, source, target in (
        ("gain", gain, gain_v),
        ("phi", phi, phi_v),
        ("coeff", coeff, coeff_v),
        ("fwd", fwd, fwd_f),
        ("skip", skip, skip_v),
        ("up", up, up_v),
        ("down", down, down_v),
        ("lift", lift, lift_v),
        ("spread", spread, spread_v),
        ("inv", inv, inv_f),
        ("coup", coup, coup_v),
    ):
        local(name, source, target)

    @pl.when(z > 0)
    def _():
        signal(ready_next, t - PLANE, x)

    for k in range(1, PLANE):

        @pl.when(own >= k)
        def _():
            signal(ready_plane, t - k, x)

    def chain(place):
        @pl.when(z == PLANES - 1 - place)
        def _():
            if not isinstance(place, int) or place > 0:
                pl.semaphore_wait(ready_later, 1)
            if not isinstance(place, int) or place < PLANES - 1:
                signal(ready_later, t - PLANE, x)

    chain(0)
    tables_near()
    pass_on(0)
    send_direct(2)
    chain(1)

    @pl.when(own < PLANE - 1)
    def _():
        pl.semaphore_wait(ready_plane, PLANE - 1 - own)

    @pl.when(z < PLANES - 1)
    def _():
        pl.semaphore_wait(ready_next, 1)

        @pl.when(y == 0)
        def _():
            signal(ready_edge, z * PLANE + 6, x)
            signal(ready_edge, z * PLANE + 7, x)

    tables_moments()
    tables_lift()
    pass_on(1)
    send_direct(3)
    chain(2)
    tables_far()
    chain(3)
    copies["inv"].wait()
    inv_v[...] = jnp.concatenate(halves(inv_f[...]), 1)
    for slot in range(4):
        copies["v", slot].wait()
        copies["g", slot].wait()
    for name in ("tok", "gain", "skip", "coup"):
        copies[name].wait()

    @pl.when((y == 3) & (z < PLANES - 1))
    def _():
        pl.semaphore_wait(ready_edge, 2)

    halo_copy = pltpu.make_async_remote_copy(
        src_ref=vals.at[pl.ds(3 * LEAF, LEAF)],
        dst_ref=halo,
        send_sem=hsem.at[0],
        recv_sem=hsem.at[1],
        device_id=(t + 1, x),
        device_id_type=MESH,
    )

    def ctx_copy(part):
        return pltpu.make_async_remote_copy(
            src_ref=ctx_out.at[pl.ds(part * 32, 32)],
            dst_ref=ctx_in.at[pl.ds(part * 32, 32)],
            send_sem=csem.at[0, part],
            recv_sem=csem.at[1, part],
            device_id=(t + 1, x),
            device_id_type=MESH,
        )

    def step(i, carry):
        wait_relayed(i)
        project(leaf_at(i))

        @pl.when((i == 0) & (t < PLANES * PLANE - 1))
        def _():
            halo_copy.start()

        @pl.when(i < 2)
        def _():
            pass_on(i + 2)

        chain(4 + i)
        return carry

    lax.fori_loop(0, 3, step, 0)

    ctx_out[:32] = jnp.concatenate([moms[3, 0:16, :], moms[0, 16:32, :] + moms[1, 16:32, :]], 0).astype(BF16)

    @pl.when(t < PLANES * PLANE - 1)
    def _():
        ctx_copy(0).start()

    summing = red_m[0, :RANK, :]

    def gathered(level, source_two, source_three=None):
        return dot(summing, coupled(level, source_two, source_three))

    far0[2] = gathered(0, moms[0, 0:16, :])
    far0[3] = gathered(0, moms[1, 0:16, :], moms[0, 0:16, :])
    near_rows(1)

    @pl.when(t > 0)
    def _():
        halo_copy.wait_recv()

    before = halo[...]
    spec[LEAVES] = dot(fwd_v[...], jnp.concatenate([before, before], 0))
    near_rows(0)

    scaled, squares = scaled_rows(2, (0, 1, 2))
    first_value = dot(scaled, weights(0, 3))
    first_gate = dot(scaled, weights(1, 3))
    wait_relayed(3)
    scaled, more_squares = scaled_rows(2, (3,))
    inverse = inverse_of(squares + more_squares)
    twice = values_of(2, first_value + dot(scaled, w[3, :, :WIDTH]), inverse)

    chain(7)

    total = moms[0, 32:48, :] + moms[1, 32:48, :] + moms[2, 32:48, :] + moms[3, 32:48, :]
    m2[own] = total.astype(BF16)

    def plane_copy(k):
        return pltpu.make_async_remote_copy(
            src_ref=m2.at[own],
            dst_ref=m2.at[own],
            send_sem=s1.at[k - 1],
            recv_sem=r1.at[k - 1],
            device_id=(z * PLANE + lax.rem(own + k, PLANE), x),
            device_id_type=MESH,
        )

    def plane_arrival(k):
        return pltpu.make_async_remote_copy(
            src_ref=m2.at[own],
            dst_ref=m2.at[lax.rem(own + PLANE - k, PLANE)],
            send_sem=s1.at[k - 1],
            recv_sem=r1.at[k - 1],
            device_id=(z * PLANE + lax.rem(own + k, PLANE), x),
            device_id_type=MESH,
        )

    for k in range(1, PLANE):
        plane_copy(k).start()

    def next_plane_copy(target, source):
        return pltpu.make_async_remote_copy(
            src_ref=m2.at[own],
            dst_ref=m2_prev.at[source],
            send_sem=s1p.at[target],
            recv_sem=r1p.at[source],
            device_id=((z + 1) * PLANE + target, x),
            device_id_type=MESH,
        )

    @pl.when((y == 3) & (z < PLANES - 1))
    def _():
        for target in range(2):
            next_plane_copy(target, core).start()

    ctx_out[32:] = jnp.concatenate([moms[2, 0:16, :], moms[2, 16:32, :] + moms[3, 16:32, :]], 0).astype(BF16)

    @pl.when(t < PLANES * PLANE - 1)
    def _():
        ctx_copy(1).start()

    gates_of(2, first_gate + dot(scaled, w[3, :, WIDTH:]), inverse)
    spec[2] = dot(fwd_v[...], twice)
    near_rows(2)

    @pl.when(t > 0)
    def _():
        ctx_copy(0).wait_recv()

    far1[0] = gathered(1, ctx_in[16:32, :].astype(F32))

    for way in range(2):
        for leaf in range(LEAVES):
            direct(leaf, way).wait_send()
            relay(leaf, way).wait_send()

    for k in range(1, PLANE):
        plane_arrival(k).wait_recv()
    stack = m2[...].reshape(PLANE * RANK, WIDTH)
    lifted = dot(lift_m[...], jnp.concatenate([stack, stack], 0))
    pack_out[...] = lifted[:80].astype(BF16)


    def pack_copy(rows):
        return pltpu.make_async_remote_copy(
            src_ref=pack_out.at[pl.ds(0, rows)],
            dst_ref=pack_in.at[pl.ds(0, rows)],
            send_sem=s2,
            recv_sem=r2,
            device_id=(t + PLANE, x),
            device_id_type=MESH,
        )

    def five_copy(k):
        return pltpu.make_async_remote_copy(
            src_ref=pack_out.at[pl.ds(64, RANK)],
            dst_ref=m5_in.at[k],
            send_sem=s5.at[k],
            recv_sem=r5.at[k],
            device_id=(t + k * PLANE, x),
            device_id_type=MESH,
        )

    @pl.when((z < PLANES - 1) & (y < 2))
    def _():
        pack_copy(64).start()

    @pl.when((z < PLANES - 1) & (y >= 2))
    def _():
        pack_copy(32).start()

    for k in range(2, PLANES):

        @pl.when(z + k < PLANES)
        def _():
            five_copy(k).start()

    near_rows(3)

    @pl.when(t > 0)
    def _():
        ctx_copy(1).wait_recv()

    prev = ctx_in[...].astype(F32)
    far0[0] = gathered(0, prev[32:48])
    far0[1] = gathered(0, prev[0:16], prev[32:48])
    far1[1] = gathered(1, prev[48:64], prev[16:32])

    for k in range(1, PLANE):
        plane_copy(k).wait_send()

    @pl.when(t < PLANES * PLANE - 1)
    def _():
        halo_copy.wait_send()
        ctx_copy(0).wait_send()
        ctx_copy(1).wait_send()

    @pl.when((y == 3) & (z < PLANES - 1))
    def _():
        for target in range(2):
            next_plane_copy(target, core).wait_send()

    @pl.when((y == 0) & (z > 0))
    def _():
        for source in range(2):
            next_plane_copy(source, source).wait_recv()

    def reduced(k, source_two, source_three):
        return dot(red_m[k], coupled(2 + k, source_two, source_three))

    at = 2 * jnp.maximum(y - 1, 0)
    inside = y > 0
    two = jnp.where(inside, m2[at + core], m2_prev[core]).astype(F32)
    three = jnp.where(inside, m2[at], m2_prev[0]).astype(F32) * core.astype(F32)
    expansion = reduced(0, two, three)

    @pl.when((z > 0) & (y < 2))
    def _():
        pack_copy(64).wait_recv()

    @pl.when((z > 0) & (y >= 2))
    def _():
        pack_copy(32).wait_recv()

    odd = lax.rem(y, 2)
    lower = y < 2
    here = jnp.where(odd == 1, lifted[96:112], lifted[80:96])
    coming = pack_in[pl.ds(pl.multiple_of(32 + odd * RANK, RANK), RANK), :].astype(F32)
    two = jnp.where(lower, coming, here)
    three = jnp.where(lower, pack_in[32:48, :].astype(F32), lifted[80:96]) * odd.astype(F32)
    expansion = expansion + reduced(1, two, three)
    odd = lax.div(y, 2)
    two = pack_in[pl.ds(pl.multiple_of(odd * RANK, RANK), RANK), :].astype(F32)
    three = pack_in[0:16, :].astype(F32) * odd.astype(F32)
    expansion = expansion + reduced(2, two, three)

    for k in range(2, PLANES):

        @pl.when(z >= k)
        def _():
            five_copy(k).wait_recv()

    odd = lax.rem(z, 2)
    expansion = expansion + reduced(
        3, m5_in[2].astype(F32), m5_in[3].astype(F32) * odd.astype(F32)
    )
    pad = jnp.zeros((64, WIDTH), BF16)

    def sixth(base):
        pair = [m5_in[base], m5_in[base - 1]]
        return dot(six_m[...], jnp.concatenate(pair + pair + [pad], 0))

    odd_six = lax.rem(lax.div(z, 2), 2)
    expansion = expansion + reduced(
        4, sixth(4 + odd), sixth(6 + odd) * odd_six.astype(F32)
    )

    expansion = expansion[:RANK] + expansion[RANK:]

    def out_copy(leaf):
        rows = leaf_rows(leaf)
        return pltpu.make_async_copy(out_v.at[rows], out.at[rows], osem.at[leaf])

    for leaf in range(LEAVES):
        rows = leaf_rows(leaf)
        high, low = halves(jnp.concatenate([far0[leaf], far1[leaf // 2], expansion], 0))
        whole = jnp.concatenate([high, low, high, jnp.zeros((112, WIDTH), BF16)], 0)
        combined = near[rows, :] + dot(far_m[leaf], whole)
        out_v[rows, :] = (gate[rows, :] * combined).astype(BF16)
        out_copy(leaf).start()

    @pl.when((z < PLANES - 1) & (y < 2))
    def _():
        pack_copy(64).wait_send()

    @pl.when((z < PLANES - 1) & (y >= 2))
    def _():
        pack_copy(32).wait_send()

    for k in range(2, PLANES):

        @pl.when(z + k < PLANES)
        def _():
            five_copy(k).wait_send()

    for leaf in range(LEAVES):
        out_copy(leaf).wait()


def per_device(
    tokens,
    norm_gain,
    w_value,
    w_gate,
    phi_taps,
    tap_coeff,
    skip_gain,
    basis_up,
    basis_down,
    lift_maps,
    spread_maps,
    couplings,
):
    forward, inverse = transform_tables()
    in_hbm = pl.BlockSpec(memory_space=pltpu.HBM)
    frames = LEAF * LEAVES
    vmem = pltpu.VMEM
    dma = pltpu.SemaphoreType.DMA
    scratch = [
        vmem((4, frames, WIDTH), BF16),
        vmem((4, WIDTH, 2 * WIDTH), BF16),
        vmem((1, 4 * WIDTH), F32),
        vmem(phi_taps.shape, F32),
        vmem(tap_coeff.shape, F32),
        vmem((1, WIDTH), F32),
        vmem(basis_up.shape, F32),
        vmem(basis_down.shape, F32),
        vmem(lift_maps.shape, F32),
        vmem(spread_maps.shape, F32),
        vmem(couplings.shape, F32),
        vmem(forward.shape, F32),
        vmem(inverse.shape, F32),
        vmem((2 * LEAF, 2 * LEAF), BF16),
        vmem((LEAF, 4 * LEAF), BF16),
        vmem((frames, WIDTH), BF16),
        vmem((LEAF, WIDTH), BF16),
        vmem((frames, WIDTH), F32),
        vmem((frames, WIDTH), F32),
        vmem((LEAVES + 1, 2 * LEAF, WIDTH), F32),
        vmem((4, LEAF, WIDTH), F32),
        vmem((LEAVES, 48, 2 * LEAF), BF16),
        vmem((112, 256), BF16),
        vmem((RANK, 128), BF16),
        vmem((LEAVES, LEAF, LEAF), BF16),
        vmem((5, 2 * RANK, LEAF), BF16),
        vmem((LEAVES, 48, WIDTH), F32),
        vmem((PLANE, RANK, WIDTH), BF16),
        vmem((2, RANK, WIDTH), BF16),
        vmem((64, WIDTH), BF16),
        vmem((64, WIDTH), BF16),
        vmem((80, WIDTH), BF16),
        vmem((64, WIDTH), BF16),
        vmem((PLANES, RANK, WIDTH), BF16),
        vmem((LEAVES, RANK, WIDTH), F32),
        vmem((2, RANK, WIDTH), F32),
        vmem((frames, WIDTH), BF16),
        dma((20,)),
        dma((2, LEAVES)),
        dma((2, LEAVES)),
        dma((2, LEAVES)),
        dma((2, LEAVES)),
        dma((2,)),
        dma((2, 2)),
        dma((PLANE - 1,)),
        dma((PLANE - 1,)),
        dma((2,)),
        dma((2,)),
        dma(()),
        dma(()),
        dma((PLANES,)),
        dma((PLANES,)),
        pltpu.SemaphoreType.REGULAR,
        pltpu.SemaphoreType.REGULAR,
        pltpu.SemaphoreType.REGULAR,
        pltpu.SemaphoreType.REGULAR,
        dma((LEAVES,)),
    ]
    return pl.pallas_call(
        body,
        out_shape=jax.ShapeDtypeStruct(tokens.shape, BF16),
        in_specs=[in_hbm] * 14,
        out_specs=in_hbm,
        scratch_shapes=scratch,
        compiler_params=pltpu.CompilerParams(
            collective_id=0, has_side_effects=True, vmem_limit_bytes=60 * 1024 * 1024
        ),
        cost_estimate=pl.CostEstimate(flops=4 * 10**9, bytes_accessed=8 * 10**6, transcendentals=10**6),
    )(
        tokens,
        norm_gain.reshape(1, -1),
        w_value,
        w_gate,
        phi_taps,
        tap_coeff,
        skip_gain.reshape(1, -1),
        basis_up,
        basis_down,
        lift_maps,
        spread_maps,
        couplings,
        jnp.asarray(forward),
        jnp.asarray(inverse),
    )


def solution(mesh):
    placed = (
        P("tm", "chan"),
        P(),
        P(None, "chan"),
        P(None, "chan"),
        P(),
        P(None, "chan"),
        P("chan"),
        P(),
        P(),
        P(),
        P(),
        P(None, None, None, None, "chan"),
    )
    return jax.shard_map(
        per_device, mesh=mesh, in_specs=placed, out_specs=P("tm", "chan"), check_vma=False
    )
```

```python
import jax
import jax.numpy as jnp
import numpy as np
from jax import lax
from jax.experimental import pallas as pl
from jax.experimental.pallas import tpu as pltpu
from jax.sharding import PartitionSpec as P

MESH = pl.DeviceIdType.MESH
F32 = jnp.float32
BF16 = jnp.bfloat16
HIGHEST = lax.Precision.HIGHEST

LEAF = 256
LEAVES = 4
WIDTH = 256
RANK = 16
PLANES = 8
PLANE = 8


def transform_tables():
    odd = np.arange(LEAF)[:, None] + 0.5
    angle = 2 * np.pi * odd * np.arange(LEAF)[None, :] / (2 * LEAF)
    forward = np.concatenate([np.cos(angle), -np.sin(angle)], 0)
    return forward.astype(np.float32), (forward.T / LEAF).astype(np.float32)


def exact_dot(left, right):
    return jnp.dot(left, right, precision=HIGHEST, preferred_element_type=F32)


def dot(left, right):
    return jnp.dot(left, right, preferred_element_type=F32)


def halves(value):
    high = value.astype(BF16)
    return high, (value - high.astype(F32)).astype(BF16)


def selector(lanes, period, shift, limit):
    row = lax.broadcasted_iota(jnp.int32, (RANK, lanes), 0)
    lane = lax.broadcasted_iota(jnp.int32, (RANK, lanes), 1)
    return ((lax.rem(lane, period) == row + shift) & (lane < limit)).astype(F32)


def body(
    tok, gain, w_value, w_gate, phi, coeff, skip, up, down, lift, spread, coup, fwd, inv,
    out,
    g, w, gain_v, phi_v, coeff_v, skip_v, up_v, down_v, lift_v, spread_v, coup_v, fwd_f, inv_f, fwd_v, inv_v,
    vals, halo, gate, near, spec, khat, mom_m, lift_m, six_m, far_m, red_m, moms,
    m2, m2_prev, ctx_out, ctx_in, pack_out, pack_in, m5_in, far0, far1, out_v, parts, part_squares,
    local_sem, dsend, drecv, rsend, rrecv, hsem, csem, s1, r1, s1p, r1p, s2, r2, s5, r5, ready_plane, ready_next, ready_edge, ready_later, osem,
):
    t = lax.axis_index("tm")
    x = lax.axis_index("chan")
    core = lax.rem(t, 2)
    y = lax.rem(lax.div(t, 2), 4)
    z = lax.div(t, PLANE)
    own = lax.rem(t, PLANE)
    right, left = lax.rem(x + 1, 4), lax.rem(x + 3, 4)

    barrier = pltpu.get_barrier_semaphore()

    def signal(semaphore, frames, chans):
        pl.semaphore_signal(semaphore, inc=1, device_id=(frames, chans), device_id_type=MESH)

    signal(barrier, t, right)
    signal(barrier, t, left)

    @pl.when(z < PLANES - 1)
    def _():
        signal(barrier, t + PLANE, x)

    for k in range(1, PLANE):

        @pl.when(own + k < PLANE)
        def _():
            signal(barrier, t + k, x)

    m2_prev[...] = jnp.zeros_like(m2_prev)
    ctx_in[...] = jnp.zeros_like(ctx_in)
    pack_in[...] = jnp.zeros_like(pack_in)
    m5_in[...] = jnp.zeros_like(m5_in)
    halo[...] = jnp.zeros_like(halo)

    pl.semaphore_wait(barrier, 2 + own + jnp.where(z > 0, 1, 0))

    owners = [x, left, right, lax.rem(x + 2, 4)]

    def leaf_at(place):
        return (place + 3) % LEAVES if isinstance(place, int) else lax.rem(place + 3, LEAVES)

    def leaf_rows(leaf):
        return pl.ds(leaf * LEAF if isinstance(leaf, int) else pl.multiple_of(leaf * LEAF, LEAF), LEAF)

    def direct(leaf, way):
        rows = leaf_rows(leaf)
        return pltpu.make_async_remote_copy(
            src_ref=tok.at[rows],
            dst_ref=g.at[1 + way, rows],
            send_sem=dsend.at[way, leaf],
            recv_sem=drecv.at[way, leaf],
            device_id=(t, left if way else right),
            device_id_type=MESH,
        )

    def relay(leaf, way):
        start = leaf * LEAF + way * (LEAF // 2)
        rows = pl.ds(start if isinstance(leaf, int) else pl.multiple_of(start, LEAF // 2), LEAF // 2)
        return pltpu.make_async_remote_copy(
            src_ref=g.at[1 + way, rows],
            dst_ref=g.at[3, rows],
            send_sem=rsend.at[way, leaf],
            recv_sem=rrecv.at[way, leaf],
            device_id=(t, left if way else right),
            device_id_type=MESH,
        )

    def send_direct(place):
        for way in range(2):
            direct(leaf_at(place), way).start()

    def pass_on(place):
        for way in range(2):
            direct(leaf_at(place), way).wait_recv()
            relay(leaf_at(place), way).start()

    def wait_relayed(place):
        for way in range(2):
            relay(leaf_at(place), way).wait_recv()

    def tables_near():
        for name in ("phi", "coeff", "fwd"):
            copies[name].wait()
        fwd_v[...] = jnp.concatenate(halves(fwd_f[...]), 1)
        taps = phi_v[...].astype(BF16).astype(F32)
        kernel_taps = lax.dot_general(
            taps, coeff_v[...], (((0,), (0,)), ((), ())), precision=HIGHEST, preferred_element_type=F32
        )
        both = jnp.concatenate([kernel_taps[:LEAF], kernel_taps[LEAF:]], 1)
        high, low = halves(both)
        hat = dot(fwd_v[...], jnp.concatenate([high, high], 0)) + dot(fwd_v[:, :LEAF], low)
        a_re, a_im = hat[:LEAF, :WIDTH], hat[LEAF:, :WIDTH]
        b_re, b_im = hat[:LEAF, WIDTH:], hat[LEAF:, WIDTH:]
        row = lax.broadcasted_iota(jnp.int32, (LEAF, WIDTH), 0)
        sign = (1 - 2 * lax.rem(row, 2)).astype(F32)
        khat[0] = a_re
        khat[1] = a_im
        khat[2] = b_re - sign * a_im
        khat[3] = b_im + sign * a_re

    def tables_moments():
        copies["up"].wait()
        copies["lift"].wait()
        base = up_v[...]
        first = [exact_dot(lift_v[0, k], base) for k in range(2)]
        for leaf in range(LEAVES):
            second = exact_dot(lift_v[1, leaf // 2], first[leaf % 2])
            high, low = halves(jnp.concatenate([base, first[leaf % 2], second], 0))
            mom_m[leaf] = jnp.concatenate([high, low], 1)

    def tables_lift():
        def pair(level):
            return exact_dot(lift_v[level, 0], selector(128, 32, 0, 128)) + exact_dot(
                lift_v[level, 1], selector(128, 32, 16, 128)
            )

        def blocks(level, copies_of):
            rows = jnp.concatenate([pair(level)] * copies_of, 0)
            row = lax.broadcasted_iota(jnp.int32, rows.shape, 0)
            lane = lax.broadcasted_iota(jnp.int32, rows.shape, 1)
            return jnp.where(lax.div(row, RANK) == lax.div(lane, 2 * RANK), rows, 0.0)

        three = blocks(2, 8)
        four = exact_dot(blocks(3, 2), three)
        five = exact_dot(blocks(4, 1), jnp.concatenate([four, jnp.zeros((96, 128), F32)], 0))
        whole = jnp.concatenate([four, three[32:64], five, three[:32]], 0)
        high, low = halves(whole)
        lift_m[...] = jnp.concatenate([high, low], 1)
        six = exact_dot(lift_v[5, 0], selector(128, 32, 0, 64)) + exact_dot(
            lift_v[5, 1], selector(128, 32, 16, 64)
        )
        high = six.astype(BF16).astype(F32)
        lane = lax.broadcasted_iota(jnp.int32, six.shape, 1)
        six_m[...] = jnp.where(lane < 32, high, six - high).astype(BF16)

    def tables_far():
        copies["spread"].wait()
        copies["down"].wait()
        row = lax.broadcasted_iota(jnp.int32, (RANK, LEAF), 0)
        lane = lax.broadcasted_iota(jnp.int32, (RANK, LEAF), 1)
        summing = (lax.div(lane, RANK) == row).astype(F32)
        chain = None
        for k in range(5):
            if k > 0:
                step = spread_v[1 + k, lax.rem(lax.div(t, 2 ** (k - 1)), 2)]
                chain = step if k == 1 else exact_dot(chain, step)
            high, low = halves(summing if k == 0 else exact_dot(chain, summing))
            red_m[k] = jnp.concatenate([high, low], 0)
        for leaf in range(LEAVES):
            near_step = spread_v[0, leaf % 2]
            both_steps = exact_dot(near_step, spread_v[1, leaf // 2])
            mix = (
                selector(LEAF, 48, 0, 144)
                + exact_dot(near_step, selector(LEAF, 48, 16, 144))
                + exact_dot(both_steps, selector(LEAF, 48, 32, 144))
            )
            whole = lax.dot_general(
                down_v[...], mix, (((0,), (0,)), ((), ())), precision=HIGHEST, preferred_element_type=F32
            )
            high = whole.astype(BF16).astype(F32)
            lane_at = lax.broadcasted_iota(jnp.int32, whole.shape, 1)
            far_m[leaf] = jnp.where(lane_at < 96, high, whole - high).astype(BF16)

    def scaled_rows(leaf, slots):
        rows = leaf_rows(leaf)
        squares = jnp.zeros((LEAF, WIDTH), F32)
        columns = []
        for slot in slots:
            tokens = g[slot, rows, :].astype(F32)
            squares = squares + tokens * tokens
            scale = gain_v[:, pl.ds(pl.multiple_of(owners[slot] * WIDTH, WIDTH), WIDTH)]
            columns.append((tokens * scale).astype(BF16))
        return jnp.concatenate(columns, 1), squares

    def inverse_of(squares):
        return lax.rsqrt(jnp.sum(squares, axis=1, keepdims=True) / 1024 + 1e-06)

    def values_of(leaf, sums, inverse):
        value = (sums * inverse).astype(BF16)
        vals[leaf_rows(leaf), :] = value
        twice = jnp.concatenate([value, value], 0)
        moms[leaf] = dot(mom_m[leaf], twice)
        return twice

    def gates_of(leaf, sums, inverse):
        gate[leaf_rows(leaf), :] = jax.nn.sigmoid(sums * inverse)

    def gather_part(leaf):
        scaled, squares = scaled_rows(leaf, (0, 1, 2))
        parts[leaf] = dot(scaled, w[:3].reshape(3 * WIDTH, 2 * WIDTH))
        part_squares[leaf] = squares[:, : WIDTH // 2] + squares[:, WIDTH // 2 :]

    def finished_sums(leaf):
        scaled, squares = scaled_rows(leaf, (3,))
        inverse = inverse_of(squares[:, : WIDTH // 2] + squares[:, WIDTH // 2 :] + part_squares[leaf])
        value_sums = parts[leaf, :, :WIDTH] + dot(scaled, w[3, :, :WIDTH])
        gate_sums = parts[leaf, :, WIDTH:] + dot(scaled, w[3, :, WIDTH:])
        return value_sums, gate_sums, inverse

    def project(leaf):
        value_sums, gate_sums, inverse = finished_sums(leaf)
        twice = values_of(leaf, value_sums, inverse)
        gates_of(leaf, gate_sums, inverse)
        spec[leaf] = dot(fwd_v[...], twice)

    def near_rows(leaf):
        rows = leaf_rows(leaf)
        before = (leaf - 1 if leaf > 0 else LEAVES) if isinstance(leaf, int) else leaf - 1
        a_re, a_im = spec[leaf, :LEAF, :], spec[leaf, LEAF:, :]
        b_re, b_im = spec[before, :LEAF, :], spec[before, LEAF:, :]
        out_re = khat[0] * a_re - khat[1] * a_im + khat[2] * b_re - khat[3] * b_im
        out_im = khat[0] * a_im + khat[1] * a_re + khat[2] * b_im + khat[3] * b_re
        high, low = halves(jnp.concatenate([out_re, out_im], 0))
        total = dot(inv_v[...], jnp.concatenate([high, high], 0)) + dot(inv_v[:, : 2 * LEAF], low)
        near[rows, :] = total + skip_v[...] * vals[rows, :].astype(F32)

    def coupled(level, source_two, source_three):
        product = coup_v[level, 0] * source_two[None]
        if source_three is not None:
            product = product + coup_v[level, 1] * source_three[None]
        return product.reshape(RANK * RANK, WIDTH).astype(BF16)

    for place in range(LEAVES):
        send_direct(place)

    copies = {}

    def local(name, source, target):
        copies[name] = pltpu.make_async_copy(source, target, local_sem.at[len(copies)])
        copies[name].start()

    local("tok", tok, g.at[0])
    for slot in range(4):
        rows = pl.ds(pl.multiple_of(owners[slot] * WIDTH, WIDTH), WIDTH)
        local(("v", slot), w_value.at[rows], w.at[slot, :, pl.ds(0, WIDTH)])
        local(("g", slot), w_gate.at[rows], w.at[slot, :, pl.ds(WIDTH, WIDTH)])
    for name, source, target in (
        ("gain", gain, gain_v),
        ("phi", phi, phi_v),
        ("coeff", coeff, coeff_v),
        ("fwd", fwd, fwd_f),
        ("skip", skip, skip_v),
        ("up", up, up_v),
        ("down", down, down_v),
        ("lift", lift, lift_v),
        ("spread", spread, spread_v),
        ("inv", inv, inv_f),
        ("coup", coup, coup_v),
    ):
        local(name, source, target)

    @pl.when(z > 0)
    def _():
        signal(ready_next, t - PLANE, x)

    for k in range(1, PLANE):

        @pl.when(own >= k)
        def _():
            signal(ready_plane, t - k, x)

    def chain(place):
        @pl.when(z == PLANES - 1 - place)
        def _():
            if not isinstance(place, int) or place > 0:
                pl.semaphore_wait(ready_later, 1)
            if not isinstance(place, int) or place < PLANES - 1:
                signal(ready_later, t - PLANE, x)

    chain(0)
    tables_near()
    chain(1)
    tables_moments()
    tables_lift()
    chain(2)

    @pl.when(own < PLANE - 1)
    def _():
        pl.semaphore_wait(ready_plane, PLANE - 1 - own)

    @pl.when(z < PLANES - 1)
    def _():
        pl.semaphore_wait(ready_next, 1)

        @pl.when(y == 0)
        def _():
            signal(ready_edge, z * PLANE + 6, x)
            signal(ready_edge, z * PLANE + 7, x)

    for slot in range(4):
        copies["v", slot].wait()
        copies["g", slot].wait()
    for name in ("tok", "gain", "skip", "coup", "inv"):
        copies[name].wait()

    def arrive(place, carry):
        pass_on(place)
        gather_part(leaf_at(place))

        @pl.when(place == 0)
        def _():
            tables_far()
            inv_v[...] = jnp.concatenate(halves(inv_f[...]), 1)

        return carry

    lax.fori_loop(0, LEAVES, arrive, 0)
    chain(3)

    @pl.when((y == 3) & (z < PLANES - 1))
    def _():
        pl.semaphore_wait(ready_edge, 2)

    halo_copy = pltpu.make_async_remote_copy(
        src_ref=vals.at[pl.ds(3 * LEAF, LEAF)],
        dst_ref=halo,
        send_sem=hsem.at[0],
        recv_sem=hsem.at[1],
        device_id=(t + 1, x),
        device_id_type=MESH,
    )

    def ctx_copy(part):
        return pltpu.make_async_remote_copy(
            src_ref=ctx_out.at[pl.ds(part * 32, 32)],
            dst_ref=ctx_in.at[pl.ds(part * 32, 32)],
            send_sem=csem.at[0, part],
            recv_sem=csem.at[1, part],
            device_id=(t + 1, x),
            device_id_type=MESH,
        )

    def step(i, carry):
        wait_relayed(i)
        project(leaf_at(i))

        @pl.when((i == 0) & (t < PLANES * PLANE - 1))
        def _():
            halo_copy.start()

        chain(4 + i)
        return carry

    lax.fori_loop(0, 3, step, 0)

    ctx_out[:32] = jnp.concatenate([moms[3, 0:16, :], moms[0, 16:32, :] + moms[1, 16:32, :]], 0).astype(BF16)

    @pl.when(t < PLANES * PLANE - 1)
    def _():
        ctx_copy(0).start()

    @pl.when(t > 0)
    def _():
        halo_copy.wait_recv()

    before = halo[...]
    spec[LEAVES] = dot(fwd_v[...], jnp.concatenate([before, before], 0))
    near_rows(0)

    wait_relayed(3)
    value_sums, gate_sums, inverse = finished_sums(2)
    twice = values_of(2, value_sums, inverse)

    chain(7)

    total = moms[0, 32:48, :] + moms[1, 32:48, :] + moms[2, 32:48, :] + moms[3, 32:48, :]
    m2[own] = total.astype(BF16)

    def plane_copy(k):
        return pltpu.make_async_remote_copy(
            src_ref=m2.at[own],
            dst_ref=m2.at[own],
            send_sem=s1.at[k - 1],
            recv_sem=r1.at[k - 1],
            device_id=(z * PLANE + lax.rem(own + k, PLANE), x),
            device_id_type=MESH,
        )

    def plane_arrival(k):
        return pltpu.make_async_remote_copy(
            src_ref=m2.at[own],
            dst_ref=m2.at[lax.rem(own + PLANE - k, PLANE)],
            send_sem=s1.at[k - 1],
            recv_sem=r1.at[k - 1],
            device_id=(z * PLANE + lax.rem(own + k, PLANE), x),
            device_id_type=MESH,
        )

    for k in range(1, PLANE):
        plane_copy(k).start()

    def next_plane_copy(target, source):
        return pltpu.make_async_remote_copy(
            src_ref=m2.at[own],
            dst_ref=m2_prev.at[source],
            send_sem=s1p.at[target],
            recv_sem=r1p.at[source],
            device_id=((z + 1) * PLANE + target, x),
            device_id_type=MESH,
        )

    @pl.when((y == 3) & (z < PLANES - 1))
    def _():
        for target in range(2):
            next_plane_copy(target, core).start()

    ctx_out[32:] = jnp.concatenate([moms[2, 0:16, :], moms[2, 16:32, :] + moms[3, 16:32, :]], 0).astype(BF16)

    @pl.when(t < PLANES * PLANE - 1)
    def _():
        ctx_copy(1).start()

    summing = red_m[0, :RANK, :]

    def gathered(level, source_two, source_three=None):
        return dot(summing, coupled(level, source_two, source_three))

    gates_of(2, gate_sums, inverse)
    spec[2] = dot(fwd_v[...], twice)
    near_rows(1)
    near_rows(2)
    far0[2] = gathered(0, moms[0, 0:16, :])
    far0[3] = gathered(0, moms[1, 0:16, :], moms[0, 0:16, :])

    for way in range(2):
        for leaf in range(LEAVES):
            direct(leaf, way).wait_send()
            relay(leaf, way).wait_send()

    for k in range(1, PLANE):
        plane_arrival(k).wait_recv()
    stack = m2[...].reshape(PLANE * RANK, WIDTH)
    lifted = dot(lift_m[...], jnp.concatenate([stack, stack], 0))
    pack_out[...] = lifted[:80].astype(BF16)


    def pack_copy(rows):
        return pltpu.make_async_remote_copy(
            src_ref=pack_out.at[pl.ds(0, rows)],
            dst_ref=pack_in.at[pl.ds(0, rows)],
            send_sem=s2,
            recv_sem=r2,
            device_id=(t + PLANE, x),
            device_id_type=MESH,
        )

    def five_copy(k):
        return pltpu.make_async_remote_copy(
            src_ref=pack_out.at[pl.ds(64, RANK)],
            dst_ref=m5_in.at[k],
            send_sem=s5.at[k],
            recv_sem=r5.at[k],
            device_id=(t + k * PLANE, x),
            device_id_type=MESH,
        )

    @pl.when((z < PLANES - 1) & (y < 2))
    def _():
        pack_copy(64).start()

    @pl.when((z < PLANES - 1) & (y >= 2))
    def _():
        pack_copy(32).start()

    for k in range(2, PLANES):

        @pl.when(z + k < PLANES)
        def _():
            five_copy(k).start()

    near_rows(3)

    @pl.when(t > 0)
    def _():
        ctx_copy(0).wait_recv()
        ctx_copy(1).wait_recv()

    prev = ctx_in[...].astype(F32)
    far1[0] = gathered(1, prev[16:32])
    far0[0] = gathered(0, prev[32:48])
    far0[1] = gathered(0, prev[0:16], prev[32:48])
    far1[1] = gathered(1, prev[48:64], prev[16:32])

    for k in range(1, PLANE):
        plane_copy(k).wait_send()

    @pl.when(t < PLANES * PLANE - 1)
    def _():
        halo_copy.wait_send()
        ctx_copy(0).wait_send()
        ctx_copy(1).wait_send()

    @pl.when((y == 3) & (z < PLANES - 1))
    def _():
        for target in range(2):
            next_plane_copy(target, core).wait_send()

    @pl.when((y == 0) & (z > 0))
    def _():
        for source in range(2):
            next_plane_copy(source, source).wait_recv()

    def reduced(k, source_two, source_three):
        return dot(red_m[k], coupled(2 + k, source_two, source_three))

    at = 2 * jnp.maximum(y - 1, 0)
    inside = y > 0
    two = jnp.where(inside, m2[at + core], m2_prev[core]).astype(F32)
    three = jnp.where(inside, m2[at], m2_prev[0]).astype(F32) * core.astype(F32)
    expansion = reduced(0, two, three)

    @pl.when((z > 0) & (y < 2))
    def _():
        pack_copy(64).wait_recv()

    @pl.when((z > 0) & (y >= 2))
    def _():
        pack_copy(32).wait_recv()

    odd = lax.rem(y, 2)
    lower = y < 2
    here = jnp.where(odd == 1, lifted[96:112], lifted[80:96])
    coming = pack_in[pl.ds(pl.multiple_of(32 + odd * RANK, RANK), RANK), :].astype(F32)
    two = jnp.where(lower, coming, here)
    three = jnp.where(lower, pack_in[32:48, :].astype(F32), lifted[80:96]) * odd.astype(F32)
    expansion = expansion + reduced(1, two, three)
    odd = lax.div(y, 2)
    two = pack_in[pl.ds(pl.multiple_of(odd * RANK, RANK), RANK), :].astype(F32)
    three = pack_in[0:16, :].astype(F32) * odd.astype(F32)
    expansion = expansion + reduced(2, two, three)

    for k in range(2, PLANES):

        @pl.when(z >= k)
        def _():
            five_copy(k).wait_recv()

    odd = lax.rem(z, 2)
    expansion = expansion + reduced(
        3, m5_in[2].astype(F32), m5_in[3].astype(F32) * odd.astype(F32)
    )
    pad = jnp.zeros((64, WIDTH), BF16)

    def sixth(base):
        pair = [m5_in[base], m5_in[base - 1]]
        return dot(six_m[...], jnp.concatenate(pair + pair + [pad], 0))

    odd_six = lax.rem(lax.div(z, 2), 2)
    expansion = expansion + reduced(
        4, sixth(4 + odd), sixth(6 + odd) * odd_six.astype(F32)
    )

    expansion = expansion[:RANK] + expansion[RANK:]

    def out_copy(leaf):
        rows = leaf_rows(leaf)
        return pltpu.make_async_copy(out_v.at[rows], out.at[rows], osem.at[leaf])

    for leaf in range(LEAVES):
        rows = leaf_rows(leaf)
        high, low = halves(jnp.concatenate([far0[leaf], far1[leaf // 2], expansion], 0))
        whole = jnp.concatenate([high, low, high, jnp.zeros((112, WIDTH), BF16)], 0)
        combined = near[rows, :] + dot(far_m[leaf], whole)
        out_v[rows, :] = (gate[rows, :] * combined).astype(BF16)
        out_copy(leaf).start()

    @pl.when((z < PLANES - 1) & (y < 2))
    def _():
        pack_copy(64).wait_send()

    @pl.when((z < PLANES - 1) & (y >= 2))
    def _():
        pack_copy(32).wait_send()

    for k in range(2, PLANES):

        @pl.when(z + k < PLANES)
        def _():
            five_copy(k).wait_send()

    for leaf in range(LEAVES):
        out_copy(leaf).wait()


def per_device(
    tokens,
    norm_gain,
    w_value,
    w_gate,
    phi_taps,
    tap_coeff,
    skip_gain,
    basis_up,
    basis_down,
    lift_maps,
    spread_maps,
    couplings,
):
    forward, inverse = transform_tables()
    in_hbm = pl.BlockSpec(memory_space=pltpu.HBM)
    frames = LEAF * LEAVES
    vmem = pltpu.VMEM
    dma = pltpu.SemaphoreType.DMA
    scratch = [
        vmem((4, frames, WIDTH), BF16),
        vmem((4, WIDTH, 2 * WIDTH), BF16),
        vmem((1, 4 * WIDTH), F32),
        vmem(phi_taps.shape, F32),
        vmem(tap_coeff.shape, F32),
        vmem((1, WIDTH), F32),
        vmem(basis_up.shape, F32),
        vmem(basis_down.shape, F32),
        vmem(lift_maps.shape, F32),
        vmem(spread_maps.shape, F32),
        vmem(couplings.shape, F32),
        vmem(forward.shape, F32),
        vmem(inverse.shape, F32),
        vmem((2 * LEAF, 2 * LEAF), BF16),
        vmem((LEAF, 4 * LEAF), BF16),
        vmem((frames, WIDTH), BF16),
        vmem((LEAF, WIDTH), BF16),
        vmem((frames, WIDTH), F32),
        vmem((frames, WIDTH), F32),
        vmem((LEAVES + 1, 2 * LEAF, WIDTH), F32),
        vmem((4, LEAF, WIDTH), F32),
        vmem((LEAVES, 48, 2 * LEAF), BF16),
        vmem((112, 256), BF16),
        vmem((RANK, 128), BF16),
        vmem((LEAVES, LEAF, LEAF), BF16),
        vmem((5, 2 * RANK, LEAF), BF16),
        vmem((LEAVES, 48, WIDTH), F32),
        vmem((PLANE, RANK, WIDTH), BF16),
        vmem((2, RANK, WIDTH), BF16),
        vmem((64, WIDTH), BF16),
        vmem((64, WIDTH), BF16),
        vmem((80, WIDTH), BF16),
        vmem((64, WIDTH), BF16),
        vmem((PLANES, RANK, WIDTH), BF16),
        vmem((LEAVES, RANK, WIDTH), F32),
        vmem((2, RANK, WIDTH), F32),
        vmem((frames, WIDTH), BF16),
        vmem((LEAVES, LEAF, 2 * WIDTH), F32),
        vmem((LEAVES, LEAF, WIDTH // 2), F32),
        dma((20,)),
        dma((2, LEAVES)),
        dma((2, LEAVES)),
        dma((2, LEAVES)),
        dma((2, LEAVES)),
        dma((2,)),
        dma((2, 2)),
        dma((PLANE - 1,)),
        dma((PLANE - 1,)),
        dma((2,)),
        dma((2,)),
        dma(()),
        dma(()),
        dma((PLANES,)),
        dma((PLANES,)),
        pltpu.SemaphoreType.REGULAR,
        pltpu.SemaphoreType.REGULAR,
        pltpu.SemaphoreType.REGULAR,
        pltpu.SemaphoreType.REGULAR,
        dma((LEAVES,)),
    ]
    return pl.pallas_call(
        body,
        out_shape=jax.ShapeDtypeStruct(tokens.shape, BF16),
        in_specs=[in_hbm] * 14,
        out_specs=in_hbm,
        scratch_shapes=scratch,
        compiler_params=pltpu.CompilerParams(
            collective_id=0, has_side_effects=True, vmem_limit_bytes=60 * 1024 * 1024
        ),
        cost_estimate=pl.CostEstimate(flops=4 * 10**9, bytes_accessed=8 * 10**6, transcendentals=10**6),
    )(
        tokens,
        norm_gain.reshape(1, -1),
        w_value,
        w_gate,
        phi_taps,
        tap_coeff,
        skip_gain.reshape(1, -1),
        basis_up,
        basis_down,
        lift_maps,
        spread_maps,
        couplings,
        jnp.asarray(forward),
        jnp.asarray(inverse),
    )


def solution(mesh):
    placed = (
        P("tm", "chan"),
        P(),
        P(None, "chan"),
        P(None, "chan"),
        P(),
        P(None, "chan"),
        P("chan"),
        P(),
        P(),
        P(),
        P(),
        P(None, None, None, None, "chan"),
    )
    return jax.shard_map(
        per_device, mesh=mesh, in_specs=placed, out_specs=P("tm", "chan"), check_vma=False
    )
```

```python
import jax
import jax.numpy as jnp
import numpy as np
from jax import lax
from jax.experimental import pallas as pl
from jax.experimental.pallas import tpu as pltpu
from jax.sharding import PartitionSpec as P

MESH = pl.DeviceIdType.MESH
F32 = jnp.float32
BF16 = jnp.bfloat16
HIGHEST = lax.Precision.HIGHEST

LEAF = 256
LEAVES = 4
BLOCK = 128
BLOCKS = 8
WINDOW = 3
WIDTH = 256
RANK = 16
PLANES = 8
PLANE = 8


def transform_tables():
    odd = np.arange(LEAF)[:, None] + 0.5
    angle = 2 * np.pi * odd * np.arange(LEAF)[None, :] / (2 * LEAF)
    forward = np.concatenate([np.cos(angle), -np.sin(angle)], 0)
    return forward.astype(np.float32), (forward.T / LEAF).astype(np.float32)


def exact_dot(left, right):
    return jnp.dot(left, right, precision=HIGHEST, preferred_element_type=F32)


def dot(left, right):
    return jnp.dot(left, right, preferred_element_type=F32)


def halves(value):
    high = value.astype(BF16)
    return high, (value - high.astype(F32)).astype(BF16)


def selector(lanes, period, shift, limit):
    row = lax.broadcasted_iota(jnp.int32, (RANK, lanes), 0)
    lane = lax.broadcasted_iota(jnp.int32, (RANK, lanes), 1)
    return ((lax.rem(lane, period) == row + shift) & (lane < limit)).astype(F32)


def body(
    tok, gain, w_value, w_gate, phi, coeff, skip, up, down, lift, spread, coup, fwd, inv,
    out,
    g, w, gain_v, phi_v, coeff_v, skip_v, up_v, down_v, lift_v, spread_v, coup_v, fwd_f, inv_f, fwd_v, inv_v,
    vals, halo, gate, near, spec, khat, mom_m, lift_m, six_m, far_m, red_m, moms,
    m2, m2_prev, ctx_out, ctx_in, pack_out, pack_in, m5_in, far0, far1, out_v, parts, part_squares,
    local_sem, dsend, drecv, rsend, rrecv, hsem, csem, s1, r1, s1p, r1p, s2, r2, s5, r5, ready_plane, ready_next, ready_edge, ready_later, osem,
):
    t = lax.axis_index("tm")
    x = lax.axis_index("chan")
    core = lax.rem(t, 2)
    y = lax.rem(lax.div(t, 2), 4)
    z = lax.div(t, PLANE)
    own = lax.rem(t, PLANE)
    right, left = lax.rem(x + 1, 4), lax.rem(x + 3, 4)

    barrier = pltpu.get_barrier_semaphore()

    def signal(semaphore, frames, chans):
        pl.semaphore_signal(semaphore, inc=1, device_id=(frames, chans), device_id_type=MESH)

    signal(barrier, t, right)
    signal(barrier, t, left)

    @pl.when(z < PLANES - 1)
    def _():
        signal(barrier, t + PLANE, x)

    for k in range(1, PLANE):

        @pl.when(own + k < PLANE)
        def _():
            signal(barrier, t + k, x)

    m2_prev[...] = jnp.zeros_like(m2_prev)
    ctx_in[...] = jnp.zeros_like(ctx_in)
    pack_in[...] = jnp.zeros_like(pack_in)
    m5_in[...] = jnp.zeros_like(m5_in)
    halo[...] = jnp.zeros_like(halo)

    pl.semaphore_wait(barrier, 2 + own + jnp.where(z > 0, 1, 0))

    owners = [x, left, right, lax.rem(x + 2, 4)]

    def leaf_of(block):
        return lax.rem(lax.div(block, 2) + 3, LEAVES) if not isinstance(block, int) else (block // 2 + 3) % LEAVES

    def start_of(block):
        if isinstance(block, int):
            return leaf_of(block) * LEAF + block % 2 * BLOCK
        return pl.multiple_of(leaf_of(block) * LEAF + lax.rem(block, 2) * BLOCK, BLOCK)

    def block_rows(block):
        return pl.ds(start_of(block), BLOCK)

    def leaf_rows(leaf):
        return pl.ds(leaf * LEAF if isinstance(leaf, int) else pl.multiple_of(leaf * LEAF, LEAF), LEAF)

    def direct(block, way):
        rows = block_rows(block)
        return pltpu.make_async_remote_copy(
            src_ref=tok.at[rows],
            dst_ref=g.at[1 + way, rows],
            send_sem=dsend.at[way, block],
            recv_sem=drecv.at[way, block],
            device_id=(t, left if way else right),
            device_id_type=MESH,
        )

    def relay(block, way):
        start = start_of(block) + way * (BLOCK // 2)
        rows = pl.ds(start if isinstance(block, int) else pl.multiple_of(start, BLOCK // 2), BLOCK // 2)
        return pltpu.make_async_remote_copy(
            src_ref=g.at[1 + way, rows],
            dst_ref=g.at[3, rows],
            send_sem=rsend.at[way, block],
            recv_sem=rrecv.at[way, block],
            device_id=(t, left if way else right),
            device_id_type=MESH,
        )

    def send_direct(block):
        for way in range(2):
            direct(block, way).start()

    def pass_on(block):
        for way in range(2):
            direct(block, way).wait_recv()
            relay(block, way).start()

    def wait_relayed(block):
        for way in range(2):
            relay(block, way).wait_recv()

    def tables_near():
        for name in ("phi", "coeff", "fwd"):
            copies[name].wait()
        fwd_v[...] = jnp.concatenate(halves(fwd_f[...]), 1)
        taps = phi_v[...].astype(BF16).astype(F32)
        kernel_taps = lax.dot_general(
            taps, coeff_v[...], (((0,), (0,)), ((), ())), precision=HIGHEST, preferred_element_type=F32
        )
        both = jnp.concatenate([kernel_taps[:LEAF], kernel_taps[LEAF:]], 1)
        high, low = halves(both)
        hat = dot(fwd_v[...], jnp.concatenate([high, high], 0)) + dot(fwd_v[:, :LEAF], low)
        a_re, a_im = hat[:LEAF, :WIDTH], hat[LEAF:, :WIDTH]
        b_re, b_im = hat[:LEAF, WIDTH:], hat[LEAF:, WIDTH:]
        row = lax.broadcasted_iota(jnp.int32, (LEAF, WIDTH), 0)
        sign = (1 - 2 * lax.rem(row, 2)).astype(F32)
        khat[0] = a_re
        khat[1] = a_im
        khat[2] = b_re - sign * a_im
        khat[3] = b_im + sign * a_re

    def tables_moments():
        copies["up"].wait()
        copies["lift"].wait()
        base = up_v[...]
        first = [exact_dot(lift_v[0, k], base) for k in range(2)]
        for leaf in range(LEAVES):
            second = exact_dot(lift_v[1, leaf // 2], first[leaf % 2])
            high, low = halves(jnp.concatenate([base, first[leaf % 2], second], 0))
            mom_m[leaf] = jnp.concatenate([high, low], 1)

    def tables_lift():
        def pair(level):
            return exact_dot(lift_v[level, 0], selector(128, 32, 0, 128)) + exact_dot(
                lift_v[level, 1], selector(128, 32, 16, 128)
            )

        def blocks(level, copies_of):
            rows = jnp.concatenate([pair(level)] * copies_of, 0)
            row = lax.broadcasted_iota(jnp.int32, rows.shape, 0)
            lane = lax.broadcasted_iota(jnp.int32, rows.shape, 1)
            return jnp.where(lax.div(row, RANK) == lax.div(lane, 2 * RANK), rows, 0.0)

        three = blocks(2, 8)
        four = exact_dot(blocks(3, 2), three)
        five = exact_dot(blocks(4, 1), jnp.concatenate([four, jnp.zeros((96, 128), F32)], 0))
        whole = jnp.concatenate([four, three[32:64], five, three[:32]], 0)
        high, low = halves(whole)
        lift_m[...] = jnp.concatenate([high, low], 1)
        six = exact_dot(lift_v[5, 0], selector(128, 32, 0, 64)) + exact_dot(
            lift_v[5, 1], selector(128, 32, 16, 64)
        )
        high = six.astype(BF16).astype(F32)
        lane = lax.broadcasted_iota(jnp.int32, six.shape, 1)
        six_m[...] = jnp.where(lane < 32, high, six - high).astype(BF16)

    def tables_far():
        copies["spread"].wait()
        copies["down"].wait()
        row = lax.broadcasted_iota(jnp.int32, (RANK, LEAF), 0)
        lane = lax.broadcasted_iota(jnp.int32, (RANK, LEAF), 1)
        summing = (lax.div(lane, RANK) == row).astype(F32)
        chain = None
        for k in range(5):
            if k > 0:
                step = spread_v[1 + k, lax.rem(lax.div(t, 2 ** (k - 1)), 2)]
                chain = step if k == 1 else exact_dot(chain, step)
            high, low = halves(summing if k == 0 else exact_dot(chain, summing))
            red_m[k] = jnp.concatenate([high, low], 0)
        for leaf in range(LEAVES):
            near_step = spread_v[0, leaf % 2]
            both_steps = exact_dot(near_step, spread_v[1, leaf // 2])
            mix = (
                selector(LEAF, 48, 0, 144)
                + exact_dot(near_step, selector(LEAF, 48, 16, 144))
                + exact_dot(both_steps, selector(LEAF, 48, 32, 144))
            )
            whole = lax.dot_general(
                down_v[...], mix, (((0,), (0,)), ((), ())), precision=HIGHEST, preferred_element_type=F32
            )
            high = whole.astype(BF16).astype(F32)
            lane_at = lax.broadcasted_iota(jnp.int32, whole.shape, 1)
            far_m[leaf] = jnp.where(lane_at < 96, high, whole - high).astype(BF16)

    def scaled_rows(block, slots):
        rows = block_rows(block)
        squares = jnp.zeros((BLOCK, WIDTH), F32)
        columns = []
        for slot in slots:
            tokens = g[slot, rows, :].astype(F32)
            squares = squares + tokens * tokens
            scale = gain_v[:, pl.ds(pl.multiple_of(owners[slot] * WIDTH, WIDTH), WIDTH)]
            columns.append((tokens * scale).astype(BF16))
        return jnp.concatenate(columns, 1), squares[:, : WIDTH // 2] + squares[:, WIDTH // 2 :]

    def gather_part(block):
        scaled, squares = scaled_rows(block, (0, 1, 2))
        parts[block] = dot(scaled, w[:3].reshape(3 * WIDTH, 2 * WIDTH))
        part_squares[block] = squares

    def finished_sums(block):
        scaled, squares = scaled_rows(block, (3,))
        squares = jnp.sum(squares + part_squares[block], axis=1, keepdims=True)
        inverse = lax.rsqrt(squares / 1024 + 1e-06)
        value_sums = parts[block, :, :WIDTH] + dot(scaled, w[3, :, :WIDTH])
        gate_sums = parts[block, :, WIDTH:] + dot(scaled, w[3, :, WIDTH:])
        return value_sums, gate_sums, inverse

    def gates_of(block, sums, inverse):
        gate[block_rows(block), :] = jax.nn.sigmoid(sums * inverse)

    def project(block):
        value_sums, gate_sums, inverse = finished_sums(block)
        vals[block_rows(block), :] = (value_sums * inverse).astype(BF16)
        gates_of(block, gate_sums, inverse)

    def twice_rows(leaf):
        value = vals[leaf_rows(leaf), :]
        return jnp.concatenate([value, value], 0)

    def moments_of(leaf):
        moms[leaf] = dot(mom_m[leaf], twice_rows(leaf))

    def spectrum_of(leaf):
        spec[leaf] = dot(fwd_v[...], twice_rows(leaf))

    def near_rows(leaf):
        rows = leaf_rows(leaf)
        before = (leaf - 1 if leaf > 0 else LEAVES) if isinstance(leaf, int) else leaf - 1
        a_re, a_im = spec[leaf, :LEAF, :], spec[leaf, LEAF:, :]
        b_re, b_im = spec[before, :LEAF, :], spec[before, LEAF:, :]
        out_re = khat[0] * a_re - khat[1] * a_im + khat[2] * b_re - khat[3] * b_im
        out_im = khat[0] * a_im + khat[1] * a_re + khat[2] * b_im + khat[3] * b_re
        high, low = halves(jnp.concatenate([out_re, out_im], 0))
        total = dot(inv_v[...], jnp.concatenate([high, high], 0)) + dot(inv_v[:, : 2 * LEAF], low)
        near[rows, :] = total + skip_v[...] * vals[rows, :].astype(F32)

    def coupled(level, source_two, source_three):
        product = coup_v[level, 0] * source_two[None]
        if source_three is not None:
            product = product + coup_v[level, 1] * source_three[None]
        return product.reshape(RANK * RANK, WIDTH).astype(BF16)

    for block in range(WINDOW):
        send_direct(block)

    copies = {}

    def local(name, source, target):
        copies[name] = pltpu.make_async_copy(source, target, local_sem.at[len(copies)])
        copies[name].start()

    local("tok", tok, g.at[0])
    for slot in range(4):
        rows = pl.ds(pl.multiple_of(owners[slot] * WIDTH, WIDTH), WIDTH)
        local(("v", slot), w_value.at[rows], w.at[slot, :, pl.ds(0, WIDTH)])
        local(("g", slot), w_gate.at[rows], w.at[slot, :, pl.ds(WIDTH, WIDTH)])
    for name, source, target in (
        ("gain", gain, gain_v),
        ("phi", phi, phi_v),
        ("coeff", coeff, coeff_v),
        ("fwd", fwd, fwd_f),
        ("skip", skip, skip_v),
        ("up", up, up_v),
        ("down", down, down_v),
        ("lift", lift, lift_v),
        ("spread", spread, spread_v),
        ("inv", inv, inv_f),
        ("coup", coup, coup_v),
    ):
        local(name, source, target)

    @pl.when(z > 0)
    def _():
        signal(ready_next, t - PLANE, x)

    for k in range(1, PLANE):

        @pl.when(own >= k)
        def _():
            signal(ready_plane, t - k, x)

    def chain(place):
        @pl.when(z == PLANES - 1 - place)
        def _():
            if not isinstance(place, int) or place > 0:
                pl.semaphore_wait(ready_later, 1)

            @pl.when(z > 0)
            def _():
                signal(ready_later, t - PLANE, x)

    chain(0)
    for slot in range(4):
        copies["v", slot].wait()
        copies["g", slot].wait()
    copies["tok"].wait()
    copies["gain"].wait()

    halo_copy = pltpu.make_async_remote_copy(
        src_ref=vals.at[pl.ds(3 * LEAF, LEAF)],
        dst_ref=halo,
        send_sem=hsem.at[0],
        recv_sem=hsem.at[1],
        device_id=(t + 1, x),
        device_id_type=MESH,
    )

    def ctx_copy(part):
        return pltpu.make_async_remote_copy(
            src_ref=ctx_out.at[pl.ds(part * 32, 32)],
            dst_ref=ctx_in.at[pl.ds(part * 32, 32)],
            send_sem=csem.at[0, part],
            recv_sem=csem.at[1, part],
            device_id=(t + 1, x),
            device_id_type=MESH,
        )

    def first_near():
        @pl.when(t > 0)
        def _():
            halo_copy.wait_recv()

        before = halo[...]
        spec[LEAVES] = dot(fwd_v[...], jnp.concatenate([before, before], 0))
        near_rows(0)

    def answers():
        @pl.when(own < PLANE - 1)
        def _():
            pl.semaphore_wait(ready_plane, PLANE - 1 - own)

        @pl.when(z < PLANES - 1)
        def _():
            pl.semaphore_wait(ready_next, 1)

            @pl.when(y == 0)
            def _():
                signal(ready_edge, z * PLANE + 6, x)
                signal(ready_edge, z * PLANE + 7, x)

    def send_halo():
        @pl.when((y == 3) & (z < PLANES - 1))
        def _():
            pl.semaphore_wait(ready_edge, 2)

        @pl.when(t < PLANES * PLANE - 1)
        def _():
            halo_copy.start()

    def step(block, carry):
        pass_on(block)

        @pl.when(block + WINDOW < BLOCKS)
        def _():
            send_direct(block + WINDOW)

        gather_part(block)

        @pl.when(block > 0)
        def _():
            chain(block)

        @pl.when(block >= 2)
        def _():
            done = block - 2
            wait_relayed(done)
            project(done)

            @pl.when(lax.rem(done, 2) == 1)
            def _():
                leaf = leaf_of(done)
                moments_of(leaf)
                spectrum_of(leaf)

        @pl.when(block == 0)
        def _():
            tables_moments()
            tables_lift()

        @pl.when(block == 1)
        def _():
            answers()
            tables_near()

        @pl.when(block == 2)
        def _():
            tables_far()
            copies["inv"].wait()
            inv_v[...] = jnp.concatenate(halves(inv_f[...]), 1)
            copies["skip"].wait()
            copies["coup"].wait()

        @pl.when(block == 3)
        def _():
            send_halo()

        @pl.when(block == 6)
        def _():
            first_near()

        return carry

    lax.fori_loop(0, BLOCKS, step, 0)

    ctx_out[:32] = jnp.concatenate([moms[3, 0:16, :], moms[0, 16:32, :] + moms[1, 16:32, :]], 0).astype(BF16)

    @pl.when(t < PLANES * PLANE - 1)
    def _():
        ctx_copy(0).start()

    wait_relayed(6)
    project(6)
    wait_relayed(7)
    value_sums, gate_sums, inverse = finished_sums(7)
    vals[block_rows(7), :] = (value_sums * inverse).astype(BF16)
    moments_of(2)

    total = moms[0, 32:48, :] + moms[1, 32:48, :] + moms[2, 32:48, :] + moms[3, 32:48, :]
    m2[own] = total.astype(BF16)

    def plane_copy(k):
        return pltpu.make_async_remote_copy(
            src_ref=m2.at[own],
            dst_ref=m2.at[own],
            send_sem=s1.at[k - 1],
            recv_sem=r1.at[k - 1],
            device_id=(z * PLANE + lax.rem(own + k, PLANE), x),
            device_id_type=MESH,
        )

    def plane_arrival(k):
        return pltpu.make_async_remote_copy(
            src_ref=m2.at[own],
            dst_ref=m2.at[lax.rem(own + PLANE - k, PLANE)],
            send_sem=s1.at[k - 1],
            recv_sem=r1.at[k - 1],
            device_id=(z * PLANE + lax.rem(own + k, PLANE), x),
            device_id_type=MESH,
        )

    for k in range(1, PLANE):
        plane_copy(k).start()

    def next_plane_copy(target, source):
        return pltpu.make_async_remote_copy(
            src_ref=m2.at[own],
            dst_ref=m2_prev.at[source],
            send_sem=s1p.at[target],
            recv_sem=r1p.at[source],
            device_id=((z + 1) * PLANE + target, x),
            device_id_type=MESH,
        )

    @pl.when((y == 3) & (z < PLANES - 1))
    def _():
        for target in range(2):
            next_plane_copy(target, core).start()

    ctx_out[32:] = jnp.concatenate([moms[2, 0:16, :], moms[2, 16:32, :] + moms[3, 16:32, :]], 0).astype(BF16)

    @pl.when(t < PLANES * PLANE - 1)
    def _():
        ctx_copy(1).start()

    summing = red_m[0, :RANK, :]

    def gathered(level, source_two, source_three=None):
        return dot(summing, coupled(level, source_two, source_three))

    gates_of(7, gate_sums, inverse)
    spectrum_of(2)
    near_rows(1)
    near_rows(2)
    far0[2] = gathered(0, moms[0, 0:16, :])
    far0[3] = gathered(0, moms[1, 0:16, :], moms[0, 0:16, :])

    for way in range(2):
        for block in range(BLOCKS):
            direct(block, way).wait_send()
            relay(block, way).wait_send()

    for k in range(1, PLANE):
        plane_arrival(k).wait_recv()
    stack = m2[...].reshape(PLANE * RANK, WIDTH)
    lifted = dot(lift_m[...], jnp.concatenate([stack, stack], 0))
    pack_out[...] = lifted[:80].astype(BF16)


    def pack_copy(rows):
        return pltpu.make_async_remote_copy(
            src_ref=pack_out.at[pl.ds(0, rows)],
            dst_ref=pack_in.at[pl.ds(0, rows)],
            send_sem=s2,
            recv_sem=r2,
            device_id=(t + PLANE, x),
            device_id_type=MESH,
        )

    def five_copy(k):
        return pltpu.make_async_remote_copy(
            src_ref=pack_out.at[pl.ds(64, RANK)],
            dst_ref=m5_in.at[k],
            send_sem=s5.at[k],
            recv_sem=r5.at[k],
            device_id=(t + k * PLANE, x),
            device_id_type=MESH,
        )

    @pl.when((z < PLANES - 1) & (y < 2))
    def _():
        pack_copy(64).start()

    @pl.when((z < PLANES - 1) & (y >= 2))
    def _():
        pack_copy(32).start()

    for k in range(2, PLANES):

        @pl.when(z + k < PLANES)
        def _():
            five_copy(k).start()

    near_rows(3)

    @pl.when(t > 0)
    def _():
        ctx_copy(0).wait_recv()
        ctx_copy(1).wait_recv()

    prev = ctx_in[...].astype(F32)
    far1[0] = gathered(1, prev[16:32])
    far0[0] = gathered(0, prev[32:48])
    far0[1] = gathered(0, prev[0:16], prev[32:48])
    far1[1] = gathered(1, prev[48:64], prev[16:32])

    for k in range(1, PLANE):
        plane_copy(k).wait_send()

    @pl.when(t < PLANES * PLANE - 1)
    def _():
        halo_copy.wait_send()
        ctx_copy(0).wait_send()
        ctx_copy(1).wait_send()

    @pl.when((y == 3) & (z < PLANES - 1))
    def _():
        for target in range(2):
            next_plane_copy(target, core).wait_send()

    @pl.when((y == 0) & (z > 0))
    def _():
        for source in range(2):
            next_plane_copy(source, source).wait_recv()

    def reduced(k, source_two, source_three):
        return dot(red_m[k], coupled(2 + k, source_two, source_three))

    at = 2 * jnp.maximum(y - 1, 0)
    inside = y > 0
    two = jnp.where(inside, m2[at + core], m2_prev[core]).astype(F32)
    three = jnp.where(inside, m2[at], m2_prev[0]).astype(F32) * core.astype(F32)
    expansion = reduced(0, two, three)

    @pl.when((z > 0) & (y < 2))
    def _():
        pack_copy(64).wait_recv()

    @pl.when((z > 0) & (y >= 2))
    def _():
        pack_copy(32).wait_recv()

    odd = lax.rem(y, 2)
    lower = y < 2
    here = jnp.where(odd == 1, lifted[96:112], lifted[80:96])
    coming = pack_in[pl.ds(pl.multiple_of(32 + odd * RANK, RANK), RANK), :].astype(F32)
    two = jnp.where(lower, coming, here)
    three = jnp.where(lower, pack_in[32:48, :].astype(F32), lifted[80:96]) * odd.astype(F32)
    expansion = expansion + reduced(1, two, three)
    odd = lax.div(y, 2)
    two = pack_in[pl.ds(pl.multiple_of(odd * RANK, RANK), RANK), :].astype(F32)
    three = pack_in[0:16, :].astype(F32) * odd.astype(F32)
    expansion = expansion + reduced(2, two, three)

    for k in range(2, PLANES):

        @pl.when(z >= k)
        def _():
            five_copy(k).wait_recv()

    odd = lax.rem(z, 2)
    expansion = expansion + reduced(
        3, m5_in[2].astype(F32), m5_in[3].astype(F32) * odd.astype(F32)
    )
    pad = jnp.zeros((64, WIDTH), BF16)

    def sixth(base):
        pair = [m5_in[base], m5_in[base - 1]]
        return dot(six_m[...], jnp.concatenate(pair + pair + [pad], 0))

    odd_six = lax.rem(lax.div(z, 2), 2)
    expansion = expansion + reduced(
        4, sixth(4 + odd), sixth(6 + odd) * odd_six.astype(F32)
    )

    expansion = expansion[:RANK] + expansion[RANK:]

    def out_copy(leaf):
        rows = leaf_rows(leaf)
        return pltpu.make_async_copy(out_v.at[rows], out.at[rows], osem.at[leaf])

    for leaf in range(LEAVES):
        rows = leaf_rows(leaf)
        high, low = halves(jnp.concatenate([far0[leaf], far1[leaf // 2], expansion], 0))
        whole = jnp.concatenate([high, low, high, jnp.zeros((112, WIDTH), BF16)], 0)
        combined = near[rows, :] + dot(far_m[leaf], whole)
        out_v[rows, :] = (gate[rows, :] * combined).astype(BF16)
        out_copy(leaf).start()

    @pl.when((z < PLANES - 1) & (y < 2))
    def _():
        pack_copy(64).wait_send()

    @pl.when((z < PLANES - 1) & (y >= 2))
    def _():
        pack_copy(32).wait_send()

    for k in range(2, PLANES):

        @pl.when(z + k < PLANES)
        def _():
            five_copy(k).wait_send()

    for leaf in range(LEAVES):
        out_copy(leaf).wait()


def per_device(
    tokens,
    norm_gain,
    w_value,
    w_gate,
    phi_taps,
    tap_coeff,
    skip_gain,
    basis_up,
    basis_down,
    lift_maps,
    spread_maps,
    couplings,
):
    forward, inverse = transform_tables()
    in_hbm = pl.BlockSpec(memory_space=pltpu.HBM)
    frames = LEAF * LEAVES
    vmem = pltpu.VMEM
    dma = pltpu.SemaphoreType.DMA
    scratch = [
        vmem((4, frames, WIDTH), BF16),
        vmem((4, WIDTH, 2 * WIDTH), BF16),
        vmem((1, 4 * WIDTH), F32),
        vmem(phi_taps.shape, F32),
        vmem(tap_coeff.shape, F32),
        vmem((1, WIDTH), F32),
        vmem(basis_up.shape, F32),
        vmem(basis_down.shape, F32),
        vmem(lift_maps.shape, F32),
        vmem(spread_maps.shape, F32),
        vmem(couplings.shape, F32),
        vmem(forward.shape, F32),
        vmem(inverse.shape, F32),
        vmem((2 * LEAF, 2 * LEAF), BF16),
        vmem((LEAF, 4 * LEAF), BF16),
        vmem((frames, WIDTH), BF16),
        vmem((LEAF, WIDTH), BF16),
        vmem((frames, WIDTH), F32),
        vmem((frames, WIDTH), F32),
        vmem((LEAVES + 1, 2 * LEAF, WIDTH), F32),
        vmem((4, LEAF, WIDTH), F32),
        vmem((LEAVES, 48, 2 * LEAF), BF16),
        vmem((112, 256), BF16),
        vmem((RANK, 128), BF16),
        vmem((LEAVES, LEAF, LEAF), BF16),
        vmem((5, 2 * RANK, LEAF), BF16),
        vmem((LEAVES, 48, WIDTH), F32),
        vmem((PLANE, RANK, WIDTH), BF16),
        vmem((2, RANK, WIDTH), BF16),
        vmem((64, WIDTH), BF16),
        vmem((64, WIDTH), BF16),
        vmem((80, WIDTH), BF16),
        vmem((64, WIDTH), BF16),
        vmem((PLANES, RANK, WIDTH), BF16),
        vmem((LEAVES, RANK, WIDTH), F32),
        vmem((2, RANK, WIDTH), F32),
        vmem((frames, WIDTH), BF16),
        vmem((BLOCKS, BLOCK, 2 * WIDTH), F32),
        vmem((BLOCKS, BLOCK, WIDTH // 2), F32),
        dma((20,)),
        dma((2, BLOCKS)),
        dma((2, BLOCKS)),
        dma((2, BLOCKS)),
        dma((2, BLOCKS)),
        dma((2,)),
        dma((2, 2)),
        dma((PLANE - 1,)),
        dma((PLANE - 1,)),
        dma((2,)),
        dma((2,)),
        dma(()),
        dma(()),
        dma((PLANES,)),
        dma((PLANES,)),
        pltpu.SemaphoreType.REGULAR,
        pltpu.SemaphoreType.REGULAR,
        pltpu.SemaphoreType.REGULAR,
        pltpu.SemaphoreType.REGULAR,
        dma((LEAVES,)),
    ]
    return pl.pallas_call(
        body,
        out_shape=jax.ShapeDtypeStruct(tokens.shape, BF16),
        in_specs=[in_hbm] * 14,
        out_specs=in_hbm,
        scratch_shapes=scratch,
        compiler_params=pltpu.CompilerParams(
            collective_id=0, has_side_effects=True, vmem_limit_bytes=60 * 1024 * 1024
        ),
        cost_estimate=pl.CostEstimate(flops=4 * 10**9, bytes_accessed=8 * 10**6, transcendentals=10**6),
    )(
        tokens,
        norm_gain.reshape(1, -1),
        w_value,
        w_gate,
        phi_taps,
        tap_coeff,
        skip_gain.reshape(1, -1),
        basis_up,
        basis_down,
        lift_maps,
        spread_maps,
        couplings,
        jnp.asarray(forward),
        jnp.asarray(inverse),
    )


def solution(mesh):
    placed = (
        P("tm", "chan"),
        P(),
        P(None, "chan"),
        P(None, "chan"),
        P(),
        P(None, "chan"),
        P("chan"),
        P(),
        P(),
        P(),
        P(),
        P(None, None, None, None, "chan"),
    )
    return jax.shard_map(
        per_device, mesh=mesh, in_specs=placed, out_specs=P("tm", "chan"), check_vma=False
    )
```

```python
import jax
import jax.numpy as jnp
import numpy as np
from jax import lax
from jax.experimental import pallas as pl
from jax.experimental.pallas import tpu as pltpu
from jax.sharding import PartitionSpec as P

MESH = pl.DeviceIdType.MESH
F32 = jnp.float32
BF16 = jnp.bfloat16
HIGHEST = lax.Precision.HIGHEST

LEAF = 256
LEAVES = 4
WIDTH = 256
RANK = 16
PLANES = 8
PLANE = 8


def transform_tables():
    odd = np.arange(LEAF)[:, None] + 0.5
    angle = 2 * np.pi * odd * np.arange(LEAF)[None, :] / (2 * LEAF)
    forward = np.concatenate([np.cos(angle), -np.sin(angle)], 0)
    return forward.astype(np.float32), (forward.T / LEAF).astype(np.float32)


def exact_dot(left, right):
    return jnp.dot(left, right, precision=HIGHEST, preferred_element_type=F32)


def dot(left, right):
    return jnp.dot(left, right, preferred_element_type=F32)


def halves(value):
    high = value.astype(BF16)
    return high, (value - high.astype(F32)).astype(BF16)


def selector(lanes, period, shift, limit):
    row = lax.broadcasted_iota(jnp.int32, (RANK, lanes), 0)
    lane = lax.broadcasted_iota(jnp.int32, (RANK, lanes), 1)
    return ((lax.rem(lane, period) == row + shift) & (lane < limit)).astype(F32)


def body(
    tok, gain, w_value, w_gate, phi, coeff, skip, up, down, lift, spread, coup, fwd, inv,
    out,
    g, w, gain_v, phi_v, coeff_v, skip_v, up_v, down_v, lift_v, spread_v, coup_v, fwd_f, inv_f, fwd_v, inv_v,
    vals, halo, gate, near, spec, khat, mom_m, lift_m, six_m, far_m, red_m, moms,
    m2, m2_prev, ctx_out, ctx_in, pack_out, pack_in, m5_in, far0, far1, out_v, parts, part_squares,
    local_sem, dsend, drecv, rsend, rrecv, hsem, csem, s1, r1, s1p, r1p, s2, r2, s5, r5, ready_plane, ready_next, ready_edge, ready_later, osem,
):
    t = lax.axis_index("tm")
    x = lax.axis_index("chan")
    core = lax.rem(t, 2)
    y = lax.rem(lax.div(t, 2), 4)
    z = lax.div(t, PLANE)
    own = lax.rem(t, PLANE)
    right, left = lax.rem(x + 1, 4), lax.rem(x + 3, 4)

    barrier = pltpu.get_barrier_semaphore()

    def signal(semaphore, frames, chans):
        pl.semaphore_signal(semaphore, inc=1, device_id=(frames, chans), device_id_type=MESH)

    signal(barrier, t, right)
    signal(barrier, t, left)

    @pl.when(z < PLANES - 1)
    def _():
        signal(barrier, t + PLANE, x)

    for k in range(1, PLANE):

        @pl.when(own + k < PLANE)
        def _():
            signal(barrier, t + k, x)

    m2_prev[...] = jnp.zeros_like(m2_prev)
    ctx_in[...] = jnp.zeros_like(ctx_in)
    pack_in[...] = jnp.zeros_like(pack_in)
    m5_in[...] = jnp.zeros_like(m5_in)
    halo[...] = jnp.zeros_like(halo)

    pl.semaphore_wait(barrier, 2 + own + jnp.where(z > 0, 1, 0))

    owners = [x, left, right, lax.rem(x + 2, 4)]

    def leaf_at(place):
        return (place + 3) % LEAVES if isinstance(place, int) else lax.rem(place + 3, LEAVES)

    def leaf_rows(leaf):
        return pl.ds(leaf * LEAF if isinstance(leaf, int) else pl.multiple_of(leaf * LEAF, LEAF), LEAF)

    def direct(leaf, way):
        rows = leaf_rows(leaf)
        return pltpu.make_async_remote_copy(
            src_ref=tok.at[rows],
            dst_ref=g.at[1 + way, rows],
            send_sem=dsend.at[way, leaf],
            recv_sem=drecv.at[way, leaf],
            device_id=(t, left if way else right),
            device_id_type=MESH,
        )

    def relay(leaf, way):
        start = leaf * LEAF + way * (LEAF // 2)
        rows = pl.ds(start if isinstance(leaf, int) else pl.multiple_of(start, LEAF // 2), LEAF // 2)
        return pltpu.make_async_remote_copy(
            src_ref=g.at[1 + way, rows],
            dst_ref=g.at[3, rows],
            send_sem=rsend.at[way, leaf],
            recv_sem=rrecv.at[way, leaf],
            device_id=(t, left if way else right),
            device_id_type=MESH,
        )

    def send_direct(place):
        for way in range(2):
            direct(leaf_at(place), way).start()

    def pass_on(place):
        for way in range(2):
            direct(leaf_at(place), way).wait_recv()
            relay(leaf_at(place), way).start()

    def wait_relayed(place):
        for way in range(2):
            relay(leaf_at(place), way).wait_recv()

    def tables_near():
        for name in ("phi", "coeff", "fwd"):
            copies[name].wait()
        fwd_v[...] = jnp.concatenate(halves(fwd_f[...]), 1)
        taps = phi_v[...].astype(BF16).astype(F32)
        kernel_taps = lax.dot_general(
            taps, coeff_v[...], (((0,), (0,)), ((), ())), precision=HIGHEST, preferred_element_type=F32
        )
        both = jnp.concatenate([kernel_taps[:LEAF], kernel_taps[LEAF:]], 1)
        high, low = halves(both)
        hat = dot(fwd_v[...], jnp.concatenate([high, high], 0)) + dot(fwd_v[:, :LEAF], low)
        a_re, a_im = hat[:LEAF, :WIDTH], hat[LEAF:, :WIDTH]
        b_re, b_im = hat[:LEAF, WIDTH:], hat[LEAF:, WIDTH:]
        row = lax.broadcasted_iota(jnp.int32, (LEAF, WIDTH), 0)
        sign = (1 - 2 * lax.rem(row, 2)).astype(F32)
        khat[0] = a_re
        khat[1] = a_im
        khat[2] = b_re - sign * a_im
        khat[3] = b_im + sign * a_re

    def tables_moments():
        copies["up"].wait()
        copies["lift"].wait()
        base = up_v[...]
        first = [exact_dot(lift_v[0, k], base) for k in range(2)]
        for leaf in range(LEAVES):
            second = exact_dot(lift_v[1, leaf // 2], first[leaf % 2])
            high, low = halves(jnp.concatenate([base, first[leaf % 2], second], 0))
            mom_m[leaf] = jnp.concatenate([high, low], 1)

    def tables_lift():
        def pair(level):
            return exact_dot(lift_v[level, 0], selector(128, 32, 0, 128)) + exact_dot(
                lift_v[level, 1], selector(128, 32, 16, 128)
            )

        def blocks(level, copies_of):
            rows = jnp.concatenate([pair(level)] * copies_of, 0)
            row = lax.broadcasted_iota(jnp.int32, rows.shape, 0)
            lane = lax.broadcasted_iota(jnp.int32, rows.shape, 1)
            return jnp.where(lax.div(row, RANK) == lax.div(lane, 2 * RANK), rows, 0.0)

        three = blocks(2, 8)
        four = exact_dot(blocks(3, 2), three)
        five = exact_dot(blocks(4, 1), jnp.concatenate([four, jnp.zeros((96, 128), F32)], 0))
        whole = jnp.concatenate([four, three[32:64], five, three[:32]], 0)
        high, low = halves(whole)
        lift_m[...] = jnp.concatenate([high, low], 1)
        six = exact_dot(lift_v[5, 0], selector(128, 32, 0, 64)) + exact_dot(
            lift_v[5, 1], selector(128, 32, 16, 64)
        )
        high = six.astype(BF16).astype(F32)
        lane = lax.broadcasted_iota(jnp.int32, six.shape, 1)
        six_m[...] = jnp.where(lane < 32, high, six - high).astype(BF16)

    def tables_far():
        copies["spread"].wait()
        copies["down"].wait()
        row = lax.broadcasted_iota(jnp.int32, (RANK, LEAF), 0)
        lane = lax.broadcasted_iota(jnp.int32, (RANK, LEAF), 1)
        summing = (lax.div(lane, RANK) == row).astype(F32)
        chain = None
        for k in range(5):
            if k > 0:
                step = spread_v[1 + k, lax.rem(lax.div(t, 2 ** (k - 1)), 2)]
                chain = step if k == 1 else exact_dot(chain, step)
            high, low = halves(summing if k == 0 else exact_dot(chain, summing))
            red_m[k] = jnp.concatenate([high, low], 0)
        for leaf in range(LEAVES):
            near_step = spread_v[0, leaf % 2]
            both_steps = exact_dot(near_step, spread_v[1, leaf // 2])
            mix = (
                selector(LEAF, 48, 0, 144)
                + exact_dot(near_step, selector(LEAF, 48, 16, 144))
                + exact_dot(both_steps, selector(LEAF, 48, 32, 144))
            )
            whole = lax.dot_general(
                down_v[...], mix, (((0,), (0,)), ((), ())), precision=HIGHEST, preferred_element_type=F32
            )
            high = whole.astype(BF16).astype(F32)
            lane_at = lax.broadcasted_iota(jnp.int32, whole.shape, 1)
            far_m[leaf] = jnp.where(lane_at < 96, high, whole - high).astype(BF16)

    def scaled_rows(leaf, slots):
        rows = leaf_rows(leaf)
        squares = jnp.zeros((LEAF, WIDTH), F32)
        columns = []
        for slot in slots:
            tokens = g[slot, rows, :].astype(F32)
            squares = squares + tokens * tokens
            scale = gain_v[:, pl.ds(pl.multiple_of(owners[slot] * WIDTH, WIDTH), WIDTH)]
            columns.append((tokens * scale).astype(BF16))
        return jnp.concatenate(columns, 1), squares

    def inverse_of(squares):
        return lax.rsqrt(jnp.sum(squares, axis=1, keepdims=True) / 1024 + 1e-06)

    def values_of(leaf, sums, inverse):
        value = (sums * inverse).astype(BF16)
        vals[leaf_rows(leaf), :] = value
        twice = jnp.concatenate([value, value], 0)
        moms[leaf] = dot(mom_m[leaf], twice)
        return twice

    def gates_of(leaf, sums, inverse):
        gate[leaf_rows(leaf), :] = jax.nn.sigmoid(sums * inverse)

    def gather_part(leaf):
        scaled, squares = scaled_rows(leaf, (0, 1, 2))
        parts[leaf] = dot(scaled, w[:3].reshape(3 * WIDTH, 2 * WIDTH))
        part_squares[leaf] = squares[:, : WIDTH // 2] + squares[:, WIDTH // 2 :]

    def finished_sums(leaf):
        scaled, squares = scaled_rows(leaf, (3,))
        inverse = inverse_of(squares[:, : WIDTH // 2] + squares[:, WIDTH // 2 :] + part_squares[leaf])
        value_sums = parts[leaf, :, :WIDTH] + dot(scaled, w[3, :, :WIDTH])
        gate_sums = parts[leaf, :, WIDTH:] + dot(scaled, w[3, :, WIDTH:])
        return value_sums, gate_sums, inverse

    def project(leaf):
        value_sums, gate_sums, inverse = finished_sums(leaf)
        twice = values_of(leaf, value_sums, inverse)
        gates_of(leaf, gate_sums, inverse)
        spec[leaf] = dot(fwd_v[...], twice)

    def near_rows(leaf):
        rows = leaf_rows(leaf)
        before = (leaf - 1 if leaf > 0 else LEAVES) if isinstance(leaf, int) else leaf - 1
        a_re, a_im = spec[leaf, :LEAF, :], spec[leaf, LEAF:, :]
        b_re, b_im = spec[before, :LEAF, :], spec[before, LEAF:, :]
        out_re = khat[0] * a_re - khat[1] * a_im + khat[2] * b_re - khat[3] * b_im
        out_im = khat[0] * a_im + khat[1] * a_re + khat[2] * b_im + khat[3] * b_re
        both = jnp.concatenate([out_re, out_im], 0).astype(BF16)
        total = dot(inv_v[...], jnp.concatenate([both, both], 0))
        near[rows, :] = total + skip_v[...] * vals[rows, :].astype(F32)

    def coupled(level, source_two, source_three):
        product = coup_v[level, 0] * source_two[None]
        if source_three is not None:
            product = product + coup_v[level, 1] * source_three[None]
        return product.reshape(RANK * RANK, WIDTH).astype(BF16)

    for place in range(LEAVES - 1):
        send_direct(place)

    copies = {}

    def local(name, source, target):
        copies[name] = pltpu.make_async_copy(source, target, local_sem.at[len(copies)])
        copies[name].start()

    local("tok", tok, g.at[0])
    for slot in range(4):
        rows = pl.ds(pl.multiple_of(owners[slot] * WIDTH, WIDTH), WIDTH)
        local(("v", slot), w_value.at[rows], w.at[slot, :, pl.ds(0, WIDTH)])
        local(("g", slot), w_gate.at[rows], w.at[slot, :, pl.ds(WIDTH, WIDTH)])
    for name, source, target in (
        ("gain", gain, gain_v),
        ("phi", phi, phi_v),
        ("coeff", coeff, coeff_v),
        ("fwd", fwd, fwd_f),
        ("skip", skip, skip_v),
        ("up", up, up_v),
        ("down", down, down_v),
        ("lift", lift, lift_v),
        ("spread", spread, spread_v),
        ("inv", inv, inv_f),
        ("coup", coup, coup_v),
    ):
        local(name, source, target)

    @pl.when(z > 0)
    def _():
        signal(ready_next, t - PLANE, x)

    for k in range(1, PLANE):

        @pl.when(own >= k)
        def _():
            signal(ready_plane, t - k, x)

    def chain(place):
        @pl.when(z == PLANES - 1 - place)
        def _():
            if not isinstance(place, int) or place > 0:
                pl.semaphore_wait(ready_later, 1)
            if not isinstance(place, int) or place < PLANES - 1:
                signal(ready_later, t - PLANE, x)

    chain(0)
    tables_near()
    chain(1)
    tables_moments()
    tables_lift()
    chain(2)

    @pl.when(own < PLANE - 1)
    def _():
        pl.semaphore_wait(ready_plane, PLANE - 1 - own)

    @pl.when(z < PLANES - 1)
    def _():
        pl.semaphore_wait(ready_next, 1)

        @pl.when(y == 0)
        def _():
            signal(ready_edge, z * PLANE + 6, x)
            signal(ready_edge, z * PLANE + 7, x)

    for slot in range(4):
        copies["v", slot].wait()
        copies["g", slot].wait()
    for name in ("tok", "gain", "skip", "coup", "inv"):
        copies[name].wait()

    def arrive(place, carry):
        gather_part(leaf_at(place))
        return carry

    tables_far()
    inv_v[...] = jnp.concatenate(halves(inv_f[...]), 1)
    pass_on(0)
    send_direct(3)
    pass_on(1)
    pass_on(2)
    lax.fori_loop(0, 3, arrive, 0)
    chain(3)

    @pl.when((y == 3) & (z < PLANES - 1))
    def _():
        pl.semaphore_wait(ready_edge, 2)

    halo_copy = pltpu.make_async_remote_copy(
        src_ref=vals.at[pl.ds(3 * LEAF, LEAF)],
        dst_ref=halo,
        send_sem=hsem.at[0],
        recv_sem=hsem.at[1],
        device_id=(t + 1, x),
        device_id_type=MESH,
    )

    def ctx_copy(part):
        return pltpu.make_async_remote_copy(
            src_ref=ctx_out.at[pl.ds(part * 32, 32)],
            dst_ref=ctx_in.at[pl.ds(part * 32, 32)],
            send_sem=csem.at[0, part],
            recv_sem=csem.at[1, part],
            device_id=(t + 1, x),
            device_id_type=MESH,
        )

    def step(i, carry):
        wait_relayed(i)
        project(leaf_at(i))

        @pl.when((i == 0) & (t < PLANES * PLANE - 1))
        def _():
            halo_copy.start()

        chain(4 + i)

        @pl.when(i == 1)
        def _():
            pass_on(3)
            gather_part(2)

        return carry

    lax.fori_loop(0, 3, step, 0)

    ctx_out[:32] = jnp.concatenate([moms[3, 0:16, :], moms[0, 16:32, :] + moms[1, 16:32, :]], 0).astype(BF16)

    @pl.when(t < PLANES * PLANE - 1)
    def _():
        ctx_copy(0).start()

    @pl.when(t > 0)
    def _():
        halo_copy.wait_recv()

    before = halo[...]
    spec[LEAVES] = dot(fwd_v[...], jnp.concatenate([before, before], 0))
    near_rows(0)

    wait_relayed(3)
    value_sums, gate_sums, inverse = finished_sums(2)
    twice = values_of(2, value_sums, inverse)

    chain(7)

    total = moms[0, 32:48, :] + moms[1, 32:48, :] + moms[2, 32:48, :] + moms[3, 32:48, :]
    m2[own] = total.astype(BF16)

    def plane_copy(k):
        return pltpu.make_async_remote_copy(
            src_ref=m2.at[own],
            dst_ref=m2.at[own],
            send_sem=s1.at[k - 1],
            recv_sem=r1.at[k - 1],
            device_id=(z * PLANE + lax.rem(own + k, PLANE), x),
            device_id_type=MESH,
        )

    def plane_arrival(k):
        return pltpu.make_async_remote_copy(
            src_ref=m2.at[own],
            dst_ref=m2.at[lax.rem(own + PLANE - k, PLANE)],
            send_sem=s1.at[k - 1],
            recv_sem=r1.at[k - 1],
            device_id=(z * PLANE + lax.rem(own + k, PLANE), x),
            device_id_type=MESH,
        )

    for k in range(1, PLANE):
        plane_copy(k).start()

    def next_plane_copy(target, source):
        return pltpu.make_async_remote_copy(
            src_ref=m2.at[own],
            dst_ref=m2_prev.at[source],
            send_sem=s1p.at[target],
            recv_sem=r1p.at[source],
            device_id=((z + 1) * PLANE + target, x),
            device_id_type=MESH,
        )

    @pl.when((y == 3) & (z < PLANES - 1))
    def _():
        for target in range(2):
            next_plane_copy(target, core).start()

    ctx_out[32:] = jnp.concatenate([moms[2, 0:16, :], moms[2, 16:32, :] + moms[3, 16:32, :]], 0).astype(BF16)

    @pl.when(t < PLANES * PLANE - 1)
    def _():
        ctx_copy(1).start()

    summing = red_m[0, :RANK, :]

    def gathered(level, source_two, source_three=None):
        return dot(summing, coupled(level, source_two, source_three))

    gates_of(2, gate_sums, inverse)
    spec[2] = dot(fwd_v[...], twice)
    near_rows(1)
    near_rows(2)
    far0[2] = gathered(0, moms[0, 0:16, :])
    far0[3] = gathered(0, moms[1, 0:16, :], moms[0, 0:16, :])

    for way in range(2):
        for leaf in range(LEAVES):
            direct(leaf, way).wait_send()
            relay(leaf, way).wait_send()

    for k in range(1, PLANE):
        plane_arrival(k).wait_recv()
    stack = m2[...].reshape(PLANE * RANK, WIDTH)
    lifted = dot(lift_m[...], jnp.concatenate([stack, stack], 0))
    pack_out[...] = lifted[:80].astype(BF16)


    def pack_copy(rows):
        return pltpu.make_async_remote_copy(
            src_ref=pack_out.at[pl.ds(0, rows)],
            dst_ref=pack_in.at[pl.ds(0, rows)],
            send_sem=s2,
            recv_sem=r2,
            device_id=(t + PLANE, x),
            device_id_type=MESH,
        )

    def five_copy(k):
        return pltpu.make_async_remote_copy(
            src_ref=pack_out.at[pl.ds(64, RANK)],
            dst_ref=m5_in.at[k],
            send_sem=s5.at[k],
            recv_sem=r5.at[k],
            device_id=(t + k * PLANE, x),
            device_id_type=MESH,
        )

    @pl.when((z < PLANES - 1) & (y < 2))
    def _():
        pack_copy(64).start()

    @pl.when((z < PLANES - 1) & (y >= 2))
    def _():
        pack_copy(32).start()

    for k in range(2, PLANES):

        @pl.when(z + k < PLANES)
        def _():
            five_copy(k).start()

    near_rows(3)

    @pl.when(t > 0)
    def _():
        ctx_copy(0).wait_recv()
        ctx_copy(1).wait_recv()

    prev = ctx_in[...].astype(F32)
    far1[0] = gathered(1, prev[16:32])
    far0[0] = gathered(0, prev[32:48])
    far0[1] = gathered(0, prev[0:16], prev[32:48])
    far1[1] = gathered(1, prev[48:64], prev[16:32])

    for k in range(1, PLANE):
        plane_copy(k).wait_send()

    @pl.when(t < PLANES * PLANE - 1)
    def _():
        halo_copy.wait_send()
        ctx_copy(0).wait_send()
        ctx_copy(1).wait_send()

    @pl.when((y == 3) & (z < PLANES - 1))
    def _():
        for target in range(2):
            next_plane_copy(target, core).wait_send()

    @pl.when((y == 0) & (z > 0))
    def _():
        for source in range(2):
            next_plane_copy(source, source).wait_recv()

    def reduced(k, source_two, source_three):
        return dot(red_m[k], coupled(2 + k, source_two, source_three))

    at = 2 * jnp.maximum(y - 1, 0)
    inside = y > 0
    two = jnp.where(inside, m2[at + core], m2_prev[core]).astype(F32)
    three = jnp.where(inside, m2[at], m2_prev[0]).astype(F32) * core.astype(F32)
    expansion = reduced(0, two, three)

    @pl.when((z > 0) & (y < 2))
    def _():
        pack_copy(64).wait_recv()

    @pl.when((z > 0) & (y >= 2))
    def _():
        pack_copy(32).wait_recv()

    odd = lax.rem(y, 2)
    lower = y < 2
    here = jnp.where(odd == 1, lifted[96:112], lifted[80:96])
    coming = pack_in[pl.ds(pl.multiple_of(32 + odd * RANK, RANK), RANK), :].astype(F32)
    two = jnp.where(lower, coming, here)
    three = jnp.where(lower, pack_in[32:48, :].astype(F32), lifted[80:96]) * odd.astype(F32)
    expansion = expansion + reduced(1, two, three)
    odd = lax.div(y, 2)
    two = pack_in[pl.ds(pl.multiple_of(odd * RANK, RANK), RANK), :].astype(F32)
    three = pack_in[0:16, :].astype(F32) * odd.astype(F32)
    expansion = expansion + reduced(2, two, three)

    for k in range(2, PLANES):

        @pl.when(z >= k)
        def _():
            five_copy(k).wait_recv()

    odd = lax.rem(z, 2)
    expansion = expansion + reduced(
        3, m5_in[2].astype(F32), m5_in[3].astype(F32) * odd.astype(F32)
    )
    pad = jnp.zeros((64, WIDTH), BF16)

    def sixth(base):
        pair = [m5_in[base], m5_in[base - 1]]
        return dot(six_m[...], jnp.concatenate(pair + pair + [pad], 0))

    odd_six = lax.rem(lax.div(z, 2), 2)
    expansion = expansion + reduced(
        4, sixth(4 + odd), sixth(6 + odd) * odd_six.astype(F32)
    )

    expansion = expansion[:RANK] + expansion[RANK:]

    def out_copy(leaf):
        rows = leaf_rows(leaf)
        return pltpu.make_async_copy(out_v.at[rows], out.at[rows], osem.at[leaf])

    for leaf in range(LEAVES):
        rows = leaf_rows(leaf)
        high, low = halves(jnp.concatenate([far0[leaf], far1[leaf // 2], expansion], 0))
        whole = jnp.concatenate([high, low, high, jnp.zeros((112, WIDTH), BF16)], 0)
        combined = near[rows, :] + dot(far_m[leaf], whole)
        out_v[rows, :] = (gate[rows, :] * combined).astype(BF16)
        out_copy(leaf).start()

    @pl.when((z < PLANES - 1) & (y < 2))
    def _():
        pack_copy(64).wait_send()

    @pl.when((z < PLANES - 1) & (y >= 2))
    def _():
        pack_copy(32).wait_send()

    for k in range(2, PLANES):

        @pl.when(z + k < PLANES)
        def _():
            five_copy(k).wait_send()

    for leaf in range(LEAVES):
        out_copy(leaf).wait()


def per_device(
    tokens,
    norm_gain,
    w_value,
    w_gate,
    phi_taps,
    tap_coeff,
    skip_gain,
    basis_up,
    basis_down,
    lift_maps,
    spread_maps,
    couplings,
):
    forward, inverse = transform_tables()
    in_hbm = pl.BlockSpec(memory_space=pltpu.HBM)
    frames = LEAF * LEAVES
    vmem = pltpu.VMEM
    dma = pltpu.SemaphoreType.DMA
    scratch = [
        vmem((4, frames, WIDTH), BF16),
        vmem((4, WIDTH, 2 * WIDTH), BF16),
        vmem((1, 4 * WIDTH), F32),
        vmem(phi_taps.shape, F32),
        vmem(tap_coeff.shape, F32),
        vmem((1, WIDTH), F32),
        vmem(basis_up.shape, F32),
        vmem(basis_down.shape, F32),
        vmem(lift_maps.shape, F32),
        vmem(spread_maps.shape, F32),
        vmem(couplings.shape, F32),
        vmem(forward.shape, F32),
        vmem(inverse.shape, F32),
        vmem((2 * LEAF, 2 * LEAF), BF16),
        vmem((LEAF, 4 * LEAF), BF16),
        vmem((frames, WIDTH), BF16),
        vmem((LEAF, WIDTH), BF16),
        vmem((frames, WIDTH), F32),
        vmem((frames, WIDTH), F32),
        vmem((LEAVES + 1, 2 * LEAF, WIDTH), F32),
        vmem((4, LEAF, WIDTH), F32),
        vmem((LEAVES, 48, 2 * LEAF), BF16),
        vmem((112, 256), BF16),
        vmem((RANK, 128), BF16),
        vmem((LEAVES, LEAF, LEAF), BF16),
        vmem((5, 2 * RANK, LEAF), BF16),
        vmem((LEAVES, 48, WIDTH), F32),
        vmem((PLANE, RANK, WIDTH), BF16),
        vmem((2, RANK, WIDTH), BF16),
        vmem((64, WIDTH), BF16),
        vmem((64, WIDTH), BF16),
        vmem((80, WIDTH), BF16),
        vmem((64, WIDTH), BF16),
        vmem((PLANES, RANK, WIDTH), BF16),
        vmem((LEAVES, RANK, WIDTH), F32),
        vmem((2, RANK, WIDTH), F32),
        vmem((frames, WIDTH), BF16),
        vmem((LEAVES, LEAF, 2 * WIDTH), F32),
        vmem((LEAVES, LEAF, WIDTH // 2), F32),
        dma((20,)),
        dma((2, LEAVES)),
        dma((2, LEAVES)),
        dma((2, LEAVES)),
        dma((2, LEAVES)),
        dma((2,)),
        dma((2, 2)),
        dma((PLANE - 1,)),
        dma((PLANE - 1,)),
        dma((2,)),
        dma((2,)),
        dma(()),
        dma(()),
        dma((PLANES,)),
        dma((PLANES,)),
        pltpu.SemaphoreType.REGULAR,
        pltpu.SemaphoreType.REGULAR,
        pltpu.SemaphoreType.REGULAR,
        pltpu.SemaphoreType.REGULAR,
        dma((LEAVES,)),
    ]
    return pl.pallas_call(
        body,
        out_shape=jax.ShapeDtypeStruct(tokens.shape, BF16),
        in_specs=[in_hbm] * 14,
        out_specs=in_hbm,
        scratch_shapes=scratch,
        compiler_params=pltpu.CompilerParams(
            collective_id=0, has_side_effects=True, vmem_limit_bytes=60 * 1024 * 1024
        ),
        cost_estimate=pl.CostEstimate(flops=4 * 10**9, bytes_accessed=8 * 10**6, transcendentals=10**6),
    )(
        tokens,
        norm_gain.reshape(1, -1),
        w_value,
        w_gate,
        phi_taps,
        tap_coeff,
        skip_gain.reshape(1, -1),
        basis_up,
        basis_down,
        lift_maps,
        spread_maps,
        couplings,
        jnp.asarray(forward),
        jnp.asarray(inverse),
    )


def solution(mesh):
    placed = (
        P("tm", "chan"),
        P(),
        P(None, "chan"),
        P(None, "chan"),
        P(),
        P(None, "chan"),
        P("chan"),
        P(),
        P(),
        P(),
        P(),
        P(None, None, None, None, "chan"),
    )
    return jax.shard_map(
        per_device, mesh=mesh, in_specs=placed, out_specs=P("tm", "chan"), check_vma=False
    )
```

```python
import jax
import jax.numpy as jnp
import numpy as np
from jax import lax
from jax.experimental import pallas as pl
from jax.experimental.pallas import tpu as pltpu
from jax.sharding import PartitionSpec as P

MESH = pl.DeviceIdType.MESH
F32 = jnp.float32
BF16 = jnp.bfloat16
HIGHEST = lax.Precision.HIGHEST

LEAF = 256
LEAVES = 4
PARTS = 2
WIDTH = 256
RANK = 16
PLANES = 8
PLANE = 8


def transform_tables():
    odd = np.arange(LEAF)[:, None] + 0.5
    angle = 2 * np.pi * odd * np.arange(LEAF)[None, :] / (2 * LEAF)
    forward = np.concatenate([np.cos(angle), -np.sin(angle)], 0)
    return forward.astype(np.float32), (forward.T / LEAF).astype(np.float32)


def exact_dot(left, right):
    return jnp.dot(left, right, precision=HIGHEST, preferred_element_type=F32)


def dot(left, right):
    return jnp.dot(left, right, preferred_element_type=F32)


def halves(value):
    high = value.astype(BF16)
    return high, (value - high.astype(F32)).astype(BF16)


def selector(lanes, period, shift, limit):
    row = lax.broadcasted_iota(jnp.int32, (RANK, lanes), 0)
    lane = lax.broadcasted_iota(jnp.int32, (RANK, lanes), 1)
    return ((lax.rem(lane, period) == row + shift) & (lane < limit)).astype(F32)


def body(
    tok, gain, w_value, w_gate, phi, coeff, skip, up, down, lift, spread, coup, fwd, inv,
    out,
    g, w, gain_v, phi_v, coeff_v, skip_v, up_v, down_v, lift_v, spread_v, coup_v, fwd_f, inv_f, fwd_v, inv_v,
    vals, halo, gate, near, spec, khat, mom_m, lift_m, six_m, far_m, red_m, moms,
    m2, m2_prev, ctx_out, ctx_in, pack_out, pack_in, m5_in, far0, far1, out_v, parts, part_squares,
    local_sem, dsend, drecv, rsend, rrecv, hsem, csem, s1, r1, s1p, r1p, s2, r2, s5, r5, ready_plane, ready_next, ready_edge, ready_later, osem,
):
    t = lax.axis_index("tm")
    x = lax.axis_index("chan")
    core = lax.rem(t, 2)
    y = lax.rem(lax.div(t, 2), 4)
    z = lax.div(t, PLANE)
    own = lax.rem(t, PLANE)
    right, left = lax.rem(x + 1, 4), lax.rem(x + 3, 4)

    barrier = pltpu.get_barrier_semaphore()

    def signal(semaphore, frames, chans):
        pl.semaphore_signal(semaphore, inc=1, device_id=(frames, chans), device_id_type=MESH)

    signal(barrier, t, right)
    signal(barrier, t, left)

    @pl.when(z < PLANES - 1)
    def _():
        signal(barrier, t + PLANE, x)

    for k in range(1, PLANE):

        @pl.when(own + k < PLANE)
        def _():
            signal(barrier, t + k, x)

    m2_prev[...] = jnp.zeros_like(m2_prev)
    ctx_in[...] = jnp.zeros_like(ctx_in)
    pack_in[...] = jnp.zeros_like(pack_in)
    m5_in[...] = jnp.zeros_like(m5_in)
    halo[...] = jnp.zeros_like(halo)

    pl.semaphore_wait(barrier, 2 + own + jnp.where(z > 0, 1, 0))

    owners = [x, left, right, lax.rem(x + 2, 4)]

    def leaf_at(place):
        return (place + 3) % LEAVES if isinstance(place, int) else lax.rem(place + 3, LEAVES)

    def leaf_rows(leaf):
        return pl.ds(leaf * LEAF if isinstance(leaf, int) else pl.multiple_of(leaf * LEAF, LEAF), LEAF)

    def part_rows(start, size):
        return pl.ds(start if isinstance(start, int) else pl.multiple_of(start, size), size)

    def direct(leaf, way, part):
        rows = part_rows(leaf * LEAF + part * (LEAF // PARTS), LEAF // PARTS)
        return pltpu.make_async_remote_copy(
            src_ref=tok.at[rows],
            dst_ref=g.at[1 + way, rows],
            send_sem=dsend.at[way, leaf, part],
            recv_sem=drecv.at[way, leaf, part],
            device_id=(t, left if way else right),
            device_id_type=MESH,
        )

    def relay(leaf, way, part):
        size = LEAF // 2 // PARTS
        rows = part_rows(leaf * LEAF + way * (LEAF // 2) + part * size, size)
        return pltpu.make_async_remote_copy(
            src_ref=g.at[1 + way, rows],
            dst_ref=g.at[3, rows],
            send_sem=rsend.at[way, leaf, part],
            recv_sem=rrecv.at[way, leaf, part],
            device_id=(t, left if way else right),
            device_id_type=MESH,
        )

    def send_direct(place):
        for part in range(PARTS):
            for way in range(2):
                direct(leaf_at(place), way, way if part == 0 else 1 - way).start()

    def pass_on(place):
        for way in range(2):
            direct(leaf_at(place), way, way).wait_recv()
            for part in range(PARTS):
                relay(leaf_at(place), way, part).start()

    def wait_relayed(place):
        for way in range(2):
            for part in range(PARTS):
                relay(leaf_at(place), way, part).wait_recv()

    def tables_near():
        for name in ("phi", "coeff", "fwd"):
            copies[name].wait()
        fwd_v[...] = jnp.concatenate(halves(fwd_f[...]), 1)
        taps = phi_v[...].astype(BF16).astype(F32)
        kernel_taps = lax.dot_general(
            taps, coeff_v[...], (((0,), (0,)), ((), ())), precision=HIGHEST, preferred_element_type=F32
        )
        both = jnp.concatenate([kernel_taps[:LEAF], kernel_taps[LEAF:]], 1)
        high, low = halves(both)
        hat = dot(fwd_v[...], jnp.concatenate([high, high], 0)) + dot(fwd_v[:, :LEAF], low)
        a_re, a_im = hat[:LEAF, :WIDTH], hat[LEAF:, :WIDTH]
        b_re, b_im = hat[:LEAF, WIDTH:], hat[LEAF:, WIDTH:]
        row = lax.broadcasted_iota(jnp.int32, (LEAF, WIDTH), 0)
        sign = (1 - 2 * lax.rem(row, 2)).astype(F32)
        khat[0] = a_re
        khat[1] = a_im
        khat[2] = b_re - sign * a_im
        khat[3] = b_im + sign * a_re

    def tables_moments():
        copies["up"].wait()
        copies["lift"].wait()
        base = up_v[...]
        first = [exact_dot(lift_v[0, k], base) for k in range(2)]
        for leaf in range(LEAVES):
            second = exact_dot(lift_v[1, leaf // 2], first[leaf % 2])
            high, low = halves(jnp.concatenate([base, first[leaf % 2], second], 0))
            mom_m[leaf] = jnp.concatenate([high, low], 1)

    def tables_lift():
        def pair(level):
            return exact_dot(lift_v[level, 0], selector(128, 32, 0, 128)) + exact_dot(
                lift_v[level, 1], selector(128, 32, 16, 128)
            )

        def blocks(level, copies_of):
            rows = jnp.concatenate([pair(level)] * copies_of, 0)
            row = lax.broadcasted_iota(jnp.int32, rows.shape, 0)
            lane = lax.broadcasted_iota(jnp.int32, rows.shape, 1)
            return jnp.where(lax.div(row, RANK) == lax.div(lane, 2 * RANK), rows, 0.0)

        three = blocks(2, 8)
        four = exact_dot(blocks(3, 2), three)
        five = exact_dot(blocks(4, 1), jnp.concatenate([four, jnp.zeros((96, 128), F32)], 0))
        whole = jnp.concatenate([four, three[32:64], five, three[:32]], 0)
        high, low = halves(whole)
        lift_m[...] = jnp.concatenate([high, low], 1)
        six = exact_dot(lift_v[5, 0], selector(128, 32, 0, 64)) + exact_dot(
            lift_v[5, 1], selector(128, 32, 16, 64)
        )
        high = six.astype(BF16).astype(F32)
        lane = lax.broadcasted_iota(jnp.int32, six.shape, 1)
        six_m[...] = jnp.where(lane < 32, high, six - high).astype(BF16)

    def tables_far():
        copies["spread"].wait()
        copies["down"].wait()
        row = lax.broadcasted_iota(jnp.int32, (RANK, LEAF), 0)
        lane = lax.broadcasted_iota(jnp.int32, (RANK, LEAF), 1)
        summing = (lax.div(lane, RANK) == row).astype(F32)
        chain = None
        for k in range(5):
            if k > 0:
                step = spread_v[1 + k, lax.rem(lax.div(t, 2 ** (k - 1)), 2)]
                chain = step if k == 1 else exact_dot(chain, step)
            high, low = halves(summing if k == 0 else exact_dot(chain, summing))
            red_m[k] = jnp.concatenate([high, low], 0)
        for leaf in range(LEAVES):
            near_step = spread_v[0, leaf % 2]
            both_steps = exact_dot(near_step, spread_v[1, leaf // 2])
            mix = (
                selector(LEAF, 48, 0, 144)
                + exact_dot(near_step, selector(LEAF, 48, 16, 144))
                + exact_dot(both_steps, selector(LEAF, 48, 32, 144))
            )
            whole = lax.dot_general(
                down_v[...], mix, (((0,), (0,)), ((), ())), precision=HIGHEST, preferred_element_type=F32
            )
            high = whole.astype(BF16).astype(F32)
            lane_at = lax.broadcasted_iota(jnp.int32, whole.shape, 1)
            far_m[leaf] = jnp.where(lane_at < 96, high, whole - high).astype(BF16)

    def scaled_rows(leaf, slots):
        rows = leaf_rows(leaf)
        squares = jnp.zeros((LEAF, WIDTH), F32)
        columns = []
        for slot in slots:
            tokens = g[slot, rows, :].astype(F32)
            squares = squares + tokens * tokens
            scale = gain_v[:, pl.ds(pl.multiple_of(owners[slot] * WIDTH, WIDTH), WIDTH)]
            columns.append((tokens * scale).astype(BF16))
        return jnp.concatenate(columns, 1), squares

    def inverse_of(squares):
        return lax.rsqrt(jnp.sum(squares, axis=1, keepdims=True) / 1024 + 1e-06)

    def values_of(leaf, sums, inverse):
        value = (sums * inverse).astype(BF16)
        vals[leaf_rows(leaf), :] = value
        twice = jnp.concatenate([value, value], 0)
        moms[leaf] = dot(mom_m[leaf], twice)
        return twice

    def gates_of(leaf, sums, inverse):
        gate[leaf_rows(leaf), :] = jax.nn.sigmoid(sums * inverse)

    def gather_part(leaf):
        for way in range(2):
            direct(leaf, way, 1 - way).wait_recv()
        scaled, squares = scaled_rows(leaf, (0, 1, 2))
        parts[leaf] = dot(scaled, w[:3].reshape(3 * WIDTH, 2 * WIDTH))
        part_squares[leaf] = squares[:, : WIDTH // 2] + squares[:, WIDTH // 2 :]

    def finished_sums(leaf):
        scaled, squares = scaled_rows(leaf, (3,))
        inverse = inverse_of(squares[:, : WIDTH // 2] + squares[:, WIDTH // 2 :] + part_squares[leaf])
        value_sums = parts[leaf, :, :WIDTH] + dot(scaled, w[3, :, :WIDTH])
        gate_sums = parts[leaf, :, WIDTH:] + dot(scaled, w[3, :, WIDTH:])
        return value_sums, gate_sums, inverse

    def project(leaf):
        value_sums, gate_sums, inverse = finished_sums(leaf)
        twice = values_of(leaf, value_sums, inverse)
        gates_of(leaf, gate_sums, inverse)
        spec[leaf] = dot(fwd_v[...], twice)

    def near_rows(leaf):
        rows = leaf_rows(leaf)
        before = (leaf - 1 if leaf > 0 else LEAVES) if isinstance(leaf, int) else leaf - 1
        a_re, a_im = spec[leaf, :LEAF, :], spec[leaf, LEAF:, :]
        b_re, b_im = spec[before, :LEAF, :], spec[before, LEAF:, :]
        out_re = khat[0] * a_re - khat[1] * a_im + khat[2] * b_re - khat[3] * b_im
        out_im = khat[0] * a_im + khat[1] * a_re + khat[2] * b_im + khat[3] * b_re
        both = jnp.concatenate([out_re, out_im], 0).astype(BF16)
        total = dot(inv_v[...], jnp.concatenate([both, both], 0))
        near[rows, :] = total + skip_v[...] * vals[rows, :].astype(F32)

    def coupled(level, source_two, source_three):
        product = coup_v[level, 0] * source_two[None]
        if source_three is not None:
            product = product + coup_v[level, 1] * source_three[None]
        return product.reshape(RANK * RANK, WIDTH).astype(BF16)

    for place in range(LEAVES - 1):
        send_direct(place)

    copies = {}

    def local(name, source, target):
        copies[name] = pltpu.make_async_copy(source, target, local_sem.at[len(copies)])
        copies[name].start()

    local("tok", tok, g.at[0])
    for slot in range(4):
        rows = pl.ds(pl.multiple_of(owners[slot] * WIDTH, WIDTH), WIDTH)
        local(("v", slot), w_value.at[rows], w.at[slot, :, pl.ds(0, WIDTH)])
        local(("g", slot), w_gate.at[rows], w.at[slot, :, pl.ds(WIDTH, WIDTH)])
    for name, source, target in (
        ("gain", gain, gain_v),
        ("phi", phi, phi_v),
        ("coeff", coeff, coeff_v),
        ("fwd", fwd, fwd_f),
        ("skip", skip, skip_v),
        ("up", up, up_v),
        ("down", down, down_v),
        ("lift", lift, lift_v),
        ("spread", spread, spread_v),
        ("inv", inv, inv_f),
        ("coup", coup, coup_v),
    ):
        local(name, source, target)

    @pl.when(z > 0)
    def _():
        signal(ready_next, t - PLANE, x)

    for k in range(1, PLANE):

        @pl.when(own >= k)
        def _():
            signal(ready_plane, t - k, x)

    def chain(place):
        @pl.when(z == PLANES - 1 - place)
        def _():
            if not isinstance(place, int) or place > 0:
                pl.semaphore_wait(ready_later, 1)
            if not isinstance(place, int) or place < PLANES - 1:
                signal(ready_later, t - PLANE, x)

    chain(0)
    tables_near()
    chain(1)
    tables_moments()
    tables_lift()
    chain(2)

    @pl.when(own < PLANE - 1)
    def _():
        pl.semaphore_wait(ready_plane, PLANE - 1 - own)

    @pl.when(z < PLANES - 1)
    def _():
        pl.semaphore_wait(ready_next, 1)

        @pl.when(y == 0)
        def _():
            signal(ready_edge, z * PLANE + 6, x)
            signal(ready_edge, z * PLANE + 7, x)

    for slot in range(4):
        copies["v", slot].wait()
        copies["g", slot].wait()
    for name in ("tok", "gain", "skip", "coup", "inv"):
        copies[name].wait()

    def arrive(place, carry):
        gather_part(leaf_at(place))
        return carry

    tables_far()
    inv_v[...] = jnp.concatenate(halves(inv_f[...]), 1)
    pass_on(0)
    send_direct(3)
    pass_on(1)
    pass_on(2)
    lax.fori_loop(0, 3, arrive, 0)
    chain(3)

    @pl.when((y == 3) & (z < PLANES - 1))
    def _():
        pl.semaphore_wait(ready_edge, 2)

    halo_copy = pltpu.make_async_remote_copy(
        src_ref=vals.at[pl.ds(3 * LEAF, LEAF)],
        dst_ref=halo,
        send_sem=hsem.at[0],
        recv_sem=hsem.at[1],
        device_id=(t + 1, x),
        device_id_type=MESH,
    )

    def ctx_copy(part):
        return pltpu.make_async_remote_copy(
            src_ref=ctx_out.at[pl.ds(part * 32, 32)],
            dst_ref=ctx_in.at[pl.ds(part * 32, 32)],
            send_sem=csem.at[0, part],
            recv_sem=csem.at[1, part],
            device_id=(t + 1, x),
            device_id_type=MESH,
        )

    def step(i, carry):
        wait_relayed(i)
        project(leaf_at(i))

        @pl.when((i == 0) & (t < PLANES * PLANE - 1))
        def _():
            halo_copy.start()

        chain(4 + i)

        @pl.when(i == 1)
        def _():
            pass_on(3)
            gather_part(2)

        return carry

    lax.fori_loop(0, 3, step, 0)

    ctx_out[:32] = jnp.concatenate([moms[3, 0:16, :], moms[0, 16:32, :] + moms[1, 16:32, :]], 0).astype(BF16)

    @pl.when(t < PLANES * PLANE - 1)
    def _():
        ctx_copy(0).start()

    @pl.when(t > 0)
    def _():
        halo_copy.wait_recv()

    before = halo[...]
    spec[LEAVES] = dot(fwd_v[...], jnp.concatenate([before, before], 0))
    near_rows(0)

    wait_relayed(3)
    value_sums, gate_sums, inverse = finished_sums(2)
    twice = values_of(2, value_sums, inverse)

    chain(7)

    total = moms[0, 32:48, :] + moms[1, 32:48, :] + moms[2, 32:48, :] + moms[3, 32:48, :]
    m2[own] = total.astype(BF16)

    def plane_copy(k):
        return pltpu.make_async_remote_copy(
            src_ref=m2.at[own],
            dst_ref=m2.at[own],
            send_sem=s1.at[k - 1],
            recv_sem=r1.at[k - 1],
            device_id=(z * PLANE + lax.rem(own + k, PLANE), x),
            device_id_type=MESH,
        )

    def plane_arrival(k):
        return pltpu.make_async_remote_copy(
            src_ref=m2.at[own],
            dst_ref=m2.at[lax.rem(own + PLANE - k, PLANE)],
            send_sem=s1.at[k - 1],
            recv_sem=r1.at[k - 1],
            device_id=(z * PLANE + lax.rem(own + k, PLANE), x),
            device_id_type=MESH,
        )

    for k in range(1, PLANE):
        plane_copy(k).start()

    def next_plane_copy(target, source):
        return pltpu.make_async_remote_copy(
            src_ref=m2.at[own],
            dst_ref=m2_prev.at[source],
            send_sem=s1p.at[target],
            recv_sem=r1p.at[source],
            device_id=((z + 1) * PLANE + target, x),
            device_id_type=MESH,
        )

    @pl.when((y == 3) & (z < PLANES - 1))
    def _():
        for target in range(2):
            next_plane_copy(target, core).start()

    ctx_out[32:] = jnp.concatenate([moms[2, 0:16, :], moms[2, 16:32, :] + moms[3, 16:32, :]], 0).astype(BF16)

    @pl.when(t < PLANES * PLANE - 1)
    def _():
        ctx_copy(1).start()

    summing = red_m[0, :RANK, :]

    def gathered(level, source_two, source_three=None):
        return dot(summing, coupled(level, source_two, source_three))

    gates_of(2, gate_sums, inverse)
    spec[2] = dot(fwd_v[...], twice)
    for k in range(1, PLANE):
        plane_arrival(k).wait_recv()
    stack = m2[...].reshape(PLANE * RANK, WIDTH)
    lifted = dot(lift_m[...], jnp.concatenate([stack, stack], 0))
    pack_out[...] = lifted[:80].astype(BF16)


    def pack_copy(rows):
        return pltpu.make_async_remote_copy(
            src_ref=pack_out.at[pl.ds(0, rows)],
            dst_ref=pack_in.at[pl.ds(0, rows)],
            send_sem=s2,
            recv_sem=r2,
            device_id=(t + PLANE, x),
            device_id_type=MESH,
        )

    def five_copy(k):
        return pltpu.make_async_remote_copy(
            src_ref=pack_out.at[pl.ds(64, RANK)],
            dst_ref=m5_in.at[k],
            send_sem=s5.at[k],
            recv_sem=r5.at[k],
            device_id=(t + k * PLANE, x),
            device_id_type=MESH,
        )

    @pl.when((z < PLANES - 1) & (y < 2))
    def _():
        pack_copy(64).start()

    @pl.when((z < PLANES - 1) & (y >= 2))
    def _():
        pack_copy(32).start()

    for k in range(2, PLANES):

        @pl.when(z + k < PLANES)
        def _():
            five_copy(k).start()

    near_rows(1)
    near_rows(2)
    far0[2] = gathered(0, moms[0, 0:16, :])
    far0[3] = gathered(0, moms[1, 0:16, :], moms[0, 0:16, :])
    near_rows(3)

    for way in range(2):
        for leaf in range(LEAVES):
            for part in range(PARTS):
                direct(leaf, way, part).wait_send()
                relay(leaf, way, part).wait_send()

    @pl.when(t > 0)
    def _():
        ctx_copy(0).wait_recv()
        ctx_copy(1).wait_recv()

    prev = ctx_in[...].astype(F32)
    far1[0] = gathered(1, prev[16:32])
    far0[0] = gathered(0, prev[32:48])
    far0[1] = gathered(0, prev[0:16], prev[32:48])
    far1[1] = gathered(1, prev[48:64], prev[16:32])

    for k in range(1, PLANE):
        plane_copy(k).wait_send()

    @pl.when(t < PLANES * PLANE - 1)
    def _():
        halo_copy.wait_send()
        ctx_copy(0).wait_send()
        ctx_copy(1).wait_send()

    @pl.when((y == 3) & (z < PLANES - 1))
    def _():
        for target in range(2):
            next_plane_copy(target, core).wait_send()

    @pl.when((y == 0) & (z > 0))
    def _():
        for source in range(2):
            next_plane_copy(source, source).wait_recv()

    def reduced(k, source_two, source_three):
        return dot(red_m[k], coupled(2 + k, source_two, source_three))

    at = 2 * jnp.maximum(y - 1, 0)
    inside = y > 0
    two = jnp.where(inside, m2[at + core], m2_prev[core]).astype(F32)
    three = jnp.where(inside, m2[at], m2_prev[0]).astype(F32) * core.astype(F32)
    expansion = reduced(0, two, three)

    @pl.when((z > 0) & (y < 2))
    def _():
        pack_copy(64).wait_recv()

    @pl.when((z > 0) & (y >= 2))
    def _():
        pack_copy(32).wait_recv()

    odd = lax.rem(y, 2)
    lower = y < 2
    here = jnp.where(odd == 1, lifted[96:112], lifted[80:96])
    coming = pack_in[pl.ds(pl.multiple_of(32 + odd * RANK, RANK), RANK), :].astype(F32)
    two = jnp.where(lower, coming, here)
    three = jnp.where(lower, pack_in[32:48, :].astype(F32), lifted[80:96]) * odd.astype(F32)
    expansion = expansion + reduced(1, two, three)
    odd = lax.div(y, 2)
    two = pack_in[pl.ds(pl.multiple_of(odd * RANK, RANK), RANK), :].astype(F32)
    three = pack_in[0:16, :].astype(F32) * odd.astype(F32)
    expansion = expansion + reduced(2, two, three)

    for k in range(2, PLANES):

        @pl.when(z >= k)
        def _():
            five_copy(k).wait_recv()

    odd = lax.rem(z, 2)
    expansion = expansion + reduced(
        3, m5_in[2].astype(F32), m5_in[3].astype(F32) * odd.astype(F32)
    )
    pad = jnp.zeros((64, WIDTH), BF16)

    def sixth(base):
        pair = [m5_in[base], m5_in[base - 1]]
        return dot(six_m[...], jnp.concatenate(pair + pair + [pad], 0))

    odd_six = lax.rem(lax.div(z, 2), 2)
    expansion = expansion + reduced(
        4, sixth(4 + odd), sixth(6 + odd) * odd_six.astype(F32)
    )

    expansion = expansion[:RANK] + expansion[RANK:]

    def out_copy(leaf):
        rows = leaf_rows(leaf)
        return pltpu.make_async_copy(out_v.at[rows], out.at[rows], osem.at[leaf])

    for leaf in range(LEAVES):
        rows = leaf_rows(leaf)
        high, low = halves(jnp.concatenate([far0[leaf], far1[leaf // 2], expansion], 0))
        whole = jnp.concatenate([high, low, high, jnp.zeros((112, WIDTH), BF16)], 0)
        combined = near[rows, :] + dot(far_m[leaf], whole)
        out_v[rows, :] = (gate[rows, :] * combined).astype(BF16)
        out_copy(leaf).start()

    @pl.when((z < PLANES - 1) & (y < 2))
    def _():
        pack_copy(64).wait_send()

    @pl.when((z < PLANES - 1) & (y >= 2))
    def _():
        pack_copy(32).wait_send()

    for k in range(2, PLANES):

        @pl.when(z + k < PLANES)
        def _():
            five_copy(k).wait_send()

    for leaf in range(LEAVES):
        out_copy(leaf).wait()


def per_device(
    tokens,
    norm_gain,
    w_value,
    w_gate,
    phi_taps,
    tap_coeff,
    skip_gain,
    basis_up,
    basis_down,
    lift_maps,
    spread_maps,
    couplings,
):
    forward, inverse = transform_tables()
    in_hbm = pl.BlockSpec(memory_space=pltpu.HBM)
    frames = LEAF * LEAVES
    vmem = pltpu.VMEM
    dma = pltpu.SemaphoreType.DMA
    scratch = [
        vmem((4, frames, WIDTH), BF16),
        vmem((4, WIDTH, 2 * WIDTH), BF16),
        vmem((1, 4 * WIDTH), F32),
        vmem(phi_taps.shape, F32),
        vmem(tap_coeff.shape, F32),
        vmem((1, WIDTH), F32),
        vmem(basis_up.shape, F32),
        vmem(basis_down.shape, F32),
        vmem(lift_maps.shape, F32),
        vmem(spread_maps.shape, F32),
        vmem(couplings.shape, F32),
        vmem(forward.shape, F32),
        vmem(inverse.shape, F32),
        vmem((2 * LEAF, 2 * LEAF), BF16),
        vmem((LEAF, 4 * LEAF), BF16),
        vmem((frames, WIDTH), BF16),
        vmem((LEAF, WIDTH), BF16),
        vmem((frames, WIDTH), F32),
        vmem((frames, WIDTH), F32),
        vmem((LEAVES + 1, 2 * LEAF, WIDTH), F32),
        vmem((4, LEAF, WIDTH), F32),
        vmem((LEAVES, 48, 2 * LEAF), BF16),
        vmem((112, 256), BF16),
        vmem((RANK, 128), BF16),
        vmem((LEAVES, LEAF, LEAF), BF16),
        vmem((5, 2 * RANK, LEAF), BF16),
        vmem((LEAVES, 48, WIDTH), F32),
        vmem((PLANE, RANK, WIDTH), BF16),
        vmem((2, RANK, WIDTH), BF16),
        vmem((64, WIDTH), BF16),
        vmem((64, WIDTH), BF16),
        vmem((80, WIDTH), BF16),
        vmem((64, WIDTH), BF16),
        vmem((PLANES, RANK, WIDTH), BF16),
        vmem((LEAVES, RANK, WIDTH), F32),
        vmem((2, RANK, WIDTH), F32),
        vmem((frames, WIDTH), BF16),
        vmem((LEAVES, LEAF, 2 * WIDTH), F32),
        vmem((LEAVES, LEAF, WIDTH // 2), F32),
        dma((20,)),
        dma((2, LEAVES, PARTS)),
        dma((2, LEAVES, PARTS)),
        dma((2, LEAVES, PARTS)),
        dma((2, LEAVES, PARTS)),
        dma((2,)),
        dma((2, 2)),
        dma((PLANE - 1,)),
        dma((PLANE - 1,)),
        dma((2,)),
        dma((2,)),
        dma(()),
        dma(()),
        dma((PLANES,)),
        dma((PLANES,)),
        pltpu.SemaphoreType.REGULAR,
        pltpu.SemaphoreType.REGULAR,
        pltpu.SemaphoreType.REGULAR,
        pltpu.SemaphoreType.REGULAR,
        dma((LEAVES,)),
    ]
    return pl.pallas_call(
        body,
        out_shape=jax.ShapeDtypeStruct(tokens.shape, BF16),
        in_specs=[in_hbm] * 14,
        out_specs=in_hbm,
        scratch_shapes=scratch,
        compiler_params=pltpu.CompilerParams(
            collective_id=0, has_side_effects=True, vmem_limit_bytes=60 * 1024 * 1024
        ),
        cost_estimate=pl.CostEstimate(flops=4 * 10**9, bytes_accessed=8 * 10**6, transcendentals=10**6),
    )(
        tokens,
        norm_gain.reshape(1, -1),
        w_value,
        w_gate,
        phi_taps,
        tap_coeff,
        skip_gain.reshape(1, -1),
        basis_up,
        basis_down,
        lift_maps,
        spread_maps,
        couplings,
        jnp.asarray(forward),
        jnp.asarray(inverse),
    )


def solution(mesh):
    placed = (
        P("tm", "chan"),
        P(),
        P(None, "chan"),
        P(None, "chan"),
        P(),
        P(None, "chan"),
        P("chan"),
        P(),
        P(),
        P(),
        P(),
        P(None, None, None, None, "chan"),
    )
    return jax.shard_map(
        per_device, mesh=mesh, in_specs=placed, out_specs=P("tm", "chan"), check_vma=False
    )
```

```python
import jax
import jax.numpy as jnp
import numpy as np
from jax import lax
from jax.experimental import pallas as pl
from jax.experimental.pallas import tpu as pltpu
from jax.sharding import PartitionSpec as P

MESH = pl.DeviceIdType.MESH
F32 = jnp.float32
BF16 = jnp.bfloat16
HIGHEST = lax.Precision.HIGHEST

LEAF = 256
LEAVES = 4
WIDTH = 256
RANK = 16
PLANES = 8
PLANE = 8


def transform_tables():
    odd = np.arange(LEAF)[:, None] + 0.5
    angle = 2 * np.pi * odd * np.arange(LEAF)[None, :] / (2 * LEAF)
    forward = np.concatenate([np.cos(angle), -np.sin(angle)], 0)
    return forward.astype(np.float32), (forward.T / LEAF).astype(np.float32)


def exact_dot(left, right):
    return jnp.dot(left, right, precision=HIGHEST, preferred_element_type=F32)


def dot(left, right):
    return jnp.dot(left, right, preferred_element_type=F32)


def halves(value):
    high = value.astype(BF16)
    return high, (value - high.astype(F32)).astype(BF16)


def selector(lanes, period, shift, limit):
    row = lax.broadcasted_iota(jnp.int32, (RANK, lanes), 0)
    lane = lax.broadcasted_iota(jnp.int32, (RANK, lanes), 1)
    return ((lax.rem(lane, period) == row + shift) & (lane < limit)).astype(F32)


def body(
    tok, gain, w_value, w_gate, phi, coeff, skip, up, down, lift, spread, coup, fwd, inv,
    out,
    g, w, gain_v, phi_v, coeff_v, skip_v, up_v, down_v, lift_v, spread_v, coup_v, fwd_f, inv_f, fwd_v, inv_v,
    vals, halo, gate, near, spec, khat, mom_m, lift_m, six_m, far_m, red_m, moms,
    m2, m2_prev, ctx_out, ctx_in, pack_out, pack_in, m5_in, far0, far1, out_v, parts, part_squares,
    local_sem, dsend, drecv, rsend, rrecv, hsem, csem, s1, r1, s1p, r1p, s2, r2, s5, r5, ready_plane, ready_next, ready_edge, ready_later, osem,
):
    t = lax.axis_index("tm")
    x = lax.axis_index("chan")
    core = lax.rem(t, 2)
    y = lax.rem(lax.div(t, 2), 4)
    z = lax.div(t, PLANE)
    own = lax.rem(t, PLANE)
    right, left = lax.rem(x + 1, 4), lax.rem(x + 3, 4)

    barrier = pltpu.get_barrier_semaphore()

    def signal(semaphore, frames, chans):
        pl.semaphore_signal(semaphore, inc=1, device_id=(frames, chans), device_id_type=MESH)

    signal(barrier, t, right)
    signal(barrier, t, left)

    @pl.when(z < PLANES - 1)
    def _():
        signal(barrier, t + PLANE, x)

    for k in range(1, PLANE):

        @pl.when(own + k < PLANE)
        def _():
            signal(barrier, t + k, x)

    m2_prev[...] = jnp.zeros_like(m2_prev)
    ctx_in[...] = jnp.zeros_like(ctx_in)
    pack_in[...] = jnp.zeros_like(pack_in)
    m5_in[...] = jnp.zeros_like(m5_in)
    halo[...] = jnp.zeros_like(halo)

    pl.semaphore_wait(barrier, 2 + own + jnp.where(z > 0, 1, 0))

    owners = [x, left, right, lax.rem(x + 2, 4)]

    def leaf_at(place):
        return (place + 3) % LEAVES if isinstance(place, int) else lax.rem(place + 3, LEAVES)

    def leaf_rows(leaf):
        return pl.ds(leaf * LEAF if isinstance(leaf, int) else pl.multiple_of(leaf * LEAF, LEAF), LEAF)

    def direct(leaf, way):
        rows = leaf_rows(leaf)
        return pltpu.make_async_remote_copy(
            src_ref=tok.at[rows],
            dst_ref=g.at[1 + way, rows],
            send_sem=dsend.at[way, leaf],
            recv_sem=drecv.at[way, leaf],
            device_id=(t, left if way else right),
            device_id_type=MESH,
        )

    def relay(leaf, way):
        start = leaf * LEAF + way * (LEAF // 2)
        rows = pl.ds(start if isinstance(leaf, int) else pl.multiple_of(start, LEAF // 2), LEAF // 2)
        return pltpu.make_async_remote_copy(
            src_ref=g.at[1 + way, rows],
            dst_ref=g.at[3, rows],
            send_sem=rsend.at[way, leaf],
            recv_sem=rrecv.at[way, leaf],
            device_id=(t, left if way else right),
            device_id_type=MESH,
        )

    def send_direct(place):
        for way in range(2):
            direct(leaf_at(place), way).start()

    def pass_on(place):
        for way in range(2):
            direct(leaf_at(place), way).wait_recv()
            relay(leaf_at(place), way).start()

    def wait_relayed(place):
        for way in range(2):
            relay(leaf_at(place), way).wait_recv()

    def tables_near():
        for name in ("phi", "coeff", "fwd"):
            copies[name].wait()
        fwd_v[...] = jnp.concatenate(halves(fwd_f[...]), 1)
        taps = phi_v[...].astype(BF16).astype(F32)
        kernel_taps = lax.dot_general(
            taps, coeff_v[...], (((0,), (0,)), ((), ())), precision=HIGHEST, preferred_element_type=F32
        )
        both = jnp.concatenate([kernel_taps[:LEAF], kernel_taps[LEAF:]], 1)
        high, low = halves(both)
        hat = dot(fwd_v[...], jnp.concatenate([high, high], 0)) + dot(fwd_v[:, :LEAF], low)
        a_re, a_im = hat[:LEAF, :WIDTH], hat[LEAF:, :WIDTH]
        b_re, b_im = hat[:LEAF, WIDTH:], hat[LEAF:, WIDTH:]
        row = lax.broadcasted_iota(jnp.int32, (LEAF, WIDTH), 0)
        sign = (1 - 2 * lax.rem(row, 2)).astype(F32)
        khat[0] = a_re
        khat[1] = a_im
        khat[2] = b_re - sign * a_im
        khat[3] = b_im + sign * a_re

    def tables_moments():
        copies["up"].wait()
        copies["lift"].wait()
        base = up_v[...]
        first = [exact_dot(lift_v[0, k], base) for k in range(2)]
        for leaf in range(LEAVES):
            second = exact_dot(lift_v[1, leaf // 2], first[leaf % 2])
            high, low = halves(jnp.concatenate([base, first[leaf % 2], second], 0))
            mom_m[leaf] = jnp.concatenate([high, low], 1)

    def tables_lift():
        def pair(level):
            return exact_dot(lift_v[level, 0], selector(128, 32, 0, 128)) + exact_dot(
                lift_v[level, 1], selector(128, 32, 16, 128)
            )

        def blocks(level, copies_of):
            rows = jnp.concatenate([pair(level)] * copies_of, 0)
            row = lax.broadcasted_iota(jnp.int32, rows.shape, 0)
            lane = lax.broadcasted_iota(jnp.int32, rows.shape, 1)
            return jnp.where(lax.div(row, RANK) == lax.div(lane, 2 * RANK), rows, 0.0)

        three = blocks(2, 8)
        four = exact_dot(blocks(3, 2), three)
        five = exact_dot(blocks(4, 1), jnp.concatenate([four, jnp.zeros((96, 128), F32)], 0))
        whole = jnp.concatenate([four, three[32:64], five, three[:32]], 0)
        high, low = halves(whole)
        lift_m[...] = jnp.concatenate([high, low], 1)
        six = exact_dot(lift_v[5, 0], selector(128, 32, 0, 64)) + exact_dot(
            lift_v[5, 1], selector(128, 32, 16, 64)
        )
        high = six.astype(BF16).astype(F32)
        lane = lax.broadcasted_iota(jnp.int32, six.shape, 1)
        six_m[...] = jnp.where(lane < 32, high, six - high).astype(BF16)

    def tables_far():
        copies["spread"].wait()
        copies["down"].wait()
        row = lax.broadcasted_iota(jnp.int32, (RANK, LEAF), 0)
        lane = lax.broadcasted_iota(jnp.int32, (RANK, LEAF), 1)
        summing = (lax.div(lane, RANK) == row).astype(F32)
        chain = None
        for k in range(5):
            if k > 0:
                step = spread_v[1 + k, lax.rem(lax.div(t, 2 ** (k - 1)), 2)]
                chain = step if k == 1 else exact_dot(chain, step)
            high, low = halves(summing if k == 0 else exact_dot(chain, summing))
            red_m[k] = jnp.concatenate([high, low], 0)
        for leaf in range(LEAVES):
            near_step = spread_v[0, leaf % 2]
            both_steps = exact_dot(near_step, spread_v[1, leaf // 2])
            mix = (
                selector(LEAF, 48, 0, 144)
                + exact_dot(near_step, selector(LEAF, 48, 16, 144))
                + exact_dot(both_steps, selector(LEAF, 48, 32, 144))
            )
            whole = lax.dot_general(
                down_v[...], mix, (((0,), (0,)), ((), ())), precision=HIGHEST, preferred_element_type=F32
            )
            high = whole.astype(BF16).astype(F32)
            lane_at = lax.broadcasted_iota(jnp.int32, whole.shape, 1)
            far_m[leaf] = jnp.where(lane_at < 96, high, whole - high).astype(BF16)

    def scaled_rows(leaf, slots):
        rows = leaf_rows(leaf)
        squares = jnp.zeros((LEAF, WIDTH), F32)
        columns = []
        for slot in slots:
            tokens = g[slot, rows, :].astype(F32)
            squares = squares + tokens * tokens
            scale = gain_v[:, pl.ds(pl.multiple_of(owners[slot] * WIDTH, WIDTH), WIDTH)]
            columns.append((tokens * scale).astype(BF16))
        return jnp.concatenate(columns, 1), squares

    def gather_part(leaf):
        scaled, squares = scaled_rows(leaf, (0, 1, 2))
        parts[leaf] = dot(scaled, w[:3].reshape(3 * WIDTH, 2 * WIDTH))
        part_squares[leaf] = squares[:, : WIDTH // 2] + squares[:, WIDTH // 2 :]

    def values_of(leaf):
        scaled, squares = scaled_rows(leaf, (3,))
        squares = squares[:, : WIDTH // 2] + squares[:, WIDTH // 2 :] + part_squares[leaf]
        inverse = lax.rsqrt(jnp.sum(squares, axis=1, keepdims=True) / 1024 + 1e-06)
        part_squares[leaf] = jnp.broadcast_to(inverse, squares.shape)
        value = ((parts[leaf, :, :WIDTH] + dot(scaled, w[3, :, :WIDTH])) * inverse).astype(BF16)
        vals[leaf_rows(leaf), :] = value
        moms[leaf] = dot(mom_m[leaf], jnp.concatenate([value, value], 0))

    def gates_of(leaf):
        scaled, _ = scaled_rows(leaf, (3,))
        inverse = part_squares[leaf]
        sums = parts[leaf, :, WIDTH:] + dot(scaled, w[3, :, WIDTH:])
        gate[leaf_rows(leaf), :] = jax.nn.sigmoid(sums * jnp.concatenate([inverse, inverse], 1))

    def spectrum_of(leaf):
        value = vals[leaf_rows(leaf), :]
        spec[leaf] = dot(fwd_v[...], jnp.concatenate([value, value], 0))

    def near_rows(leaf):
        rows = leaf_rows(leaf)
        before = (leaf - 1 if leaf > 0 else LEAVES) if isinstance(leaf, int) else leaf - 1
        a_re, a_im = spec[leaf, :LEAF, :], spec[leaf, LEAF:, :]
        b_re, b_im = spec[before, :LEAF, :], spec[before, LEAF:, :]
        out_re = khat[0] * a_re - khat[1] * a_im + khat[2] * b_re - khat[3] * b_im
        out_im = khat[0] * a_im + khat[1] * a_re + khat[2] * b_im + khat[3] * b_re
        both = jnp.concatenate([out_re, out_im], 0).astype(BF16)
        total = dot(inv_v[...], jnp.concatenate([both, both], 0))
        near[rows, :] = total + skip_v[...] * vals[rows, :].astype(F32)

    def coupled(level, source_two, source_three):
        product = coup_v[level, 0] * source_two[None]
        if source_three is not None:
            product = product + coup_v[level, 1] * source_three[None]
        return product.reshape(RANK * RANK, WIDTH).astype(BF16)

    for place in range(LEAVES):
        send_direct(place)

    copies = {}

    def local(name, source, target):
        copies[name] = pltpu.make_async_copy(source, target, local_sem.at[len(copies)])
        copies[name].start()

    local("tok", tok, g.at[0])
    for slot in range(4):
        rows = pl.ds(pl.multiple_of(owners[slot] * WIDTH, WIDTH), WIDTH)
        local(("v", slot), w_value.at[rows], w.at[slot, :, pl.ds(0, WIDTH)])
        local(("g", slot), w_gate.at[rows], w.at[slot, :, pl.ds(WIDTH, WIDTH)])
    for name, source, target in (
        ("gain", gain, gain_v),
        ("phi", phi, phi_v),
        ("coeff", coeff, coeff_v),
        ("fwd", fwd, fwd_f),
        ("skip", skip, skip_v),
        ("up", up, up_v),
        ("down", down, down_v),
        ("lift", lift, lift_v),
        ("spread", spread, spread_v),
        ("inv", inv, inv_f),
        ("coup", coup, coup_v),
    ):
        local(name, source, target)

    @pl.when(z > 0)
    def _():
        signal(ready_next, t - PLANE, x)

    for k in range(1, PLANE):

        @pl.when(own >= k)
        def _():
            signal(ready_plane, t - k, x)

    def chain(place):
        @pl.when(z == PLANES - 1 - place)
        def _():
            if not isinstance(place, int) or place > 0:
                pl.semaphore_wait(ready_later, 1)
            if not isinstance(place, int) or place < PLANES - 1:
                signal(ready_later, t - PLANE, x)

    chain(0)
    tables_near()
    chain(1)
    tables_moments()
    tables_lift()
    chain(2)

    @pl.when(own < PLANE - 1)
    def _():
        pl.semaphore_wait(ready_plane, PLANE - 1 - own)

    @pl.when(z < PLANES - 1)
    def _():
        pl.semaphore_wait(ready_next, 1)

        @pl.when(y == 0)
        def _():
            signal(ready_edge, z * PLANE + 6, x)
            signal(ready_edge, z * PLANE + 7, x)

    tables_far()
    copies["inv"].wait()
    inv_v[...] = jnp.concatenate(halves(inv_f[...]), 1)
    chain(3)
    for slot in range(4):
        copies["v", slot].wait()
        copies["g", slot].wait()
    for name in ("tok", "gain", "skip", "coup"):
        copies[name].wait()
    chain(4)
    pass_on(0)
    chain(5)
    pass_on(1)
    pass_on(2)
    pass_on(3)
    chain(6)

    def sum_parts(leaf, carry):
        gather_part(leaf)
        return carry

    lax.fori_loop(0, LEAVES, sum_parts, 0)

    @pl.when((y == 3) & (z < PLANES - 1))
    def _():
        pl.semaphore_wait(ready_edge, 2)

    chain(7)

    halo_copy = pltpu.make_async_remote_copy(
        src_ref=vals.at[pl.ds(3 * LEAF, LEAF)],
        dst_ref=halo,
        send_sem=hsem.at[0],
        recv_sem=hsem.at[1],
        device_id=(t + 1, x),
        device_id_type=MESH,
    )

    ctx_copy = pltpu.make_async_remote_copy(
        src_ref=ctx_out,
        dst_ref=ctx_in,
        send_sem=csem.at[0],
        recv_sem=csem.at[1],
        device_id=(t + 1, x),
        device_id_type=MESH,
    )

    def step(place, carry):
        wait_relayed(place)
        values_of(leaf_at(place))

        @pl.when((place == 0) & (t < PLANES * PLANE - 1))
        def _():
            halo_copy.start()

        return carry

    lax.fori_loop(0, LEAVES, step, 0)

    total = moms[0, 32:48, :] + moms[1, 32:48, :] + moms[2, 32:48, :] + moms[3, 32:48, :]
    m2[own] = total.astype(BF16)

    def plane_copy(k):
        return pltpu.make_async_remote_copy(
            src_ref=m2.at[own],
            dst_ref=m2.at[own],
            send_sem=s1.at[k - 1],
            recv_sem=r1.at[k - 1],
            device_id=(z * PLANE + lax.rem(own + k, PLANE), x),
            device_id_type=MESH,
        )

    def plane_arrival(k):
        return pltpu.make_async_remote_copy(
            src_ref=m2.at[own],
            dst_ref=m2.at[lax.rem(own + PLANE - k, PLANE)],
            send_sem=s1.at[k - 1],
            recv_sem=r1.at[k - 1],
            device_id=(z * PLANE + lax.rem(own + k, PLANE), x),
            device_id_type=MESH,
        )

    for k in range(1, PLANE):
        plane_copy(k).start()

    def next_plane_copy(target, source):
        return pltpu.make_async_remote_copy(
            src_ref=m2.at[own],
            dst_ref=m2_prev.at[source],
            send_sem=s1p.at[target],
            recv_sem=r1p.at[source],
            device_id=((z + 1) * PLANE + target, x),
            device_id_type=MESH,
        )

    @pl.when((y == 3) & (z < PLANES - 1))
    def _():
        for target in range(2):
            next_plane_copy(target, core).start()

    ctx_out[...] = jnp.concatenate(
        [
            moms[2, 0:16, :],
            moms[3, 0:16, :],
            moms[0, 16:32, :] + moms[1, 16:32, :],
            moms[2, 16:32, :] + moms[3, 16:32, :],
        ],
        0,
    ).astype(BF16)

    @pl.when(t < PLANES * PLANE - 1)
    def _():
        ctx_copy.start()

    def gate_step(leaf, carry):
        gates_of(leaf)
        return carry

    lax.fori_loop(0, LEAVES, gate_step, 0)

    for k in range(1, PLANE):
        plane_arrival(k).wait_recv()
    stack = m2[...].reshape(PLANE * RANK, WIDTH)
    lifted = dot(lift_m[...], jnp.concatenate([stack, stack], 0))
    pack_out[...] = lifted[:80].astype(BF16)


    def pack_copy(rows):
        return pltpu.make_async_remote_copy(
            src_ref=pack_out.at[pl.ds(0, rows)],
            dst_ref=pack_in.at[pl.ds(0, rows)],
            send_sem=s2,
            recv_sem=r2,
            device_id=(t + PLANE, x),
            device_id_type=MESH,
        )

    def five_copy(k):
        return pltpu.make_async_remote_copy(
            src_ref=pack_out.at[pl.ds(64, RANK)],
            dst_ref=m5_in.at[k],
            send_sem=s5.at[k],
            recv_sem=r5.at[k],
            device_id=(t + k * PLANE, x),
            device_id_type=MESH,
        )

    @pl.when((z < PLANES - 1) & (y < 2))
    def _():
        pack_copy(64).start()

    @pl.when((z < PLANES - 1) & (y >= 2))
    def _():
        pack_copy(32).start()

    for k in range(2, PLANES):

        @pl.when(z + k < PLANES)
        def _():
            five_copy(k).start()

    def spectrum_step(leaf, carry):
        spectrum_of(leaf)
        return carry

    lax.fori_loop(0, LEAVES, spectrum_step, 0)

    def near_step(leaf, carry):
        near_rows(leaf)
        return carry

    lax.fori_loop(1, LEAVES, near_step, 0)

    @pl.when(t > 0)
    def _():
        halo_copy.wait_recv()

    before = halo[...]
    spec[LEAVES] = dot(fwd_v[...], jnp.concatenate([before, before], 0))
    near_rows(0)

    summing = red_m[0, :RANK, :]

    def gathered(level, source_two, source_three=None):
        return dot(summing, coupled(level, source_two, source_three))

    @pl.when(t > 0)
    def _():
        ctx_copy.wait_recv()

    prev = ctx_in[...].astype(F32)
    far0[0] = gathered(0, prev[0:16])
    far0[1] = gathered(0, prev[16:32], prev[0:16])
    far0[2] = gathered(0, moms[0, 0:16, :])
    far0[3] = gathered(0, moms[1, 0:16, :], moms[0, 0:16, :])
    far1[0] = gathered(1, prev[32:48])
    far1[1] = gathered(1, prev[48:64], prev[32:48])

    for way in range(2):
        for leaf in range(LEAVES):
            direct(leaf, way).wait_send()
            relay(leaf, way).wait_send()

    for k in range(1, PLANE):
        plane_copy(k).wait_send()

    @pl.when(t < PLANES * PLANE - 1)
    def _():
        halo_copy.wait_send()
        ctx_copy.wait_send()

    @pl.when((y == 3) & (z < PLANES - 1))
    def _():
        for target in range(2):
            next_plane_copy(target, core).wait_send()

    @pl.when((y == 0) & (z > 0))
    def _():
        for source in range(2):
            next_plane_copy(source, source).wait_recv()

    def reduced(k, source_two, source_three):
        return dot(red_m[k], coupled(2 + k, source_two, source_three))

    at = 2 * jnp.maximum(y - 1, 0)
    inside = y > 0
    two = jnp.where(inside, m2[at + core], m2_prev[core]).astype(F32)
    three = jnp.where(inside, m2[at], m2_prev[0]).astype(F32) * core.astype(F32)
    expansion = reduced(0, two, three)

    @pl.when((z > 0) & (y < 2))
    def _():
        pack_copy(64).wait_recv()

    @pl.when((z > 0) & (y >= 2))
    def _():
        pack_copy(32).wait_recv()

    odd = lax.rem(y, 2)
    lower = y < 2
    here = jnp.where(odd == 1, lifted[96:112], lifted[80:96])
    coming = pack_in[pl.ds(pl.multiple_of(32 + odd * RANK, RANK), RANK), :].astype(F32)
    two = jnp.where(lower, coming, here)
    three = jnp.where(lower, pack_in[32:48, :].astype(F32), lifted[80:96]) * odd.astype(F32)
    expansion = expansion + reduced(1, two, three)
    odd = lax.div(y, 2)
    two = pack_in[pl.ds(pl.multiple_of(odd * RANK, RANK), RANK), :].astype(F32)
    three = pack_in[0:16, :].astype(F32) * odd.astype(F32)
    expansion = expansion + reduced(2, two, three)

    for k in range(2, PLANES):

        @pl.when(z >= k)
        def _():
            five_copy(k).wait_recv()

    odd = lax.rem(z, 2)
    expansion = expansion + reduced(
        3, m5_in[2].astype(F32), m5_in[3].astype(F32) * odd.astype(F32)
    )
    pad = jnp.zeros((64, WIDTH), BF16)

    def sixth(base):
        pair = [m5_in[base], m5_in[base - 1]]
        return dot(six_m[...], jnp.concatenate(pair + pair + [pad], 0))

    odd_six = lax.rem(lax.div(z, 2), 2)
    expansion = expansion + reduced(
        4, sixth(4 + odd), sixth(6 + odd) * odd_six.astype(F32)
    )

    expansion = expansion[:RANK] + expansion[RANK:]

    def out_copy(leaf):
        rows = leaf_rows(leaf)
        return pltpu.make_async_copy(out_v.at[rows], out.at[rows], osem.at[leaf])

    for leaf in range(LEAVES):
        rows = leaf_rows(leaf)
        high, low = halves(jnp.concatenate([far0[leaf], far1[leaf // 2], expansion], 0))
        whole = jnp.concatenate([high, low, high, jnp.zeros((112, WIDTH), BF16)], 0)
        combined = near[rows, :] + dot(far_m[leaf], whole)
        out_v[rows, :] = (gate[rows, :] * combined).astype(BF16)
        out_copy(leaf).start()

    @pl.when((z < PLANES - 1) & (y < 2))
    def _():
        pack_copy(64).wait_send()

    @pl.when((z < PLANES - 1) & (y >= 2))
    def _():
        pack_copy(32).wait_send()

    for k in range(2, PLANES):

        @pl.when(z + k < PLANES)
        def _():
            five_copy(k).wait_send()

    for leaf in range(LEAVES):
        out_copy(leaf).wait()


def per_device(
    tokens,
    norm_gain,
    w_value,
    w_gate,
    phi_taps,
    tap_coeff,
    skip_gain,
    basis_up,
    basis_down,
    lift_maps,
    spread_maps,
    couplings,
):
    forward, inverse = transform_tables()
    in_hbm = pl.BlockSpec(memory_space=pltpu.HBM)
    frames = LEAF * LEAVES
    vmem = pltpu.VMEM
    dma = pltpu.SemaphoreType.DMA
    scratch = [
        vmem((4, frames, WIDTH), BF16),
        vmem((4, WIDTH, 2 * WIDTH), BF16),
        vmem((1, 4 * WIDTH), F32),
        vmem(phi_taps.shape, F32),
        vmem(tap_coeff.shape, F32),
        vmem((1, WIDTH), F32),
        vmem(basis_up.shape, F32),
        vmem(basis_down.shape, F32),
        vmem(lift_maps.shape, F32),
        vmem(spread_maps.shape, F32),
        vmem(couplings.shape, F32),
        vmem(forward.shape, F32),
        vmem(inverse.shape, F32),
        vmem((2 * LEAF, 2 * LEAF), BF16),
        vmem((LEAF, 4 * LEAF), BF16),
        vmem((frames, WIDTH), BF16),
        vmem((LEAF, WIDTH), BF16),
        vmem((frames, WIDTH), F32),
        vmem((frames, WIDTH), F32),
        vmem((LEAVES + 1, 2 * LEAF, WIDTH), F32),
        vmem((4, LEAF, WIDTH), F32),
        vmem((LEAVES, 48, 2 * LEAF), BF16),
        vmem((112, 256), BF16),
        vmem((RANK, 128), BF16),
        vmem((LEAVES, LEAF, LEAF), BF16),
        vmem((5, 2 * RANK, LEAF), BF16),
        vmem((LEAVES, 48, WIDTH), F32),
        vmem((PLANE, RANK, WIDTH), BF16),
        vmem((2, RANK, WIDTH), BF16),
        vmem((64, WIDTH), BF16),
        vmem((64, WIDTH), BF16),
        vmem((80, WIDTH), BF16),
        vmem((64, WIDTH), BF16),
        vmem((PLANES, RANK, WIDTH), BF16),
        vmem((LEAVES, RANK, WIDTH), F32),
        vmem((2, RANK, WIDTH), F32),
        vmem((frames, WIDTH), BF16),
        vmem((LEAVES, LEAF, 2 * WIDTH), F32),
        vmem((LEAVES, LEAF, WIDTH // 2), F32),
        dma((20,)),
        dma((2, LEAVES)),
        dma((2, LEAVES)),
        dma((2, LEAVES)),
        dma((2, LEAVES)),
        dma((2,)),
        dma((2,)),
        dma((PLANE - 1,)),
        dma((PLANE - 1,)),
        dma((2,)),
        dma((2,)),
        dma(()),
        dma(()),
        dma((PLANES,)),
        dma((PLANES,)),
        pltpu.SemaphoreType.REGULAR,
        pltpu.SemaphoreType.REGULAR,
        pltpu.SemaphoreType.REGULAR,
        pltpu.SemaphoreType.REGULAR,
        dma((LEAVES,)),
    ]
    return pl.pallas_call(
        body,
        out_shape=jax.ShapeDtypeStruct(tokens.shape, BF16),
        in_specs=[in_hbm] * 14,
        out_specs=in_hbm,
        scratch_shapes=scratch,
        compiler_params=pltpu.CompilerParams(
            collective_id=0, has_side_effects=True, vmem_limit_bytes=60 * 1024 * 1024
        ),
        cost_estimate=pl.CostEstimate(flops=4 * 10**9, bytes_accessed=8 * 10**6, transcendentals=10**6),
    )(
        tokens,
        norm_gain.reshape(1, -1),
        w_value,
        w_gate,
        phi_taps,
        tap_coeff,
        skip_gain.reshape(1, -1),
        basis_up,
        basis_down,
        lift_maps,
        spread_maps,
        couplings,
        jnp.asarray(forward),
        jnp.asarray(inverse),
    )


def solution(mesh):
    placed = (
        P("tm", "chan"),
        P(),
        P(None, "chan"),
        P(None, "chan"),
        P(),
        P(None, "chan"),
        P("chan"),
        P(),
        P(),
        P(),
        P(),
        P(None, None, None, None, "chan"),
    )
    return jax.shard_map(
        per_device, mesh=mesh, in_specs=placed, out_specs=P("tm", "chan"), check_vma=False
    )
```

```python
import jax
import jax.numpy as jnp
import numpy as np
from jax import lax
from jax.experimental import pallas as pl
from jax.experimental.pallas import tpu as pltpu
from jax.sharding import PartitionSpec as P

MESH = pl.DeviceIdType.MESH
F32 = jnp.float32
BF16 = jnp.bfloat16
HIGHEST = lax.Precision.HIGHEST

LEAF = 256
LEAVES = 4
WIDTH = 256
RANK = 16
PLANES = 8
PLANE = 8


def transform_tables():
    odd = np.arange(LEAF)[:, None] + 0.5
    angle = 2 * np.pi * odd * np.arange(LEAF)[None, :] / (2 * LEAF)
    forward = np.concatenate([np.cos(angle), -np.sin(angle)], 0)
    return forward.astype(np.float32), (forward.T / LEAF).astype(np.float32)


def exact_dot(left, right):
    return jnp.dot(left, right, precision=HIGHEST, preferred_element_type=F32)


def dot(left, right):
    return jnp.dot(left, right, preferred_element_type=F32)


def halves(value):
    high = value.astype(BF16)
    return high, (value - high.astype(F32)).astype(BF16)


def selector(lanes, period, shift, limit):
    row = lax.broadcasted_iota(jnp.int32, (RANK, lanes), 0)
    lane = lax.broadcasted_iota(jnp.int32, (RANK, lanes), 1)
    return ((lax.rem(lane, period) == row + shift) & (lane < limit)).astype(F32)


def body(
    tok, gain, w_value, w_gate, phi, coeff, skip, up, down, lift, spread, coup, fwd, inv,
    out,
    g, w, gain_v, phi_v, coeff_v, skip_v, up_v, down_v, lift_v, spread_v, coup_v, fwd_f, inv_f, fwd_v, inv_v,
    vals, halo, gate, near, spec, khat, mom_m, lift_m, six_m, far_m, red_m, moms,
    m2, m2_prev, ctx_out, ctx_in, pack_out, pack_in, m5_in, far0, far1, out_v, parts, part_squares,
    local_sem, dsend, drecv, rsend, rrecv, hsem, csem, s1, r1, s1p, r1p, s2, r2, s5, r5, ready_plane, ready_next, ready_edge, ready_later, osem,
):
    t = lax.axis_index("tm")
    x = lax.axis_index("chan")
    core = lax.rem(t, 2)
    y = lax.rem(lax.div(t, 2), 4)
    z = lax.div(t, PLANE)
    own = lax.rem(t, PLANE)
    right, left = lax.rem(x + 1, 4), lax.rem(x + 3, 4)

    barrier = pltpu.get_barrier_semaphore()

    def signal(semaphore, frames, chans):
        pl.semaphore_signal(semaphore, inc=1, device_id=(frames, chans), device_id_type=MESH)

    signal(barrier, t, right)
    signal(barrier, t, left)

    @pl.when(z < PLANES - 1)
    def _():
        signal(barrier, t + PLANE, x)

    for k in range(1, PLANE):

        @pl.when(own + k < PLANE)
        def _():
            signal(barrier, t + k, x)

    m2_prev[...] = jnp.zeros_like(m2_prev)
    ctx_in[...] = jnp.zeros_like(ctx_in)
    pack_in[...] = jnp.zeros_like(pack_in)
    m5_in[...] = jnp.zeros_like(m5_in)
    halo[...] = jnp.zeros_like(halo)

    pl.semaphore_wait(barrier, 2 + own + jnp.where(z > 0, 1, 0))

    owners = [x, left, right, lax.rem(x + 2, 4)]

    def leaf_rows(leaf):
        return pl.ds(leaf * LEAF if isinstance(leaf, int) else pl.multiple_of(leaf * LEAF, LEAF), LEAF)

    def direct(group, way):
        rows = pl.ds((1 - group) * 2 * LEAF, 2 * LEAF)
        return pltpu.make_async_remote_copy(
            src_ref=tok.at[rows],
            dst_ref=g.at[1 + way, rows],
            send_sem=dsend.at[way, group],
            recv_sem=drecv.at[way, group],
            device_id=(t, left if way else right),
            device_id_type=MESH,
        )

    def relay(group, way):
        rows = leaf_rows((1 - group) * 2 + way)
        return pltpu.make_async_remote_copy(
            src_ref=g.at[1 + way, rows],
            dst_ref=g.at[3, rows],
            send_sem=rsend.at[way, group],
            recv_sem=rrecv.at[way, group],
            device_id=(t, left if way else right),
            device_id_type=MESH,
        )

    def send_direct(group):
        for way in range(2):
            direct(group, way).start()

    def pass_on(group):
        for way in range(2):
            direct(group, way).wait_recv()
            relay(group, way).start()

    def wait_relayed(group):
        for way in range(2):
            relay(group, way).wait_recv()

    def tables_near():
        for name in ("phi", "coeff", "fwd"):
            copies[name].wait()
        fwd_v[...] = jnp.concatenate(halves(fwd_f[...]), 1)
        taps = phi_v[...].astype(BF16).astype(F32)
        kernel_taps = lax.dot_general(
            taps, coeff_v[...], (((0,), (0,)), ((), ())), precision=HIGHEST, preferred_element_type=F32
        )
        both = jnp.concatenate([kernel_taps[:LEAF], kernel_taps[LEAF:]], 1)
        high, low = halves(both)
        hat = dot(fwd_v[...], jnp.concatenate([high, high], 0)) + dot(fwd_v[:, :LEAF], low)
        a_re, a_im = hat[:LEAF, :WIDTH], hat[LEAF:, :WIDTH]
        b_re, b_im = hat[:LEAF, WIDTH:], hat[LEAF:, WIDTH:]
        row = lax.broadcasted_iota(jnp.int32, (LEAF, WIDTH), 0)
        sign = (1 - 2 * lax.rem(row, 2)).astype(F32)
        khat[0] = a_re
        khat[1] = a_im
        khat[2] = b_re - sign * a_im
        khat[3] = b_im + sign * a_re

    def tables_moments():
        copies["up"].wait()
        copies["lift"].wait()
        base = up_v[...]
        first = [exact_dot(lift_v[0, k], base) for k in range(2)]
        for leaf in range(LEAVES):
            second = exact_dot(lift_v[1, leaf // 2], first[leaf % 2])
            high, low = halves(jnp.concatenate([base, first[leaf % 2], second], 0))
            mom_m[leaf] = jnp.concatenate([high, low], 1)

    def tables_lift():
        def pair(level):
            return exact_dot(lift_v[level, 0], selector(128, 32, 0, 128)) + exact_dot(
                lift_v[level, 1], selector(128, 32, 16, 128)
            )

        def blocks(level, copies_of):
            rows = jnp.concatenate([pair(level)] * copies_of, 0)
            row = lax.broadcasted_iota(jnp.int32, rows.shape, 0)
            lane = lax.broadcasted_iota(jnp.int32, rows.shape, 1)
            return jnp.where(lax.div(row, RANK) == lax.div(lane, 2 * RANK), rows, 0.0)

        three = blocks(2, 8)
        four = exact_dot(blocks(3, 2), three)
        five = exact_dot(blocks(4, 1), jnp.concatenate([four, jnp.zeros((96, 128), F32)], 0))
        whole = jnp.concatenate([four, three[32:64], five, three[:32]], 0)
        high, low = halves(whole)
        lift_m[...] = jnp.concatenate([high, low], 1)
        six = exact_dot(lift_v[5, 0], selector(128, 32, 0, 64)) + exact_dot(
            lift_v[5, 1], selector(128, 32, 16, 64)
        )
        high = six.astype(BF16).astype(F32)
        lane = lax.broadcasted_iota(jnp.int32, six.shape, 1)
        six_m[...] = jnp.where(lane < 32, high, six - high).astype(BF16)

    def tables_far():
        copies["spread"].wait()
        copies["down"].wait()
        row = lax.broadcasted_iota(jnp.int32, (RANK, LEAF), 0)
        lane = lax.broadcasted_iota(jnp.int32, (RANK, LEAF), 1)
        summing = (lax.div(lane, RANK) == row).astype(F32)
        chain = None
        for k in range(5):
            if k > 0:
                step = spread_v[1 + k, lax.rem(lax.div(t, 2 ** (k - 1)), 2)]
                chain = step if k == 1 else exact_dot(chain, step)
            high, low = halves(summing if k == 0 else exact_dot(chain, summing))
            red_m[k] = jnp.concatenate([high, low], 0)
        for leaf in range(LEAVES):
            near_step = spread_v[0, leaf % 2]
            both_steps = exact_dot(near_step, spread_v[1, leaf // 2])
            mix = (
                selector(LEAF, 48, 0, 144)
                + exact_dot(near_step, selector(LEAF, 48, 16, 144))
                + exact_dot(both_steps, selector(LEAF, 48, 32, 144))
            )
            whole = lax.dot_general(
                down_v[...], mix, (((0,), (0,)), ((), ())), precision=HIGHEST, preferred_element_type=F32
            )
            high = whole.astype(BF16).astype(F32)
            lane_at = lax.broadcasted_iota(jnp.int32, whole.shape, 1)
            far_m[leaf] = jnp.where(lane_at < 96, high, whole - high).astype(BF16)

    def scaled_rows(leaf, slots):
        rows = leaf_rows(leaf)
        squares = jnp.zeros((LEAF, WIDTH), F32)
        columns = []
        for slot in slots:
            tokens = g[slot, rows, :].astype(F32)
            squares = squares + tokens * tokens
            scale = gain_v[:, pl.ds(pl.multiple_of(owners[slot] * WIDTH, WIDTH), WIDTH)]
            columns.append((tokens * scale).astype(BF16))
        return jnp.concatenate(columns, 1), squares

    def gather_part(leaf):
        scaled, squares = scaled_rows(leaf, (0, 1, 2))
        parts[leaf] = dot(scaled, w[:3].reshape(3 * WIDTH, 2 * WIDTH))
        part_squares[leaf] = squares[:, : WIDTH // 2] + squares[:, WIDTH // 2 :]

    def values_of(leaf):
        scaled, squares = scaled_rows(leaf, (3,))
        squares = squares[:, : WIDTH // 2] + squares[:, WIDTH // 2 :] + part_squares[leaf]
        inverse = lax.rsqrt(jnp.sum(squares, axis=1, keepdims=True) / 1024 + 1e-06)
        part_squares[leaf] = jnp.broadcast_to(inverse, squares.shape)
        value = ((parts[leaf, :, :WIDTH] + dot(scaled, w[3, :, :WIDTH])) * inverse).astype(BF16)
        vals[leaf_rows(leaf), :] = value
        moms[leaf] = dot(mom_m[leaf], jnp.concatenate([value, value], 0))

    def gates_of(leaf):
        scaled, _ = scaled_rows(leaf, (3,))
        inverse = part_squares[leaf]
        sums = parts[leaf, :, WIDTH:] + dot(scaled, w[3, :, WIDTH:])
        gate[leaf_rows(leaf), :] = jax.nn.sigmoid(sums * jnp.concatenate([inverse, inverse], 1))

    def spectrum_of(leaf):
        value = vals[leaf_rows(leaf), :]
        spec[leaf] = dot(fwd_v[...], jnp.concatenate([value, value], 0))

    def near_rows(leaf):
        rows = leaf_rows(leaf)
        before = (leaf - 1 if leaf > 0 else LEAVES) if isinstance(leaf, int) else leaf - 1
        a_re, a_im = spec[leaf, :LEAF, :], spec[leaf, LEAF:, :]
        b_re, b_im = spec[before, :LEAF, :], spec[before, LEAF:, :]
        out_re = khat[0] * a_re - khat[1] * a_im + khat[2] * b_re - khat[3] * b_im
        out_im = khat[0] * a_im + khat[1] * a_re + khat[2] * b_im + khat[3] * b_re
        both = jnp.concatenate([out_re, out_im], 0).astype(BF16)
        total = dot(inv_v[...], jnp.concatenate([both, both], 0))
        near[rows, :] = total + skip_v[...] * vals[rows, :].astype(F32)

    def coupled(level, source_two, source_three):
        product = coup_v[level, 0] * source_two[None]
        if source_three is not None:
            product = product + coup_v[level, 1] * source_three[None]
        return product.reshape(RANK * RANK, WIDTH).astype(BF16)

    send_direct(0)

    copies = {}

    def local(name, source, target):
        copies[name] = pltpu.make_async_copy(source, target, local_sem.at[len(copies)])
        copies[name].start()

    local("tok", tok, g.at[0])
    for slot in range(4):
        rows = pl.ds(pl.multiple_of(owners[slot] * WIDTH, WIDTH), WIDTH)
        local(("v", slot), w_value.at[rows], w.at[slot, :, pl.ds(0, WIDTH)])
        local(("g", slot), w_gate.at[rows], w.at[slot, :, pl.ds(WIDTH, WIDTH)])
    for name, source, target in (
        ("gain", gain, gain_v),
        ("phi", phi, phi_v),
        ("coeff", coeff, coeff_v),
        ("fwd", fwd, fwd_f),
        ("skip", skip, skip_v),
        ("up", up, up_v),
        ("down", down, down_v),
        ("lift", lift, lift_v),
        ("spread", spread, spread_v),
        ("inv", inv, inv_f),
        ("coup", coup, coup_v),
    ):
        local(name, source, target)

    @pl.when(z > 0)
    def _():
        signal(ready_next, t - PLANE, x)

    for k in range(1, PLANE):

        @pl.when(own >= k)
        def _():
            signal(ready_plane, t - k, x)

    def chain(place):
        @pl.when(z == PLANES - 1 - place)
        def _():
            if not isinstance(place, int) or place > 0:
                pl.semaphore_wait(ready_later, 1)
            if not isinstance(place, int) or place < PLANES - 1:
                signal(ready_later, t - PLANE, x)

    def over(first, last, work):
        def step(leaf, carry):
            work(leaf)
            return carry

        lax.fori_loop(first, last, step, 0)

    chain(0)
    tables_near()
    send_direct(1)
    chain(1)
    tables_moments()
    tables_lift()
    chain(2)

    @pl.when(own < PLANE - 1)
    def _():
        pl.semaphore_wait(ready_plane, PLANE - 1 - own)

    @pl.when(z < PLANES - 1)
    def _():
        pl.semaphore_wait(ready_next, 1)

        @pl.when(y == 0)
        def _():
            signal(ready_edge, z * PLANE + 6, x)
            signal(ready_edge, z * PLANE + 7, x)

    for slot in range(4):
        copies["v", slot].wait()
        copies["g", slot].wait()
    for name in ("tok", "gain", "skip", "coup", "inv"):
        copies[name].wait()
    chain(3)
    pass_on(0)
    chain(4)
    over(2, 4, gather_part)
    tables_far()
    inv_v[...] = jnp.concatenate(halves(inv_f[...]), 1)
    chain(5)

    @pl.when((y == 3) & (z < PLANES - 1))
    def _():
        pl.semaphore_wait(ready_edge, 2)

    pass_on(1)
    chain(6)
    over(0, 2, gather_part)
    chain(7)

    halo_copy = pltpu.make_async_remote_copy(
        src_ref=vals.at[pl.ds(3 * LEAF, LEAF)],
        dst_ref=halo,
        send_sem=hsem.at[0],
        recv_sem=hsem.at[1],
        device_id=(t + 1, x),
        device_id_type=MESH,
    )

    ctx_copy = pltpu.make_async_remote_copy(
        src_ref=ctx_out,
        dst_ref=ctx_in,
        send_sem=csem.at[0],
        recv_sem=csem.at[1],
        device_id=(t + 1, x),
        device_id_type=MESH,
    )

    wait_relayed(0)
    over(2, 4, values_of)

    @pl.when(t < PLANES * PLANE - 1)
    def _():
        halo_copy.start()

    over(2, 4, spectrum_of)
    over(2, 4, gates_of)
    near_rows(3)

    wait_relayed(1)
    over(0, 2, values_of)

    total = moms[0, 32:48, :] + moms[1, 32:48, :] + moms[2, 32:48, :] + moms[3, 32:48, :]
    m2[own] = total.astype(BF16)

    def plane_copy(k):
        return pltpu.make_async_remote_copy(
            src_ref=m2.at[own],
            dst_ref=m2.at[own],
            send_sem=s1.at[k - 1],
            recv_sem=r1.at[k - 1],
            device_id=(z * PLANE + lax.rem(own + k, PLANE), x),
            device_id_type=MESH,
        )

    def plane_arrival(k):
        return pltpu.make_async_remote_copy(
            src_ref=m2.at[own],
            dst_ref=m2.at[lax.rem(own + PLANE - k, PLANE)],
            send_sem=s1.at[k - 1],
            recv_sem=r1.at[k - 1],
            device_id=(z * PLANE + lax.rem(own + k, PLANE), x),
            device_id_type=MESH,
        )

    for k in range(1, PLANE):
        plane_copy(k).start()

    def next_plane_copy(target, source):
        return pltpu.make_async_remote_copy(
            src_ref=m2.at[own],
            dst_ref=m2_prev.at[source],
            send_sem=s1p.at[target],
            recv_sem=r1p.at[source],
            device_id=((z + 1) * PLANE + target, x),
            device_id_type=MESH,
        )

    @pl.when((y == 3) & (z < PLANES - 1))
    def _():
        for target in range(2):
            next_plane_copy(target, core).start()

    ctx_out[...] = jnp.concatenate(
        [
            moms[2, 0:16, :],
            moms[3, 0:16, :],
            moms[0, 16:32, :] + moms[1, 16:32, :],
            moms[2, 16:32, :] + moms[3, 16:32, :],
        ],
        0,
    ).astype(BF16)

    @pl.when(t < PLANES * PLANE - 1)
    def _():
        ctx_copy.start()

    over(0, 2, gates_of)

    for k in range(1, PLANE):
        plane_arrival(k).wait_recv()
    stack = m2[...].reshape(PLANE * RANK, WIDTH)
    lifted = dot(lift_m[...], jnp.concatenate([stack, stack], 0))
    pack_out[...] = lifted[:80].astype(BF16)


    def pack_copy(rows):
        return pltpu.make_async_remote_copy(
            src_ref=pack_out.at[pl.ds(0, rows)],
            dst_ref=pack_in.at[pl.ds(0, rows)],
            send_sem=s2,
            recv_sem=r2,
            device_id=(t + PLANE, x),
            device_id_type=MESH,
        )

    def five_copy(k):
        return pltpu.make_async_remote_copy(
            src_ref=pack_out.at[pl.ds(64, RANK)],
            dst_ref=m5_in.at[k],
            send_sem=s5.at[k],
            recv_sem=r5.at[k],
            device_id=(t + k * PLANE, x),
            device_id_type=MESH,
        )

    @pl.when((z < PLANES - 1) & (y < 2))
    def _():
        pack_copy(64).start()

    @pl.when((z < PLANES - 1) & (y >= 2))
    def _():
        pack_copy(32).start()

    for k in range(2, PLANES):

        @pl.when(z + k < PLANES)
        def _():
            five_copy(k).start()

    over(0, 2, spectrum_of)
    over(1, 3, near_rows)

    @pl.when(t > 0)
    def _():
        halo_copy.wait_recv()

    before = halo[...]
    spec[LEAVES] = dot(fwd_v[...], jnp.concatenate([before, before], 0))
    near_rows(0)

    summing = red_m[0, :RANK, :]

    def gathered(level, source_two, source_three=None):
        return dot(summing, coupled(level, source_two, source_three))

    @pl.when(t > 0)
    def _():
        ctx_copy.wait_recv()

    prev = ctx_in[...].astype(F32)
    far0[0] = gathered(0, prev[0:16])
    far0[1] = gathered(0, prev[16:32], prev[0:16])
    far0[2] = gathered(0, moms[0, 0:16, :])
    far0[3] = gathered(0, moms[1, 0:16, :], moms[0, 0:16, :])
    far1[0] = gathered(1, prev[32:48])
    far1[1] = gathered(1, prev[48:64], prev[32:48])

    for way in range(2):
        for group in range(2):
            direct(group, way).wait_send()
            relay(group, way).wait_send()

    for k in range(1, PLANE):
        plane_copy(k).wait_send()

    @pl.when(t < PLANES * PLANE - 1)
    def _():
        halo_copy.wait_send()
        ctx_copy.wait_send()

    @pl.when((y == 3) & (z < PLANES - 1))
    def _():
        for target in range(2):
            next_plane_copy(target, core).wait_send()

    @pl.when((y == 0) & (z > 0))
    def _():
        for source in range(2):
            next_plane_copy(source, source).wait_recv()

    def reduced(k, source_two, source_three):
        return dot(red_m[k], coupled(2 + k, source_two, source_three))

    at = 2 * jnp.maximum(y - 1, 0)
    inside = y > 0
    two = jnp.where(inside, m2[at + core], m2_prev[core]).astype(F32)
    three = jnp.where(inside, m2[at], m2_prev[0]).astype(F32) * core.astype(F32)
    expansion = reduced(0, two, three)

    @pl.when((z > 0) & (y < 2))
    def _():
        pack_copy(64).wait_recv()

    @pl.when((z > 0) & (y >= 2))
    def _():
        pack_copy(32).wait_recv()

    odd = lax.rem(y, 2)
    lower = y < 2
    here = jnp.where(odd == 1, lifted[96:112], lifted[80:96])
    coming = pack_in[pl.ds(pl.multiple_of(32 + odd * RANK, RANK), RANK), :].astype(F32)
    two = jnp.where(lower, coming, here)
    three = jnp.where(lower, pack_in[32:48, :].astype(F32), lifted[80:96]) * odd.astype(F32)
    expansion = expansion + reduced(1, two, three)
    odd = lax.div(y, 2)
    two = pack_in[pl.ds(pl.multiple_of(odd * RANK, RANK), RANK), :].astype(F32)
    three = pack_in[0:16, :].astype(F32) * odd.astype(F32)
    expansion = expansion + reduced(2, two, three)

    for k in range(2, PLANES):

        @pl.when(z >= k)
        def _():
            five_copy(k).wait_recv()

    odd = lax.rem(z, 2)
    expansion = expansion + reduced(
        3, m5_in[2].astype(F32), m5_in[3].astype(F32) * odd.astype(F32)
    )
    pad = jnp.zeros((64, WIDTH), BF16)

    def sixth(base):
        pair = [m5_in[base], m5_in[base - 1]]
        return dot(six_m[...], jnp.concatenate(pair + pair + [pad], 0))

    odd_six = lax.rem(lax.div(z, 2), 2)
    expansion = expansion + reduced(
        4, sixth(4 + odd), sixth(6 + odd) * odd_six.astype(F32)
    )

    expansion = expansion[:RANK] + expansion[RANK:]

    def out_copy(leaf):
        rows = leaf_rows(leaf)
        return pltpu.make_async_copy(out_v.at[rows], out.at[rows], osem.at[leaf])

    for leaf in range(LEAVES):
        rows = leaf_rows(leaf)
        high, low = halves(jnp.concatenate([far0[leaf], far1[leaf // 2], expansion], 0))
        whole = jnp.concatenate([high, low, high, jnp.zeros((112, WIDTH), BF16)], 0)
        combined = near[rows, :] + dot(far_m[leaf], whole)
        out_v[rows, :] = (gate[rows, :] * combined).astype(BF16)
        out_copy(leaf).start()

    @pl.when((z < PLANES - 1) & (y < 2))
    def _():
        pack_copy(64).wait_send()

    @pl.when((z < PLANES - 1) & (y >= 2))
    def _():
        pack_copy(32).wait_send()

    for k in range(2, PLANES):

        @pl.when(z + k < PLANES)
        def _():
            five_copy(k).wait_send()

    for leaf in range(LEAVES):
        out_copy(leaf).wait()


def per_device(
    tokens,
    norm_gain,
    w_value,
    w_gate,
    phi_taps,
    tap_coeff,
    skip_gain,
    basis_up,
    basis_down,
    lift_maps,
    spread_maps,
    couplings,
):
    forward, inverse = transform_tables()
    in_hbm = pl.BlockSpec(memory_space=pltpu.HBM)
    frames = LEAF * LEAVES
    vmem = pltpu.VMEM
    dma = pltpu.SemaphoreType.DMA
    scratch = [
        vmem((4, frames, WIDTH), BF16),
        vmem((4, WIDTH, 2 * WIDTH), BF16),
        vmem((1, 4 * WIDTH), F32),
        vmem(phi_taps.shape, F32),
        vmem(tap_coeff.shape, F32),
        vmem((1, WIDTH), F32),
        vmem(basis_up.shape, F32),
        vmem(basis_down.shape, F32),
        vmem(lift_maps.shape, F32),
        vmem(spread_maps.shape, F32),
        vmem(couplings.shape, F32),
        vmem(forward.shape, F32),
        vmem(inverse.shape, F32),
        vmem((2 * LEAF, 2 * LEAF), BF16),
        vmem((LEAF, 4 * LEAF), BF16),
        vmem((frames, WIDTH), BF16),
        vmem((LEAF, WIDTH), BF16),
        vmem((frames, WIDTH), F32),
        vmem((frames, WIDTH), F32),
        vmem((LEAVES + 1, 2 * LEAF, WIDTH), F32),
        vmem((4, LEAF, WIDTH), F32),
        vmem((LEAVES, 48, 2 * LEAF), BF16),
        vmem((112, 256), BF16),
        vmem((RANK, 128), BF16),
        vmem((LEAVES, LEAF, LEAF), BF16),
        vmem((5, 2 * RANK, LEAF), BF16),
        vmem((LEAVES, 48, WIDTH), F32),
        vmem((PLANE, RANK, WIDTH), BF16),
        vmem((2, RANK, WIDTH), BF16),
        vmem((64, WIDTH), BF16),
        vmem((64, WIDTH), BF16),
        vmem((80, WIDTH), BF16),
        vmem((64, WIDTH), BF16),
        vmem((PLANES, RANK, WIDTH), BF16),
        vmem((LEAVES, RANK, WIDTH), F32),
        vmem((2, RANK, WIDTH), F32),
        vmem((frames, WIDTH), BF16),
        vmem((LEAVES, LEAF, 2 * WIDTH), F32),
        vmem((LEAVES, LEAF, WIDTH // 2), F32),
        dma((20,)),
        dma((2, 2)),
        dma((2, 2)),
        dma((2, 2)),
        dma((2, 2)),
        dma((2,)),
        dma((2,)),
        dma((PLANE - 1,)),
        dma((PLANE - 1,)),
        dma((2,)),
        dma((2,)),
        dma(()),
        dma(()),
        dma((PLANES,)),
        dma((PLANES,)),
        pltpu.SemaphoreType.REGULAR,
        pltpu.SemaphoreType.REGULAR,
        pltpu.SemaphoreType.REGULAR,
        pltpu.SemaphoreType.REGULAR,
        dma((LEAVES,)),
    ]
    return pl.pallas_call(
        body,
        out_shape=jax.ShapeDtypeStruct(tokens.shape, BF16),
        in_specs=[in_hbm] * 14,
        out_specs=in_hbm,
        scratch_shapes=scratch,
        compiler_params=pltpu.CompilerParams(
            collective_id=0, has_side_effects=True, vmem_limit_bytes=60 * 1024 * 1024
        ),
        cost_estimate=pl.CostEstimate(flops=4 * 10**9, bytes_accessed=8 * 10**6, transcendentals=10**6),
    )(
        tokens,
        norm_gain.reshape(1, -1),
        w_value,
        w_gate,
        phi_taps,
        tap_coeff,
        skip_gain.reshape(1, -1),
        basis_up,
        basis_down,
        lift_maps,
        spread_maps,
        couplings,
        jnp.asarray(forward),
        jnp.asarray(inverse),
    )


def solution(mesh):
    placed = (
        P("tm", "chan"),
        P(),
        P(None, "chan"),
        P(None, "chan"),
        P(),
        P(None, "chan"),
        P("chan"),
        P(),
        P(),
        P(),
        P(),
        P(None, None, None, None, "chan"),
    )
    return jax.shard_map(
        per_device, mesh=mesh, in_specs=placed, out_specs=P("tm", "chan"), check_vma=False
    )
```

```python
import jax
import jax.numpy as jnp
import numpy as np
from jax import lax
from jax.experimental import pallas as pl
from jax.experimental.pallas import tpu as pltpu
from jax.sharding import PartitionSpec as P

MESH = pl.DeviceIdType.MESH
F32 = jnp.float32
BF16 = jnp.bfloat16

LEAF = 256
LEAVES = 4
WIDTH = 256
RANK = 16
PLANES = 8
PLANE = 8


def transform_tables():
    odd = np.arange(LEAF)[:, None] + 0.5
    angle = 2 * np.pi * odd * np.arange(LEAF)[None, :] / (2 * LEAF)
    forward = np.concatenate([np.cos(angle), -np.sin(angle)], 0)
    return forward.astype(np.float32), (forward.T / LEAF).astype(np.float32)


def dot(left, right):
    return jnp.dot(left, right, preferred_element_type=F32)


def halves(value):
    high = value.astype(BF16)
    return high, (value - high.astype(F32)).astype(BF16)


def fine_dot(left, right):
    left_high, left_low = halves(left)
    right_high, right_low = halves(right)
    return dot(left_high, right_high) + dot(left_high, right_low) + dot(left_low, right_high)


def place_dot(left, right):
    left_high, left_low = halves(left)
    ones = right.astype(BF16)
    return dot(left_high, ones) + dot(left_low, ones)


def selector(lanes, period, shift, limit):
    row = lax.broadcasted_iota(jnp.int32, (RANK, lanes), 0)
    lane = lax.broadcasted_iota(jnp.int32, (RANK, lanes), 1)
    return ((lax.rem(lane, period) == row + shift) & (lane < limit)).astype(F32)


def body(
    tok, gain, w_value, w_gate, phi, coeff, skip, up, down, lift, spread, coup, fwd, inv,
    out,
    g, w, gain_v, phi_v, coeff_v, skip_v, up_v, down_v, lift_v, spread_v, coup_v, fwd_f, inv_f, fwd_v, inv_v,
    vals, halo, gate, near, spec, khat, mom_m, lift_m, six_m, far_m, red_m, moms,
    m2, m2_prev, ctx_out, ctx_in, pack_out, pack_in, m5_in, far0, far1, out_v, parts, part_squares,
    local_sem, dsend, drecv, rsend, rrecv, hsem, csem, s1, r1, s1p, r1p, s2, r2, s5, r5, ready_plane, ready_next, ready_edge, ready_later, osem,
):
    t = lax.axis_index("tm")
    x = lax.axis_index("chan")
    core = lax.rem(t, 2)
    y = lax.rem(lax.div(t, 2), 4)
    z = lax.div(t, PLANE)
    own = lax.rem(t, PLANE)
    right, left = lax.rem(x + 1, 4), lax.rem(x + 3, 4)

    barrier = pltpu.get_barrier_semaphore()

    def signal(semaphore, frames, chans):
        pl.semaphore_signal(semaphore, inc=1, device_id=(frames, chans), device_id_type=MESH)

    signal(barrier, t, right)
    signal(barrier, t, left)

    @pl.when(z < PLANES - 1)
    def _():
        signal(barrier, t + PLANE, x)

    for k in range(1, PLANE):

        @pl.when(own + k < PLANE)
        def _():
            signal(barrier, t + k, x)

    m2_prev[...] = jnp.zeros_like(m2_prev)
    ctx_in[...] = jnp.zeros_like(ctx_in)
    pack_in[...] = jnp.zeros_like(pack_in)
    m5_in[...] = jnp.zeros_like(m5_in)
    halo[...] = jnp.zeros_like(halo)

    pl.semaphore_wait(barrier, 2 + own + jnp.where(z > 0, 1, 0))

    owners = [x, left, right, lax.rem(x + 2, 4)]

    def leaf_rows(leaf):
        return pl.ds(leaf * LEAF if isinstance(leaf, int) else pl.multiple_of(leaf * LEAF, LEAF), LEAF)

    def direct(group, way):
        rows = pl.ds((1 - group) * 2 * LEAF, 2 * LEAF)
        return pltpu.make_async_remote_copy(
            src_ref=tok.at[rows],
            dst_ref=g.at[1 + way, rows],
            send_sem=dsend.at[way, group],
            recv_sem=drecv.at[way, group],
            device_id=(t, left if way else right),
            device_id_type=MESH,
        )

    def relay(group, way):
        rows = leaf_rows((1 - group) * 2 + way)
        return pltpu.make_async_remote_copy(
            src_ref=g.at[1 + way, rows],
            dst_ref=g.at[3, rows],
            send_sem=rsend.at[way, group],
            recv_sem=rrecv.at[way, group],
            device_id=(t, left if way else right),
            device_id_type=MESH,
        )

    def send_direct(group):
        for way in range(2):
            direct(group, way).start()

    def pass_on(group):
        for way in range(2):
            direct(group, way).wait_recv()
            relay(group, way).start()

    def wait_relayed(group):
        for way in range(2):
            relay(group, way).wait_recv()

    def tables_near():
        for name in ("phi", "coeff", "fwd"):
            copies[name].wait()
        fwd_v[...] = jnp.concatenate(halves(fwd_f[...]), 1)
        taps = phi_v[...].astype(BF16).astype(F32).T.astype(BF16)
        coeff_high, coeff_low = halves(coeff_v[...])
        kernel_taps = dot(taps, coeff_high) + dot(taps, coeff_low)
        both = jnp.concatenate([kernel_taps[:LEAF], kernel_taps[LEAF:]], 1)
        high, low = halves(both)
        hat = dot(fwd_v[...], jnp.concatenate([high, high], 0)) + dot(fwd_v[:, :LEAF], low)
        a_re, a_im = hat[:LEAF, :WIDTH], hat[LEAF:, :WIDTH]
        b_re, b_im = hat[:LEAF, WIDTH:], hat[LEAF:, WIDTH:]
        row = lax.broadcasted_iota(jnp.int32, (LEAF, WIDTH), 0)
        sign = (1 - 2 * lax.rem(row, 2)).astype(F32)
        khat[0] = a_re
        khat[1] = a_im
        khat[2] = b_re - sign * a_im
        khat[3] = b_im + sign * a_re

    def tables_moments():
        copies["up"].wait()
        copies["lift"].wait()
        base = up_v[...]
        first = [fine_dot(lift_v[0, k], base) for k in range(2)]
        for leaf in range(LEAVES):
            second = fine_dot(lift_v[1, leaf // 2], first[leaf % 2])
            high, low = halves(jnp.concatenate([base, first[leaf % 2], second], 0))
            mom_m[leaf] = jnp.concatenate([high, low], 1)

    def tables_lift():
        def pair(level):
            return place_dot(lift_v[level, 0], selector(128, 32, 0, 128)) + place_dot(
                lift_v[level, 1], selector(128, 32, 16, 128)
            )

        def blocks(level, copies_of):
            rows = jnp.concatenate([pair(level)] * copies_of, 0)
            row = lax.broadcasted_iota(jnp.int32, rows.shape, 0)
            lane = lax.broadcasted_iota(jnp.int32, rows.shape, 1)
            return jnp.where(lax.div(row, RANK) == lax.div(lane, 2 * RANK), rows, 0.0)

        three = blocks(2, 8)
        four = fine_dot(blocks(3, 2), three)
        five = fine_dot(blocks(4, 1), jnp.concatenate([four, jnp.zeros((96, 128), F32)], 0))
        whole = jnp.concatenate([four, three[32:64], five, three[:32]], 0)
        high, low = halves(whole)
        lift_m[...] = jnp.concatenate([high, low], 1)
        six = place_dot(lift_v[5, 0], selector(128, 32, 0, 64)) + place_dot(
            lift_v[5, 1], selector(128, 32, 16, 64)
        )
        high = six.astype(BF16).astype(F32)
        lane = lax.broadcasted_iota(jnp.int32, six.shape, 1)
        six_m[...] = jnp.where(lane < 32, high, six - high).astype(BF16)

    def tables_far():
        copies["spread"].wait()
        copies["down"].wait()
        row = lax.broadcasted_iota(jnp.int32, (RANK, LEAF), 0)
        lane = lax.broadcasted_iota(jnp.int32, (RANK, LEAF), 1)
        summing = (lax.div(lane, RANK) == row).astype(F32)
        chain = None
        for k in range(5):
            if k > 0:
                step = spread_v[1 + k, lax.rem(lax.div(t, 2 ** (k - 1)), 2)]
                chain = step if k == 1 else fine_dot(chain, step)
            high, low = halves(summing if k == 0 else place_dot(chain, summing))
            red_m[k] = jnp.concatenate([high, low], 0)
        turned = down_v[...].T
        for leaf in range(LEAVES):
            near_step = spread_v[0, leaf % 2]
            both_steps = fine_dot(near_step, spread_v[1, leaf // 2])
            mix = (
                selector(LEAF, 48, 0, 144)
                + place_dot(near_step, selector(LEAF, 48, 16, 144))
                + place_dot(both_steps, selector(LEAF, 48, 32, 144))
            )
            whole = fine_dot(turned, mix)
            high = whole.astype(BF16).astype(F32)
            lane_at = lax.broadcasted_iota(jnp.int32, whole.shape, 1)
            far_m[leaf] = jnp.where(lane_at < 96, high, whole - high).astype(BF16)

    def scaled_rows(leaf, slots):
        rows = leaf_rows(leaf)
        squares = jnp.zeros((LEAF, WIDTH), F32)
        columns = []
        for slot in slots:
            tokens = g[slot, rows, :].astype(F32)
            squares = squares + tokens * tokens
            scale = gain_v[:, pl.ds(pl.multiple_of(owners[slot] * WIDTH, WIDTH), WIDTH)]
            columns.append((tokens * scale).astype(BF16))
        return jnp.concatenate(columns, 1), squares

    def gather_part(leaf):
        scaled, squares = scaled_rows(leaf, (0, 1, 2))
        parts[leaf] = dot(scaled, w[:3].reshape(3 * WIDTH, 2 * WIDTH))
        part_squares[leaf] = squares[:, : WIDTH // 2] + squares[:, WIDTH // 2 :]

    def values_of(leaf):
        scaled, squares = scaled_rows(leaf, (3,))
        squares = squares[:, : WIDTH // 2] + squares[:, WIDTH // 2 :] + part_squares[leaf]
        inverse = lax.rsqrt(jnp.sum(squares, axis=1, keepdims=True) / 1024 + 1e-06)
        part_squares[leaf] = jnp.broadcast_to(inverse, squares.shape)
        value = ((parts[leaf, :, :WIDTH] + dot(scaled, w[3, :, :WIDTH])) * inverse).astype(BF16)
        vals[leaf_rows(leaf), :] = value
        moms[leaf] = dot(mom_m[leaf], jnp.concatenate([value, value], 0))

    def gates_of(leaf):
        scaled, _ = scaled_rows(leaf, (3,))
        inverse = part_squares[leaf]
        sums = parts[leaf, :, WIDTH:] + dot(scaled, w[3, :, WIDTH:])
        gate[leaf_rows(leaf), :] = jax.nn.sigmoid(sums * jnp.concatenate([inverse, inverse], 1))

    def spectrum_of(leaf):
        value = vals[leaf_rows(leaf), :]
        spec[leaf] = dot(fwd_v[...], jnp.concatenate([value, value], 0))

    def near_rows(leaf):
        rows = leaf_rows(leaf)
        before = (leaf - 1 if leaf > 0 else LEAVES) if isinstance(leaf, int) else leaf - 1
        a_re, a_im = spec[leaf, :LEAF, :], spec[leaf, LEAF:, :]
        b_re, b_im = spec[before, :LEAF, :], spec[before, LEAF:, :]
        out_re = khat[0] * a_re - khat[1] * a_im + khat[2] * b_re - khat[3] * b_im
        out_im = khat[0] * a_im + khat[1] * a_re + khat[2] * b_im + khat[3] * b_re
        both = jnp.concatenate([out_re, out_im], 0).astype(BF16)
        total = dot(inv_v[...], jnp.concatenate([both, both], 0))
        near[rows, :] = total + skip_v[...] * vals[rows, :].astype(F32)

    def coupled(level, source_two, source_three):
        product = coup_v[level, 0] * source_two[None]
        if source_three is not None:
            product = product + coup_v[level, 1] * source_three[None]
        return product.reshape(RANK * RANK, WIDTH).astype(BF16)

    send_direct(0)

    copies = {}

    def local(name, source, target):
        copies[name] = pltpu.make_async_copy(source, target, local_sem.at[len(copies)])
        copies[name].start()

    local("tok", tok, g.at[0])
    for slot in range(4):
        rows = pl.ds(pl.multiple_of(owners[slot] * WIDTH, WIDTH), WIDTH)
        local(("v", slot), w_value.at[rows], w.at[slot, :, pl.ds(0, WIDTH)])
        local(("g", slot), w_gate.at[rows], w.at[slot, :, pl.ds(WIDTH, WIDTH)])
    for name, source, target in (
        ("gain", gain, gain_v),
        ("phi", phi, phi_v),
        ("coeff", coeff, coeff_v),
        ("fwd", fwd, fwd_f),
        ("skip", skip, skip_v),
        ("up", up, up_v),
        ("down", down, down_v),
        ("lift", lift, lift_v),
        ("spread", spread, spread_v),
        ("inv", inv, inv_f),
        ("coup", coup, coup_v),
    ):
        local(name, source, target)

    @pl.when(z > 0)
    def _():
        signal(ready_next, t - PLANE, x)

    for k in range(1, PLANE):

        @pl.when(own >= k)
        def _():
            signal(ready_plane, t - k, x)

    def chain(place):
        @pl.when(z == PLANES - 1 - place)
        def _():
            if not isinstance(place, int) or place > 0:
                pl.semaphore_wait(ready_later, 1)
            if not isinstance(place, int) or place < PLANES - 1:
                signal(ready_later, t - PLANE, x)

    def over(first, last, work):
        def step(leaf, carry):
            work(leaf)
            return carry

        lax.fori_loop(first, last, step, 0)

    chain(0)
    tables_near()
    send_direct(1)
    chain(1)
    tables_moments()
    tables_lift()
    chain(2)

    @pl.when(own < PLANE - 1)
    def _():
        pl.semaphore_wait(ready_plane, PLANE - 1 - own)

    @pl.when(z < PLANES - 1)
    def _():
        pl.semaphore_wait(ready_next, 1)

        @pl.when(y == 0)
        def _():
            signal(ready_edge, z * PLANE + 6, x)
            signal(ready_edge, z * PLANE + 7, x)

    for slot in range(4):
        copies["v", slot].wait()
        copies["g", slot].wait()
    for name in ("tok", "gain", "skip", "coup", "inv"):
        copies[name].wait()
    chain(3)
    pass_on(0)
    chain(4)
    over(2, 4, gather_part)
    tables_far()
    inv_v[...] = jnp.concatenate(halves(inv_f[...]), 1)
    chain(5)

    @pl.when((y == 3) & (z < PLANES - 1))
    def _():
        pl.semaphore_wait(ready_edge, 2)

    pass_on(1)
    chain(6)
    over(0, 2, gather_part)
    chain(7)

    halo_copy = pltpu.make_async_remote_copy(
        src_ref=vals.at[pl.ds(3 * LEAF, LEAF)],
        dst_ref=halo,
        send_sem=hsem.at[0],
        recv_sem=hsem.at[1],
        device_id=(t + 1, x),
        device_id_type=MESH,
    )

    ctx_copy = pltpu.make_async_remote_copy(
        src_ref=ctx_out,
        dst_ref=ctx_in,
        send_sem=csem.at[0],
        recv_sem=csem.at[1],
        device_id=(t + 1, x),
        device_id_type=MESH,
    )

    wait_relayed(0)
    over(2, 4, values_of)

    @pl.when(t < PLANES * PLANE - 1)
    def _():
        halo_copy.start()

    over(2, 4, spectrum_of)
    over(2, 4, gates_of)
    near_rows(3)

    wait_relayed(1)
    over(0, 2, values_of)

    total = moms[0, 32:48, :] + moms[1, 32:48, :] + moms[2, 32:48, :] + moms[3, 32:48, :]
    m2[own] = total.astype(BF16)

    def plane_copy(k):
        return pltpu.make_async_remote_copy(
            src_ref=m2.at[own],
            dst_ref=m2.at[own],
            send_sem=s1.at[k - 1],
            recv_sem=r1.at[k - 1],
            device_id=(z * PLANE + lax.rem(own + k, PLANE), x),
            device_id_type=MESH,
        )

    def plane_arrival(k):
        return pltpu.make_async_remote_copy(
            src_ref=m2.at[own],
            dst_ref=m2.at[lax.rem(own + PLANE - k, PLANE)],
            send_sem=s1.at[k - 1],
            recv_sem=r1.at[k - 1],
            device_id=(z * PLANE + lax.rem(own + k, PLANE), x),
            device_id_type=MESH,
        )

    for k in range(1, PLANE):
        plane_copy(k).start()

    def next_plane_copy(target, source):
        return pltpu.make_async_remote_copy(
            src_ref=m2.at[own],
            dst_ref=m2_prev.at[source],
            send_sem=s1p.at[target],
            recv_sem=r1p.at[source],
            device_id=((z + 1) * PLANE + target, x),
            device_id_type=MESH,
        )

    @pl.when((y == 3) & (z < PLANES - 1))
    def _():
        for target in range(2):
            next_plane_copy(target, core).start()

    ctx_out[...] = jnp.concatenate(
        [
            moms[2, 0:16, :],
            moms[3, 0:16, :],
            moms[0, 16:32, :] + moms[1, 16:32, :],
            moms[2, 16:32, :] + moms[3, 16:32, :],
        ],
        0,
    ).astype(BF16)

    @pl.when(t < PLANES * PLANE - 1)
    def _():
        ctx_copy.start()

    over(0, 2, gates_of)

    for k in range(1, PLANE):
        plane_arrival(k).wait_recv()
    stack = m2[...].reshape(PLANE * RANK, WIDTH)
    lifted = dot(lift_m[...], jnp.concatenate([stack, stack], 0))
    pack_out[...] = lifted[:80].astype(BF16)


    def pack_copy(rows):
        return pltpu.make_async_remote_copy(
            src_ref=pack_out.at[pl.ds(0, rows)],
            dst_ref=pack_in.at[pl.ds(0, rows)],
            send_sem=s2,
            recv_sem=r2,
            device_id=(t + PLANE, x),
            device_id_type=MESH,
        )

    def five_copy(k):
        return pltpu.make_async_remote_copy(
            src_ref=pack_out.at[pl.ds(64, RANK)],
            dst_ref=m5_in.at[k],
            send_sem=s5.at[k],
            recv_sem=r5.at[k],
            device_id=(t + k * PLANE, x),
            device_id_type=MESH,
        )

    for k in range(PLANES - 1, 1, -1):

        @pl.when(z + k < PLANES)
        def _():
            five_copy(k).start()

    @pl.when((z < PLANES - 1) & (y < 2))
    def _():
        pack_copy(64).start()

    @pl.when((z < PLANES - 1) & (y >= 2))
    def _():
        pack_copy(32).start()

    over(0, 2, spectrum_of)
    over(1, 3, near_rows)

    @pl.when(t > 0)
    def _():
        halo_copy.wait_recv()

    before = halo[...]
    spec[LEAVES] = dot(fwd_v[...], jnp.concatenate([before, before], 0))
    near_rows(0)

    summing = red_m[0, :RANK, :]

    def gathered(level, source_two, source_three=None):
        return dot(summing, coupled(level, source_two, source_three))

    @pl.when(t > 0)
    def _():
        ctx_copy.wait_recv()

    prev = ctx_in[...].astype(F32)
    far0[0] = gathered(0, prev[0:16])
    far0[1] = gathered(0, prev[16:32], prev[0:16])
    far0[2] = gathered(0, moms[0, 0:16, :])
    far0[3] = gathered(0, moms[1, 0:16, :], moms[0, 0:16, :])
    far1[0] = gathered(1, prev[32:48])
    far1[1] = gathered(1, prev[48:64], prev[32:48])

    for way in range(2):
        for group in range(2):
            direct(group, way).wait_send()
            relay(group, way).wait_send()

    for k in range(1, PLANE):
        plane_copy(k).wait_send()

    @pl.when(t < PLANES * PLANE - 1)
    def _():
        halo_copy.wait_send()
        ctx_copy.wait_send()

    @pl.when((y == 3) & (z < PLANES - 1))
    def _():
        for target in range(2):
            next_plane_copy(target, core).wait_send()

    @pl.when((y == 0) & (z > 0))
    def _():
        for source in range(2):
            next_plane_copy(source, source).wait_recv()

    def reduced(k, source_two, source_three):
        return dot(red_m[k], coupled(2 + k, source_two, source_three))

    at = 2 * jnp.maximum(y - 1, 0)
    inside = y > 0
    two = jnp.where(inside, m2[at + core], m2_prev[core]).astype(F32)
    three = jnp.where(inside, m2[at], m2_prev[0]).astype(F32) * core.astype(F32)
    expansion = reduced(0, two, three)

    @pl.when((z > 0) & (y < 2))
    def _():
        pack_copy(64).wait_recv()

    @pl.when((z > 0) & (y >= 2))
    def _():
        pack_copy(32).wait_recv()

    odd = lax.rem(y, 2)
    lower = y < 2
    here = jnp.where(odd == 1, lifted[96:112], lifted[80:96])
    coming = pack_in[pl.ds(pl.multiple_of(32 + odd * RANK, RANK), RANK), :].astype(F32)
    two = jnp.where(lower, coming, here)
    three = jnp.where(lower, pack_in[32:48, :].astype(F32), lifted[80:96]) * odd.astype(F32)
    expansion = expansion + reduced(1, two, three)
    odd = lax.div(y, 2)
    two = pack_in[pl.ds(pl.multiple_of(odd * RANK, RANK), RANK), :].astype(F32)
    three = pack_in[0:16, :].astype(F32) * odd.astype(F32)
    expansion = expansion + reduced(2, two, three)

    for k in range(2, PLANES):

        @pl.when(z >= k)
        def _():
            five_copy(k).wait_recv()

    odd = lax.rem(z, 2)
    expansion = expansion + reduced(
        3, m5_in[2].astype(F32), m5_in[3].astype(F32) * odd.astype(F32)
    )
    pad = jnp.zeros((64, WIDTH), BF16)

    def sixth(base):
        pair = [m5_in[base], m5_in[base - 1]]
        return dot(six_m[...], jnp.concatenate(pair + pair + [pad], 0))

    odd_six = lax.rem(lax.div(z, 2), 2)
    expansion = expansion + reduced(
        4, sixth(4 + odd), sixth(6 + odd) * odd_six.astype(F32)
    )

    expansion = expansion[:RANK] + expansion[RANK:]

    def out_copy(leaf):
        rows = leaf_rows(leaf)
        return pltpu.make_async_copy(out_v.at[rows], out.at[rows], osem.at[leaf])

    for leaf in range(LEAVES):
        rows = leaf_rows(leaf)
        high, low = halves(jnp.concatenate([far0[leaf], far1[leaf // 2], expansion], 0))
        whole = jnp.concatenate([high, low, high, jnp.zeros((112, WIDTH), BF16)], 0)
        combined = near[rows, :] + dot(far_m[leaf], whole)
        out_v[rows, :] = (gate[rows, :] * combined).astype(BF16)
        out_copy(leaf).start()

    @pl.when((z < PLANES - 1) & (y < 2))
    def _():
        pack_copy(64).wait_send()

    @pl.when((z < PLANES - 1) & (y >= 2))
    def _():
        pack_copy(32).wait_send()

    for k in range(2, PLANES):

        @pl.when(z + k < PLANES)
        def _():
            five_copy(k).wait_send()

    for leaf in range(LEAVES):
        out_copy(leaf).wait()


def per_device(
    tokens,
    norm_gain,
    w_value,
    w_gate,
    phi_taps,
    tap_coeff,
    skip_gain,
    basis_up,
    basis_down,
    lift_maps,
    spread_maps,
    couplings,
):
    forward, inverse = transform_tables()
    in_hbm = pl.BlockSpec(memory_space=pltpu.HBM)
    frames = LEAF * LEAVES
    vmem = pltpu.VMEM
    dma = pltpu.SemaphoreType.DMA
    scratch = [
        vmem((4, frames, WIDTH), BF16),
        vmem((4, WIDTH, 2 * WIDTH), BF16),
        vmem((1, 4 * WIDTH), F32),
        vmem(phi_taps.shape, F32),
        vmem(tap_coeff.shape, F32),
        vmem((1, WIDTH), F32),
        vmem(basis_up.shape, F32),
        vmem(basis_down.shape, F32),
        vmem(lift_maps.shape, F32),
        vmem(spread_maps.shape, F32),
        vmem(couplings.shape, F32),
        vmem(forward.shape, F32),
        vmem(inverse.shape, F32),
        vmem((2 * LEAF, 2 * LEAF), BF16),
        vmem((LEAF, 4 * LEAF), BF16),
        vmem((frames, WIDTH), BF16),
        vmem((LEAF, WIDTH), BF16),
        vmem((frames, WIDTH), F32),
        vmem((frames, WIDTH), F32),
        vmem((LEAVES + 1, 2 * LEAF, WIDTH), F32),
        vmem((4, LEAF, WIDTH), F32),
        vmem((LEAVES, 48, 2 * LEAF), BF16),
        vmem((112, 256), BF16),
        vmem((RANK, 128), BF16),
        vmem((LEAVES, LEAF, LEAF), BF16),
        vmem((5, 2 * RANK, LEAF), BF16),
        vmem((LEAVES, 48, WIDTH), F32),
        vmem((PLANE, RANK, WIDTH), BF16),
        vmem((2, RANK, WIDTH), BF16),
        vmem((64, WIDTH), BF16),
        vmem((64, WIDTH), BF16),
        vmem((80, WIDTH), BF16),
        vmem((64, WIDTH), BF16),
        vmem((PLANES, RANK, WIDTH), BF16),
        vmem((LEAVES, RANK, WIDTH), F32),
        vmem((2, RANK, WIDTH), F32),
        vmem((frames, WIDTH), BF16),
        vmem((LEAVES, LEAF, 2 * WIDTH), F32),
        vmem((LEAVES, LEAF, WIDTH // 2), F32),
        dma((20,)),
        dma((2, 2)),
        dma((2, 2)),
        dma((2, 2)),
        dma((2, 2)),
        dma((2,)),
        dma((2,)),
        dma((PLANE - 1,)),
        dma((PLANE - 1,)),
        dma((2,)),
        dma((2,)),
        dma(()),
        dma(()),
        dma((PLANES,)),
        dma((PLANES,)),
        pltpu.SemaphoreType.REGULAR,
        pltpu.SemaphoreType.REGULAR,
        pltpu.SemaphoreType.REGULAR,
        pltpu.SemaphoreType.REGULAR,
        dma((LEAVES,)),
    ]
    return pl.pallas_call(
        body,
        out_shape=jax.ShapeDtypeStruct(tokens.shape, BF16),
        in_specs=[in_hbm] * 14,
        out_specs=in_hbm,
        scratch_shapes=scratch,
        compiler_params=pltpu.CompilerParams(
            collective_id=0, has_side_effects=True, vmem_limit_bytes=60 * 1024 * 1024
        ),
        cost_estimate=pl.CostEstimate(flops=4 * 10**9, bytes_accessed=8 * 10**6, transcendentals=10**6),
    )(
        tokens,
        norm_gain.reshape(1, -1),
        w_value,
        w_gate,
        phi_taps,
        tap_coeff,
        skip_gain.reshape(1, -1),
        basis_up,
        basis_down,
        lift_maps,
        spread_maps,
        couplings,
        jnp.asarray(forward),
        jnp.asarray(inverse),
    )


def solution(mesh):
    placed = (
        P("tm", "chan"),
        P(),
        P(None, "chan"),
        P(None, "chan"),
        P(),
        P(None, "chan"),
        P("chan"),
        P(),
        P(),
        P(),
        P(),
        P(None, None, None, None, "chan"),
    )
    return jax.shard_map(
        per_device, mesh=mesh, in_specs=placed, out_specs=P("tm", "chan"), check_vma=False
    )
```

```python
import jax
import jax.numpy as jnp
import numpy as np
from jax import lax
from jax.experimental import pallas as pl
from jax.experimental.pallas import tpu as pltpu
from jax.sharding import PartitionSpec as P

MESH = pl.DeviceIdType.MESH
F32 = jnp.float32
BF16 = jnp.bfloat16

LEAF = 256
LEAVES = 4
WIDTH = 256
RANK = 16
PLANES = 8
PLANE = 8


def transform_tables():
    odd = np.arange(LEAF)[:, None] + 0.5
    angle = 2 * np.pi * odd * np.arange(LEAF)[None, :] / (2 * LEAF)
    forward = np.concatenate([np.cos(angle), -np.sin(angle)], 0)
    return forward.astype(np.float32), (forward.T / LEAF).astype(np.float32)


def dot(left, right):
    return jnp.dot(left, right, preferred_element_type=F32)


def halves(value):
    high = value.astype(BF16)
    return high, (value - high.astype(F32)).astype(BF16)


def fine_dot(left, right):
    left_high, left_low = halves(left)
    right_high, right_low = halves(right)
    return dot(left_high, right_high) + dot(left_high, right_low) + dot(left_low, right_high)


def place_dot(left, right):
    left_high, left_low = halves(left)
    ones = right.astype(BF16)
    return dot(left_high, ones) + dot(left_low, ones)


def selector(lanes, period, shift, limit):
    row = lax.broadcasted_iota(jnp.int32, (RANK, lanes), 0)
    lane = lax.broadcasted_iota(jnp.int32, (RANK, lanes), 1)
    return ((lax.rem(lane, period) == row + shift) & (lane < limit)).astype(F32)


def body(
    tok, gain, w_value, w_gate, phi, coeff, skip, up, down, lift, spread, coup, fwd, inv,
    out,
    g, w, gain_v, phi_v, coeff_v, skip_v, up_v, down_v, lift_v, spread_v, coup_v, fwd_f, inv_f, fwd_v, inv_v,
    vals, halo, gate, near, spec, khat, mom_m, lift_m, six_m, far_m, red_m, moms,
    m2, m2_prev, ctx_out, ctx_in, pack_out, pack_in, m5_in, far0, far1, out_v, parts, part_squares,
    local_sem, gsend, drecv, rrecv, hsem, csem, s1, r1, s1p, r1p, s2, r2, s5, r5, ready_plane, ready_next, ready_edge, ready_later, osem,
):
    t = lax.axis_index("tm")
    x = lax.axis_index("chan")
    core = lax.rem(t, 2)
    y = lax.rem(lax.div(t, 2), 4)
    z = lax.div(t, PLANE)
    own = lax.rem(t, PLANE)
    right, left = lax.rem(x + 1, 4), lax.rem(x + 3, 4)

    barrier = pltpu.get_barrier_semaphore()

    def signal(semaphore, frames, chans):
        pl.semaphore_signal(semaphore, inc=1, device_id=(frames, chans), device_id_type=MESH)

    signal(barrier, t, right)
    signal(barrier, t, left)

    @pl.when(z < PLANES - 1)
    def _():
        signal(barrier, t + PLANE, x)

    for k in range(1, PLANE):

        @pl.when(own + k < PLANE)
        def _():
            signal(barrier, t + k, x)

    m2_prev[...] = jnp.zeros_like(m2_prev)
    ctx_in[...] = jnp.zeros_like(ctx_in)
    pack_in[...] = jnp.zeros_like(pack_in)
    m5_in[...] = jnp.zeros_like(m5_in)
    halo[...] = jnp.zeros_like(halo)

    pl.semaphore_wait(barrier, 2 + own + jnp.where(z > 0, 1, 0))

    owners = [x, left, right, lax.rem(x + 2, 4)]

    def leaf_rows(leaf):
        return pl.ds(leaf * LEAF if isinstance(leaf, int) else pl.multiple_of(leaf * LEAF, LEAF), LEAF)

    def direct(piece, way):
        rows = pl.ds(2 * LEAF, 2 * LEAF) if piece == 0 else leaf_rows(way if piece == 1 else 1 - way)
        return pltpu.make_async_remote_copy(
            src_ref=tok.at[rows],
            dst_ref=g.at[1 + way, rows],
            send_sem=gsend,
            recv_sem=drecv.at[way, piece],
            device_id=(t, left if way else right),
            device_id_type=MESH,
        )

    def relay(group, way):
        rows = leaf_rows((1 - group) * 2 + way)
        return pltpu.make_async_remote_copy(
            src_ref=g.at[1 + way, rows],
            dst_ref=g.at[3, rows],
            send_sem=gsend,
            recv_sem=rrecv.at[way, group],
            device_id=(t, left if way else right),
            device_id_type=MESH,
        )

    def send_direct(piece):
        for way in range(2):
            direct(piece, way).start()

    def pass_on(group):
        for way in range(2):
            direct(group, way).wait_recv()
            relay(group, way).start()

    def wait_relayed(group):
        for way in range(2):
            relay(group, way).wait_recv()

    def tables_near():
        for name in ("phi", "coeff", "fwd"):
            copies[name].wait()
        fwd_v[...] = jnp.concatenate(halves(fwd_f[...]), 1)
        taps = phi_v[...].astype(BF16).astype(F32).T.astype(BF16)
        coeff_high, coeff_low = halves(coeff_v[...])
        kernel_taps = dot(taps, coeff_high) + dot(taps, coeff_low)
        both = jnp.concatenate([kernel_taps[:LEAF], kernel_taps[LEAF:]], 1)
        high, low = halves(both)
        hat = dot(fwd_v[...], jnp.concatenate([high, high], 0)) + dot(fwd_v[:, :LEAF], low)
        a_re, a_im = hat[:LEAF, :WIDTH], hat[LEAF:, :WIDTH]
        b_re, b_im = hat[:LEAF, WIDTH:], hat[LEAF:, WIDTH:]
        row = lax.broadcasted_iota(jnp.int32, (LEAF, WIDTH), 0)
        sign = (1 - 2 * lax.rem(row, 2)).astype(F32)
        khat[0] = a_re
        khat[1] = a_im
        khat[2] = b_re - sign * a_im
        khat[3] = b_im + sign * a_re

    def tables_moments():
        copies["up"].wait()
        copies["lift"].wait()
        base = up_v[...]
        first = [fine_dot(lift_v[0, k], base) for k in range(2)]
        for leaf in range(LEAVES):
            second = fine_dot(lift_v[1, leaf // 2], first[leaf % 2])
            high, low = halves(jnp.concatenate([base, first[leaf % 2], second], 0))
            mom_m[leaf] = jnp.concatenate([high, low], 1)

    def tables_lift():
        def pair(level):
            return place_dot(lift_v[level, 0], selector(128, 32, 0, 128)) + place_dot(
                lift_v[level, 1], selector(128, 32, 16, 128)
            )

        def blocks(level, copies_of):
            rows = jnp.concatenate([pair(level)] * copies_of, 0)
            row = lax.broadcasted_iota(jnp.int32, rows.shape, 0)
            lane = lax.broadcasted_iota(jnp.int32, rows.shape, 1)
            return jnp.where(lax.div(row, RANK) == lax.div(lane, 2 * RANK), rows, 0.0)

        three = blocks(2, 8)
        four = fine_dot(blocks(3, 2), three)
        five = fine_dot(blocks(4, 1), jnp.concatenate([four, jnp.zeros((96, 128), F32)], 0))
        whole = jnp.concatenate([four, three[32:64], five, three[:32]], 0)
        high, low = halves(whole)
        lift_m[...] = jnp.concatenate([high, low], 1)
        six = place_dot(lift_v[5, 0], selector(128, 32, 0, 64)) + place_dot(
            lift_v[5, 1], selector(128, 32, 16, 64)
        )
        high = six.astype(BF16).astype(F32)
        lane = lax.broadcasted_iota(jnp.int32, six.shape, 1)
        six_m[...] = jnp.where(lane < 32, high, six - high).astype(BF16)

    def tables_far():
        copies["spread"].wait()
        copies["down"].wait()
        row = lax.broadcasted_iota(jnp.int32, (RANK, LEAF), 0)
        lane = lax.broadcasted_iota(jnp.int32, (RANK, LEAF), 1)
        summing = (lax.div(lane, RANK) == row).astype(F32)
        chain = None
        for k in range(5):
            if k > 0:
                step = spread_v[1 + k, lax.rem(lax.div(t, 2 ** (k - 1)), 2)]
                chain = step if k == 1 else fine_dot(chain, step)
            high, low = halves(summing if k == 0 else place_dot(chain, summing))
            red_m[k] = jnp.concatenate([high, low], 0)
        turned = down_v[...].T
        for leaf in range(LEAVES):
            near_step = spread_v[0, leaf % 2]
            both_steps = fine_dot(near_step, spread_v[1, leaf // 2])
            mix = (
                selector(LEAF, 48, 0, 144)
                + place_dot(near_step, selector(LEAF, 48, 16, 144))
                + place_dot(both_steps, selector(LEAF, 48, 32, 144))
            )
            whole = fine_dot(turned, mix)
            high = whole.astype(BF16).astype(F32)
            lane_at = lax.broadcasted_iota(jnp.int32, whole.shape, 1)
            far_m[leaf] = jnp.where(lane_at < 96, high, whole - high).astype(BF16)

    def scaled_rows(leaf, slots):
        rows = leaf_rows(leaf)
        squares = jnp.zeros((LEAF, WIDTH), F32)
        columns = []
        for slot in slots:
            tokens = g[slot, rows, :].astype(F32)
            squares = squares + tokens * tokens
            scale = gain_v[:, pl.ds(pl.multiple_of(owners[slot] * WIDTH, WIDTH), WIDTH)]
            columns.append((tokens * scale).astype(BF16))
        return jnp.concatenate(columns, 1), squares

    def gather_part(leaf):
        scaled, squares = scaled_rows(leaf, (0, 1, 2))
        parts[leaf] = dot(scaled, w[:3].reshape(3 * WIDTH, 2 * WIDTH))
        part_squares[leaf] = squares[:, : WIDTH // 2] + squares[:, WIDTH // 2 :]

    def values_of(leaf):
        scaled, squares = scaled_rows(leaf, (3,))
        squares = squares[:, : WIDTH // 2] + squares[:, WIDTH // 2 :] + part_squares[leaf]
        inverse = lax.rsqrt(jnp.sum(squares, axis=1, keepdims=True) / 1024 + 1e-06)
        part_squares[leaf] = jnp.broadcast_to(inverse, squares.shape)
        value = ((parts[leaf, :, :WIDTH] + dot(scaled, w[3, :, :WIDTH])) * inverse).astype(BF16)
        vals[leaf_rows(leaf), :] = value
        moms[leaf] = dot(mom_m[leaf], jnp.concatenate([value, value], 0))

    def gates_of(leaf):
        scaled, _ = scaled_rows(leaf, (3,))
        inverse = part_squares[leaf]
        sums = parts[leaf, :, WIDTH:] + dot(scaled, w[3, :, WIDTH:])
        gate[leaf_rows(leaf), :] = jax.nn.sigmoid(sums * jnp.concatenate([inverse, inverse], 1))

    def spectrum_of(leaf):
        value = vals[leaf_rows(leaf), :]
        spec[leaf] = dot(fwd_v[...], jnp.concatenate([value, value], 0))

    def near_rows(leaf):
        rows = leaf_rows(leaf)
        before = (leaf - 1 if leaf > 0 else LEAVES) if isinstance(leaf, int) else leaf - 1
        a_re, a_im = spec[leaf, :LEAF, :], spec[leaf, LEAF:, :]
        b_re, b_im = spec[before, :LEAF, :], spec[before, LEAF:, :]
        out_re = khat[0] * a_re - khat[1] * a_im + khat[2] * b_re - khat[3] * b_im
        out_im = khat[0] * a_im + khat[1] * a_re + khat[2] * b_im + khat[3] * b_re
        both = jnp.concatenate([out_re, out_im], 0).astype(BF16)
        total = dot(inv_v[...], jnp.concatenate([both, both], 0))
        near[rows, :] = total + skip_v[...] * vals[rows, :].astype(F32)

    def coupled(level, source_two, source_three):
        product = coup_v[level, 0] * source_two[None]
        if source_three is not None:
            product = product + coup_v[level, 1] * source_three[None]
        return product.reshape(RANK * RANK, WIDTH).astype(BF16)

    send_direct(0)

    copies = {}

    def local(name, source, target):
        copies[name] = pltpu.make_async_copy(source, target, local_sem.at[len(copies)])
        copies[name].start()

    local("tok", tok, g.at[0])
    for slot in range(4):
        rows = pl.ds(pl.multiple_of(owners[slot] * WIDTH, WIDTH), WIDTH)
        local(("v", slot), w_value.at[rows], w.at[slot, :, pl.ds(0, WIDTH)])
        local(("g", slot), w_gate.at[rows], w.at[slot, :, pl.ds(WIDTH, WIDTH)])
    for name, source, target in (
        ("gain", gain, gain_v),
        ("phi", phi, phi_v),
        ("coeff", coeff, coeff_v),
        ("fwd", fwd, fwd_f),
        ("skip", skip, skip_v),
        ("up", up, up_v),
        ("down", down, down_v),
        ("lift", lift, lift_v),
        ("spread", spread, spread_v),
        ("inv", inv, inv_f),
        ("coup", coup, coup_v),
    ):
        local(name, source, target)

    @pl.when(z > 0)
    def _():
        signal(ready_next, t - PLANE, x)

    for k in range(1, PLANE):

        @pl.when(own >= k)
        def _():
            signal(ready_plane, t - k, x)

    def chain(place):
        @pl.when(z == PLANES - 1 - place)
        def _():
            if not isinstance(place, int) or place > 0:
                pl.semaphore_wait(ready_later, 1)
            if not isinstance(place, int) or place < PLANES - 1:
                signal(ready_later, t - PLANE, x)

    def over(first, last, work):
        def step(leaf, carry):
            work(leaf)
            return carry

        lax.fori_loop(first, last, step, 0)

    chain(0)
    tables_near()
    send_direct(1)
    chain(1)
    tables_moments()
    tables_lift()
    chain(2)

    @pl.when(own < PLANE - 1)
    def _():
        pl.semaphore_wait(ready_plane, PLANE - 1 - own)

    @pl.when(z < PLANES - 1)
    def _():
        pl.semaphore_wait(ready_next, 1)

        @pl.when(y == 0)
        def _():
            signal(ready_edge, z * PLANE + 6, x)
            signal(ready_edge, z * PLANE + 7, x)

    for slot in range(4):
        copies["v", slot].wait()
        copies["g", slot].wait()
    for name in ("tok", "gain", "skip", "coup", "inv"):
        copies[name].wait()
    chain(3)
    pass_on(0)
    send_direct(2)
    chain(4)
    over(2, 4, gather_part)
    pass_on(1)
    tables_far()
    inv_v[...] = jnp.concatenate(halves(inv_f[...]), 1)
    chain(5)

    @pl.when((y == 3) & (z < PLANES - 1))
    def _():
        pl.semaphore_wait(ready_edge, 2)

    for way in range(2):
        direct(2, way).wait_recv()
    chain(6)
    over(0, 2, gather_part)
    chain(7)

    halo_copy = pltpu.make_async_remote_copy(
        src_ref=vals.at[pl.ds(3 * LEAF, LEAF)],
        dst_ref=halo,
        send_sem=hsem.at[0],
        recv_sem=hsem.at[1],
        device_id=(t + 1, x),
        device_id_type=MESH,
    )

    ctx_copy = pltpu.make_async_remote_copy(
        src_ref=ctx_out,
        dst_ref=ctx_in,
        send_sem=csem.at[0],
        recv_sem=csem.at[1],
        device_id=(t + 1, x),
        device_id_type=MESH,
    )

    wait_relayed(0)
    over(2, 4, values_of)

    @pl.when(t < PLANES * PLANE - 1)
    def _():
        halo_copy.start()

    over(2, 4, spectrum_of)
    over(2, 4, gates_of)
    near_rows(3)

    wait_relayed(1)
    over(0, 2, values_of)

    total = moms[0, 32:48, :] + moms[1, 32:48, :] + moms[2, 32:48, :] + moms[3, 32:48, :]
    m2[own] = total.astype(BF16)

    def plane_copy(k):
        return pltpu.make_async_remote_copy(
            src_ref=m2.at[own],
            dst_ref=m2.at[own],
            send_sem=s1,
            recv_sem=r1,
            device_id=(z * PLANE + lax.rem(own + k, PLANE), x),
            device_id_type=MESH,
        )

    plane_all = pltpu.make_async_remote_copy(
        src_ref=m2.at[pl.ds(0, PLANE - 1)],
        dst_ref=m2.at[pl.ds(0, PLANE - 1)],
        send_sem=s1,
        recv_sem=r1,
        device_id=(t, right),
        device_id_type=MESH,
    )

    for k in range(1, PLANE):
        plane_copy(k).start()

    def next_plane_copy(target, source):
        return pltpu.make_async_remote_copy(
            src_ref=m2.at[own],
            dst_ref=m2_prev.at[source],
            send_sem=s1p.at[target],
            recv_sem=r1p.at[source],
            device_id=((z + 1) * PLANE + target, x),
            device_id_type=MESH,
        )

    @pl.when((y == 3) & (z < PLANES - 1))
    def _():
        for target in range(2):
            next_plane_copy(target, core).start()

    ctx_out[...] = jnp.concatenate(
        [
            moms[2, 0:16, :],
            moms[3, 0:16, :],
            moms[0, 16:32, :] + moms[1, 16:32, :],
            moms[2, 16:32, :] + moms[3, 16:32, :],
        ],
        0,
    ).astype(BF16)

    @pl.when(t < PLANES * PLANE - 1)
    def _():
        ctx_copy.start()

    over(0, 2, gates_of)

    early = jnp.where(y == 0, 2, jnp.where(y == 1, 1, 0))
    over(0, jnp.minimum(2 * early, 2), spectrum_of)
    over(1, 1 + early, near_rows)

    plane_all.wait_recv()
    stack = m2[...].reshape(PLANE * RANK, WIDTH)
    lifted = dot(lift_m[...], jnp.concatenate([stack, stack], 0))
    pack_out[...] = lifted[:80].astype(BF16)


    def pack_copy(rows):
        return pltpu.make_async_remote_copy(
            src_ref=pack_out.at[pl.ds(0, rows)],
            dst_ref=pack_in.at[pl.ds(0, rows)],
            send_sem=s2,
            recv_sem=r2,
            device_id=(t + PLANE, x),
            device_id_type=MESH,
        )

    def five_copy(k):
        return pltpu.make_async_remote_copy(
            src_ref=pack_out.at[pl.ds(64, RANK)],
            dst_ref=m5_in.at[k],
            send_sem=s5.at[k],
            recv_sem=r5.at[k],
            device_id=(t + k * PLANE, x),
            device_id_type=MESH,
        )

    for k in range(PLANES - 1, 1, -1):

        @pl.when(z + k < PLANES)
        def _():
            five_copy(k).start()

    @pl.when((z < PLANES - 1) & (y < 2))
    def _():
        pack_copy(64).start()

    @pl.when((z < PLANES - 1) & (y >= 2))
    def _():
        pack_copy(32).start()

    over(jnp.minimum(2 * early, 2), 2, spectrum_of)
    over(1 + early, 3, near_rows)

    @pl.when(t > 0)
    def _():
        halo_copy.wait_recv()

    before = halo[...]
    spec[LEAVES] = dot(fwd_v[...], jnp.concatenate([before, before], 0))
    near_rows(0)

    summing = red_m[0, :RANK, :]

    def gathered(level, source_two, source_three=None):
        return dot(summing, coupled(level, source_two, source_three))

    @pl.when(t > 0)
    def _():
        ctx_copy.wait_recv()

    prev = ctx_in[...].astype(F32)
    far0[0] = gathered(0, prev[0:16])
    far0[1] = gathered(0, prev[16:32], prev[0:16])
    far0[2] = gathered(0, moms[0, 0:16, :])
    far0[3] = gathered(0, moms[1, 0:16, :], moms[0, 0:16, :])
    far1[0] = gathered(1, prev[32:48])
    far1[1] = gathered(1, prev[48:64], prev[32:48])

    gather_sent = g.at[pl.ds(0, 3)]
    pltpu.make_async_remote_copy(
        src_ref=gather_sent,
        dst_ref=gather_sent,
        send_sem=gsend,
        recv_sem=drecv.at[0, 0],
        device_id=(t, right),
        device_id_type=MESH,
    ).wait_send()

    plane_all.wait_send()

    @pl.when(t < PLANES * PLANE - 1)
    def _():
        halo_copy.wait_send()
        ctx_copy.wait_send()

    @pl.when((y == 3) & (z < PLANES - 1))
    def _():
        for target in range(2):
            next_plane_copy(target, core).wait_send()

    @pl.when((y == 0) & (z > 0))
    def _():
        for source in range(2):
            next_plane_copy(source, source).wait_recv()

    def reduced(k, source_two, source_three):
        return dot(red_m[k], coupled(2 + k, source_two, source_three))

    at = 2 * jnp.maximum(y - 1, 0)
    inside = y > 0
    two = jnp.where(inside, m2[at + core], m2_prev[core]).astype(F32)
    three = jnp.where(inside, m2[at], m2_prev[0]).astype(F32) * core.astype(F32)
    expansion = reduced(0, two, three)

    @pl.when((z > 0) & (y < 2))
    def _():
        pack_copy(64).wait_recv()

    @pl.when((z > 0) & (y >= 2))
    def _():
        pack_copy(32).wait_recv()

    odd = lax.rem(y, 2)
    lower = y < 2
    here = jnp.where(odd == 1, lifted[96:112], lifted[80:96])
    coming = pack_in[pl.ds(pl.multiple_of(32 + odd * RANK, RANK), RANK), :].astype(F32)
    two = jnp.where(lower, coming, here)
    three = jnp.where(lower, pack_in[32:48, :].astype(F32), lifted[80:96]) * odd.astype(F32)
    expansion = expansion + reduced(1, two, three)
    odd = lax.div(y, 2)
    two = pack_in[pl.ds(pl.multiple_of(odd * RANK, RANK), RANK), :].astype(F32)
    three = pack_in[0:16, :].astype(F32) * odd.astype(F32)
    expansion = expansion + reduced(2, two, three)

    for k in range(2, PLANES):

        @pl.when(z >= k)
        def _():
            five_copy(k).wait_recv()

    odd = lax.rem(z, 2)
    expansion = expansion + reduced(
        3, m5_in[2].astype(F32), m5_in[3].astype(F32) * odd.astype(F32)
    )
    pad = jnp.zeros((64, WIDTH), BF16)

    def sixth(base):
        pair = [m5_in[base], m5_in[base - 1]]
        return dot(six_m[...], jnp.concatenate(pair + pair + [pad], 0))

    odd_six = lax.rem(lax.div(z, 2), 2)
    expansion = expansion + reduced(
        4, sixth(4 + odd), sixth(6 + odd) * odd_six.astype(F32)
    )

    expansion = expansion[:RANK] + expansion[RANK:]

    def out_copy(leaf):
        rows = leaf_rows(leaf)
        return pltpu.make_async_copy(out_v.at[rows], out.at[rows], osem.at[leaf])

    for leaf in range(LEAVES):
        rows = leaf_rows(leaf)
        high, low = halves(jnp.concatenate([far0[leaf], far1[leaf // 2], expansion], 0))
        whole = jnp.concatenate([high, low, high, jnp.zeros((112, WIDTH), BF16)], 0)
        combined = near[rows, :] + dot(far_m[leaf], whole)
        out_v[rows, :] = (gate[rows, :] * combined).astype(BF16)
        out_copy(leaf).start()

    @pl.when((z < PLANES - 1) & (y < 2))
    def _():
        pack_copy(64).wait_send()

    @pl.when((z < PLANES - 1) & (y >= 2))
    def _():
        pack_copy(32).wait_send()

    for k in range(2, PLANES):

        @pl.when(z + k < PLANES)
        def _():
            five_copy(k).wait_send()

    for leaf in range(LEAVES):
        out_copy(leaf).wait()


def per_device(
    tokens,
    norm_gain,
    w_value,
    w_gate,
    phi_taps,
    tap_coeff,
    skip_gain,
    basis_up,
    basis_down,
    lift_maps,
    spread_maps,
    couplings,
):
    forward, inverse = transform_tables()
    in_hbm = pl.BlockSpec(memory_space=pltpu.HBM)
    frames = LEAF * LEAVES
    vmem = pltpu.VMEM
    dma = pltpu.SemaphoreType.DMA
    scratch = [
        vmem((4, frames, WIDTH), BF16),
        vmem((4, WIDTH, 2 * WIDTH), BF16),
        vmem((1, 4 * WIDTH), F32),
        vmem(phi_taps.shape, F32),
        vmem(tap_coeff.shape, F32),
        vmem((1, WIDTH), F32),
        vmem(basis_up.shape, F32),
        vmem(basis_down.shape, F32),
        vmem(lift_maps.shape, F32),
        vmem(spread_maps.shape, F32),
        vmem(couplings.shape, F32),
        vmem(forward.shape, F32),
        vmem(inverse.shape, F32),
        vmem((2 * LEAF, 2 * LEAF), BF16),
        vmem((LEAF, 4 * LEAF), BF16),
        vmem((frames, WIDTH), BF16),
        vmem((LEAF, WIDTH), BF16),
        vmem((frames, WIDTH), F32),
        vmem((frames, WIDTH), F32),
        vmem((LEAVES + 1, 2 * LEAF, WIDTH), F32),
        vmem((4, LEAF, WIDTH), F32),
        vmem((LEAVES, 48, 2 * LEAF), BF16),
        vmem((112, 256), BF16),
        vmem((RANK, 128), BF16),
        vmem((LEAVES, LEAF, LEAF), BF16),
        vmem((5, 2 * RANK, LEAF), BF16),
        vmem((LEAVES, 48, WIDTH), F32),
        vmem((PLANE, RANK, WIDTH), BF16),
        vmem((2, RANK, WIDTH), BF16),
        vmem((64, WIDTH), BF16),
        vmem((64, WIDTH), BF16),
        vmem((80, WIDTH), BF16),
        vmem((64, WIDTH), BF16),
        vmem((PLANES, RANK, WIDTH), BF16),
        vmem((LEAVES, RANK, WIDTH), F32),
        vmem((2, RANK, WIDTH), F32),
        vmem((frames, WIDTH), BF16),
        vmem((LEAVES, LEAF, 2 * WIDTH), F32),
        vmem((LEAVES, LEAF, WIDTH // 2), F32),
        dma((20,)),
        dma(()),
        dma((2, 3)),
        dma((2, 2)),
        dma((2,)),
        dma((2,)),
        dma(()),
        dma(()),
        dma((2,)),
        dma((2,)),
        dma(()),
        dma(()),
        dma((PLANES,)),
        dma((PLANES,)),
        pltpu.SemaphoreType.REGULAR,
        pltpu.SemaphoreType.REGULAR,
        pltpu.SemaphoreType.REGULAR,
        pltpu.SemaphoreType.REGULAR,
        dma((LEAVES,)),
    ]
    return pl.pallas_call(
        body,
        out_shape=jax.ShapeDtypeStruct(tokens.shape, BF16),
        in_specs=[in_hbm] * 14,
        out_specs=in_hbm,
        scratch_shapes=scratch,
        compiler_params=pltpu.CompilerParams(
            collective_id=0, has_side_effects=True, vmem_limit_bytes=60 * 1024 * 1024
        ),
        cost_estimate=pl.CostEstimate(flops=4 * 10**9, bytes_accessed=8 * 10**6, transcendentals=10**6),
    )(
        tokens,
        norm_gain.reshape(1, -1),
        w_value,
        w_gate,
        phi_taps,
        tap_coeff,
        skip_gain.reshape(1, -1),
        basis_up,
        basis_down,
        lift_maps,
        spread_maps,
        couplings,
        jnp.asarray(forward),
        jnp.asarray(inverse),
    )


def solution(mesh):
    placed = (
        P("tm", "chan"),
        P(),
        P(None, "chan"),
        P(None, "chan"),
        P(),
        P(None, "chan"),
        P("chan"),
        P(),
        P(),
        P(),
        P(),
        P(None, None, None, None, "chan"),
    )
    return jax.shard_map(
        per_device, mesh=mesh, in_specs=placed, out_specs=P("tm", "chan"), check_vma=False
    )
```

```python
import jax
import jax.numpy as jnp
import numpy as np
from jax import lax
from jax.experimental import pallas as pl
from jax.experimental.pallas import tpu as pltpu
from jax.sharding import PartitionSpec as P

MESH = pl.DeviceIdType.MESH
F32 = jnp.float32
BF16 = jnp.bfloat16

LEAF = 256
LEAVES = 4
WIDTH = 256
RANK = 16
PLANES = 8
PLANE = 8


def transform_tables():
    odd = np.arange(LEAF)[:, None] + 0.5
    angle = 2 * np.pi * odd * np.arange(LEAF)[None, :] / (2 * LEAF)
    forward = np.concatenate([np.cos(angle), -np.sin(angle)], 0)
    return forward.astype(np.float32), (forward.T / LEAF).astype(np.float32)


def dot(left, right):
    return jnp.dot(left, right, preferred_element_type=F32)


def halves(value):
    high = value.astype(BF16)
    return high, (value - high.astype(F32)).astype(BF16)


def fine_dot(left, right):
    left_high, left_low = halves(left)
    right_high, right_low = halves(right)
    return dot(left_high, right_high) + dot(left_high, right_low) + dot(left_low, right_high)


def place_dot(left, right):
    left_high, left_low = halves(left)
    ones = right.astype(BF16)
    return dot(left_high, ones) + dot(left_low, ones)


def selector(lanes, period, shift, limit):
    row = lax.broadcasted_iota(jnp.int32, (RANK, lanes), 0)
    lane = lax.broadcasted_iota(jnp.int32, (RANK, lanes), 1)
    return ((lax.rem(lane, period) == row + shift) & (lane < limit)).astype(F32)


def body(
    tok, gain, w_value, w_gate, phi, coeff, skip, up, down, lift, spread, coup, fwd, inv,
    out,
    g, w, gain_v, phi_v, coeff_v, skip_v, up_v, down_v, lift_v, spread_v, coup_v, fwd_f, inv_f, fwd_v, inv_v,
    vals, halo, gate, near, spec, khat, mom_m, lift_m, six_m, far_m, red_m, moms,
    m2, m2_prev, ctx_out, ctx_in, pack_out, pack_in, m5_in, far0, far1, out_v, parts, part_squares,
    local_sem, gsend, drecv, rrecv, hsem, csem, s1, r1, s1p, r1p, s2, r2, s5, r5, ready_plane, ready_next, ready_edge, ready_later, osem,
):
    t = lax.axis_index("tm")
    x = lax.axis_index("chan")
    core = lax.rem(t, 2)
    y = lax.rem(lax.div(t, 2), 4)
    z = lax.div(t, PLANE)
    own = lax.rem(t, PLANE)
    right, left = lax.rem(x + 1, 4), lax.rem(x + 3, 4)

    barrier = pltpu.get_barrier_semaphore()

    def signal(semaphore, frames, chans):
        pl.semaphore_signal(semaphore, inc=1, device_id=(frames, chans), device_id_type=MESH)

    signal(barrier, t, right)
    signal(barrier, t, left)

    @pl.when(z < PLANES - 1)
    def _():
        signal(barrier, t + PLANE, x)

    for k in range(1, PLANE):

        @pl.when(own + k < PLANE)
        def _():
            signal(barrier, t + k, x)

    m2_prev[...] = jnp.zeros_like(m2_prev)
    ctx_in[...] = jnp.zeros_like(ctx_in)
    pack_in[...] = jnp.zeros_like(pack_in)
    m5_in[...] = jnp.zeros_like(m5_in)
    halo[...] = jnp.zeros_like(halo)

    pl.semaphore_wait(barrier, 2 + own + jnp.where(z > 0, 1, 0))

    owners = [x, left, right, lax.rem(x + 2, 4)]

    def leaf_rows(leaf):
        return pl.ds(leaf * LEAF if isinstance(leaf, int) else pl.multiple_of(leaf * LEAF, LEAF), LEAF)

    def direct(group, way):
        rows = pl.ds((1 - group) * 2 * LEAF, 2 * LEAF)
        return pltpu.make_async_remote_copy(
            src_ref=tok.at[rows],
            dst_ref=g.at[1 + way, rows],
            send_sem=gsend,
            recv_sem=drecv.at[way, group],
            device_id=(t, left if way else right),
            device_id_type=MESH,
        )

    def relay(group, way):
        rows = leaf_rows((1 - group) * 2 + way)
        return pltpu.make_async_remote_copy(
            src_ref=g.at[1 + way, rows],
            dst_ref=g.at[3, rows],
            send_sem=gsend,
            recv_sem=rrecv.at[way, group],
            device_id=(t, left if way else right),
            device_id_type=MESH,
        )

    def send_direct(group):
        for way in range(2):
            direct(group, way).start()

    def pass_on(group):
        for way in range(2):
            direct(group, way).wait_recv()
            relay(group, way).start()

    def wait_relayed(group):
        for way in range(2):
            relay(group, way).wait_recv()

    def tables_near():
        for name in ("phi", "coeff", "fwd"):
            copies[name].wait()
        fwd_v[...] = jnp.concatenate(halves(fwd_f[...]), 1)
        taps = phi_v[...].astype(BF16).astype(F32).T.astype(BF16)
        coeff_high, coeff_low = halves(coeff_v[...])
        kernel_taps = dot(taps, coeff_high) + dot(taps, coeff_low)
        both = jnp.concatenate([kernel_taps[:LEAF], kernel_taps[LEAF:]], 1)
        high, low = halves(both)
        hat = dot(fwd_v[...], jnp.concatenate([high, high], 0)) + dot(fwd_v[:, :LEAF], low)
        a_re, a_im = hat[:LEAF, :WIDTH], hat[LEAF:, :WIDTH]
        b_re, b_im = hat[:LEAF, WIDTH:], hat[LEAF:, WIDTH:]
        row = lax.broadcasted_iota(jnp.int32, (LEAF, WIDTH), 0)
        sign = (1 - 2 * lax.rem(row, 2)).astype(F32)
        khat[0] = a_re
        khat[1] = a_im
        khat[2] = b_re - sign * a_im
        khat[3] = b_im + sign * a_re

    def tables_moments():
        copies["up"].wait()
        copies["lift"].wait()
        base = up_v[...]
        first = [fine_dot(lift_v[0, k], base) for k in range(2)]
        for leaf in range(LEAVES):
            second = fine_dot(lift_v[1, leaf // 2], first[leaf % 2])
            high, low = halves(jnp.concatenate([base, first[leaf % 2], second], 0))
            mom_m[leaf] = jnp.concatenate([high, low], 1)

    def tables_lift():
        def pair(level):
            return place_dot(lift_v[level, 0], selector(128, 32, 0, 128)) + place_dot(
                lift_v[level, 1], selector(128, 32, 16, 128)
            )

        def blocks(level, copies_of):
            rows = jnp.concatenate([pair(level)] * copies_of, 0)
            row = lax.broadcasted_iota(jnp.int32, rows.shape, 0)
            lane = lax.broadcasted_iota(jnp.int32, rows.shape, 1)
            return jnp.where(lax.div(row, RANK) == lax.div(lane, 2 * RANK), rows, 0.0)

        three = blocks(2, 8)
        four = fine_dot(blocks(3, 2), three)
        five = fine_dot(blocks(4, 1), jnp.concatenate([four, jnp.zeros((96, 128), F32)], 0))
        whole = jnp.concatenate([four, three[32:64], five, three[:32]], 0)
        high, low = halves(whole)
        lift_m[...] = jnp.concatenate([high, low], 1)
        six = place_dot(lift_v[5, 0], selector(128, 32, 0, 64)) + place_dot(
            lift_v[5, 1], selector(128, 32, 16, 64)
        )
        high = six.astype(BF16).astype(F32)
        lane = lax.broadcasted_iota(jnp.int32, six.shape, 1)
        six_m[...] = jnp.where(lane < 32, high, six - high).astype(BF16)

    def tables_far():
        copies["spread"].wait()
        copies["down"].wait()
        row = lax.broadcasted_iota(jnp.int32, (RANK, LEAF), 0)
        lane = lax.broadcasted_iota(jnp.int32, (RANK, LEAF), 1)
        summing = (lax.div(lane, RANK) == row).astype(F32)
        chain = None
        for k in range(5):
            if k > 0:
                step = spread_v[1 + k, lax.rem(lax.div(t, 2 ** (k - 1)), 2)]
                chain = step if k == 1 else fine_dot(chain, step)
            high, low = halves(summing if k == 0 else place_dot(chain, summing))
            red_m[k] = jnp.concatenate([high, low], 0)
        turned = down_v[...].T
        for leaf in range(LEAVES):
            near_step = spread_v[0, leaf % 2]
            both_steps = fine_dot(near_step, spread_v[1, leaf // 2])
            mix = (
                selector(LEAF, 48, 0, 144)
                + place_dot(near_step, selector(LEAF, 48, 16, 144))
                + place_dot(both_steps, selector(LEAF, 48, 32, 144))
            )
            whole = fine_dot(turned, mix)
            high = whole.astype(BF16).astype(F32)
            lane_at = lax.broadcasted_iota(jnp.int32, whole.shape, 1)
            far_m[leaf] = jnp.where(lane_at < 96, high, whole - high).astype(BF16)

    def scaled_rows(leaf, slots):
        rows = leaf_rows(leaf)
        squares = jnp.zeros((LEAF, WIDTH), F32)
        columns = []
        for slot in slots:
            tokens = g[slot, rows, :].astype(F32)
            squares = squares + tokens * tokens
            scale = gain_v[:, pl.ds(pl.multiple_of(owners[slot] * WIDTH, WIDTH), WIDTH)]
            columns.append((tokens * scale).astype(BF16))
        return jnp.concatenate(columns, 1), squares

    def gather_part(leaf):
        scaled, squares = scaled_rows(leaf, (0, 1, 2))
        parts[leaf] = dot(scaled, w[:3].reshape(3 * WIDTH, 2 * WIDTH))
        part_squares[leaf] = squares[:, : WIDTH // 2] + squares[:, WIDTH // 2 :]

    def values_of(leaf):
        scaled, squares = scaled_rows(leaf, (3,))
        squares = squares[:, : WIDTH // 2] + squares[:, WIDTH // 2 :] + part_squares[leaf]
        inverse = lax.rsqrt(jnp.sum(squares, axis=1, keepdims=True) / 1024 + 1e-06)
        part_squares[leaf] = jnp.broadcast_to(inverse, squares.shape)
        value = ((parts[leaf, :, :WIDTH] + dot(scaled, w[3, :, :WIDTH])) * inverse).astype(BF16)
        vals[leaf_rows(leaf), :] = value
        moms[leaf] = dot(mom_m[leaf], jnp.concatenate([value, value], 0))

    def gates_of(leaf):
        scaled, _ = scaled_rows(leaf, (3,))
        inverse = part_squares[leaf]
        sums = parts[leaf, :, WIDTH:] + dot(scaled, w[3, :, WIDTH:])
        half = 0.5 * jnp.concatenate([inverse, inverse], 1)
        gate[leaf_rows(leaf), :] = 0.5 * jnp.tanh(sums * half) + 0.5

    def spectrum_of(leaf):
        value = vals[leaf_rows(leaf), :]
        spec[leaf] = dot(fwd_v[...], jnp.concatenate([value, value], 0))

    def near_rows(leaf):
        rows = leaf_rows(leaf)
        before = (leaf - 1 if leaf > 0 else LEAVES) if isinstance(leaf, int) else leaf - 1
        a_re, a_im = spec[leaf, :LEAF, :], spec[leaf, LEAF:, :]
        b_re, b_im = spec[before, :LEAF, :], spec[before, LEAF:, :]
        out_re = khat[0] * a_re - khat[1] * a_im + khat[2] * b_re - khat[3] * b_im
        out_im = khat[0] * a_im + khat[1] * a_re + khat[2] * b_im + khat[3] * b_re
        both = jnp.concatenate([out_re, out_im], 0).astype(BF16)
        total = dot(inv_v[...], both)
        near[rows, :] = total + skip_v[...] * vals[rows, :].astype(F32)

    def coupled(level, source_two, source_three):
        product = coup_v[level, 0] * source_two[None]
        if source_three is not None:
            product = product + coup_v[level, 1] * source_three[None]
        return product.reshape(RANK * RANK, WIDTH).astype(BF16)

    send_direct(0)

    copies = {}

    def local(name, source, target):
        copies[name] = pltpu.make_async_copy(source, target, local_sem.at[len(copies)])
        copies[name].start()

    local("tok", tok, g.at[0])
    for slot in range(4):
        rows = pl.ds(pl.multiple_of(owners[slot] * WIDTH, WIDTH), WIDTH)
        local(("v", slot), w_value.at[rows], w.at[slot, :, pl.ds(0, WIDTH)])
        local(("g", slot), w_gate.at[rows], w.at[slot, :, pl.ds(WIDTH, WIDTH)])
    for name, source, target in (
        ("gain", gain, gain_v),
        ("phi", phi, phi_v),
        ("coeff", coeff, coeff_v),
        ("fwd", fwd, fwd_f),
        ("skip", skip, skip_v),
        ("up", up, up_v),
        ("down", down, down_v),
        ("lift", lift, lift_v),
        ("spread", spread, spread_v),
        ("inv", inv, inv_f),
        ("coup", coup, coup_v),
    ):
        local(name, source, target)

    @pl.when(z > 0)
    def _():
        signal(ready_next, t - PLANE, x)

    for k in range(1, PLANE):

        @pl.when(own >= k)
        def _():
            signal(ready_plane, t - k, x)

    def chain(place):
        @pl.when(z == PLANES - 1 - place)
        def _():
            if not isinstance(place, int) or place > 0:
                pl.semaphore_wait(ready_later, 1)
            if not isinstance(place, int) or place < PLANES - 1:
                signal(ready_later, t - PLANE, x)

    def over(first, last, work):
        def step(leaf, carry):
            work(leaf)
            return carry

        lax.fori_loop(first, last, step, 0)

    def over(first, last, work):
        def step(leaf, carry):
            work(leaf)
            return carry

        lax.fori_loop(first, last, step, 0)

    chain(0)
    tables_near()
    send_direct(1)
    chain(1)
    tables_moments()
    chain(2)
    tables_lift()
    chain(3)
    for slot in range(4):
        copies["v", slot].wait()
        copies["g", slot].wait()
    for name in ("tok", "gain", "skip", "coup", "inv"):
        copies[name].wait()
    pass_on(0)
    chain(4)

    @pl.when(own < PLANE - 1)
    def _():
        pl.semaphore_wait(ready_plane, PLANE - 1 - own)

    @pl.when(z < PLANES - 1)
    def _():
        pl.semaphore_wait(ready_next, 1)

        @pl.when(y == 0)
        def _():
            signal(ready_edge, z * PLANE + 6, x)
            signal(ready_edge, z * PLANE + 7, x)

    over(2, 4, gather_part)
    chain(5)
    tables_far()
    inv_v[...] = inv_f[...].astype(BF16)
    chain(6)
    pass_on(1)
    over(0, 2, gather_part)

    @pl.when((y == 3) & (z < PLANES - 1))
    def _():
        pl.semaphore_wait(ready_edge, 2)

    halo_copy = pltpu.make_async_remote_copy(
        src_ref=vals.at[pl.ds(3 * LEAF, LEAF)],
        dst_ref=halo,
        send_sem=hsem.at[0],
        recv_sem=hsem.at[1],
        device_id=(t + 1, x),
        device_id_type=MESH,
    )

    def ctx_copy(part):
        rows = pl.ds(0, 48) if part == 0 else pl.ds(48, 16)
        return pltpu.make_async_remote_copy(
            src_ref=ctx_out.at[rows],
            dst_ref=ctx_in.at[rows],
            send_sem=csem.at[0, part],
            recv_sem=csem.at[1, part],
            device_id=(t + 1, x),
            device_id_type=MESH,
        )

    summing = red_m[0, :RANK, :]

    def gathered(level, source_two, source_three=None):
        return dot(summing, coupled(level, source_two, source_three))

    wait_relayed(0)
    over(2, 4, values_of)
    ctx_out[:48] = jnp.concatenate(
        [moms[2, 0:16, :], moms[3, 0:16, :], moms[2, 16:32, :] + moms[3, 16:32, :]], 0
    ).astype(BF16)

    @pl.when(t < PLANES * PLANE - 1)
    def _():
        halo_copy.start()
        ctx_copy(0).start()

    over(2, 4, spectrum_of)
    over(2, 4, gates_of)
    near_rows(3)

    @pl.when(t > 0)
    def _():
        ctx_copy(0).wait_recv()
        halo_copy.wait_recv()

    prev = ctx_in[:32].astype(F32)
    far0[0] = gathered(0, prev[0:16])
    far0[1] = gathered(0, prev[16:32], prev[0:16])
    spec[LEAVES] = dot(fwd_v[...], jnp.concatenate([halo[...], halo[...]], 0))

    wait_relayed(1)
    over(0, 2, values_of)

    total = moms[0, 32:48, :] + moms[1, 32:48, :] + moms[2, 32:48, :] + moms[3, 32:48, :]
    m2[own] = total.astype(BF16)

    def plane_copy(k):
        return pltpu.make_async_remote_copy(
            src_ref=m2.at[own],
            dst_ref=m2.at[own],
            send_sem=s1,
            recv_sem=r1,
            device_id=(z * PLANE + lax.rem(own + k, PLANE), x),
            device_id_type=MESH,
        )

    plane_all = pltpu.make_async_remote_copy(
        src_ref=m2.at[pl.ds(0, PLANE - 1)],
        dst_ref=m2.at[pl.ds(0, PLANE - 1)],
        send_sem=s1,
        recv_sem=r1,
        device_id=(t, right),
        device_id_type=MESH,
    )

    for k in range(1, PLANE):
        plane_copy(k).start()

    def next_plane_copy(target, source):
        return pltpu.make_async_remote_copy(
            src_ref=m2.at[own],
            dst_ref=m2_prev.at[source],
            send_sem=s1p.at[target],
            recv_sem=r1p.at[source],
            device_id=((z + 1) * PLANE + target, x),
            device_id_type=MESH,
        )

    @pl.when((y == 3) & (z < PLANES - 1))
    def _():
        for target in range(2):
            next_plane_copy(target, core).start()

    ctx_out[48:] = (moms[0, 16:32, :] + moms[1, 16:32, :]).astype(BF16)

    @pl.when(t < PLANES * PLANE - 1)
    def _():
        ctx_copy(1).start()

    over(0, 2, gates_of)

    plane_all.wait_recv()
    stack = m2[...].reshape(PLANE * RANK, WIDTH)
    lifted = dot(lift_m[...], jnp.concatenate([stack, stack], 0))
    pack_out[...] = lifted[:80].astype(BF16)


    def pack_copy(rows):
        return pltpu.make_async_remote_copy(
            src_ref=pack_out.at[pl.ds(0, rows)],
            dst_ref=pack_in.at[pl.ds(0, rows)],
            send_sem=s2,
            recv_sem=r2,
            device_id=(t + PLANE, x),
            device_id_type=MESH,
        )

    def five_copy(k):
        return pltpu.make_async_remote_copy(
            src_ref=pack_out.at[pl.ds(64, RANK)],
            dst_ref=m5_in.at[k],
            send_sem=s5.at[k],
            recv_sem=r5.at[k],
            device_id=(t + k * PLANE, x),
            device_id_type=MESH,
        )

    chain(7)

    for k in range(PLANES - 1, 1, -1):

        @pl.when(z + k < PLANES)
        def _():
            five_copy(k).start()

    @pl.when((z < PLANES - 1) & (y < 2))
    def _():
        pack_copy(64).start()

    @pl.when((z < PLANES - 1) & (y >= 2))
    def _():
        pack_copy(32).start()

    over(0, 2, spectrum_of)
    over(1, 3, near_rows)

    near_rows(0)

    @pl.when(t > 0)
    def _():
        ctx_copy(1).wait_recv()

    prev = ctx_in[32:].astype(F32)
    far0[2] = gathered(0, moms[0, 0:16, :])
    far0[3] = gathered(0, moms[1, 0:16, :], moms[0, 0:16, :])
    far1[0] = gathered(1, prev[16:32])
    far1[1] = gathered(1, prev[0:16], prev[16:32])

    gather_sent = g.at[pl.ds(0, 3)]
    pltpu.make_async_remote_copy(
        src_ref=gather_sent,
        dst_ref=gather_sent,
        send_sem=gsend,
        recv_sem=drecv.at[0, 0],
        device_id=(t, right),
        device_id_type=MESH,
    ).wait_send()

    plane_all.wait_send()

    @pl.when(t < PLANES * PLANE - 1)
    def _():
        halo_copy.wait_send()
        ctx_copy(0).wait_send()
        ctx_copy(1).wait_send()

    @pl.when((y == 3) & (z < PLANES - 1))
    def _():
        for target in range(2):
            next_plane_copy(target, core).wait_send()

    @pl.when((y == 0) & (z > 0))
    def _():
        for source in range(2):
            next_plane_copy(source, source).wait_recv()

    def reduced(k, source_two, source_three):
        return dot(red_m[k], coupled(2 + k, source_two, source_three))

    at = 2 * jnp.maximum(y - 1, 0)
    inside = y > 0
    two = jnp.where(inside, m2[at + core], m2_prev[core]).astype(F32)
    three = jnp.where(inside, m2[at], m2_prev[0]).astype(F32) * core.astype(F32)
    expansion = reduced(0, two, three)

    @pl.when((z > 0) & (y < 2))
    def _():
        pack_copy(64).wait_recv()

    @pl.when((z > 0) & (y >= 2))
    def _():
        pack_copy(32).wait_recv()

    odd = lax.rem(y, 2)
    lower = y < 2
    here = jnp.where(odd == 1, lifted[96:112], lifted[80:96])
    coming = pack_in[pl.ds(pl.multiple_of(32 + odd * RANK, RANK), RANK), :].astype(F32)
    two = jnp.where(lower, coming, here)
    three = jnp.where(lower, pack_in[32:48, :].astype(F32), lifted[80:96]) * odd.astype(F32)
    expansion = expansion + reduced(1, two, three)
    odd = lax.div(y, 2)
    two = pack_in[pl.ds(pl.multiple_of(odd * RANK, RANK), RANK), :].astype(F32)
    three = pack_in[0:16, :].astype(F32) * odd.astype(F32)
    expansion = expansion + reduced(2, two, three)

    for k in range(2, PLANES):

        @pl.when(z >= k)
        def _():
            five_copy(k).wait_recv()

    odd = lax.rem(z, 2)
    expansion = expansion + reduced(
        3, m5_in[2].astype(F32), m5_in[3].astype(F32) * odd.astype(F32)
    )
    pad = jnp.zeros((64, WIDTH), BF16)

    def sixth(base):
        pair = [m5_in[base], m5_in[base - 1]]
        return dot(six_m[...], jnp.concatenate(pair + pair + [pad], 0))

    odd_six = lax.rem(lax.div(z, 2), 2)
    expansion = expansion + reduced(
        4, sixth(4 + odd), sixth(6 + odd) * odd_six.astype(F32)
    )

    expansion = expansion[:RANK] + expansion[RANK:]

    def out_copy(leaf):
        rows = leaf_rows(leaf)
        return pltpu.make_async_copy(out_v.at[rows], out.at[rows], osem.at[leaf])

    for leaf in range(LEAVES):
        rows = leaf_rows(leaf)
        high, low = halves(jnp.concatenate([far0[leaf], far1[leaf // 2], expansion], 0))
        whole = jnp.concatenate([high, low, high, jnp.zeros((112, WIDTH), BF16)], 0)
        combined = near[rows, :] + dot(far_m[leaf], whole)
        out_v[rows, :] = (gate[rows, :] * combined).astype(BF16)
        out_copy(leaf).start()

    @pl.when((z < PLANES - 1) & (y < 2))
    def _():
        pack_copy(64).wait_send()

    @pl.when((z < PLANES - 1) & (y >= 2))
    def _():
        pack_copy(32).wait_send()

    for k in range(2, PLANES):

        @pl.when(z + k < PLANES)
        def _():
            five_copy(k).wait_send()

    for leaf in range(LEAVES):
        out_copy(leaf).wait()


def per_device(
    tokens,
    norm_gain,
    w_value,
    w_gate,
    phi_taps,
    tap_coeff,
    skip_gain,
    basis_up,
    basis_down,
    lift_maps,
    spread_maps,
    couplings,
):
    forward, inverse = transform_tables()
    in_hbm = pl.BlockSpec(memory_space=pltpu.HBM)
    frames = LEAF * LEAVES
    vmem = pltpu.VMEM
    dma = pltpu.SemaphoreType.DMA
    scratch = [
        vmem((4, frames, WIDTH), BF16),
        vmem((4, WIDTH, 2 * WIDTH), BF16),
        vmem((1, 4 * WIDTH), F32),
        vmem(phi_taps.shape, F32),
        vmem(tap_coeff.shape, F32),
        vmem((1, WIDTH), F32),
        vmem(basis_up.shape, F32),
        vmem(basis_down.shape, F32),
        vmem(lift_maps.shape, F32),
        vmem(spread_maps.shape, F32),
        vmem(couplings.shape, F32),
        vmem(forward.shape, F32),
        vmem(inverse.shape, F32),
        vmem((2 * LEAF, 2 * LEAF), BF16),
        vmem((LEAF, 2 * LEAF), BF16),
        vmem((frames, WIDTH), BF16),
        vmem((LEAF, WIDTH), BF16),
        vmem((frames, WIDTH), F32),
        vmem((frames, WIDTH), F32),
        vmem((LEAVES + 1, 2 * LEAF, WIDTH), F32),
        vmem((4, LEAF, WIDTH), F32),
        vmem((LEAVES, 48, 2 * LEAF), BF16),
        vmem((112, 256), BF16),
        vmem((RANK, 128), BF16),
        vmem((LEAVES, LEAF, LEAF), BF16),
        vmem((5, 2 * RANK, LEAF), BF16),
        vmem((LEAVES, 48, WIDTH), F32),
        vmem((PLANE, RANK, WIDTH), BF16),
        vmem((2, RANK, WIDTH), BF16),
        vmem((64, WIDTH), BF16),
        vmem((64, WIDTH), BF16),
        vmem((80, WIDTH), BF16),
        vmem((64, WIDTH), BF16),
        vmem((PLANES, RANK, WIDTH), BF16),
        vmem((LEAVES, RANK, WIDTH), F32),
        vmem((2, RANK, WIDTH), F32),
        vmem((frames, WIDTH), BF16),
        vmem((LEAVES, LEAF, 2 * WIDTH), F32),
        vmem((LEAVES, LEAF, WIDTH // 2), F32),
        dma((20,)),
        dma(()),
        dma((2, 2)),
        dma((2, 2)),
        dma((2,)),
        dma((2, 2)),
        dma(()),
        dma(()),
        dma((2,)),
        dma((2,)),
        dma(()),
        dma(()),
        dma((PLANES,)),
        dma((PLANES,)),
        pltpu.SemaphoreType.REGULAR,
        pltpu.SemaphoreType.REGULAR,
        pltpu.SemaphoreType.REGULAR,
        pltpu.SemaphoreType.REGULAR,
        dma((LEAVES,)),
    ]
    return pl.pallas_call(
        body,
        out_shape=jax.ShapeDtypeStruct(tokens.shape, BF16),
        in_specs=[in_hbm] * 14,
        out_specs=in_hbm,
        scratch_shapes=scratch,
        compiler_params=pltpu.CompilerParams(
            collective_id=0, has_side_effects=True, vmem_limit_bytes=60 * 1024 * 1024
        ),
        cost_estimate=pl.CostEstimate(flops=4 * 10**9, bytes_accessed=8 * 10**6, transcendentals=10**6),
    )(
        tokens,
        norm_gain.reshape(1, -1),
        w_value,
        w_gate,
        phi_taps,
        tap_coeff,
        skip_gain.reshape(1, -1),
        basis_up,
        basis_down,
        lift_maps,
        spread_maps,
        couplings,
        jnp.asarray(forward),
        jnp.asarray(inverse),
    )


def solution(mesh):
    placed = (
        P("tm", "chan"),
        P(),
        P(None, "chan"),
        P(None, "chan"),
        P(),
        P(None, "chan"),
        P("chan"),
        P(),
        P(),
        P(),
        P(),
        P(None, None, None, None, "chan"),
    )
    return jax.shard_map(
        per_device, mesh=mesh, in_specs=placed, out_specs=P("tm", "chan"), check_vma=False
    )
```

```python
import jax
import jax.numpy as jnp
import numpy as np
from jax import lax
from jax.experimental import pallas as pl
from jax.experimental.pallas import tpu as pltpu
from jax.sharding import PartitionSpec as P

MESH = pl.DeviceIdType.MESH
F32 = jnp.float32
BF16 = jnp.bfloat16

LEAF = 256
LEAVES = 4
WIDTH = 256
RANK = 16
PLANES = 8
PLANE = 8


def transform_tables():
    odd = np.arange(LEAF)[:, None] + 0.5
    angle = 2 * np.pi * odd * np.arange(LEAF)[None, :] / (2 * LEAF)
    forward = np.concatenate([np.cos(angle), -np.sin(angle)], 0)
    return forward.astype(np.float32), (forward.T / LEAF).astype(np.float32)


def dot(left, right):
    return jnp.dot(left, right, preferred_element_type=F32)


def halves(value):
    high = value.astype(BF16)
    return high, (value - high.astype(F32)).astype(BF16)


def fine_dot(left, right):
    left_high, left_low = halves(left)
    right_high, right_low = halves(right)
    return dot(left_high, right_high) + dot(left_high, right_low) + dot(left_low, right_high)


def place_dot(left, right):
    left_high, left_low = halves(left)
    ones = right.astype(BF16)
    return dot(left_high, ones) + dot(left_low, ones)


def selector(lanes, period, shift, limit):
    row = lax.broadcasted_iota(jnp.int32, (RANK, lanes), 0)
    lane = lax.broadcasted_iota(jnp.int32, (RANK, lanes), 1)
    return ((lax.rem(lane, period) == row + shift) & (lane < limit)).astype(F32)


def body(
    tok, gain, w_value, w_gate, phi, coeff, skip, up, down, lift, spread, coup, fwd, inv,
    out,
    g, w, gain_v, phi_v, coeff_v, skip_v, up_v, down_v, lift_v, spread_v, coup_v, fwd_f, inv_f, fwd_v, inv_v,
    vals, halo, gate, near, spec, khat, mom_m, lift_m, six_m, far_m, red_m, moms,
    m2, m2_prev, ctx_out, ctx_in, pack_out, pack_in, m5_in, far0, far1, out_v, parts, part_squares,
    local_sem, gsend, drecv, rrecv, hsem, csem, s1, r1, s1p, r1p, s2, r2, s5, r5, ready_plane, ready_next, ready_edge, ready_later, osem,
):
    t = lax.axis_index("tm")
    x = lax.axis_index("chan")
    core = lax.rem(t, 2)
    y = lax.rem(lax.div(t, 2), 4)
    z = lax.div(t, PLANE)
    own = lax.rem(t, PLANE)
    right, left = lax.rem(x + 1, 4), lax.rem(x + 3, 4)

    barrier = pltpu.get_barrier_semaphore()

    def signal(semaphore, frames, chans):
        pl.semaphore_signal(semaphore, inc=1, device_id=(frames, chans), device_id_type=MESH)

    signal(barrier, t, right)
    signal(barrier, t, left)

    @pl.when(z < PLANES - 1)
    def _():
        signal(barrier, t + PLANE, x)

    for k in range(1, PLANE):

        @pl.when(own + k < PLANE)
        def _():
            signal(barrier, t + k, x)

    m2_prev[...] = jnp.zeros_like(m2_prev)
    ctx_in[...] = jnp.zeros_like(ctx_in)
    pack_in[...] = jnp.zeros_like(pack_in)
    m5_in[...] = jnp.zeros_like(m5_in)
    halo[...] = jnp.zeros_like(halo)

    pl.semaphore_wait(barrier, 2 + own + jnp.where(z > 0, 1, 0))

    owners = [x, left, right, lax.rem(x + 2, 4)]

    def leaf_rows(leaf):
        return pl.ds(leaf * LEAF if isinstance(leaf, int) else pl.multiple_of(leaf * LEAF, LEAF), LEAF)

    def direct(group, way):
        rows = pl.ds((1 - group) * 2 * LEAF, 2 * LEAF)
        return pltpu.make_async_remote_copy(
            src_ref=tok.at[rows],
            dst_ref=g.at[1 + way, rows],
            send_sem=gsend,
            recv_sem=drecv.at[way, group],
            device_id=(t, left if way else right),
            device_id_type=MESH,
        )

    def relay(group, way):
        rows = leaf_rows((1 - group) * 2 + way)
        return pltpu.make_async_remote_copy(
            src_ref=g.at[1 + way, rows],
            dst_ref=g.at[3, rows],
            send_sem=gsend,
            recv_sem=rrecv.at[way, group],
            device_id=(t, left if way else right),
            device_id_type=MESH,
        )

    def send_direct(group):
        for way in range(2):
            direct(group, way).start()

    def pass_on(group):
        for way in range(2):
            direct(group, way).wait_recv()
            relay(group, way).start()

    def wait_relayed(group):
        for way in range(2):
            relay(group, way).wait_recv()

    def tables_near():
        for name in ("phi", "coeff", "fwd"):
            copies[name].wait()
        fwd_v[...] = jnp.concatenate(halves(fwd_f[...]), 1)
        taps = phi_v[...].astype(BF16).astype(F32).T.astype(BF16)
        coeff_high, coeff_low = halves(coeff_v[...])
        kernel_taps = dot(taps, coeff_high) + dot(taps, coeff_low)
        both = jnp.concatenate([kernel_taps[:LEAF], kernel_taps[LEAF:]], 1)
        high, low = halves(both)
        hat = dot(fwd_v[...], jnp.concatenate([high, high], 0)) + dot(fwd_v[:, :LEAF], low)
        a_re, a_im = hat[:LEAF, :WIDTH], hat[LEAF:, :WIDTH]
        b_re, b_im = hat[:LEAF, WIDTH:], hat[LEAF:, WIDTH:]
        row = lax.broadcasted_iota(jnp.int32, (LEAF, WIDTH), 0)
        sign = (1 - 2 * lax.rem(row, 2)).astype(F32)
        khat[0] = a_re
        khat[1] = a_im
        khat[2] = b_re - sign * a_im
        khat[3] = b_im + sign * a_re

    def tables_moments():
        copies["up"].wait()
        copies["lift"].wait()
        base = up_v[...]
        first = [fine_dot(lift_v[0, k], base) for k in range(2)]
        for leaf in range(LEAVES):
            second = fine_dot(lift_v[1, leaf // 2], first[leaf % 2])
            high, low = halves(jnp.concatenate([base, first[leaf % 2], second], 0))
            mom_m[leaf] = jnp.concatenate([high, low], 1)

    def tables_lift():
        def pair(level):
            return place_dot(lift_v[level, 0], selector(128, 32, 0, 128)) + place_dot(
                lift_v[level, 1], selector(128, 32, 16, 128)
            )

        def blocks(level, copies_of):
            rows = jnp.concatenate([pair(level)] * copies_of, 0)
            row = lax.broadcasted_iota(jnp.int32, rows.shape, 0)
            lane = lax.broadcasted_iota(jnp.int32, rows.shape, 1)
            return jnp.where(lax.div(row, RANK) == lax.div(lane, 2 * RANK), rows, 0.0)

        three = blocks(2, 8)
        four = fine_dot(blocks(3, 2), three)
        five = fine_dot(blocks(4, 1), jnp.concatenate([four, jnp.zeros((96, 128), F32)], 0))
        whole = jnp.concatenate([four, three[32:64], five, three[:32]], 0)
        high, low = halves(whole)
        lift_m[...] = jnp.concatenate([high, low], 1)
        six = place_dot(lift_v[5, 0], selector(128, 32, 0, 64)) + place_dot(
            lift_v[5, 1], selector(128, 32, 16, 64)
        )
        high = six.astype(BF16).astype(F32)
        lane = lax.broadcasted_iota(jnp.int32, six.shape, 1)
        six_m[...] = jnp.where(lane < 32, high, six - high).astype(BF16)

    def tables_far():
        copies["spread"].wait()
        copies["down"].wait()
        row = lax.broadcasted_iota(jnp.int32, (RANK, LEAF), 0)
        lane = lax.broadcasted_iota(jnp.int32, (RANK, LEAF), 1)
        summing = (lax.div(lane, RANK) == row).astype(F32)
        chain = None
        for k in range(5):
            if k > 0:
                step = spread_v[1 + k, lax.rem(lax.div(t, 2 ** (k - 1)), 2)]
                chain = step if k == 1 else fine_dot(chain, step)
            high, low = halves(summing if k == 0 else place_dot(chain, summing))
            red_m[k] = jnp.concatenate([high, low], 0)
        turned = down_v[...].T
        for leaf in range(LEAVES):
            near_step = spread_v[0, leaf % 2]
            both_steps = fine_dot(near_step, spread_v[1, leaf // 2])
            mix = (
                selector(LEAF, 48, 0, 144)
                + place_dot(near_step, selector(LEAF, 48, 16, 144))
                + place_dot(both_steps, selector(LEAF, 48, 32, 144))
            )
            whole = fine_dot(turned, mix)
            high = whole.astype(BF16).astype(F32)
            lane_at = lax.broadcasted_iota(jnp.int32, whole.shape, 1)
            far_m[leaf] = jnp.where(lane_at < 96, high, whole - high).astype(BF16)

    def pair_rows(first):
        return pl.ds(first * LEAF, 2 * LEAF)

    def scaled_rows(first, slots):
        rows = pair_rows(first)
        squares = jnp.zeros((2 * LEAF, WIDTH), F32)
        columns = []
        for slot in slots:
            tokens = g[slot, rows, :].astype(F32)
            squares = squares + tokens * tokens
            scale = gain_v[:, pl.ds(pl.multiple_of(owners[slot] * WIDTH, WIDTH), WIDTH)]
            columns.append((tokens * scale).astype(BF16))
        return jnp.concatenate(columns, 1), squares

    def gather_pair(first):
        scaled, squares = scaled_rows(first, (0, 1, 2))
        parts[pair_rows(first), :] = dot(scaled, w[:3].reshape(3 * WIDTH, 2 * WIDTH))
        part_squares[pair_rows(first), :] = squares[:, : WIDTH // 2] + squares[:, WIDTH // 2 :]

    def values_of(first):
        rows = pair_rows(first)
        scaled, squares = scaled_rows(first, (3,))
        squares = squares[:, : WIDTH // 2] + squares[:, WIDTH // 2 :] + part_squares[rows, :]
        inverse = lax.rsqrt(jnp.sum(squares, axis=1, keepdims=True) / 1024 + 1e-06)
        part_squares[rows, :] = jnp.broadcast_to(inverse, squares.shape)
        value = ((parts[rows, :WIDTH] + dot(scaled, w[3, :, :WIDTH])) * inverse).astype(BF16)
        vals[rows, :] = value
        for k in range(2):
            leaf_value = value[k * LEAF : (k + 1) * LEAF]
            moms[first + k] = dot(mom_m[first + k], jnp.concatenate([leaf_value, leaf_value], 0))

    def gates_of(first):
        rows = pair_rows(first)
        scaled, _ = scaled_rows(first, (3,))
        half = 0.5 * part_squares[rows, :]
        sums = parts[rows, WIDTH:] + dot(scaled, w[3, :, WIDTH:])
        gate[rows, :] = 0.5 * jnp.tanh(sums * jnp.concatenate([half, half], 1)) + 0.5

    def spectra(first):
        both = jnp.concatenate([vals[leaf_rows(first), :], vals[leaf_rows(first + 1), :]], 1)
        result = dot(fwd_v[...], jnp.concatenate([both, both], 0))
        spec[first] = result[:, :WIDTH]
        spec[first + 1] = result[:, WIDTH:]

    def near_rows(leaves):
        columns = []
        for leaf in leaves:
            before = leaf - 1 if leaf > 0 else LEAVES
            a_re, a_im = spec[leaf, :LEAF, :], spec[leaf, LEAF:, :]
            b_re, b_im = spec[before, :LEAF, :], spec[before, LEAF:, :]
            out_re = khat[0] * a_re - khat[1] * a_im + khat[2] * b_re - khat[3] * b_im
            out_im = khat[0] * a_im + khat[1] * a_re + khat[2] * b_im + khat[3] * b_re
            columns.append(jnp.concatenate([out_re, out_im], 0).astype(BF16))
        total = dot(inv_v[...], jnp.concatenate(columns, 1))
        for k, leaf in enumerate(leaves):
            rows = leaf_rows(leaf)
            direct_term = skip_v[...] * vals[rows, :].astype(F32)
            near[rows, :] = total[:, k * WIDTH : (k + 1) * WIDTH] + direct_term

    def coupled(level, source_two, source_three):
        product = coup_v[level, 0] * source_two[None]
        if source_three is not None:
            product = product + coup_v[level, 1] * source_three[None]
        return product.reshape(RANK * RANK, WIDTH).astype(BF16)

    send_direct(0)

    copies = {}

    def local(name, source, target):
        copies[name] = pltpu.make_async_copy(source, target, local_sem.at[len(copies)])
        copies[name].start()

    local("tok", tok, g.at[0])
    for slot in range(4):
        rows = pl.ds(pl.multiple_of(owners[slot] * WIDTH, WIDTH), WIDTH)
        local(("v", slot), w_value.at[rows], w.at[slot, :, pl.ds(0, WIDTH)])
        local(("g", slot), w_gate.at[rows], w.at[slot, :, pl.ds(WIDTH, WIDTH)])
    for name, source, target in (
        ("gain", gain, gain_v),
        ("phi", phi, phi_v),
        ("coeff", coeff, coeff_v),
        ("fwd", fwd, fwd_f),
        ("skip", skip, skip_v),
        ("up", up, up_v),
        ("down", down, down_v),
        ("lift", lift, lift_v),
        ("spread", spread, spread_v),
        ("inv", inv, inv_f),
        ("coup", coup, coup_v),
    ):
        local(name, source, target)

    @pl.when(z > 0)
    def _():
        signal(ready_next, t - PLANE, x)

    for k in range(1, PLANE):

        @pl.when(own >= k)
        def _():
            signal(ready_plane, t - k, x)

    def chain(place):
        @pl.when(z == PLANES - 1 - place)
        def _():
            if not isinstance(place, int) or place > 0:
                pl.semaphore_wait(ready_later, 1)
            if not isinstance(place, int) or place < PLANES - 1:
                signal(ready_later, t - PLANE, x)

    chain(0)
    tables_near()
    send_direct(1)
    chain(1)
    tables_moments()
    chain(2)
    tables_lift()
    chain(3)
    for slot in range(4):
        copies["v", slot].wait()
        copies["g", slot].wait()
    for name in ("tok", "gain", "skip", "coup", "inv"):
        copies[name].wait()
    pass_on(0)
    chain(4)

    @pl.when(own < PLANE - 1)
    def _():
        pl.semaphore_wait(ready_plane, PLANE - 1 - own)

    @pl.when(z < PLANES - 1)
    def _():
        pl.semaphore_wait(ready_next, 1)

        @pl.when(y == 0)
        def _():
            signal(ready_edge, z * PLANE + 6, x)
            signal(ready_edge, z * PLANE + 7, x)

    gather_pair(2)
    chain(5)
    tables_far()
    inv_v[...] = inv_f[...].astype(BF16)
    chain(6)
    pass_on(1)
    gather_pair(0)

    @pl.when((y == 3) & (z < PLANES - 1))
    def _():
        pl.semaphore_wait(ready_edge, 2)

    halo_copy = pltpu.make_async_remote_copy(
        src_ref=vals.at[pl.ds(3 * LEAF, LEAF)],
        dst_ref=halo,
        send_sem=hsem.at[0],
        recv_sem=hsem.at[1],
        device_id=(t + 1, x),
        device_id_type=MESH,
    )

    def ctx_copy(part):
        rows = pl.ds(0, 48) if part == 0 else pl.ds(48, 16)
        return pltpu.make_async_remote_copy(
            src_ref=ctx_out.at[rows],
            dst_ref=ctx_in.at[rows],
            send_sem=csem.at[0, part],
            recv_sem=csem.at[1, part],
            device_id=(t + 1, x),
            device_id_type=MESH,
        )

    summing = red_m[0, :RANK, :]

    def gathered(level, source_two, source_three=None):
        return dot(summing, coupled(level, source_two, source_three))

    wait_relayed(0)
    values_of(2)
    ctx_out[:48] = jnp.concatenate(
        [moms[2, 0:16, :], moms[3, 0:16, :], moms[2, 16:32, :] + moms[3, 16:32, :]], 0
    ).astype(BF16)

    @pl.when(t < PLANES * PLANE - 1)
    def _():
        halo_copy.start()
        ctx_copy(0).start()

    spectra(2)
    gates_of(2)
    near_rows((3,))

    wait_relayed(1)
    values_of(0)

    total = moms[0, 32:48, :] + moms[1, 32:48, :] + moms[2, 32:48, :] + moms[3, 32:48, :]
    m2[own] = total.astype(BF16)

    def plane_copy(k):
        return pltpu.make_async_remote_copy(
            src_ref=m2.at[own],
            dst_ref=m2.at[own],
            send_sem=s1,
            recv_sem=r1,
            device_id=(z * PLANE + lax.rem(own + k, PLANE), x),
            device_id_type=MESH,
        )

    plane_all = pltpu.make_async_remote_copy(
        src_ref=m2.at[pl.ds(0, PLANE - 1)],
        dst_ref=m2.at[pl.ds(0, PLANE - 1)],
        send_sem=s1,
        recv_sem=r1,
        device_id=(t, right),
        device_id_type=MESH,
    )

    for k in range(1, PLANE):
        plane_copy(k).start()

    def next_plane_copy(target, source):
        return pltpu.make_async_remote_copy(
            src_ref=m2.at[own],
            dst_ref=m2_prev.at[source],
            send_sem=s1p.at[target],
            recv_sem=r1p.at[source],
            device_id=((z + 1) * PLANE + target, x),
            device_id_type=MESH,
        )

    @pl.when((y == 3) & (z < PLANES - 1))
    def _():
        for target in range(2):
            next_plane_copy(target, core).start()

    ctx_out[48:] = (moms[0, 16:32, :] + moms[1, 16:32, :]).astype(BF16)

    @pl.when(t < PLANES * PLANE - 1)
    def _():
        ctx_copy(1).start()

    gates_of(0)

    plane_all.wait_recv()
    stack = m2[...].reshape(PLANE * RANK, WIDTH)
    lifted = dot(lift_m[...], jnp.concatenate([stack, stack], 0))
    pack_out[...] = lifted[:80].astype(BF16)


    def pack_copy(rows):
        return pltpu.make_async_remote_copy(
            src_ref=pack_out.at[pl.ds(0, rows)],
            dst_ref=pack_in.at[pl.ds(0, rows)],
            send_sem=s2,
            recv_sem=r2,
            device_id=(t + PLANE, x),
            device_id_type=MESH,
        )

    def five_copy(k):
        return pltpu.make_async_remote_copy(
            src_ref=pack_out.at[pl.ds(64, RANK)],
            dst_ref=m5_in.at[k],
            send_sem=s5.at[k],
            recv_sem=r5.at[k],
            device_id=(t + k * PLANE, x),
            device_id_type=MESH,
        )

    chain(7)

    for k in range(PLANES - 1, 1, -1):

        @pl.when(z + k < PLANES)
        def _():
            five_copy(k).start()

    @pl.when((z < PLANES - 1) & (y < 2))
    def _():
        pack_copy(64).start()

    @pl.when((z < PLANES - 1) & (y >= 2))
    def _():
        pack_copy(32).start()

    spectra(0)

    @pl.when(t > 0)
    def _():
        halo_copy.wait_recv()

    spec[LEAVES] = dot(fwd_v[...], jnp.concatenate([halo[...], halo[...]], 0))
    near_rows((0, 1, 2))

    @pl.when(t > 0)
    def _():
        ctx_copy(0).wait_recv()
        ctx_copy(1).wait_recv()

    prev = ctx_in[...].astype(F32)
    far0[0] = gathered(0, prev[0:16])
    far0[1] = gathered(0, prev[16:32], prev[0:16])
    far0[2] = gathered(0, moms[0, 0:16, :])
    far0[3] = gathered(0, moms[1, 0:16, :], moms[0, 0:16, :])
    far1[0] = gathered(1, prev[48:64])
    far1[1] = gathered(1, prev[32:48], prev[48:64])

    gather_sent = g.at[pl.ds(0, 3)]
    pltpu.make_async_remote_copy(
        src_ref=gather_sent,
        dst_ref=gather_sent,
        send_sem=gsend,
        recv_sem=drecv.at[0, 0],
        device_id=(t, right),
        device_id_type=MESH,
    ).wait_send()

    plane_all.wait_send()

    @pl.when(t < PLANES * PLANE - 1)
    def _():
        halo_copy.wait_send()
        ctx_copy(0).wait_send()
        ctx_copy(1).wait_send()

    @pl.when((y == 3) & (z < PLANES - 1))
    def _():
        for target in range(2):
            next_plane_copy(target, core).wait_send()

    @pl.when((y == 0) & (z > 0))
    def _():
        for source in range(2):
            next_plane_copy(source, source).wait_recv()

    def reduced(k, source_two, source_three):
        return dot(red_m[k], coupled(2 + k, source_two, source_three))

    at = 2 * jnp.maximum(y - 1, 0)
    inside = y > 0
    two = jnp.where(inside, m2[at + core], m2_prev[core]).astype(F32)
    three = jnp.where(inside, m2[at], m2_prev[0]).astype(F32) * core.astype(F32)
    expansion = reduced(0, two, three)

    @pl.when((z > 0) & (y < 2))
    def _():
        pack_copy(64).wait_recv()

    @pl.when((z > 0) & (y >= 2))
    def _():
        pack_copy(32).wait_recv()

    odd = lax.rem(y, 2)
    lower = y < 2
    here = jnp.where(odd == 1, lifted[96:112], lifted[80:96])
    coming = pack_in[pl.ds(pl.multiple_of(32 + odd * RANK, RANK), RANK), :].astype(F32)
    two = jnp.where(lower, coming, here)
    three = jnp.where(lower, pack_in[32:48, :].astype(F32), lifted[80:96]) * odd.astype(F32)
    expansion = expansion + reduced(1, two, three)
    odd = lax.div(y, 2)
    two = pack_in[pl.ds(pl.multiple_of(odd * RANK, RANK), RANK), :].astype(F32)
    three = pack_in[0:16, :].astype(F32) * odd.astype(F32)
    expansion = expansion + reduced(2, two, three)

    for k in range(2, PLANES):

        @pl.when(z >= k)
        def _():
            five_copy(k).wait_recv()

    odd = lax.rem(z, 2)
    expansion = expansion + reduced(
        3, m5_in[2].astype(F32), m5_in[3].astype(F32) * odd.astype(F32)
    )
    pad = jnp.zeros((64, WIDTH), BF16)

    def sixth(base):
        pair = [m5_in[base], m5_in[base - 1]]
        return dot(six_m[...], jnp.concatenate(pair + pair + [pad], 0))

    odd_six = lax.rem(lax.div(z, 2), 2)
    expansion = expansion + reduced(
        4, sixth(4 + odd), sixth(6 + odd) * odd_six.astype(F32)
    )

    expansion = expansion[:RANK] + expansion[RANK:]

    def out_copy(leaf):
        rows = leaf_rows(leaf)
        return pltpu.make_async_copy(out_v.at[rows], out.at[rows], osem.at[leaf])

    for leaf in range(LEAVES):
        rows = leaf_rows(leaf)
        high, low = halves(jnp.concatenate([far0[leaf], far1[leaf // 2], expansion], 0))
        whole = jnp.concatenate([high, low, high, jnp.zeros((112, WIDTH), BF16)], 0)
        combined = near[rows, :] + dot(far_m[leaf], whole)
        out_v[rows, :] = (gate[rows, :] * combined).astype(BF16)
        out_copy(leaf).start()

    @pl.when((z < PLANES - 1) & (y < 2))
    def _():
        pack_copy(64).wait_send()

    @pl.when((z < PLANES - 1) & (y >= 2))
    def _():
        pack_copy(32).wait_send()

    for k in range(2, PLANES):

        @pl.when(z + k < PLANES)
        def _():
            five_copy(k).wait_send()

    for leaf in range(LEAVES):
        out_copy(leaf).wait()


def per_device(
    tokens,
    norm_gain,
    w_value,
    w_gate,
    phi_taps,
    tap_coeff,
    skip_gain,
    basis_up,
    basis_down,
    lift_maps,
    spread_maps,
    couplings,
):
    forward, inverse = transform_tables()
    in_hbm = pl.BlockSpec(memory_space=pltpu.HBM)
    frames = LEAF * LEAVES
    vmem = pltpu.VMEM
    dma = pltpu.SemaphoreType.DMA
    scratch = [
        vmem((4, frames, WIDTH), BF16),
        vmem((4, WIDTH, 2 * WIDTH), BF16),
        vmem((1, 4 * WIDTH), F32),
        vmem(phi_taps.shape, F32),
        vmem(tap_coeff.shape, F32),
        vmem((1, WIDTH), F32),
        vmem(basis_up.shape, F32),
        vmem(basis_down.shape, F32),
        vmem(lift_maps.shape, F32),
        vmem(spread_maps.shape, F32),
        vmem(couplings.shape, F32),
        vmem(forward.shape, F32),
        vmem(inverse.shape, F32),
        vmem((2 * LEAF, 2 * LEAF), BF16),
        vmem((LEAF, 2 * LEAF), BF16),
        vmem((frames, WIDTH), BF16),
        vmem((LEAF, WIDTH), BF16),
        vmem((frames, WIDTH), F32),
        vmem((frames, WIDTH), F32),
        vmem((LEAVES + 1, 2 * LEAF, WIDTH), F32),
        vmem((4, LEAF, WIDTH), F32),
        vmem((LEAVES, 48, 2 * LEAF), BF16),
        vmem((112, 256), BF16),
        vmem((RANK, 128), BF16),
        vmem((LEAVES, LEAF, LEAF), BF16),
        vmem((5, 2 * RANK, LEAF), BF16),
        vmem((LEAVES, 48, WIDTH), F32),
        vmem((PLANE, RANK, WIDTH), BF16),
        vmem((2, RANK, WIDTH), BF16),
        vmem((64, WIDTH), BF16),
        vmem((64, WIDTH), BF16),
        vmem((80, WIDTH), BF16),
        vmem((64, WIDTH), BF16),
        vmem((PLANES, RANK, WIDTH), BF16),
        vmem((LEAVES, RANK, WIDTH), F32),
        vmem((2, RANK, WIDTH), F32),
        vmem((frames, WIDTH), BF16),
        vmem((frames, 2 * WIDTH), F32),
        vmem((frames, WIDTH // 2), F32),
        dma((20,)),
        dma(()),
        dma((2, 2)),
        dma((2, 2)),
        dma((2,)),
        dma((2, 2)),
        dma(()),
        dma(()),
        dma((2,)),
        dma((2,)),
        dma(()),
        dma(()),
        dma((PLANES,)),
        dma((PLANES,)),
        pltpu.SemaphoreType.REGULAR,
        pltpu.SemaphoreType.REGULAR,
        pltpu.SemaphoreType.REGULAR,
        pltpu.SemaphoreType.REGULAR,
        dma((LEAVES,)),
    ]
    return pl.pallas_call(
        body,
        out_shape=jax.ShapeDtypeStruct(tokens.shape, BF16),
        in_specs=[in_hbm] * 14,
        out_specs=in_hbm,
        scratch_shapes=scratch,
        compiler_params=pltpu.CompilerParams(
            collective_id=0, has_side_effects=True, vmem_limit_bytes=60 * 1024 * 1024
        ),
        cost_estimate=pl.CostEstimate(flops=4 * 10**9, bytes_accessed=8 * 10**6, transcendentals=10**6),
    )(
        tokens,
        norm_gain.reshape(1, -1),
        w_value,
        w_gate,
        phi_taps,
        tap_coeff,
        skip_gain.reshape(1, -1),
        basis_up,
        basis_down,
        lift_maps,
        spread_maps,
        couplings,
        jnp.asarray(forward),
        jnp.asarray(inverse),
    )


def solution(mesh):
    placed = (
        P("tm", "chan"),
        P(),
        P(None, "chan"),
        P(None, "chan"),
        P(),
        P(None, "chan"),
        P("chan"),
        P(),
        P(),
        P(),
        P(),
        P(None, None, None, None, "chan"),
    )
    return jax.shard_map(
        per_device, mesh=mesh, in_specs=placed, out_specs=P("tm", "chan"), check_vma=False
    )
```

```python
import jax
import jax.numpy as jnp
import numpy as np
from jax import lax
from jax.experimental import pallas as pl
from jax.experimental.pallas import tpu as pltpu
from jax.sharding import PartitionSpec as P

MESH = pl.DeviceIdType.MESH
F32 = jnp.float32
BF16 = jnp.bfloat16

LEAF = 256
LEAVES = 4
WIDTH = 256
RANK = 16
PLANES = 8
PLANE = 8


def transform_tables():
    odd = np.arange(LEAF)[:, None] + 0.5
    angle = 2 * np.pi * odd * np.arange(LEAF)[None, :] / (2 * LEAF)
    forward = np.concatenate([np.cos(angle), -np.sin(angle)], 0)
    return forward.astype(np.float32), (forward.T / LEAF).astype(np.float32)


def dot(left, right):
    return jnp.dot(left, right, preferred_element_type=F32)


def halves(value):
    high = value.astype(BF16)
    return high, (value - high.astype(F32)).astype(BF16)


def fine_dot(left, right):
    left_high, left_low = halves(left)
    right_high, right_low = halves(right)
    return dot(left_high, right_high) + dot(left_high, right_low) + dot(left_low, right_high)


def place_dot(left, right):
    left_high, left_low = halves(left)
    ones = right.astype(BF16)
    return dot(left_high, ones) + dot(left_low, ones)


def selector(lanes, period, shift, limit):
    row = lax.broadcasted_iota(jnp.int32, (RANK, lanes), 0)
    lane = lax.broadcasted_iota(jnp.int32, (RANK, lanes), 1)
    return ((lax.rem(lane, period) == row + shift) & (lane < limit)).astype(F32)


def body(
    tok, gain, w_value, w_gate, phi, coeff, skip, up, down, lift, spread, coup, fwd, inv,
    out,
    g, w, gain_v, phi_v, coeff_v, skip_v, up_v, down_v, lift_v, spread_v, coup_v, fwd_f, inv_f, fwd_v, inv_v,
    vals, halo, gate, near, spec, khat, mom_m, lift_m, six_m, far_m, red_m, moms,
    m2, m2_prev, ctx_out, ctx_in, pack_out, pack_in, m5_in, far0, far1, out_v, parts, part_squares,
    local_sem, gsend, drecv, rrecv, hsem, csem, s1, r1, s1p, r1p, s2, r2, s5, r5, ready_plane, ready_next, ready_edge, ready_later, osem,
):
    t = lax.axis_index("tm")
    x = lax.axis_index("chan")
    core = lax.rem(t, 2)
    y = lax.rem(lax.div(t, 2), 4)
    z = lax.div(t, PLANE)
    own = lax.rem(t, PLANE)
    right, left = lax.rem(x + 1, 4), lax.rem(x + 3, 4)

    barrier = pltpu.get_barrier_semaphore()

    def signal(semaphore, frames, chans):
        pl.semaphore_signal(semaphore, inc=1, device_id=(frames, chans), device_id_type=MESH)

    signal(barrier, t, right)
    signal(barrier, t, left)

    @pl.when(z < PLANES - 1)
    def _():
        signal(barrier, t + PLANE, x)

    for k in range(1, PLANE):

        @pl.when(own + k < PLANE)
        def _():
            signal(barrier, t + k, x)

    m2_prev[...] = jnp.zeros_like(m2_prev)
    ctx_in[...] = jnp.zeros_like(ctx_in)
    pack_in[...] = jnp.zeros_like(pack_in)
    m5_in[...] = jnp.zeros_like(m5_in)
    halo[...] = jnp.zeros_like(halo)

    pl.semaphore_wait(barrier, 2 + own + jnp.where(z > 0, 1, 0))

    owners = [x, left, right, lax.rem(x + 2, 4)]

    def leaf_rows(leaf):
        return pl.ds(leaf * LEAF if isinstance(leaf, int) else pl.multiple_of(leaf * LEAF, LEAF), LEAF)

    def direct(group, way):
        rows = pl.ds((1 - group) * 2 * LEAF, 2 * LEAF)
        return pltpu.make_async_remote_copy(
            src_ref=tok.at[rows],
            dst_ref=g.at[1 + way, rows],
            send_sem=gsend,
            recv_sem=drecv.at[way, group],
            device_id=(t, left if way else right),
            device_id_type=MESH,
        )

    def relay(group, way):
        rows = leaf_rows((1 - group) * 2 + way)
        return pltpu.make_async_remote_copy(
            src_ref=g.at[1 + way, rows],
            dst_ref=g.at[3, rows],
            send_sem=gsend,
            recv_sem=rrecv.at[way, group],
            device_id=(t, left if way else right),
            device_id_type=MESH,
        )

    def send_direct(group):
        for way in range(2):
            direct(group, way).start()

    def arrive(group):
        for way in range(2):
            direct(group, way).wait_recv()

    def pass_on(group):
        for way in range(2):
            relay(group, way).start()

    def wait_relayed(group):
        for way in range(2):
            relay(group, way).wait_recv()

    def tables_near():
        for name in ("phi", "coeff", "fwd"):
            copies[name].wait()
        fwd_v[...] = jnp.concatenate(halves(fwd_f[...]), 1)
        taps = phi_v[...].astype(BF16).astype(F32).T.astype(BF16)
        coeff_high, coeff_low = halves(coeff_v[...])
        kernel_taps = dot(taps, coeff_high) + dot(taps, coeff_low)
        both = jnp.concatenate([kernel_taps[:LEAF], kernel_taps[LEAF:]], 1)
        high, low = halves(both)
        hat = dot(fwd_v[...], jnp.concatenate([high, high], 0)) + dot(fwd_v[:, :LEAF], low)
        a_re, a_im = hat[:LEAF, :WIDTH], hat[LEAF:, :WIDTH]
        b_re, b_im = hat[:LEAF, WIDTH:], hat[LEAF:, WIDTH:]
        row = lax.broadcasted_iota(jnp.int32, (LEAF, WIDTH), 0)
        sign = (1 - 2 * lax.rem(row, 2)).astype(F32)
        khat[0] = a_re
        khat[1] = a_im
        khat[2] = b_re - sign * a_im
        khat[3] = b_im + sign * a_re

    def tables_moments():
        copies["up"].wait()
        copies["lift"].wait()
        base = up_v[...]
        first = [fine_dot(lift_v[0, k], base) for k in range(2)]
        for leaf in range(LEAVES):
            second = fine_dot(lift_v[1, leaf // 2], first[leaf % 2])
            high, low = halves(jnp.concatenate([base, first[leaf % 2], second], 0))
            mom_m[leaf] = jnp.concatenate([high, low], 1)

    def tables_lift():
        def pair(level):
            return place_dot(lift_v[level, 0], selector(128, 32, 0, 128)) + place_dot(
                lift_v[level, 1], selector(128, 32, 16, 128)
            )

        def blocks(level, copies_of):
            rows = jnp.concatenate([pair(level)] * copies_of, 0)
            row = lax.broadcasted_iota(jnp.int32, rows.shape, 0)
            lane = lax.broadcasted_iota(jnp.int32, rows.shape, 1)
            return jnp.where(lax.div(row, RANK) == lax.div(lane, 2 * RANK), rows, 0.0)

        three = blocks(2, 8)
        four = fine_dot(blocks(3, 2), three)
        five = fine_dot(blocks(4, 1), jnp.concatenate([four, jnp.zeros((96, 128), F32)], 0))
        whole = jnp.concatenate([four, three[32:64], five, three[:32]], 0)
        high, low = halves(whole)
        lift_m[...] = jnp.concatenate([high, low], 1)
        six = place_dot(lift_v[5, 0], selector(128, 32, 0, 64)) + place_dot(
            lift_v[5, 1], selector(128, 32, 16, 64)
        )
        high = six.astype(BF16).astype(F32)
        lane = lax.broadcasted_iota(jnp.int32, six.shape, 1)
        six_m[...] = jnp.where(lane < 32, high, six - high).astype(BF16)

    def tables_far():
        copies["spread"].wait()
        copies["down"].wait()
        row = lax.broadcasted_iota(jnp.int32, (RANK, LEAF), 0)
        lane = lax.broadcasted_iota(jnp.int32, (RANK, LEAF), 1)
        summing = (lax.div(lane, RANK) == row).astype(F32)
        chain = None
        for k in range(5):
            if k > 0:
                step = spread_v[1 + k, lax.rem(lax.div(t, 2 ** (k - 1)), 2)]
                chain = step if k == 1 else fine_dot(chain, step)
            high, low = halves(summing if k == 0 else place_dot(chain, summing))
            red_m[k] = jnp.concatenate([high, low], 0)
        turned = down_v[...].T
        for leaf in range(LEAVES):
            near_step = spread_v[0, leaf % 2]
            both_steps = fine_dot(near_step, spread_v[1, leaf // 2])
            mix = (
                selector(LEAF, 48, 0, 144)
                + place_dot(near_step, selector(LEAF, 48, 16, 144))
                + place_dot(both_steps, selector(LEAF, 48, 32, 144))
            )
            whole = fine_dot(turned, mix)
            high = whole.astype(BF16).astype(F32)
            lane_at = lax.broadcasted_iota(jnp.int32, whole.shape, 1)
            far_m[leaf] = jnp.where(lane_at < 96, high, whole - high).astype(BF16)

    def pair_rows(first):
        return pl.ds(first * LEAF, 2 * LEAF)

    def scaled_rows(first, slots):
        rows = pair_rows(first)
        squares = jnp.zeros((2 * LEAF, WIDTH), F32)
        columns = []
        for slot in slots:
            tokens = g[slot, rows, :].astype(F32)
            squares = squares + tokens * tokens
            scale = gain_v[:, pl.ds(pl.multiple_of(owners[slot] * WIDTH, WIDTH), WIDTH)]
            columns.append((tokens * scale).astype(BF16))
        return jnp.concatenate(columns, 1), squares

    def gather_pair(first):
        scaled, squares = scaled_rows(first, (0, 1, 2))
        parts[pair_rows(first), :] = dot(scaled, w[:3].reshape(3 * WIDTH, 2 * WIDTH))
        part_squares[pair_rows(first), :] = squares[:, : WIDTH // 2] + squares[:, WIDTH // 2 :]

    def values_of(first):
        rows = pair_rows(first)
        scaled, squares = scaled_rows(first, (3,))
        squares = squares[:, : WIDTH // 2] + squares[:, WIDTH // 2 :] + part_squares[rows, :]
        inverse = lax.rsqrt(jnp.sum(squares, axis=1, keepdims=True) / 1024 + 1e-06)
        part_squares[rows, :] = jnp.broadcast_to(inverse, squares.shape)
        value = ((parts[rows, :WIDTH] + dot(scaled, w[3, :, :WIDTH])) * inverse).astype(BF16)
        vals[rows, :] = value
        for k in range(2):
            leaf_value = value[k * LEAF : (k + 1) * LEAF]
            moms[first + k] = dot(mom_m[first + k], jnp.concatenate([leaf_value, leaf_value], 0))

    def gates_of(first):
        rows = pair_rows(first)
        scaled, _ = scaled_rows(first, (3,))
        half = 0.5 * part_squares[rows, :]
        sums = parts[rows, WIDTH:] + dot(scaled, w[3, :, WIDTH:])
        gate[rows, :] = 0.5 * jnp.tanh(sums * jnp.concatenate([half, half], 1)) + 0.5

    def spectra(first):
        both = jnp.concatenate([vals[leaf_rows(first), :], vals[leaf_rows(first + 1), :]], 1)
        result = dot(fwd_v[...], jnp.concatenate([both, both], 0))
        spec[first] = result[:, :WIDTH]
        spec[first + 1] = result[:, WIDTH:]

    def near_rows(leaves):
        columns = []
        for leaf in leaves:
            before = leaf - 1 if leaf > 0 else LEAVES
            a_re, a_im = spec[leaf, :LEAF, :], spec[leaf, LEAF:, :]
            b_re, b_im = spec[before, :LEAF, :], spec[before, LEAF:, :]
            out_re = khat[0] * a_re - khat[1] * a_im + khat[2] * b_re - khat[3] * b_im
            out_im = khat[0] * a_im + khat[1] * a_re + khat[2] * b_im + khat[3] * b_re
            columns.append(jnp.concatenate([out_re, out_im], 0).astype(BF16))
        total = dot(inv_v[...], jnp.concatenate(columns, 1))
        for k, leaf in enumerate(leaves):
            rows = leaf_rows(leaf)
            direct_term = skip_v[...] * vals[rows, :].astype(F32)
            near[rows, :] = total[:, k * WIDTH : (k + 1) * WIDTH] + direct_term

    def coupled(level, source_two, source_three):
        product = coup_v[level, 0] * source_two[None]
        if source_three is not None:
            product = product + coup_v[level, 1] * source_three[None]
        return product.reshape(RANK * RANK, WIDTH).astype(BF16)

    send_direct(0)
    send_direct(1)

    copies = {}

    def local(name, source, target):
        copies[name] = pltpu.make_async_copy(source, target, local_sem.at[len(copies)])
        copies[name].start()

    local("tok", tok, g.at[0])
    for slot in range(4):
        rows = pl.ds(pl.multiple_of(owners[slot] * WIDTH, WIDTH), WIDTH)
        local(("v", slot), w_value.at[rows], w.at[slot, :, pl.ds(0, WIDTH)])
        local(("g", slot), w_gate.at[rows], w.at[slot, :, pl.ds(WIDTH, WIDTH)])
    for name, source, target in (
        ("gain", gain, gain_v),
        ("phi", phi, phi_v),
        ("coeff", coeff, coeff_v),
        ("fwd", fwd, fwd_f),
        ("skip", skip, skip_v),
        ("up", up, up_v),
        ("down", down, down_v),
        ("lift", lift, lift_v),
        ("spread", spread, spread_v),
        ("inv", inv, inv_f),
        ("coup", coup, coup_v),
    ):
        local(name, source, target)

    @pl.when(z > 0)
    def _():
        signal(ready_next, t - PLANE, x)

    for k in range(1, PLANE):

        @pl.when(own >= k)
        def _():
            signal(ready_plane, t - k, x)

    def chain(place):
        @pl.when(z == PLANES - 1 - place)
        def _():
            if not isinstance(place, int) or place > 0:
                pl.semaphore_wait(ready_later, 1)
            if not isinstance(place, int) or place < PLANES - 1:
                signal(ready_later, t - PLANE, x)

    chain(0)
    tables_near()
    chain(1)
    tables_moments()
    chain(2)
    tables_lift()
    chain(3)
    tables_far()
    for name in ("tok", "gain", "skip", "coup", "inv"):
        copies[name].wait()
    inv_v[...] = inv_f[...].astype(BF16)
    for slot in range(4):
        copies["v", slot].wait()
        copies["g", slot].wait()
    chain(4)

    @pl.when(own < PLANE - 1)
    def _():
        pl.semaphore_wait(ready_plane, PLANE - 1 - own)

    @pl.when(z < PLANES - 1)
    def _():
        pl.semaphore_wait(ready_next, 1)

        @pl.when(y == 0)
        def _():
            signal(ready_edge, z * PLANE + 6, x)
            signal(ready_edge, z * PLANE + 7, x)

    chain(5)
    arrive(0)
    pass_on(0)
    gather_pair(2)
    chain(6)
    arrive(1)
    gather_pair(0)
    pass_on(1)

    @pl.when((y == 3) & (z < PLANES - 1))
    def _():
        pl.semaphore_wait(ready_edge, 2)

    halo_copy = pltpu.make_async_remote_copy(
        src_ref=vals.at[pl.ds(3 * LEAF, LEAF)],
        dst_ref=halo,
        send_sem=hsem.at[0],
        recv_sem=hsem.at[1],
        device_id=(t + 1, x),
        device_id_type=MESH,
    )

    def ctx_copy(part):
        rows = pl.ds(0, 48) if part == 0 else pl.ds(48, 16)
        return pltpu.make_async_remote_copy(
            src_ref=ctx_out.at[rows],
            dst_ref=ctx_in.at[rows],
            send_sem=csem.at[0, part],
            recv_sem=csem.at[1, part],
            device_id=(t + 1, x),
            device_id_type=MESH,
        )

    summing = red_m[0, :RANK, :]

    def gathered(level, source_two, source_three=None):
        return dot(summing, coupled(level, source_two, source_three))

    wait_relayed(0)
    values_of(2)
    ctx_out[:48] = jnp.concatenate(
        [moms[2, 0:16, :], moms[3, 0:16, :], moms[2, 16:32, :] + moms[3, 16:32, :]], 0
    ).astype(BF16)

    @pl.when(t < PLANES * PLANE - 1)
    def _():
        halo_copy.start()
        ctx_copy(0).start()

    spectra(2)
    gates_of(2)
    near_rows((3,))

    wait_relayed(1)
    values_of(0)

    total = moms[0, 32:48, :] + moms[1, 32:48, :] + moms[2, 32:48, :] + moms[3, 32:48, :]
    m2[own] = total.astype(BF16)

    def plane_copy(k):
        return pltpu.make_async_remote_copy(
            src_ref=m2.at[own],
            dst_ref=m2.at[own],
            send_sem=s1,
            recv_sem=r1,
            device_id=(z * PLANE + lax.rem(own + k, PLANE), x),
            device_id_type=MESH,
        )

    plane_all = pltpu.make_async_remote_copy(
        src_ref=m2.at[pl.ds(0, PLANE - 1)],
        dst_ref=m2.at[pl.ds(0, PLANE - 1)],
        send_sem=s1,
        recv_sem=r1,
        device_id=(t, right),
        device_id_type=MESH,
    )

    for k in range(1, PLANE):
        plane_copy(k).start()

    def next_plane_copy(target, source):
        return pltpu.make_async_remote_copy(
            src_ref=m2.at[own],
            dst_ref=m2_prev.at[source],
            send_sem=s1p.at[target],
            recv_sem=r1p.at[source],
            device_id=((z + 1) * PLANE + target, x),
            device_id_type=MESH,
        )

    @pl.when((y == 3) & (z < PLANES - 1))
    def _():
        for target in range(2):
            next_plane_copy(target, core).start()

    ctx_out[48:] = (moms[0, 16:32, :] + moms[1, 16:32, :]).astype(BF16)

    @pl.when(t < PLANES * PLANE - 1)
    def _():
        ctx_copy(1).start()

    gates_of(0)

    def own_work():
        spectra(0)
        near_rows((1, 2))
        far0[2] = gathered(0, moms[0, 0:16, :])
        far0[3] = gathered(0, moms[1, 0:16, :], moms[0, 0:16, :])

    @pl.when(y == 0)
    def _():
        own_work()

    plane_all.wait_recv()
    stack = m2[...].reshape(PLANE * RANK, WIDTH)
    lifted = dot(lift_m[...], jnp.concatenate([stack, stack], 0))
    pack_out[...] = lifted[:80].astype(BF16)


    def pack_copy(rows):
        return pltpu.make_async_remote_copy(
            src_ref=pack_out.at[pl.ds(0, rows)],
            dst_ref=pack_in.at[pl.ds(0, rows)],
            send_sem=s2,
            recv_sem=r2,
            device_id=(t + PLANE, x),
            device_id_type=MESH,
        )

    def five_copy(k):
        return pltpu.make_async_remote_copy(
            src_ref=pack_out.at[pl.ds(64, RANK)],
            dst_ref=m5_in.at[k],
            send_sem=s5.at[k],
            recv_sem=r5.at[k],
            device_id=(t + k * PLANE, x),
            device_id_type=MESH,
        )

    chain(7)

    for k in range(PLANES - 1, 1, -1):

        @pl.when(z + k < PLANES)
        def _():
            five_copy(k).start()

    @pl.when((z < PLANES - 1) & (y < 2))
    def _():
        pack_copy(64).start()

    @pl.when((z < PLANES - 1) & (y >= 2))
    def _():
        pack_copy(32).start()

    @pl.when(y > 0)
    def _():
        own_work()

    @pl.when(t > 0)
    def _():
        halo_copy.wait_recv()

    spec[LEAVES] = dot(fwd_v[...], jnp.concatenate([halo[...], halo[...]], 0))
    near_rows((0,))

    @pl.when(t > 0)
    def _():
        ctx_copy(0).wait_recv()
        ctx_copy(1).wait_recv()

    prev = ctx_in[...].astype(F32)
    far0[0] = gathered(0, prev[0:16])
    far0[1] = gathered(0, prev[16:32], prev[0:16])
    far1[0] = gathered(1, prev[48:64])
    far1[1] = gathered(1, prev[32:48], prev[48:64])

    gather_sent = g.at[pl.ds(0, 3)]
    pltpu.make_async_remote_copy(
        src_ref=gather_sent,
        dst_ref=gather_sent,
        send_sem=gsend,
        recv_sem=drecv.at[0, 0],
        device_id=(t, right),
        device_id_type=MESH,
    ).wait_send()

    plane_all.wait_send()

    @pl.when(t < PLANES * PLANE - 1)
    def _():
        halo_copy.wait_send()
        ctx_copy(0).wait_send()
        ctx_copy(1).wait_send()

    @pl.when((y == 3) & (z < PLANES - 1))
    def _():
        for target in range(2):
            next_plane_copy(target, core).wait_send()

    @pl.when((y == 0) & (z > 0))
    def _():
        for source in range(2):
            next_plane_copy(source, source).wait_recv()

    def reduced(k, source_two, source_three):
        return dot(red_m[k], coupled(2 + k, source_two, source_three))

    at = 2 * jnp.maximum(y - 1, 0)
    inside = y > 0
    two = jnp.where(inside, m2[at + core], m2_prev[core]).astype(F32)
    three = jnp.where(inside, m2[at], m2_prev[0]).astype(F32) * core.astype(F32)
    expansion = reduced(0, two, three)

    @pl.when((z > 0) & (y < 2))
    def _():
        pack_copy(64).wait_recv()

    @pl.when((z > 0) & (y >= 2))
    def _():
        pack_copy(32).wait_recv()

    odd = lax.rem(y, 2)
    lower = y < 2
    here = jnp.where(odd == 1, lifted[96:112], lifted[80:96])
    coming = pack_in[pl.ds(pl.multiple_of(32 + odd * RANK, RANK), RANK), :].astype(F32)
    two = jnp.where(lower, coming, here)
    three = jnp.where(lower, pack_in[32:48, :].astype(F32), lifted[80:96]) * odd.astype(F32)
    expansion = expansion + reduced(1, two, three)
    odd = lax.div(y, 2)
    two = pack_in[pl.ds(pl.multiple_of(odd * RANK, RANK), RANK), :].astype(F32)
    three = pack_in[0:16, :].astype(F32) * odd.astype(F32)
    expansion = expansion + reduced(2, two, three)

    for k in range(2, PLANES):

        @pl.when(z >= k)
        def _():
            five_copy(k).wait_recv()

    odd = lax.rem(z, 2)
    expansion = expansion + reduced(
        3, m5_in[2].astype(F32), m5_in[3].astype(F32) * odd.astype(F32)
    )
    pad = jnp.zeros((64, WIDTH), BF16)

    def sixth(base):
        pair = [m5_in[base], m5_in[base - 1]]
        return dot(six_m[...], jnp.concatenate(pair + pair + [pad], 0))

    odd_six = lax.rem(lax.div(z, 2), 2)
    expansion = expansion + reduced(
        4, sixth(4 + odd), sixth(6 + odd) * odd_six.astype(F32)
    )

    expansion = expansion[:RANK] + expansion[RANK:]

    def out_copy(leaf):
        rows = leaf_rows(leaf)
        return pltpu.make_async_copy(out_v.at[rows], out.at[rows], osem.at[leaf])

    for leaf in range(LEAVES):
        rows = leaf_rows(leaf)
        high, low = halves(jnp.concatenate([far0[leaf], far1[leaf // 2], expansion], 0))
        whole = jnp.concatenate([high, low, high, jnp.zeros((112, WIDTH), BF16)], 0)
        combined = near[rows, :] + dot(far_m[leaf], whole)
        out_v[rows, :] = (gate[rows, :] * combined).astype(BF16)
        out_copy(leaf).start()

    @pl.when((z < PLANES - 1) & (y < 2))
    def _():
        pack_copy(64).wait_send()

    @pl.when((z < PLANES - 1) & (y >= 2))
    def _():
        pack_copy(32).wait_send()

    for k in range(2, PLANES):

        @pl.when(z + k < PLANES)
        def _():
            five_copy(k).wait_send()

    for leaf in range(LEAVES):
        out_copy(leaf).wait()


def per_device(
    tokens,
    norm_gain,
    w_value,
    w_gate,
    phi_taps,
    tap_coeff,
    skip_gain,
    basis_up,
    basis_down,
    lift_maps,
    spread_maps,
    couplings,
):
    forward, inverse = transform_tables()
    in_hbm = pl.BlockSpec(memory_space=pltpu.HBM)
    frames = LEAF * LEAVES
    vmem = pltpu.VMEM
    dma = pltpu.SemaphoreType.DMA
    scratch = [
        vmem((4, frames, WIDTH), BF16),
        vmem((4, WIDTH, 2 * WIDTH), BF16),
        vmem((1, 4 * WIDTH), F32),
        vmem(phi_taps.shape, F32),
        vmem(tap_coeff.shape, F32),
        vmem((1, WIDTH), F32),
        vmem(basis_up.shape, F32),
        vmem(basis_down.shape, F32),
        vmem(lift_maps.shape, F32),
        vmem(spread_maps.shape, F32),
        vmem(couplings.shape, F32),
        vmem(forward.shape, F32),
        vmem(inverse.shape, F32),
        vmem((2 * LEAF, 2 * LEAF), BF16),
        vmem((LEAF, 2 * LEAF), BF16),
        vmem((frames, WIDTH), BF16),
        vmem((LEAF, WIDTH), BF16),
        vmem((frames, WIDTH), F32),
        vmem((frames, WIDTH), F32),
        vmem((LEAVES + 1, 2 * LEAF, WIDTH), F32),
        vmem((4, LEAF, WIDTH), F32),
        vmem((LEAVES, 48, 2 * LEAF), BF16),
        vmem((112, 256), BF16),
        vmem((RANK, 128), BF16),
        vmem((LEAVES, LEAF, LEAF), BF16),
        vmem((5, 2 * RANK, LEAF), BF16),
        vmem((LEAVES, 48, WIDTH), F32),
        vmem((PLANE, RANK, WIDTH), BF16),
        vmem((2, RANK, WIDTH), BF16),
        vmem((64, WIDTH), BF16),
        vmem((64, WIDTH), BF16),
        vmem((80, WIDTH), BF16),
        vmem((64, WIDTH), BF16),
        vmem((PLANES, RANK, WIDTH), BF16),
        vmem((LEAVES, RANK, WIDTH), F32),
        vmem((2, RANK, WIDTH), F32),
        vmem((frames, WIDTH), BF16),
        vmem((frames, 2 * WIDTH), F32),
        vmem((frames, WIDTH // 2), F32),
        dma((20,)),
        dma(()),
        dma((2, 2)),
        dma((2, 2)),
        dma((2,)),
        dma((2, 2)),
        dma(()),
        dma(()),
        dma((2,)),
        dma((2,)),
        dma(()),
        dma(()),
        dma((PLANES,)),
        dma((PLANES,)),
        pltpu.SemaphoreType.REGULAR,
        pltpu.SemaphoreType.REGULAR,
        pltpu.SemaphoreType.REGULAR,
        pltpu.SemaphoreType.REGULAR,
        dma((LEAVES,)),
    ]
    return pl.pallas_call(
        body,
        out_shape=jax.ShapeDtypeStruct(tokens.shape, BF16),
        in_specs=[in_hbm] * 14,
        out_specs=in_hbm,
        scratch_shapes=scratch,
        compiler_params=pltpu.CompilerParams(
            collective_id=0, has_side_effects=True, vmem_limit_bytes=60 * 1024 * 1024
        ),
        cost_estimate=pl.CostEstimate(flops=4 * 10**9, bytes_accessed=8 * 10**6, transcendentals=10**6),
    )(
        tokens,
        norm_gain.reshape(1, -1),
        w_value,
        w_gate,
        phi_taps,
        tap_coeff,
        skip_gain.reshape(1, -1),
        basis_up,
        basis_down,
        lift_maps,
        spread_maps,
        couplings,
        jnp.asarray(forward),
        jnp.asarray(inverse),
    )


def solution(mesh):
    placed = (
        P("tm", "chan"),
        P(),
        P(None, "chan"),
        P(None, "chan"),
        P(),
        P(None, "chan"),
        P("chan"),
        P(),
        P(),
        P(),
        P(),
        P(None, None, None, None, "chan"),
    )
    return jax.shard_map(
        per_device, mesh=mesh, in_specs=placed, out_specs=P("tm", "chan"), check_vma=False
    )
```

```python
import jax
import jax.numpy as jnp
import numpy as np
from jax import lax
from jax.experimental import pallas as pl
from jax.experimental.pallas import tpu as pltpu
from jax.sharding import PartitionSpec as P

MESH = pl.DeviceIdType.MESH
F32 = jnp.float32
BF16 = jnp.bfloat16

LEAF = 256
LEAVES = 4
WIDTH = 256
RANK = 16
PLANES = 8
PLANE = 8


def transform_tables():
    odd = np.arange(LEAF)[:, None] + 0.5
    angle = 2 * np.pi * odd * np.arange(LEAF)[None, :] / (2 * LEAF)
    forward = np.concatenate([np.cos(angle), -np.sin(angle)], 0)
    return forward.astype(np.float32), (forward.T / LEAF).astype(np.float32)


def dot(left, right):
    return jnp.dot(left, right, preferred_element_type=F32)


def halves(value):
    high = value.astype(BF16)
    return high, (value - high.astype(F32)).astype(BF16)


def fine_dot(left, right):
    left_high, left_low = halves(left)
    right_high, right_low = halves(right)
    return dot(left_high, right_high) + dot(left_high, right_low) + dot(left_low, right_high)


def place_dot(left, right):
    left_high, left_low = halves(left)
    ones = right.astype(BF16)
    return dot(left_high, ones) + dot(left_low, ones)


def selector(lanes, period, shift, limit):
    row = lax.broadcasted_iota(jnp.int32, (RANK, lanes), 0)
    lane = lax.broadcasted_iota(jnp.int32, (RANK, lanes), 1)
    return ((lax.rem(lane, period) == row + shift) & (lane < limit)).astype(F32)


def body(
    tok, gain, w_value, w_gate, phi, coeff, skip, up, down, lift, spread, coup, fwd, inv,
    gate_out, near_out, far_out, expansion_out,
    g, w, gain_v, phi_v, coeff_v, skip_v, up_v, down_v, lift_v, spread_v, coup_v, fwd_f, inv_f, fwd_v, inv_v,
    vals, halo, gate, near, spec, khat, mom_m, lift_m, six_m, far_m, red_m, moms,
    m2, m2_prev, ctx_out, ctx_in, pack_out, pack_in, m5_in, expansions, parts, part_squares,
    local_sem, gsend, drecv, rrecv, hsem, csem, s1, r1, s1p, r1p, s2, r2, s5, r5, ready_plane, ready_next, ready_edge, ready_later, osem,
):
    t = lax.axis_index("tm")
    x = lax.axis_index("chan")
    core = lax.rem(t, 2)
    y = lax.rem(lax.div(t, 2), 4)
    z = lax.div(t, PLANE)
    own = lax.rem(t, PLANE)
    right, left = lax.rem(x + 1, 4), lax.rem(x + 3, 4)

    barrier = pltpu.get_barrier_semaphore()

    def signal(semaphore, frames, chans):
        pl.semaphore_signal(semaphore, inc=1, device_id=(frames, chans), device_id_type=MESH)

    signal(barrier, t, right)
    signal(barrier, t, left)

    @pl.when(z < PLANES - 1)
    def _():
        signal(barrier, t + PLANE, x)

    for k in range(1, PLANE):

        @pl.when(own + k < PLANE)
        def _():
            signal(barrier, t + k, x)

    m2_prev[...] = jnp.zeros_like(m2_prev)
    ctx_in[...] = jnp.zeros_like(ctx_in)
    pack_in[...] = jnp.zeros_like(pack_in)
    m5_in[...] = jnp.zeros_like(m5_in)
    halo[...] = jnp.zeros_like(halo)

    pl.semaphore_wait(barrier, 2 + own + jnp.where(z > 0, 1, 0))

    owners = [x, left, right, lax.rem(x + 2, 4)]

    def leaf_rows(leaf):
        return pl.ds(leaf * LEAF if isinstance(leaf, int) else pl.multiple_of(leaf * LEAF, LEAF), LEAF)

    def pair_rows(first):
        return pl.ds(first * LEAF, 2 * LEAF)

    def direct(group, way):
        rows = pl.ds((1 - group) * 2 * LEAF, 2 * LEAF)
        return pltpu.make_async_remote_copy(
            src_ref=tok.at[rows],
            dst_ref=g.at[1 + way, rows],
            send_sem=gsend,
            recv_sem=drecv.at[way, group],
            device_id=(t, left if way else right),
            device_id_type=MESH,
        )

    def relay(group, way):
        rows = leaf_rows((1 - group) * 2 + way)
        return pltpu.make_async_remote_copy(
            src_ref=g.at[1 + way, rows],
            dst_ref=g.at[3, rows],
            send_sem=gsend,
            recv_sem=rrecv.at[way, group],
            device_id=(t, left if way else right),
            device_id_type=MESH,
        )

    def send_direct(group):
        for way in range(2):
            direct(group, way).start()

    def pass_on(group):
        for way in range(2):
            direct(group, way).wait_recv()
            relay(group, way).start()

    def wait_relayed(group):
        for way in range(2):
            relay(group, way).wait_recv()

    def handed(part):
        source, target = (
            (far_m, far_out),
            (gate.at[pair_rows(2)], gate_out.at[pair_rows(2)]),
            (gate.at[pair_rows(0)], gate_out.at[pair_rows(0)]),
            (near.at[leaf_rows(3)], near_out.at[leaf_rows(3)]),
            (near.at[pl.ds(0, 3 * LEAF)], near_out.at[pl.ds(0, 3 * LEAF)]),
            (expansions.at[pl.ds(0, 6)], expansion_out.at[pl.ds(0, 6)]),
            (expansions.at[pl.ds(6, 1)], expansion_out.at[pl.ds(6, 1)]),
        )[part]
        return pltpu.make_async_copy(source, target, osem.at[part])

    def tables_near():
        for name in ("phi", "coeff", "fwd"):
            copies[name].wait()
        fwd_v[...] = jnp.concatenate(halves(fwd_f[...]), 1)
        taps = phi_v[...].astype(BF16).astype(F32).T.astype(BF16)
        coeff_high, coeff_low = halves(coeff_v[...])
        kernel_taps = dot(taps, coeff_high) + dot(taps, coeff_low)
        both = jnp.concatenate([kernel_taps[:LEAF], kernel_taps[LEAF:]], 1)
        high, low = halves(both)
        hat = dot(fwd_v[...], jnp.concatenate([high, high], 0)) + dot(fwd_v[:, :LEAF], low)
        a_re, a_im = hat[:LEAF, :WIDTH], hat[LEAF:, :WIDTH]
        b_re, b_im = hat[:LEAF, WIDTH:], hat[LEAF:, WIDTH:]
        row = lax.broadcasted_iota(jnp.int32, (LEAF, WIDTH), 0)
        sign = (1 - 2 * lax.rem(row, 2)).astype(F32)
        khat[0] = a_re
        khat[1] = a_im
        khat[2] = b_re - sign * a_im
        khat[3] = b_im + sign * a_re

    def tables_moments():
        copies["up"].wait()
        copies["lift"].wait()
        base = up_v[...]
        first = [fine_dot(lift_v[0, k], base) for k in range(2)]
        for leaf in range(LEAVES):
            second = fine_dot(lift_v[1, leaf // 2], first[leaf % 2])
            high, low = halves(jnp.concatenate([base, first[leaf % 2], second], 0))
            mom_m[leaf] = jnp.concatenate([high, low], 1)

    def tables_lift():
        def pair(level):
            return place_dot(lift_v[level, 0], selector(128, 32, 0, 128)) + place_dot(
                lift_v[level, 1], selector(128, 32, 16, 128)
            )

        def blocks(level, copies_of):
            rows = jnp.concatenate([pair(level)] * copies_of, 0)
            row = lax.broadcasted_iota(jnp.int32, rows.shape, 0)
            lane = lax.broadcasted_iota(jnp.int32, rows.shape, 1)
            return jnp.where(lax.div(row, RANK) == lax.div(lane, 2 * RANK), rows, 0.0)

        three = blocks(2, 8)
        four = fine_dot(blocks(3, 2), three)
        five = fine_dot(blocks(4, 1), jnp.concatenate([four, jnp.zeros((96, 128), F32)], 0))
        whole = jnp.concatenate([four, three[32:64], five, three[:32]], 0)
        high, low = halves(whole)
        lift_m[...] = jnp.concatenate([high, low], 1)
        six = place_dot(lift_v[5, 0], selector(128, 32, 0, 64)) + place_dot(
            lift_v[5, 1], selector(128, 32, 16, 64)
        )
        high = six.astype(BF16).astype(F32)
        lane = lax.broadcasted_iota(jnp.int32, six.shape, 1)
        six_m[...] = jnp.where(lane < 32, high, six - high).astype(BF16)

    def tables_far():
        copies["spread"].wait()
        copies["down"].wait()
        row = lax.broadcasted_iota(jnp.int32, (RANK, LEAF), 0)
        lane = lax.broadcasted_iota(jnp.int32, (RANK, LEAF), 1)
        summing = (lax.div(lane, RANK) == row).astype(F32)
        chain = None
        for k in range(5):
            if k > 0:
                step = spread_v[1 + k, lax.rem(lax.div(t, 2 ** (k - 1)), 2)]
                chain = step if k == 1 else fine_dot(chain, step)
            high, low = halves(summing if k == 0 else place_dot(chain, summing))
            red_m[k] = jnp.concatenate([high, low], 0)
        turned = down_v[...].T
        for leaf in range(LEAVES):
            near_step = spread_v[0, leaf % 2]
            both_steps = fine_dot(near_step, spread_v[1, leaf // 2])
            mix = (
                selector(LEAF, 48, 0, 144)
                + place_dot(near_step, selector(LEAF, 48, 16, 144))
                + place_dot(both_steps, selector(LEAF, 48, 32, 144))
            )
            whole = fine_dot(turned, mix)
            high = whole.astype(BF16).astype(F32)
            lane_at = lax.broadcasted_iota(jnp.int32, whole.shape, 1)
            far_m[leaf] = jnp.where(lane_at < 96, high, whole - high).astype(BF16)

    def scaled_rows(first, slots):
        rows = pair_rows(first)
        squares = jnp.zeros((2 * LEAF, WIDTH), F32)
        columns = []
        for slot in slots:
            tokens = g[slot, rows, :].astype(F32)
            squares = squares + tokens * tokens
            scale = gain_v[:, pl.ds(pl.multiple_of(owners[slot] * WIDTH, WIDTH), WIDTH)]
            columns.append((tokens * scale).astype(BF16))
        return jnp.concatenate(columns, 1), squares

    def gather_pair(first):
        scaled, squares = scaled_rows(first, (0, 1, 2))
        parts[pair_rows(first), :] = dot(scaled, w[:3].reshape(3 * WIDTH, 2 * WIDTH))
        part_squares[pair_rows(first), :] = squares[:, : WIDTH // 2] + squares[:, WIDTH // 2 :]

    def values_of(first):
        rows = pair_rows(first)
        scaled, squares = scaled_rows(first, (3,))
        squares = squares[:, : WIDTH // 2] + squares[:, WIDTH // 2 :] + part_squares[rows, :]
        inverse = lax.rsqrt(jnp.sum(squares, axis=1, keepdims=True) / 1024 + 1e-06)
        part_squares[rows, :] = jnp.broadcast_to(inverse, squares.shape)
        value = ((parts[rows, :WIDTH] + dot(scaled, w[3, :, :WIDTH])) * inverse).astype(BF16)
        vals[rows, :] = value
        for k in range(2):
            leaf_value = value[k * LEAF : (k + 1) * LEAF]
            moms[first + k] = dot(mom_m[first + k], jnp.concatenate([leaf_value, leaf_value], 0))

    def gates_of(first):
        rows = pair_rows(first)
        scaled, _ = scaled_rows(first, (3,))
        half = 0.5 * part_squares[rows, :]
        sums = parts[rows, WIDTH:] + dot(scaled, w[3, :, WIDTH:])
        gate[rows, :] = (0.5 * jnp.tanh(sums * jnp.concatenate([half, half], 1)) + 0.5).astype(BF16)

    def spectra(first):
        both = jnp.concatenate([vals[leaf_rows(first), :], vals[leaf_rows(first + 1), :]], 1)
        result = dot(fwd_v[...], jnp.concatenate([both, both], 0))
        spec[first] = result[:, :WIDTH]
        spec[first + 1] = result[:, WIDTH:]

    def near_rows(leaves):
        columns = []
        for leaf in leaves:
            before = leaf - 1 if leaf > 0 else LEAVES
            a_re, a_im = spec[leaf, :LEAF, :], spec[leaf, LEAF:, :]
            b_re, b_im = spec[before, :LEAF, :], spec[before, LEAF:, :]
            out_re = khat[0] * a_re - khat[1] * a_im + khat[2] * b_re - khat[3] * b_im
            out_im = khat[0] * a_im + khat[1] * a_re + khat[2] * b_im + khat[3] * b_re
            columns.append(jnp.concatenate([out_re, out_im], 0).astype(BF16))
        total = dot(inv_v[...], jnp.concatenate(columns, 1))
        for k, leaf in enumerate(leaves):
            rows = leaf_rows(leaf)
            direct_term = skip_v[...] * vals[rows, :].astype(F32)
            near[rows, :] = (total[:, k * WIDTH : (k + 1) * WIDTH] + direct_term).astype(BF16)

    def coupled(level, source_two, source_three):
        product = coup_v[level, 0] * source_two[None]
        if source_three is not None:
            product = product + coup_v[level, 1] * source_three[None]
        return product.reshape(RANK * RANK, WIDTH).astype(BF16)

    send_direct(0)

    copies = {}

    def local(name, source, target):
        copies[name] = pltpu.make_async_copy(source, target, local_sem.at[len(copies)])
        copies[name].start()

    local("tok", tok, g.at[0])
    for slot in range(4):
        rows = pl.ds(pl.multiple_of(owners[slot] * WIDTH, WIDTH), WIDTH)
        local(("v", slot), w_value.at[rows], w.at[slot, :, pl.ds(0, WIDTH)])
        local(("g", slot), w_gate.at[rows], w.at[slot, :, pl.ds(WIDTH, WIDTH)])
    for name, source, target in (
        ("gain", gain, gain_v),
        ("phi", phi, phi_v),
        ("coeff", coeff, coeff_v),
        ("fwd", fwd, fwd_f),
        ("skip", skip, skip_v),
        ("up", up, up_v),
        ("down", down, down_v),
        ("lift", lift, lift_v),
        ("spread", spread, spread_v),
        ("inv", inv, inv_f),
        ("coup", coup, coup_v),
    ):
        local(name, source, target)

    @pl.when(z > 0)
    def _():
        signal(ready_next, t - PLANE, x)

    for k in range(1, PLANE):

        @pl.when(own >= k)
        def _():
            signal(ready_plane, t - k, x)

    def chain(place):
        @pl.when(z == PLANES - 1 - place)
        def _():
            if not isinstance(place, int) or place > 0:
                pl.semaphore_wait(ready_later, 1)
            if not isinstance(place, int) or place < PLANES - 1:
                signal(ready_later, t - PLANE, x)

    chain(0)
    tables_near()
    send_direct(1)
    chain(1)
    tables_moments()
    chain(2)
    tables_lift()
    chain(3)
    for slot in range(4):
        copies["v", slot].wait()
        copies["g", slot].wait()
    for name in ("tok", "gain", "skip", "coup", "inv"):
        copies[name].wait()
    pass_on(0)
    chain(4)

    @pl.when(own < PLANE - 1)
    def _():
        pl.semaphore_wait(ready_plane, PLANE - 1 - own)

    @pl.when(z < PLANES - 1)
    def _():
        pl.semaphore_wait(ready_next, 1)

        @pl.when(y == 0)
        def _():
            signal(ready_edge, z * PLANE + 6, x)
            signal(ready_edge, z * PLANE + 7, x)

    gather_pair(2)
    chain(5)
    tables_far()
    handed(0).start()
    inv_v[...] = inv_f[...].astype(BF16)
    chain(6)
    pass_on(1)
    gather_pair(0)

    @pl.when((y == 3) & (z < PLANES - 1))
    def _():
        pl.semaphore_wait(ready_edge, 2)

    halo_copy = pltpu.make_async_remote_copy(
        src_ref=vals.at[pl.ds(3 * LEAF, LEAF)],
        dst_ref=halo,
        send_sem=hsem.at[0],
        recv_sem=hsem.at[1],
        device_id=(t + 1, x),
        device_id_type=MESH,
    )

    def ctx_copy(part):
        rows = pl.ds(0, 48) if part == 0 else pl.ds(48, 16)
        return pltpu.make_async_remote_copy(
            src_ref=ctx_out.at[rows],
            dst_ref=ctx_in.at[rows],
            send_sem=csem.at[0, part],
            recv_sem=csem.at[1, part],
            device_id=(t + 1, x),
            device_id_type=MESH,
        )

    summing = red_m[0, :RANK, :]

    def gathered(level, source_two, source_three=None):
        return dot(summing, coupled(level, source_two, source_three))

    wait_relayed(0)
    values_of(2)
    ctx_out[:48] = jnp.concatenate(
        [moms[2, 0:16, :], moms[3, 0:16, :], moms[2, 16:32, :] + moms[3, 16:32, :]], 0
    ).astype(BF16)

    @pl.when(t < PLANES * PLANE - 1)
    def _():
        halo_copy.start()
        ctx_copy(0).start()

    spectra(2)
    gates_of(2)
    handed(1).start()
    near_rows((3,))
    handed(3).start()

    wait_relayed(1)
    values_of(0)

    total = moms[0, 32:48, :] + moms[1, 32:48, :] + moms[2, 32:48, :] + moms[3, 32:48, :]
    m2[own] = total.astype(BF16)

    def plane_copy(k):
        return pltpu.make_async_remote_copy(
            src_ref=m2.at[own],
            dst_ref=m2.at[own],
            send_sem=s1,
            recv_sem=r1,
            device_id=(z * PLANE + lax.rem(own + k, PLANE), x),
            device_id_type=MESH,
        )

    plane_all = pltpu.make_async_remote_copy(
        src_ref=m2.at[pl.ds(0, PLANE - 1)],
        dst_ref=m2.at[pl.ds(0, PLANE - 1)],
        send_sem=s1,
        recv_sem=r1,
        device_id=(t, right),
        device_id_type=MESH,
    )

    for k in range(1, PLANE):
        plane_copy(k).start()

    def next_plane_copy(target, source):
        return pltpu.make_async_remote_copy(
            src_ref=m2.at[own],
            dst_ref=m2_prev.at[source],
            send_sem=s1p.at[target],
            recv_sem=r1p.at[source],
            device_id=((z + 1) * PLANE + target, x),
            device_id_type=MESH,
        )

    @pl.when((y == 3) & (z < PLANES - 1))
    def _():
        for target in range(2):
            next_plane_copy(target, core).start()

    ctx_out[48:] = (moms[0, 16:32, :] + moms[1, 16:32, :]).astype(BF16)

    @pl.when(t < PLANES * PLANE - 1)
    def _():
        ctx_copy(1).start()

    gates_of(0)
    handed(2).start()

    plane_all.wait_recv()
    stack = m2[...].reshape(PLANE * RANK, WIDTH)
    lifted = dot(lift_m[...], jnp.concatenate([stack, stack], 0))
    pack_out[...] = lifted[:80].astype(BF16)


    def pack_copy(rows):
        return pltpu.make_async_remote_copy(
            src_ref=pack_out.at[pl.ds(0, rows)],
            dst_ref=pack_in.at[pl.ds(0, rows)],
            send_sem=s2,
            recv_sem=r2,
            device_id=(t + PLANE, x),
            device_id_type=MESH,
        )

    def five_copy(k):
        return pltpu.make_async_remote_copy(
            src_ref=pack_out.at[pl.ds(64, RANK)],
            dst_ref=m5_in.at[k],
            send_sem=s5.at[k],
            recv_sem=r5.at[k],
            device_id=(t + k * PLANE, x),
            device_id_type=MESH,
        )

    chain(7)

    for k in range(PLANES - 1, 1, -1):

        @pl.when(z + k < PLANES)
        def _():
            five_copy(k).start()

    @pl.when((z < PLANES - 1) & (y < 2))
    def _():
        pack_copy(64).start()

    @pl.when((z < PLANES - 1) & (y >= 2))
    def _():
        pack_copy(32).start()

    spectra(0)

    @pl.when(t > 0)
    def _():
        halo_copy.wait_recv()

    spec[LEAVES] = dot(fwd_v[...], jnp.concatenate([halo[...], halo[...]], 0))
    near_rows((0, 1, 2))
    handed(4).start()

    @pl.when(t > 0)
    def _():
        ctx_copy(0).wait_recv()
        ctx_copy(1).wait_recv()

    prev = ctx_in[...].astype(F32)
    expansions[0] = gathered(0, prev[0:16])
    expansions[1] = gathered(0, prev[16:32], prev[0:16])
    expansions[2] = gathered(0, moms[0, 0:16, :])
    expansions[3] = gathered(0, moms[1, 0:16, :], moms[0, 0:16, :])
    expansions[4] = gathered(1, prev[48:64])
    expansions[5] = gathered(1, prev[32:48], prev[48:64])
    handed(5).start()

    gather_sent = g.at[pl.ds(0, 3)]
    pltpu.make_async_remote_copy(
        src_ref=gather_sent,
        dst_ref=gather_sent,
        send_sem=gsend,
        recv_sem=drecv.at[0, 0],
        device_id=(t, right),
        device_id_type=MESH,
    ).wait_send()

    plane_all.wait_send()

    @pl.when(t < PLANES * PLANE - 1)
    def _():
        halo_copy.wait_send()
        ctx_copy(0).wait_send()
        ctx_copy(1).wait_send()

    @pl.when((y == 3) & (z < PLANES - 1))
    def _():
        for target in range(2):
            next_plane_copy(target, core).wait_send()

    @pl.when((y == 0) & (z > 0))
    def _():
        for source in range(2):
            next_plane_copy(source, source).wait_recv()

    def reduced(k, source_two, source_three):
        return dot(red_m[k], coupled(2 + k, source_two, source_three))

    at = 2 * jnp.maximum(y - 1, 0)
    inside = y > 0
    two = jnp.where(inside, m2[at + core], m2_prev[core]).astype(F32)
    three = jnp.where(inside, m2[at], m2_prev[0]).astype(F32) * core.astype(F32)
    expansion = reduced(0, two, three)

    @pl.when((z > 0) & (y < 2))
    def _():
        pack_copy(64).wait_recv()

    @pl.when((z > 0) & (y >= 2))
    def _():
        pack_copy(32).wait_recv()

    odd = lax.rem(y, 2)
    lower = y < 2
    here = jnp.where(odd == 1, lifted[96:112], lifted[80:96])
    coming = pack_in[pl.ds(pl.multiple_of(32 + odd * RANK, RANK), RANK), :].astype(F32)
    two = jnp.where(lower, coming, here)
    three = jnp.where(lower, pack_in[32:48, :].astype(F32), lifted[80:96]) * odd.astype(F32)
    expansion = expansion + reduced(1, two, three)
    odd = lax.div(y, 2)
    two = pack_in[pl.ds(pl.multiple_of(odd * RANK, RANK), RANK), :].astype(F32)
    three = pack_in[0:16, :].astype(F32) * odd.astype(F32)
    expansion = expansion + reduced(2, two, three)

    for k in range(2, PLANES):

        @pl.when(z >= k)
        def _():
            five_copy(k).wait_recv()

    odd = lax.rem(z, 2)
    expansion = expansion + reduced(
        3, m5_in[2].astype(F32), m5_in[3].astype(F32) * odd.astype(F32)
    )
    pad = jnp.zeros((64, WIDTH), BF16)

    def sixth(base):
        pair = [m5_in[base], m5_in[base - 1]]
        return dot(six_m[...], jnp.concatenate(pair + pair + [pad], 0))

    odd_six = lax.rem(lax.div(z, 2), 2)
    expansion = expansion + reduced(
        4, sixth(4 + odd), sixth(6 + odd) * odd_six.astype(F32)
    )

    expansions[6] = expansion[:RANK] + expansion[RANK:]
    handed(6).start()

    @pl.when((z < PLANES - 1) & (y < 2))
    def _():
        pack_copy(64).wait_send()

    @pl.when((z < PLANES - 1) & (y >= 2))
    def _():
        pack_copy(32).wait_send()

    for k in range(2, PLANES):

        @pl.when(z + k < PLANES)
        def _():
            five_copy(k).wait_send()

    for part in range(7):
        handed(part).wait()


def finish(gate, near, far, expansions, out, gate_v, near_v, far_v, expansions_v, out_v, sems):
    def rows_of(leaf):
        return pl.ds(leaf * LEAF, LEAF)

    incoming = [
        pltpu.make_async_copy(expansions, expansions_v, sems.at[0]),
        pltpu.make_async_copy(far, far_v, sems.at[1]),
    ]
    for leaf in range(LEAVES):
        rows = rows_of(leaf)
        incoming.append(pltpu.make_async_copy(near.at[rows], near_v.at[rows], sems.at[2 + 2 * leaf]))
        incoming.append(pltpu.make_async_copy(gate.at[rows], gate_v.at[rows], sems.at[3 + 2 * leaf]))
    for copy in incoming:
        copy.start()
    incoming[0].wait()
    incoming[1].wait()
    outgoing = []
    for leaf in range(LEAVES):
        rows = rows_of(leaf)
        stack = jnp.concatenate([expansions_v[leaf], expansions_v[4 + leaf // 2], expansions_v[6]], 0)
        high, low = halves(stack)
        whole = jnp.concatenate([high, low, high, jnp.zeros((112, WIDTH), BF16)], 0)
        far_rows = dot(far_v[leaf], whole)
        incoming[2 + 2 * leaf].wait()
        incoming[3 + 2 * leaf].wait()
        combined = near_v[rows, :].astype(F32) + far_rows
        out_v[rows, :] = (gate_v[rows, :].astype(F32) * combined).astype(BF16)
        outgoing.append(pltpu.make_async_copy(out_v.at[rows], out.at[rows], sems.at[10 + leaf]))
        outgoing[leaf].start()
    for copy in outgoing:
        copy.wait()


def per_device(
    tokens,
    norm_gain,
    w_value,
    w_gate,
    phi_taps,
    tap_coeff,
    skip_gain,
    basis_up,
    basis_down,
    lift_maps,
    spread_maps,
    couplings,
):
    forward, inverse = transform_tables()
    in_hbm = pl.BlockSpec(memory_space=pltpu.HBM)
    frames = LEAF * LEAVES
    vmem = pltpu.VMEM
    dma = pltpu.SemaphoreType.DMA
    scratch = [
        vmem((4, frames, WIDTH), BF16),
        vmem((4, WIDTH, 2 * WIDTH), BF16),
        vmem((1, 4 * WIDTH), F32),
        vmem(phi_taps.shape, F32),
        vmem(tap_coeff.shape, F32),
        vmem((1, WIDTH), F32),
        vmem(basis_up.shape, F32),
        vmem(basis_down.shape, F32),
        vmem(lift_maps.shape, F32),
        vmem(spread_maps.shape, F32),
        vmem(couplings.shape, F32),
        vmem(forward.shape, F32),
        vmem(inverse.shape, F32),
        vmem((2 * LEAF, 2 * LEAF), BF16),
        vmem((LEAF, 2 * LEAF), BF16),
        vmem((frames, WIDTH), BF16),
        vmem((LEAF, WIDTH), BF16),
        vmem((frames, WIDTH), BF16),
        vmem((frames, WIDTH), BF16),
        vmem((LEAVES + 1, 2 * LEAF, WIDTH), F32),
        vmem((4, LEAF, WIDTH), F32),
        vmem((LEAVES, 48, 2 * LEAF), BF16),
        vmem((112, 256), BF16),
        vmem((RANK, 128), BF16),
        vmem((LEAVES, LEAF, LEAF), BF16),
        vmem((5, 2 * RANK, LEAF), BF16),
        vmem((LEAVES, 48, WIDTH), F32),
        vmem((PLANE, RANK, WIDTH), BF16),
        vmem((2, RANK, WIDTH), BF16),
        vmem((64, WIDTH), BF16),
        vmem((64, WIDTH), BF16),
        vmem((80, WIDTH), BF16),
        vmem((64, WIDTH), BF16),
        vmem((PLANES, RANK, WIDTH), BF16),
        vmem((7, RANK, WIDTH), F32),
        vmem((frames, 2 * WIDTH), F32),
        vmem((frames, WIDTH // 2), F32),
        dma((20,)),
        dma(()),
        dma((2, 2)),
        dma((2, 2)),
        dma((2,)),
        dma((2, 2)),
        dma(()),
        dma(()),
        dma((2,)),
        dma((2,)),
        dma(()),
        dma(()),
        dma((PLANES,)),
        dma((PLANES,)),
        pltpu.SemaphoreType.REGULAR,
        pltpu.SemaphoreType.REGULAR,
        pltpu.SemaphoreType.REGULAR,
        pltpu.SemaphoreType.REGULAR,
        dma((7,)),
    ]
    handed = [
        jax.ShapeDtypeStruct((frames, WIDTH), BF16),
        jax.ShapeDtypeStruct((frames, WIDTH), BF16),
        jax.ShapeDtypeStruct((LEAVES, LEAF, LEAF), BF16),
        jax.ShapeDtypeStruct((7, RANK, WIDTH), F32),
    ]
    results = pl.pallas_call(
        body,
        out_shape=handed,
        in_specs=[in_hbm] * 14,
        out_specs=[in_hbm] * 4,
        scratch_shapes=scratch,
        compiler_params=pltpu.CompilerParams(
            collective_id=0, has_side_effects=True, vmem_limit_bytes=60 * 1024 * 1024
        ),
        cost_estimate=pl.CostEstimate(flops=4 * 10**9, bytes_accessed=8 * 10**6, transcendentals=10**6),
    )(
        tokens,
        norm_gain.reshape(1, -1),
        w_value,
        w_gate,
        phi_taps,
        tap_coeff,
        skip_gain.reshape(1, -1),
        basis_up,
        basis_down,
        lift_maps,
        spread_maps,
        couplings,
        jnp.asarray(forward),
        jnp.asarray(inverse),
    )
    return pl.pallas_call(
        finish,
        out_shape=jax.ShapeDtypeStruct(tokens.shape, BF16),
        in_specs=[in_hbm] * 4,
        out_specs=in_hbm,
        scratch_shapes=[vmem(item.shape, item.dtype) for item in handed]
        + [vmem((frames, WIDTH), BF16), dma((10 + LEAVES,))],
        compiler_params=pltpu.CompilerParams(vmem_limit_bytes=60 * 1024 * 1024),
        cost_estimate=pl.CostEstimate(flops=2 * 10**8, bytes_accessed=2 * 10**6, transcendentals=0),
    )(*results)


def solution(mesh):
    placed = (
        P("tm", "chan"),
        P(),
        P(None, "chan"),
        P(None, "chan"),
        P(),
        P(None, "chan"),
        P("chan"),
        P(),
        P(),
        P(),
        P(),
        P(None, None, None, None, "chan"),
    )
    return jax.shard_map(
        per_device, mesh=mesh, in_specs=placed, out_specs=P("tm", "chan"), check_vma=False
    )
```

```python
import jax
import jax.numpy as jnp
import numpy as np
from jax import lax
from jax.experimental import pallas as pl
from jax.experimental.pallas import tpu as pltpu
from jax.sharding import PartitionSpec as P

MESH = pl.DeviceIdType.MESH
F32 = jnp.float32
BF16 = jnp.bfloat16

LEAF = 256
LEAVES = 4
WIDTH = 256
RANK = 16
PLANES = 8
PLANE = 8


def transform_tables():
    odd = np.arange(LEAF)[:, None] + 0.5
    angle = 2 * np.pi * odd * np.arange(LEAF)[None, :] / (2 * LEAF)
    forward = np.concatenate([np.cos(angle), -np.sin(angle)], 0)
    return forward.astype(np.float32), (forward.T / LEAF).astype(np.float32)


def dot(left, right):
    return jnp.dot(left, right, preferred_element_type=F32)


def halves(value):
    high = value.astype(BF16)
    return high, (value - high.astype(F32)).astype(BF16)


def fine_dot(left, right):
    left_high, left_low = halves(left)
    right_high, right_low = halves(right)
    return dot(left_high, right_high) + dot(left_high, right_low) + dot(left_low, right_high)


def place_dot(left, right):
    left_high, left_low = halves(left)
    ones = right.astype(BF16)
    return dot(left_high, ones) + dot(left_low, ones)


def selector(lanes, period, shift, limit):
    row = lax.broadcasted_iota(jnp.int32, (RANK, lanes), 0)
    lane = lax.broadcasted_iota(jnp.int32, (RANK, lanes), 1)
    return ((lax.rem(lane, period) == row + shift) & (lane < limit)).astype(F32)


def body(
    tok, gain, w_value, w_gate, phi, coeff, skip, up, down, lift, spread, coup, fwd, inv,
    out,
    g, w, gain_v, phi_v, coeff_v, skip_v, up_v, down_v, lift_v, spread_v, coup_v, fwd_f, inv_f, fwd_v, inv_v,
    vals, halo, gate, near, spec, khat, mom_m, lift_m, six_m, far_m, red_m, moms,
    m2, m2_prev, ctx_out, ctx_in, pack_out, pack_in, m5_in, far0, far1, out_v, parts, part_squares,
    local_sem, gsend, drecv, rrecv, hsem, csem, s1, r1, s1p, r1p, s2, r2, s5, r5, ready_plane, ready_next, ready_edge, ready_later, osem,
):
    t = lax.axis_index("tm")
    x = lax.axis_index("chan")
    core = lax.rem(t, 2)
    y = lax.rem(lax.div(t, 2), 4)
    z = lax.div(t, PLANE)
    own = lax.rem(t, PLANE)
    rank = 2 * y + 1 - core
    right, left = lax.rem(x + 1, 4), lax.rem(x + 3, 4)

    barrier = pltpu.get_barrier_semaphore()

    def signal(semaphore, frames, chans):
        pl.semaphore_signal(semaphore, inc=1, device_id=(frames, chans), device_id_type=MESH)

    signal(barrier, t, right)
    signal(barrier, t, left)

    @pl.when(z < PLANES - 1)
    def _():
        signal(barrier, t + PLANE, x)

    m2_prev[...] = jnp.zeros_like(m2_prev)
    ctx_in[...] = jnp.zeros_like(ctx_in)
    pack_in[...] = jnp.zeros_like(pack_in)
    m5_in[...] = jnp.zeros_like(m5_in)
    halo[...] = jnp.zeros_like(halo)

    def at_rank(other):
        return z * PLANE + 2 * lax.div(other, 2) + 1 - lax.rem(other, 2)

    for k in range(1, PLANE):

        @pl.when(rank + k < PLANE)
        def _():
            signal(barrier, at_rank(rank + k), x)

    pl.semaphore_wait(barrier, 2 + rank + jnp.where(z > 0, 1, 0))

    owners = [x, left, right, lax.rem(x + 2, 4)]

    def leaf_rows(leaf):
        return pl.ds(leaf * LEAF if isinstance(leaf, int) else pl.multiple_of(leaf * LEAF, LEAF), LEAF)

    def direct(group, way):
        rows = pl.ds((1 - group) * 2 * LEAF, 2 * LEAF)
        return pltpu.make_async_remote_copy(
            src_ref=tok.at[rows],
            dst_ref=g.at[1 + way, rows],
            send_sem=gsend,
            recv_sem=drecv.at[way, group],
            device_id=(t, left if way else right),
            device_id_type=MESH,
        )

    def relay(group, way):
        rows = leaf_rows((1 - group) * 2 + way)
        return pltpu.make_async_remote_copy(
            src_ref=g.at[1 + way, rows],
            dst_ref=g.at[3, rows],
            send_sem=gsend,
            recv_sem=rrecv.at[way, group],
            device_id=(t, left if way else right),
            device_id_type=MESH,
        )

    def send_direct(group):
        for way in range(2):
            direct(group, way).start()

    def pass_on(group):
        for way in range(2):
            direct(group, way).wait_recv()
            relay(group, way).start()

    def wait_relayed(group):
        for way in range(2):
            relay(group, way).wait_recv()

    def tables_near():
        for name in ("phi", "coeff", "fwd"):
            copies[name].wait()
        fwd_v[...] = jnp.concatenate(halves(fwd_f[...]), 1)
        taps = phi_v[...].astype(BF16).astype(F32).T.astype(BF16)
        coeff_high, coeff_low = halves(coeff_v[...])
        kernel_taps = dot(taps, coeff_high) + dot(taps, coeff_low)
        both = jnp.concatenate([kernel_taps[:LEAF], kernel_taps[LEAF:]], 1)
        high, low = halves(both)
        hat = dot(fwd_v[...], jnp.concatenate([high, high], 0)) + dot(fwd_v[:, :LEAF], low)
        a_re, a_im = hat[:LEAF, :WIDTH], hat[LEAF:, :WIDTH]
        b_re, b_im = hat[:LEAF, WIDTH:], hat[LEAF:, WIDTH:]
        row = lax.broadcasted_iota(jnp.int32, (LEAF, WIDTH), 0)
        sign = (1 - 2 * lax.rem(row, 2)).astype(F32)
        khat[0] = a_re
        khat[1] = a_im
        khat[2] = b_re - sign * a_im
        khat[3] = b_im + sign * a_re

    def tables_moments():
        copies["up"].wait()
        copies["lift"].wait()
        base = up_v[...]
        first = [fine_dot(lift_v[0, k], base) for k in range(2)]
        for leaf in range(LEAVES):
            second = fine_dot(lift_v[1, leaf // 2], first[leaf % 2])
            high, low = halves(jnp.concatenate([base, first[leaf % 2], second], 0))
            mom_m[leaf] = jnp.concatenate([high, low], 1)

    def tables_lift():
        def pair(level):
            return place_dot(lift_v[level, 0], selector(128, 32, 0, 128)) + place_dot(
                lift_v[level, 1], selector(128, 32, 16, 128)
            )

        def blocks(level, copies_of):
            rows = jnp.concatenate([pair(level)] * copies_of, 0)
            row = lax.broadcasted_iota(jnp.int32, rows.shape, 0)
            lane = lax.broadcasted_iota(jnp.int32, rows.shape, 1)
            return jnp.where(lax.div(row, RANK) == lax.div(lane, 2 * RANK), rows, 0.0)

        three = blocks(2, 8)
        four = fine_dot(blocks(3, 2), three)
        five = fine_dot(blocks(4, 1), jnp.concatenate([four, jnp.zeros((96, 128), F32)], 0))
        whole = jnp.concatenate([four, three[32:64], five, three[:32]], 0)
        high, low = halves(whole)
        lift_m[...] = jnp.concatenate([high, low], 1)
        six = place_dot(lift_v[5, 0], selector(128, 32, 0, 64)) + place_dot(
            lift_v[5, 1], selector(128, 32, 16, 64)
        )
        high = six.astype(BF16).astype(F32)
        lane = lax.broadcasted_iota(jnp.int32, six.shape, 1)
        six_m[...] = jnp.where(lane < 32, high, six - high).astype(BF16)

    def tables_far():
        copies["spread"].wait()
        copies["down"].wait()
        row = lax.broadcasted_iota(jnp.int32, (RANK, LEAF), 0)
        lane = lax.broadcasted_iota(jnp.int32, (RANK, LEAF), 1)
        summing = (lax.div(lane, RANK) == row).astype(F32)
        chain = None
        for k in range(5):
            if k > 0:
                step = spread_v[1 + k, lax.rem(lax.div(t, 2 ** (k - 1)), 2)]
                chain = step if k == 1 else fine_dot(chain, step)
            high, low = halves(summing if k == 0 else place_dot(chain, summing))
            red_m[k] = jnp.concatenate([high, low], 0)
        turned = down_v[...].T
        for leaf in range(LEAVES):
            near_step = spread_v[0, leaf % 2]
            both_steps = fine_dot(near_step, spread_v[1, leaf // 2])
            mix = (
                selector(LEAF, 48, 0, 144)
                + place_dot(near_step, selector(LEAF, 48, 16, 144))
                + place_dot(both_steps, selector(LEAF, 48, 32, 144))
            )
            whole = fine_dot(turned, mix)
            high = whole.astype(BF16).astype(F32)
            lane_at = lax.broadcasted_iota(jnp.int32, whole.shape, 1)
            far_m[leaf] = jnp.where(lane_at < 96, high, whole - high).astype(BF16)

    def pair_rows(first):
        return pl.ds(first * LEAF, 2 * LEAF)

    def scaled_rows(first, slots):
        rows = pair_rows(first)
        squares = jnp.zeros((2 * LEAF, WIDTH), F32)
        columns = []
        for slot in slots:
            tokens = g[slot, rows, :].astype(F32)
            squares = squares + tokens * tokens
            scale = gain_v[:, pl.ds(pl.multiple_of(owners[slot] * WIDTH, WIDTH), WIDTH)]
            columns.append((tokens * scale).astype(BF16))
        return jnp.concatenate(columns, 1), squares

    def gather_pair(first):
        scaled, squares = scaled_rows(first, (0, 1, 2))
        parts[pair_rows(first), :] = dot(scaled, w[:3].reshape(3 * WIDTH, 2 * WIDTH))
        part_squares[pair_rows(first), :] = squares[:, : WIDTH // 2] + squares[:, WIDTH // 2 :]

    def values_of(first):
        rows = pair_rows(first)
        scaled, squares = scaled_rows(first, (3,))
        squares = squares[:, : WIDTH // 2] + squares[:, WIDTH // 2 :] + part_squares[rows, :]
        inverse = lax.rsqrt(jnp.sum(squares, axis=1, keepdims=True) / 1024 + 1e-06)
        part_squares[rows, :] = jnp.broadcast_to(inverse, squares.shape)
        value = ((parts[rows, :WIDTH] + dot(scaled, w[3, :, :WIDTH])) * inverse).astype(BF16)
        vals[rows, :] = value
        for k in range(2):
            leaf_value = value[k * LEAF : (k + 1) * LEAF]
            moms[first + k] = dot(mom_m[first + k], jnp.concatenate([leaf_value, leaf_value], 0))

    def gates_of(first):
        rows = pair_rows(first)
        scaled, _ = scaled_rows(first, (3,))
        half = 0.5 * part_squares[rows, :]
        sums = parts[rows, WIDTH:] + dot(scaled, w[3, :, WIDTH:])
        gate[rows, :] = 0.5 * jnp.tanh(sums * jnp.concatenate([half, half], 1)) + 0.5

    def spectra(first):
        both = jnp.concatenate([vals[leaf_rows(first), :], vals[leaf_rows(first + 1), :]], 1)
        result = dot(fwd_v[...], jnp.concatenate([both, both], 0))
        spec[first] = result[:, :WIDTH]
        spec[first + 1] = result[:, WIDTH:]

    def near_rows(leaves):
        columns = []
        for leaf in leaves:
            before = leaf - 1 if leaf > 0 else LEAVES
            a_re, a_im = spec[leaf, :LEAF, :], spec[leaf, LEAF:, :]
            b_re, b_im = spec[before, :LEAF, :], spec[before, LEAF:, :]
            out_re = khat[0] * a_re - khat[1] * a_im + khat[2] * b_re - khat[3] * b_im
            out_im = khat[0] * a_im + khat[1] * a_re + khat[2] * b_im + khat[3] * b_re
            columns.append(jnp.concatenate([out_re, out_im], 0).astype(BF16))
        total = dot(inv_v[...], jnp.concatenate(columns, 1))
        for k, leaf in enumerate(leaves):
            rows = leaf_rows(leaf)
            direct_term = skip_v[...] * vals[rows, :].astype(F32)
            near[rows, :] = total[:, k * WIDTH : (k + 1) * WIDTH] + direct_term

    def coupled(level, source_two, source_three):
        product = coup_v[level, 0] * source_two[None]
        if source_three is not None:
            product = product + coup_v[level, 1] * source_three[None]
        return product.reshape(RANK * RANK, WIDTH).astype(BF16)

    send_direct(0)

    copies = {}

    def local(name, source, target):
        copies[name] = pltpu.make_async_copy(source, target, local_sem.at[len(copies)])
        copies[name].start()

    local("tok", tok, g.at[0])
    for slot in range(4):
        rows = pl.ds(pl.multiple_of(owners[slot] * WIDTH, WIDTH), WIDTH)
        local(("v", slot), w_value.at[rows], w.at[slot, :, pl.ds(0, WIDTH)])
        local(("g", slot), w_gate.at[rows], w.at[slot, :, pl.ds(WIDTH, WIDTH)])
    for name, source, target in (
        ("gain", gain, gain_v),
        ("phi", phi, phi_v),
        ("coeff", coeff, coeff_v),
        ("fwd", fwd, fwd_f),
        ("skip", skip, skip_v),
        ("up", up, up_v),
        ("down", down, down_v),
        ("lift", lift, lift_v),
        ("spread", spread, spread_v),
        ("inv", inv, inv_f),
        ("coup", coup, coup_v),
    ):
        local(name, source, target)

    @pl.when(z > 0)
    def _():
        signal(ready_next, t - PLANE, x)

    for k in range(1, PLANE):

        @pl.when(rank >= k)
        def _():
            signal(ready_plane, at_rank(rank - k), x)

    def chain(place):
        @pl.when(z == PLANES - 1 - place)
        def _():
            if not isinstance(place, int) or place > 0:
                pl.semaphore_wait(ready_later, 1)
            if not isinstance(place, int) or place < PLANES - 1:
                signal(ready_later, t - PLANE, x)

    chain(0)
    tables_near()
    send_direct(1)
    chain(1)
    tables_moments()
    chain(2)
    tables_lift()
    chain(3)
    for slot in range(4):
        copies["v", slot].wait()
        copies["g", slot].wait()
    for name in ("tok", "gain", "skip", "coup", "inv"):
        copies[name].wait()
    pass_on(0)
    chain(4)

    @pl.when(rank < PLANE - 1)
    def _():
        pl.semaphore_wait(ready_plane, PLANE - 1 - rank)

    @pl.when(z < PLANES - 1)
    def _():
        pl.semaphore_wait(ready_next, 1)

        @pl.when(y == 0)
        def _():
            signal(ready_edge, z * PLANE + 6, x)
            signal(ready_edge, z * PLANE + 7, x)

    gather_pair(2)
    chain(5)
    tables_far()
    inv_v[...] = inv_f[...].astype(BF16)
    chain(6)
    pass_on(1)
    gather_pair(0)

    @pl.when((y == 3) & (z < PLANES - 1))
    def _():
        pl.semaphore_wait(ready_edge, 2)

    halo_copy = pltpu.make_async_remote_copy(
        src_ref=vals.at[pl.ds(3 * LEAF, LEAF)],
        dst_ref=halo,
        send_sem=hsem.at[0],
        recv_sem=hsem.at[1],
        device_id=(t + 1, x),
        device_id_type=MESH,
    )

    def ctx_copy(part):
        rows = pl.ds(0, 48) if part == 0 else pl.ds(48, 16)
        return pltpu.make_async_remote_copy(
            src_ref=ctx_out.at[rows],
            dst_ref=ctx_in.at[rows],
            send_sem=csem.at[0, part],
            recv_sem=csem.at[1, part],
            device_id=(t + 1, x),
            device_id_type=MESH,
        )

    summing = red_m[0, :RANK, :]

    def gathered(level, source_two, source_three=None):
        return dot(summing, coupled(level, source_two, source_three))

    wait_relayed(0)
    values_of(2)
    ctx_out[:48] = jnp.concatenate(
        [moms[2, 0:16, :], moms[3, 0:16, :], moms[2, 16:32, :] + moms[3, 16:32, :]], 0
    ).astype(BF16)

    @pl.when(t < PLANES * PLANE - 1)
    def _():
        halo_copy.start()
        ctx_copy(0).start()

    spectra(2)
    gates_of(2)
    near_rows((3,))

    wait_relayed(1)
    values_of(0)

    total = moms[0, 32:48, :] + moms[1, 32:48, :] + moms[2, 32:48, :] + moms[3, 32:48, :]
    m2[own] = total.astype(BF16)

    def plane_copy(k):
        return pltpu.make_async_remote_copy(
            src_ref=m2.at[own],
            dst_ref=m2.at[own],
            send_sem=s1,
            recv_sem=r1,
            device_id=(z * PLANE + lax.rem(own + k, PLANE), x),
            device_id_type=MESH,
        )

    plane_all = pltpu.make_async_remote_copy(
        src_ref=m2.at[pl.ds(0, PLANE - 1)],
        dst_ref=m2.at[pl.ds(0, PLANE - 1)],
        send_sem=s1,
        recv_sem=r1,
        device_id=(t, right),
        device_id_type=MESH,
    )

    for k in range(1, PLANE):
        plane_copy(k).start()

    def next_plane_copy(target, source):
        return pltpu.make_async_remote_copy(
            src_ref=m2.at[own],
            dst_ref=m2_prev.at[source],
            send_sem=s1p.at[target],
            recv_sem=r1p.at[source],
            device_id=((z + 1) * PLANE + target, x),
            device_id_type=MESH,
        )

    @pl.when((y == 3) & (z < PLANES - 1))
    def _():
        for target in range(2):
            next_plane_copy(target, core).start()

    ctx_out[48:] = (moms[0, 16:32, :] + moms[1, 16:32, :]).astype(BF16)

    @pl.when(t < PLANES * PLANE - 1)
    def _():
        ctx_copy(1).start()

    gates_of(0)

    plane_all.wait_recv()
    stack = m2[...].reshape(PLANE * RANK, WIDTH)
    lifted = dot(lift_m[...], jnp.concatenate([stack, stack], 0))
    pack_out[...] = lifted[:80].astype(BF16)


    def pack_copy(rows):
        return pltpu.make_async_remote_copy(
            src_ref=pack_out.at[pl.ds(0, rows)],
            dst_ref=pack_in.at[pl.ds(0, rows)],
            send_sem=s2,
            recv_sem=r2,
            device_id=(t + PLANE, x),
            device_id_type=MESH,
        )

    def five_copy(k):
        return pltpu.make_async_remote_copy(
            src_ref=pack_out.at[pl.ds(64, RANK)],
            dst_ref=m5_in.at[k],
            send_sem=s5.at[k],
            recv_sem=r5.at[k],
            device_id=(t + k * PLANE, x),
            device_id_type=MESH,
        )

    chain(7)

    for k in range(PLANES - 1, 1, -1):

        @pl.when(z + k < PLANES)
        def _():
            five_copy(k).start()

    @pl.when((z < PLANES - 1) & (y == 0))
    def _():
        pack_copy(48).start()

    @pl.when((z < PLANES - 1) & (y == 1))
    def _():
        pack_copy(64).start()

    @pl.when((z < PLANES - 1) & (y >= 2))
    def _():
        pack_copy(32).start()

    spectra(0)

    @pl.when(t > 0)
    def _():
        halo_copy.wait_recv()

    spec[LEAVES] = dot(fwd_v[...], jnp.concatenate([halo[...], halo[...]], 0))
    near_rows((0, 1, 2))

    @pl.when(t > 0)
    def _():
        ctx_copy(0).wait_recv()
        ctx_copy(1).wait_recv()

    prev = ctx_in[...].astype(F32)
    far0[0] = gathered(0, prev[0:16])
    far0[1] = gathered(0, prev[16:32], prev[0:16])
    far0[2] = gathered(0, moms[0, 0:16, :])
    far0[3] = gathered(0, moms[1, 0:16, :], moms[0, 0:16, :])
    far1[0] = gathered(1, prev[48:64])
    far1[1] = gathered(1, prev[32:48], prev[48:64])

    gather_sent = g.at[pl.ds(0, 3)]
    pltpu.make_async_remote_copy(
        src_ref=gather_sent,
        dst_ref=gather_sent,
        send_sem=gsend,
        recv_sem=drecv.at[0, 0],
        device_id=(t, right),
        device_id_type=MESH,
    ).wait_send()

    plane_all.wait_send()

    @pl.when(t < PLANES * PLANE - 1)
    def _():
        halo_copy.wait_send()
        ctx_copy(0).wait_send()
        ctx_copy(1).wait_send()

    @pl.when((y == 3) & (z < PLANES - 1))
    def _():
        for target in range(2):
            next_plane_copy(target, core).wait_send()

    @pl.when((y == 0) & (z > 0))
    def _():
        for source in range(2):
            next_plane_copy(source, source).wait_recv()

    def reduced(k, source_two, source_three):
        return dot(red_m[k], coupled(2 + k, source_two, source_three))

    at = 2 * jnp.maximum(y - 1, 0)
    inside = y > 0
    two = jnp.where(inside, m2[at + core], m2_prev[core]).astype(F32)
    three = jnp.where(inside, m2[at], m2_prev[0]).astype(F32) * core.astype(F32)
    expansion = reduced(0, two, three)

    @pl.when((z > 0) & (y == 0))
    def _():
        pack_copy(48).wait_recv()

    @pl.when((z > 0) & (y == 1))
    def _():
        pack_copy(64).wait_recv()

    @pl.when((z > 0) & (y >= 2))
    def _():
        pack_copy(32).wait_recv()

    odd = lax.rem(y, 2)
    lower = y < 2
    here = jnp.where(odd == 1, lifted[96:112], lifted[80:96])
    coming = pack_in[pl.ds(pl.multiple_of(32 + odd * RANK, RANK), RANK), :].astype(F32)
    two = jnp.where(lower, coming, here)
    three = jnp.where(lower, pack_in[32:48, :].astype(F32), lifted[80:96]) * odd.astype(F32)
    expansion = expansion + reduced(1, two, three)
    odd = lax.div(y, 2)
    two = pack_in[pl.ds(pl.multiple_of(odd * RANK, RANK), RANK), :].astype(F32)
    three = pack_in[0:16, :].astype(F32) * odd.astype(F32)
    expansion = expansion + reduced(2, two, three)

    for k in range(2, PLANES):

        @pl.when(z >= k)
        def _():
            five_copy(k).wait_recv()

    odd = lax.rem(z, 2)
    expansion = expansion + reduced(
        3, m5_in[2].astype(F32), m5_in[3].astype(F32) * odd.astype(F32)
    )
    pad = jnp.zeros((64, WIDTH), BF16)

    def sixth(base):
        pair = [m5_in[base], m5_in[base - 1]]
        return dot(six_m[...], jnp.concatenate(pair + pair + [pad], 0))

    odd_six = lax.rem(lax.div(z, 2), 2)
    expansion = expansion + reduced(
        4, sixth(4 + odd), sixth(6 + odd) * odd_six.astype(F32)
    )

    expansion = expansion[:RANK] + expansion[RANK:]

    def out_copy(leaf):
        rows = leaf_rows(leaf)
        return pltpu.make_async_copy(out_v.at[rows], out.at[rows], osem.at[leaf])

    for leaf in range(LEAVES):
        rows = leaf_rows(leaf)
        high, low = halves(jnp.concatenate([far0[leaf], far1[leaf // 2], expansion], 0))
        whole = jnp.concatenate([high, low, high, jnp.zeros((112, WIDTH), BF16)], 0)
        combined = near[rows, :] + dot(far_m[leaf], whole)
        out_v[rows, :] = (gate[rows, :] * combined).astype(BF16)
        out_copy(leaf).start()

    @pl.when((z < PLANES - 1) & (y == 0))
    def _():
        pack_copy(48).wait_send()

    @pl.when((z < PLANES - 1) & (y == 1))
    def _():
        pack_copy(64).wait_send()

    @pl.when((z < PLANES - 1) & (y >= 2))
    def _():
        pack_copy(32).wait_send()

    for k in range(2, PLANES):

        @pl.when(z + k < PLANES)
        def _():
            five_copy(k).wait_send()

    for leaf in range(LEAVES):
        out_copy(leaf).wait()


def per_device(
    tokens,
    norm_gain,
    w_value,
    w_gate,
    phi_taps,
    tap_coeff,
    skip_gain,
    basis_up,
    basis_down,
    lift_maps,
    spread_maps,
    couplings,
):
    forward, inverse = transform_tables()
    in_hbm = pl.BlockSpec(memory_space=pltpu.HBM)
    frames = LEAF * LEAVES
    vmem = pltpu.VMEM
    dma = pltpu.SemaphoreType.DMA
    scratch = [
        vmem((4, frames, WIDTH), BF16),
        vmem((4, WIDTH, 2 * WIDTH), BF16),
        vmem((1, 4 * WIDTH), F32),
        vmem(phi_taps.shape, F32),
        vmem(tap_coeff.shape, F32),
        vmem((1, WIDTH), F32),
        vmem(basis_up.shape, F32),
        vmem(basis_down.shape, F32),
        vmem(lift_maps.shape, F32),
        vmem(spread_maps.shape, F32),
        vmem(couplings.shape, F32),
        vmem(forward.shape, F32),
        vmem(inverse.shape, F32),
        vmem((2 * LEAF, 2 * LEAF), BF16),
        vmem((LEAF, 2 * LEAF), BF16),
        vmem((frames, WIDTH), BF16),
        vmem((LEAF, WIDTH), BF16),
        vmem((frames, WIDTH), F32),
        vmem((frames, WIDTH), F32),
        vmem((LEAVES + 1, 2 * LEAF, WIDTH), F32),
        vmem((4, LEAF, WIDTH), F32),
        vmem((LEAVES, 48, 2 * LEAF), BF16),
        vmem((112, 256), BF16),
        vmem((RANK, 128), BF16),
        vmem((LEAVES, LEAF, LEAF), BF16),
        vmem((5, 2 * RANK, LEAF), BF16),
        vmem((LEAVES, 48, WIDTH), F32),
        vmem((PLANE, RANK, WIDTH), BF16),
        vmem((2, RANK, WIDTH), BF16),
        vmem((64, WIDTH), BF16),
        vmem((64, WIDTH), BF16),
        vmem((80, WIDTH), BF16),
        vmem((64, WIDTH), BF16),
        vmem((PLANES, RANK, WIDTH), BF16),
        vmem((LEAVES, RANK, WIDTH), F32),
        vmem((2, RANK, WIDTH), F32),
        vmem((frames, WIDTH), BF16),
        vmem((frames, 2 * WIDTH), F32),
        vmem((frames, WIDTH // 2), F32),
        dma((20,)),
        dma(()),
        dma((2, 2)),
        dma((2, 2)),
        dma((2,)),
        dma((2, 2)),
        dma(()),
        dma(()),
        dma((2,)),
        dma((2,)),
        dma(()),
        dma(()),
        dma((PLANES,)),
        dma((PLANES,)),
        pltpu.SemaphoreType.REGULAR,
        pltpu.SemaphoreType.REGULAR,
        pltpu.SemaphoreType.REGULAR,
        pltpu.SemaphoreType.REGULAR,
        dma((LEAVES,)),
    ]
    return pl.pallas_call(
        body,
        out_shape=jax.ShapeDtypeStruct(tokens.shape, BF16),
        in_specs=[in_hbm] * 14,
        out_specs=in_hbm,
        scratch_shapes=scratch,
        compiler_params=pltpu.CompilerParams(
            collective_id=0, has_side_effects=True, vmem_limit_bytes=60 * 1024 * 1024
        ),
        cost_estimate=pl.CostEstimate(flops=4 * 10**9, bytes_accessed=8 * 10**6, transcendentals=10**6),
    )(
        tokens,
        norm_gain.reshape(1, -1),
        w_value,
        w_gate,
        phi_taps,
        tap_coeff,
        skip_gain.reshape(1, -1),
        basis_up,
        basis_down,
        lift_maps,
        spread_maps,
        couplings,
        jnp.asarray(forward),
        jnp.asarray(inverse),
    )


def solution(mesh):
    placed = (
        P("tm", "chan"),
        P(),
        P(None, "chan"),
        P(None, "chan"),
        P(),
        P(None, "chan"),
        P("chan"),
        P(),
        P(),
        P(),
        P(),
        P(None, None, None, None, "chan"),
    )
    return jax.shard_map(
        per_device, mesh=mesh, in_specs=placed, out_specs=P("tm", "chan"), check_vma=False
    )
```

```python
import jax
import jax.numpy as jnp
import numpy as np
from jax import lax
from jax.experimental import pallas as pl
from jax.experimental.pallas import tpu as pltpu
from jax.sharding import PartitionSpec as P

MESH = pl.DeviceIdType.MESH
F32 = jnp.float32
BF16 = jnp.bfloat16

LEAF = 256
LEAVES = 4
WIDTH = 256
RANK = 16
PLANES = 8
PLANE = 8


def transform_tables():
    odd = np.arange(LEAF)[:, None] + 0.5
    angle = 2 * np.pi * odd * np.arange(LEAF)[None, :] / (2 * LEAF)
    forward = np.concatenate([np.cos(angle), -np.sin(angle)], 0)
    return forward.astype(np.float32), (forward.T / LEAF).astype(np.float32)


def dot(left, right):
    return jnp.dot(left, right, preferred_element_type=F32)


def halves(value):
    high = value.astype(BF16)
    return high, (value - high.astype(F32)).astype(BF16)


def fine_dot(left, right):
    left_high, left_low = halves(left)
    right_high, right_low = halves(right)
    return dot(left_high, right_high) + dot(left_high, right_low) + dot(left_low, right_high)


def place_dot(left, right):
    left_high, left_low = halves(left)
    ones = right.astype(BF16)
    return dot(left_high, ones) + dot(left_low, ones)


def selector(lanes, period, shift, limit):
    row = lax.broadcasted_iota(jnp.int32, (RANK, lanes), 0)
    lane = lax.broadcasted_iota(jnp.int32, (RANK, lanes), 1)
    return ((lax.rem(lane, period) == row + shift) & (lane < limit)).astype(F32)


def body(
    tok, gain, w_value, w_gate, phi, coeff, skip, up, down, lift, spread, coup, fwd, inv,
    out,
    g, w, gain_v, phi_v, coeff_v, skip_v, up_v, down_v, lift_v, spread_v, coup_v, fwd_f, inv_f, fwd_v, inv_v,
    vals, halo, gate, near, spec, khat, mom_m, lift_m, six_m, far_m, red_m, moms,
    m2, m2_prev, ctx_out, ctx_in, pack_out, pack_in, m5_in, far0, far1, out_v, parts, part_squares,
    local_sem, tsem, gsend, drecv, rrecv, hsem, csem, s1, r1, s1p, r1p, s2, r2, s5, r5, ready_plane, ready_next, ready_edge, ready_later, osem,
):
    t = lax.axis_index("tm")
    x = lax.axis_index("chan")
    core = lax.rem(t, 2)
    y = lax.rem(lax.div(t, 2), 4)
    z = lax.div(t, PLANE)
    own = lax.rem(t, PLANE)
    rank = 2 * y + 1 - core
    right, left = lax.rem(x + 1, 4), lax.rem(x + 3, 4)

    def own_tokens(group):
        rows = pl.ds((1 - group) * 2 * LEAF, 2 * LEAF)
        return pltpu.make_async_copy(tok.at[rows], g.at[0, rows], tsem.at[group])

    for group in range(2):
        own_tokens(group).start()

    barrier = pltpu.get_barrier_semaphore()

    def signal(semaphore, frames, chans):
        pl.semaphore_signal(semaphore, inc=1, device_id=(frames, chans), device_id_type=MESH)

    signal(barrier, t, right)
    signal(barrier, t, left)

    @pl.when(z < PLANES - 1)
    def _():
        signal(barrier, t + PLANE, x)

    m2_prev[...] = jnp.zeros_like(m2_prev)
    ctx_in[...] = jnp.zeros_like(ctx_in)
    pack_in[...] = jnp.zeros_like(pack_in)
    m5_in[...] = jnp.zeros_like(m5_in)
    halo[...] = jnp.zeros_like(halo)

    def at_rank(other):
        return z * PLANE + 2 * lax.div(other, 2) + 1 - lax.rem(other, 2)

    for k in range(1, PLANE):

        @pl.when(rank + k < PLANE)
        def _():
            signal(barrier, at_rank(rank + k), x)

    pl.semaphore_wait(barrier, 2 + rank + jnp.where(z > 0, 1, 0))

    owners = [x, left, right, lax.rem(x + 2, 4)]

    def leaf_rows(leaf):
        return pl.ds(leaf * LEAF if isinstance(leaf, int) else pl.multiple_of(leaf * LEAF, LEAF), LEAF)

    def direct(group, way):
        rows = pl.ds((1 - group) * 2 * LEAF, 2 * LEAF)
        return pltpu.make_async_remote_copy(
            src_ref=g.at[0, rows],
            dst_ref=g.at[1 + way, rows],
            send_sem=gsend,
            recv_sem=drecv.at[way, group],
            device_id=(t, left if way else right),
            device_id_type=MESH,
        )

    def relay(group, way):
        rows = leaf_rows((1 - group) * 2 + way)
        return pltpu.make_async_remote_copy(
            src_ref=g.at[1 + way, rows],
            dst_ref=g.at[3, rows],
            send_sem=gsend,
            recv_sem=rrecv.at[way, group],
            device_id=(t, left if way else right),
            device_id_type=MESH,
        )

    def send_direct(group):
        own_tokens(group).wait()
        for way in range(2):
            direct(group, way).start()

    def pass_on(group):
        for way in range(2):
            direct(group, way).wait_recv()
            relay(group, way).start()

    def wait_relayed(group):
        for way in range(2):
            relay(group, way).wait_recv()

    def tables_near():
        for name in ("phi", "coeff", "fwd"):
            copies[name].wait()
        fwd_v[...] = jnp.concatenate(halves(fwd_f[...]), 1)
        taps = phi_v[...].astype(BF16).astype(F32).T.astype(BF16)
        coeff_high, coeff_low = halves(coeff_v[...])
        kernel_taps = dot(taps, coeff_high) + dot(taps, coeff_low)
        both = jnp.concatenate([kernel_taps[:LEAF], kernel_taps[LEAF:]], 1)
        high, low = halves(both)
        hat = dot(fwd_v[...], jnp.concatenate([high, high], 0)) + dot(fwd_v[:, :LEAF], low)
        a_re, a_im = hat[:LEAF, :WIDTH], hat[LEAF:, :WIDTH]
        b_re, b_im = hat[:LEAF, WIDTH:], hat[LEAF:, WIDTH:]
        row = lax.broadcasted_iota(jnp.int32, (LEAF, WIDTH), 0)
        sign = (1 - 2 * lax.rem(row, 2)).astype(F32)
        khat[0] = a_re
        khat[1] = a_im
        khat[2] = b_re - sign * a_im
        khat[3] = b_im + sign * a_re

    def tables_moments():
        copies["up"].wait()
        copies["lift"].wait()
        base = up_v[...]
        first = [fine_dot(lift_v[0, k], base) for k in range(2)]
        for leaf in range(LEAVES):
            second = fine_dot(lift_v[1, leaf // 2], first[leaf % 2])
            high, low = halves(jnp.concatenate([base, first[leaf % 2], second], 0))
            mom_m[leaf] = jnp.concatenate([high, low], 1)

    def tables_lift():
        def pair(level):
            return place_dot(lift_v[level, 0], selector(128, 32, 0, 128)) + place_dot(
                lift_v[level, 1], selector(128, 32, 16, 128)
            )

        def blocks(level, copies_of):
            rows = jnp.concatenate([pair(level)] * copies_of, 0)
            row = lax.broadcasted_iota(jnp.int32, rows.shape, 0)
            lane = lax.broadcasted_iota(jnp.int32, rows.shape, 1)
            return jnp.where(lax.div(row, RANK) == lax.div(lane, 2 * RANK), rows, 0.0)

        three = blocks(2, 8)
        four = fine_dot(blocks(3, 2), three)
        five = fine_dot(blocks(4, 1), jnp.concatenate([four, jnp.zeros((96, 128), F32)], 0))
        whole = jnp.concatenate([four, three[32:64], five, three[:32]], 0)
        high, low = halves(whole)
        lift_m[...] = jnp.concatenate([high, low], 1)
        six = place_dot(lift_v[5, 0], selector(128, 32, 0, 64)) + place_dot(
            lift_v[5, 1], selector(128, 32, 16, 64)
        )
        high = six.astype(BF16).astype(F32)
        lane = lax.broadcasted_iota(jnp.int32, six.shape, 1)
        six_m[...] = jnp.where(lane < 32, high, six - high).astype(BF16)

    def tables_far():
        copies["spread"].wait()
        copies["down"].wait()
        row = lax.broadcasted_iota(jnp.int32, (RANK, LEAF), 0)
        lane = lax.broadcasted_iota(jnp.int32, (RANK, LEAF), 1)
        summing = (lax.div(lane, RANK) == row).astype(F32)
        chain = None
        for k in range(5):
            if k > 0:
                step = spread_v[1 + k, lax.rem(lax.div(t, 2 ** (k - 1)), 2)]
                chain = step if k == 1 else fine_dot(chain, step)
            high, low = halves(summing if k == 0 else place_dot(chain, summing))
            red_m[k] = jnp.concatenate([high, low], 0)
        turned = down_v[...].T
        for leaf in range(LEAVES):
            near_step = spread_v[0, leaf % 2]
            both_steps = fine_dot(near_step, spread_v[1, leaf // 2])
            mix = (
                selector(LEAF, 48, 0, 144)
                + place_dot(near_step, selector(LEAF, 48, 16, 144))
                + place_dot(both_steps, selector(LEAF, 48, 32, 144))
            )
            whole = fine_dot(turned, mix)
            high = whole.astype(BF16).astype(F32)
            lane_at = lax.broadcasted_iota(jnp.int32, whole.shape, 1)
            far_m[leaf] = jnp.where(lane_at < 96, high, whole - high).astype(BF16)

    def pair_rows(first):
        return pl.ds(first * LEAF, 2 * LEAF)

    def scaled_rows(first, slots):
        rows = pair_rows(first)
        squares = jnp.zeros((2 * LEAF, WIDTH), F32)
        columns = []
        for slot in slots:
            tokens = g[slot, rows, :].astype(F32)
            squares = squares + tokens * tokens
            scale = gain_v[:, pl.ds(pl.multiple_of(owners[slot] * WIDTH, WIDTH), WIDTH)]
            columns.append((tokens * scale).astype(BF16))
        return jnp.concatenate(columns, 1), squares

    def gather_pair(first):
        scaled, squares = scaled_rows(first, (0, 1, 2))
        parts[pair_rows(first), :] = dot(scaled, w[:3].reshape(3 * WIDTH, 2 * WIDTH))
        part_squares[pair_rows(first), :] = squares[:, : WIDTH // 2] + squares[:, WIDTH // 2 :]

    def values_of(first):
        rows = pair_rows(first)
        scaled, squares = scaled_rows(first, (3,))
        squares = squares[:, : WIDTH // 2] + squares[:, WIDTH // 2 :] + part_squares[rows, :]
        inverse = lax.rsqrt(jnp.sum(squares, axis=1, keepdims=True) / 1024 + 1e-06)
        part_squares[rows, :] = jnp.broadcast_to(inverse, squares.shape)
        value = ((parts[rows, :WIDTH] + dot(scaled, w[3, :, :WIDTH])) * inverse).astype(BF16)
        vals[rows, :] = value
        for k in range(2):
            leaf_value = value[k * LEAF : (k + 1) * LEAF]
            moms[first + k] = dot(mom_m[first + k], jnp.concatenate([leaf_value, leaf_value], 0))

    def gates_of(first):
        rows = pair_rows(first)
        scaled, _ = scaled_rows(first, (3,))
        half = 0.5 * part_squares[rows, :]
        sums = parts[rows, WIDTH:] + dot(scaled, w[3, :, WIDTH:])
        gate[rows, :] = 0.5 * jnp.tanh(sums * jnp.concatenate([half, half], 1)) + 0.5

    def spectra(first):
        both = jnp.concatenate([vals[leaf_rows(first), :], vals[leaf_rows(first + 1), :]], 1)
        result = dot(fwd_v[...], jnp.concatenate([both, both], 0))
        spec[first] = result[:, :WIDTH]
        spec[first + 1] = result[:, WIDTH:]

    def near_rows(leaves):
        columns = []
        for leaf in leaves:
            before = leaf - 1 if leaf > 0 else LEAVES
            a_re, a_im = spec[leaf, :LEAF, :], spec[leaf, LEAF:, :]
            b_re, b_im = spec[before, :LEAF, :], spec[before, LEAF:, :]
            out_re = khat[0] * a_re - khat[1] * a_im + khat[2] * b_re - khat[3] * b_im
            out_im = khat[0] * a_im + khat[1] * a_re + khat[2] * b_im + khat[3] * b_re
            columns.append(jnp.concatenate([out_re, out_im], 0).astype(BF16))
        total = dot(inv_v[...], jnp.concatenate(columns, 1))
        for k, leaf in enumerate(leaves):
            rows = leaf_rows(leaf)
            direct_term = skip_v[...] * vals[rows, :].astype(F32)
            near[rows, :] = total[:, k * WIDTH : (k + 1) * WIDTH] + direct_term

    def coupled(level, source_two, source_three):
        product = coup_v[level, 0] * source_two[None]
        if source_three is not None:
            product = product + coup_v[level, 1] * source_three[None]
        return product.reshape(RANK * RANK, WIDTH).astype(BF16)

    send_direct(0)

    copies = {}

    def local(name, source, target):
        copies[name] = pltpu.make_async_copy(source, target, local_sem.at[len(copies)])
        copies[name].start()

    for slot in range(4):
        rows = pl.ds(pl.multiple_of(owners[slot] * WIDTH, WIDTH), WIDTH)
        local(("v", slot), w_value.at[rows], w.at[slot, :, pl.ds(0, WIDTH)])
        local(("g", slot), w_gate.at[rows], w.at[slot, :, pl.ds(WIDTH, WIDTH)])
    for name, source, target in (
        ("gain", gain, gain_v),
        ("phi", phi, phi_v),
        ("coeff", coeff, coeff_v),
        ("fwd", fwd, fwd_f),
        ("skip", skip, skip_v),
        ("up", up, up_v),
        ("down", down, down_v),
        ("lift", lift, lift_v),
        ("spread", spread, spread_v),
        ("inv", inv, inv_f),
        ("coup", coup, coup_v),
    ):
        local(name, source, target)

    @pl.when(z > 0)
    def _():
        signal(ready_next, t - PLANE, x)

    for k in range(1, PLANE):

        @pl.when(rank >= k)
        def _():
            signal(ready_plane, at_rank(rank - k), x)

    def chain(place):
        @pl.when(z == PLANES - 1 - place)
        def _():
            if not isinstance(place, int) or place > 0:
                pl.semaphore_wait(ready_later, 1)
            if not isinstance(place, int) or place < PLANES - 1:
                signal(ready_later, t - PLANE, x)

    chain(0)
    tables_near()
    send_direct(1)
    chain(1)
    tables_moments()
    chain(2)
    tables_lift()
    chain(3)
    for slot in range(4):
        copies["v", slot].wait()
        copies["g", slot].wait()
    for name in ("gain", "skip", "coup", "inv"):
        copies[name].wait()
    pass_on(0)
    chain(4)

    @pl.when(rank < PLANE - 1)
    def _():
        pl.semaphore_wait(ready_plane, PLANE - 1 - rank)

    @pl.when(z < PLANES - 1)
    def _():
        pl.semaphore_wait(ready_next, 1)

        @pl.when(y == 0)
        def _():
            signal(ready_edge, z * PLANE + 6, x)
            signal(ready_edge, z * PLANE + 7, x)

    gather_pair(2)
    chain(5)
    tables_far()
    inv_v[...] = inv_f[...].astype(BF16)
    chain(6)
    pass_on(1)
    gather_pair(0)

    @pl.when((y == 3) & (z < PLANES - 1))
    def _():
        pl.semaphore_wait(ready_edge, 2)

    halo_copy = pltpu.make_async_remote_copy(
        src_ref=vals.at[pl.ds(3 * LEAF, LEAF)],
        dst_ref=halo,
        send_sem=hsem.at[0],
        recv_sem=hsem.at[1],
        device_id=(t + 1, x),
        device_id_type=MESH,
    )

    def ctx_copy(part):
        rows = pl.ds(0, 48) if part == 0 else pl.ds(48, 16)
        return pltpu.make_async_remote_copy(
            src_ref=ctx_out.at[rows],
            dst_ref=ctx_in.at[rows],
            send_sem=csem.at[0, part],
            recv_sem=csem.at[1, part],
            device_id=(t + 1, x),
            device_id_type=MESH,
        )

    summing = red_m[0, :RANK, :]

    def gathered(level, source_two, source_three=None):
        return dot(summing, coupled(level, source_two, source_three))

    wait_relayed(0)
    values_of(2)
    ctx_out[:48] = jnp.concatenate(
        [moms[2, 0:16, :], moms[3, 0:16, :], moms[2, 16:32, :] + moms[3, 16:32, :]], 0
    ).astype(BF16)

    @pl.when(t < PLANES * PLANE - 1)
    def _():
        halo_copy.start()
        ctx_copy(0).start()

    spectra(2)
    gates_of(2)
    near_rows((3,))

    wait_relayed(1)
    values_of(0)

    total = moms[0, 32:48, :] + moms[1, 32:48, :] + moms[2, 32:48, :] + moms[3, 32:48, :]
    m2[own] = total.astype(BF16)

    def plane_copy(k):
        return pltpu.make_async_remote_copy(
            src_ref=m2.at[own],
            dst_ref=m2.at[own],
            send_sem=s1,
            recv_sem=r1,
            device_id=(z * PLANE + lax.rem(own + k, PLANE), x),
            device_id_type=MESH,
        )

    plane_all = pltpu.make_async_remote_copy(
        src_ref=m2.at[pl.ds(0, PLANE - 1)],
        dst_ref=m2.at[pl.ds(0, PLANE - 1)],
        send_sem=s1,
        recv_sem=r1,
        device_id=(t, right),
        device_id_type=MESH,
    )

    for k in range(1, PLANE):
        plane_copy(k).start()

    def next_plane_copy(target, source):
        return pltpu.make_async_remote_copy(
            src_ref=m2.at[own],
            dst_ref=m2_prev.at[source],
            send_sem=s1p.at[target],
            recv_sem=r1p.at[source],
            device_id=((z + 1) * PLANE + target, x),
            device_id_type=MESH,
        )

    @pl.when((y == 3) & (z < PLANES - 1))
    def _():
        for target in range(2):
            next_plane_copy(target, core).start()

    ctx_out[48:] = (moms[0, 16:32, :] + moms[1, 16:32, :]).astype(BF16)

    @pl.when(t < PLANES * PLANE - 1)
    def _():
        ctx_copy(1).start()

    gates_of(0)

    plane_all.wait_recv()
    stack = m2[...].reshape(PLANE * RANK, WIDTH)
    lifted = dot(lift_m[...], jnp.concatenate([stack, stack], 0))
    pack_out[...] = lifted[:80].astype(BF16)


    def pack_copy(rows):
        return pltpu.make_async_remote_copy(
            src_ref=pack_out.at[pl.ds(0, rows)],
            dst_ref=pack_in.at[pl.ds(0, rows)],
            send_sem=s2,
            recv_sem=r2,
            device_id=(t + PLANE, x),
            device_id_type=MESH,
        )

    def five_copy(k):
        return pltpu.make_async_remote_copy(
            src_ref=pack_out.at[pl.ds(64, RANK)],
            dst_ref=m5_in.at[k],
            send_sem=s5.at[k],
            recv_sem=r5.at[k],
            device_id=(t + k * PLANE, x),
            device_id_type=MESH,
        )

    chain(7)

    for k in range(PLANES - 1, 1, -1):

        @pl.when(z + k < PLANES)
        def _():
            five_copy(k).start()

    @pl.when((z < PLANES - 1) & (y == 0))
    def _():
        pack_copy(48).start()

    @pl.when((z < PLANES - 1) & (y == 1))
    def _():
        pack_copy(64).start()

    @pl.when((z < PLANES - 1) & (y >= 2))
    def _():
        pack_copy(32).start()

    spectra(0)

    @pl.when(t > 0)
    def _():
        halo_copy.wait_recv()

    spec[LEAVES] = dot(fwd_v[...], jnp.concatenate([halo[...], halo[...]], 0))
    near_rows((0, 1, 2))

    @pl.when(t > 0)
    def _():
        ctx_copy(0).wait_recv()
        ctx_copy(1).wait_recv()

    prev = ctx_in[...].astype(F32)
    far0[0] = gathered(0, prev[0:16])
    far0[1] = gathered(0, prev[16:32], prev[0:16])
    far0[2] = gathered(0, moms[0, 0:16, :])
    far0[3] = gathered(0, moms[1, 0:16, :], moms[0, 0:16, :])
    far1[0] = gathered(1, prev[48:64])
    far1[1] = gathered(1, prev[32:48], prev[48:64])

    gather_sent = g.at[pl.ds(0, 3)]
    pltpu.make_async_remote_copy(
        src_ref=gather_sent,
        dst_ref=gather_sent,
        send_sem=gsend,
        recv_sem=drecv.at[0, 0],
        device_id=(t, right),
        device_id_type=MESH,
    ).wait_send()

    plane_all.wait_send()

    @pl.when(t < PLANES * PLANE - 1)
    def _():
        halo_copy.wait_send()
        ctx_copy(0).wait_send()
        ctx_copy(1).wait_send()

    @pl.when((y == 3) & (z < PLANES - 1))
    def _():
        for target in range(2):
            next_plane_copy(target, core).wait_send()

    @pl.when((y == 0) & (z > 0))
    def _():
        for source in range(2):
            next_plane_copy(source, source).wait_recv()

    def reduced(k, source_two, source_three):
        return dot(red_m[k], coupled(2 + k, source_two, source_three))

    at = 2 * jnp.maximum(y - 1, 0)
    inside = y > 0
    two = jnp.where(inside, m2[at + core], m2_prev[core]).astype(F32)
    three = jnp.where(inside, m2[at], m2_prev[0]).astype(F32) * core.astype(F32)
    expansion = reduced(0, two, three)

    @pl.when((z > 0) & (y == 0))
    def _():
        pack_copy(48).wait_recv()

    @pl.when((z > 0) & (y == 1))
    def _():
        pack_copy(64).wait_recv()

    @pl.when((z > 0) & (y >= 2))
    def _():
        pack_copy(32).wait_recv()

    odd = lax.rem(y, 2)
    lower = y < 2
    here = jnp.where(odd == 1, lifted[96:112], lifted[80:96])
    coming = pack_in[pl.ds(pl.multiple_of(32 + odd * RANK, RANK), RANK), :].astype(F32)
    two = jnp.where(lower, coming, here)
    three = jnp.where(lower, pack_in[32:48, :].astype(F32), lifted[80:96]) * odd.astype(F32)
    expansion = expansion + reduced(1, two, three)
    odd = lax.div(y, 2)
    two = pack_in[pl.ds(pl.multiple_of(odd * RANK, RANK), RANK), :].astype(F32)
    three = pack_in[0:16, :].astype(F32) * odd.astype(F32)
    expansion = expansion + reduced(2, two, three)

    for k in range(2, PLANES):

        @pl.when(z >= k)
        def _():
            five_copy(k).wait_recv()

    odd = lax.rem(z, 2)
    expansion = expansion + reduced(
        3, m5_in[2].astype(F32), m5_in[3].astype(F32) * odd.astype(F32)
    )
    pad = jnp.zeros((64, WIDTH), BF16)

    def sixth(base):
        pair = [m5_in[base], m5_in[base - 1]]
        return dot(six_m[...], jnp.concatenate(pair + pair + [pad], 0))

    odd_six = lax.rem(lax.div(z, 2), 2)
    expansion = expansion + reduced(
        4, sixth(4 + odd), sixth(6 + odd) * odd_six.astype(F32)
    )

    expansion = expansion[:RANK] + expansion[RANK:]

    def out_copy(leaf):
        rows = leaf_rows(leaf)
        return pltpu.make_async_copy(out_v.at[rows], out.at[rows], osem.at[leaf])

    for leaf in range(LEAVES):
        rows = leaf_rows(leaf)
        high, low = halves(jnp.concatenate([far0[leaf], far1[leaf // 2], expansion], 0))
        whole = jnp.concatenate([high, low, high, jnp.zeros((112, WIDTH), BF16)], 0)
        combined = near[rows, :] + dot(far_m[leaf], whole)
        out_v[rows, :] = (gate[rows, :] * combined).astype(BF16)
        out_copy(leaf).start()

    @pl.when((z < PLANES - 1) & (y == 0))
    def _():
        pack_copy(48).wait_send()

    @pl.when((z < PLANES - 1) & (y == 1))
    def _():
        pack_copy(64).wait_send()

    @pl.when((z < PLANES - 1) & (y >= 2))
    def _():
        pack_copy(32).wait_send()

    for k in range(2, PLANES):

        @pl.when(z + k < PLANES)
        def _():
            five_copy(k).wait_send()

    for leaf in range(LEAVES):
        out_copy(leaf).wait()


def per_device(
    tokens,
    norm_gain,
    w_value,
    w_gate,
    phi_taps,
    tap_coeff,
    skip_gain,
    basis_up,
    basis_down,
    lift_maps,
    spread_maps,
    couplings,
):
    forward, inverse = transform_tables()
    in_hbm = pl.BlockSpec(memory_space=pltpu.HBM)
    frames = LEAF * LEAVES
    vmem = pltpu.VMEM
    dma = pltpu.SemaphoreType.DMA
    scratch = [
        vmem((4, frames, WIDTH), BF16),
        vmem((4, WIDTH, 2 * WIDTH), BF16),
        vmem((1, 4 * WIDTH), F32),
        vmem(phi_taps.shape, F32),
        vmem(tap_coeff.shape, F32),
        vmem((1, WIDTH), F32),
        vmem(basis_up.shape, F32),
        vmem(basis_down.shape, F32),
        vmem(lift_maps.shape, F32),
        vmem(spread_maps.shape, F32),
        vmem(couplings.shape, F32),
        vmem(forward.shape, F32),
        vmem(inverse.shape, F32),
        vmem((2 * LEAF, 2 * LEAF), BF16),
        vmem((LEAF, 2 * LEAF), BF16),
        vmem((frames, WIDTH), BF16),
        vmem((LEAF, WIDTH), BF16),
        vmem((frames, WIDTH), F32),
        vmem((frames, WIDTH), F32),
        vmem((LEAVES + 1, 2 * LEAF, WIDTH), F32),
        vmem((4, LEAF, WIDTH), F32),
        vmem((LEAVES, 48, 2 * LEAF), BF16),
        vmem((112, 256), BF16),
        vmem((RANK, 128), BF16),
        vmem((LEAVES, LEAF, LEAF), BF16),
        vmem((5, 2 * RANK, LEAF), BF16),
        vmem((LEAVES, 48, WIDTH), F32),
        vmem((PLANE, RANK, WIDTH), BF16),
        vmem((2, RANK, WIDTH), BF16),
        vmem((64, WIDTH), BF16),
        vmem((64, WIDTH), BF16),
        vmem((80, WIDTH), BF16),
        vmem((64, WIDTH), BF16),
        vmem((PLANES, RANK, WIDTH), BF16),
        vmem((LEAVES, RANK, WIDTH), F32),
        vmem((2, RANK, WIDTH), F32),
        vmem((frames, WIDTH), BF16),
        vmem((frames, 2 * WIDTH), F32),
        vmem((frames, WIDTH // 2), F32),
        dma((20,)),
        dma((2,)),
        dma(()),
        dma((2, 2)),
        dma((2, 2)),
        dma((2,)),
        dma((2, 2)),
        dma(()),
        dma(()),
        dma((2,)),
        dma((2,)),
        dma(()),
        dma(()),
        dma((PLANES,)),
        dma((PLANES,)),
        pltpu.SemaphoreType.REGULAR,
        pltpu.SemaphoreType.REGULAR,
        pltpu.SemaphoreType.REGULAR,
        pltpu.SemaphoreType.REGULAR,
        dma((LEAVES,)),
    ]
    return pl.pallas_call(
        body,
        out_shape=jax.ShapeDtypeStruct(tokens.shape, BF16),
        in_specs=[in_hbm] * 14,
        out_specs=in_hbm,
        scratch_shapes=scratch,
        compiler_params=pltpu.CompilerParams(
            collective_id=0, has_side_effects=True, vmem_limit_bytes=60 * 1024 * 1024
        ),
        cost_estimate=pl.CostEstimate(flops=4 * 10**9, bytes_accessed=8 * 10**6, transcendentals=10**6),
    )(
        tokens,
        norm_gain.reshape(1, -1),
        w_value,
        w_gate,
        phi_taps,
        tap_coeff,
        skip_gain.reshape(1, -1),
        basis_up,
        basis_down,
        lift_maps,
        spread_maps,
        couplings,
        jnp.asarray(forward),
        jnp.asarray(inverse),
    )


def solution(mesh):
    placed = (
        P("tm", "chan"),
        P(),
        P(None, "chan"),
        P(None, "chan"),
        P(),
        P(None, "chan"),
        P("chan"),
        P(),
        P(),
        P(),
        P(),
        P(None, None, None, None, "chan"),
    )
    return jax.shard_map(
        per_device, mesh=mesh, in_specs=placed, out_specs=P("tm", "chan"), check_vma=False
    )
```

```python
import jax
import jax.numpy as jnp
import numpy as np
from jax import lax
from jax.experimental import pallas as pl
from jax.experimental.pallas import tpu as pltpu
from jax.sharding import PartitionSpec as P

MESH = pl.DeviceIdType.MESH
F32 = jnp.float32
BF16 = jnp.bfloat16

LEAF = 256
LEAVES = 4
WIDTH = 256
RANK = 16
PLANES = 8
PLANE = 8


def transform_tables():
    odd = np.arange(LEAF)[:, None] + 0.5
    angle = 2 * np.pi * odd * np.arange(LEAF)[None, :] / (2 * LEAF)
    forward = np.concatenate([np.cos(angle), -np.sin(angle)], 0)
    return forward.astype(np.float32), (forward.T / LEAF).astype(np.float32)


def dot(left, right):
    return jnp.dot(left, right, preferred_element_type=F32)


def halves(value):
    high = value.astype(BF16)
    return high, (value - high.astype(F32)).astype(BF16)


def fine_dot(left, right):
    left_high, left_low = halves(left)
    right_high, right_low = halves(right)
    return dot(left_high, right_high) + dot(left_high, right_low) + dot(left_low, right_high)


def place_dot(left, right):
    left_high, left_low = halves(left)
    ones = right.astype(BF16)
    return dot(left_high, ones) + dot(left_low, ones)


def selector(lanes, period, shift, limit):
    row = lax.broadcasted_iota(jnp.int32, (RANK, lanes), 0)
    lane = lax.broadcasted_iota(jnp.int32, (RANK, lanes), 1)
    return ((lax.rem(lane, period) == row + shift) & (lane < limit)).astype(F32)


def body(
    tok, gain, w_value, w_gate, phi, coeff, skip, up, down, lift, spread, coup, fwd, inv,
    out,
    g, w, gain_v, phi_v, coeff_v, skip_v, up_v, down_v, lift_v, spread_v, coup_v, fwd_f, inv_f, fwd_v, inv_v,
    vals, halo, gate, near, spec, khat, mom_m, lift_m, six_m, far_m, red_m, moms,
    m2, m2_prev, ctx_out, ctx_in, pack_out, pack_in, m5_in, far0, far1, out_v, parts, part_squares,
    local_sem, gsend, drecv, rrecv, hsem, csem, s1, r1, s1p, r1p, s2, r2, s5, r5, ready_plane, ready_next, ready_edge, ready_later, osem,
):
    t = lax.axis_index("tm")
    x = lax.axis_index("chan")
    core = lax.rem(t, 2)
    y = lax.rem(lax.div(t, 2), 4)
    z = lax.div(t, PLANE)
    own = lax.rem(t, PLANE)
    rank = 2 * y + 1 - core
    right, left = lax.rem(x + 1, 4), lax.rem(x + 3, 4)

    barrier = pltpu.get_barrier_semaphore()

    def signal(semaphore, frames, chans):
        pl.semaphore_signal(semaphore, inc=1, device_id=(frames, chans), device_id_type=MESH)

    signal(barrier, t, right)
    signal(barrier, t, left)

    @pl.when(z < PLANES - 1)
    def _():
        signal(barrier, t + PLANE, x)

    m2_prev[...] = jnp.zeros_like(m2_prev)
    ctx_in[...] = jnp.zeros_like(ctx_in)
    pack_in[...] = jnp.zeros_like(pack_in)
    m5_in[...] = jnp.zeros_like(m5_in)
    halo[...] = jnp.zeros_like(halo)

    def at_rank(other):
        return z * PLANE + 2 * lax.div(other, 2) + 1 - lax.rem(other, 2)

    for k in range(1, PLANE):

        @pl.when(rank + k < PLANE)
        def _():
            signal(barrier, at_rank(rank + k), x)

    pl.semaphore_wait(barrier, 2 + rank + jnp.where(z > 0, 1, 0))

    owners = [x, left, right, lax.rem(x + 2, 4)]

    def leaf_rows(leaf):
        return pl.ds(leaf * LEAF if isinstance(leaf, int) else pl.multiple_of(leaf * LEAF, LEAF), LEAF)

    def direct(group, way):
        rows = pl.ds((1 - group) * 2 * LEAF, 2 * LEAF)
        return pltpu.make_async_remote_copy(
            src_ref=tok.at[rows],
            dst_ref=g.at[1 + way, rows],
            send_sem=gsend,
            recv_sem=drecv.at[way, group],
            device_id=(t, left if way else right),
            device_id_type=MESH,
        )

    def relay(group, way):
        rows = leaf_rows((1 - group) * 2 + way)
        return pltpu.make_async_remote_copy(
            src_ref=g.at[1 + way, rows],
            dst_ref=g.at[3, rows],
            send_sem=gsend,
            recv_sem=rrecv.at[way, group],
            device_id=(t, left if way else right),
            device_id_type=MESH,
        )

    def send_direct(group):
        for way in range(2):
            direct(group, way).start()

    def pass_on(group):
        for way in range(2):
            direct(group, way).wait_recv()
            relay(group, way).start()

    def wait_relayed(group):
        for way in range(2):
            relay(group, way).wait_recv()

    def tables_near():
        for name in ("phi", "coeff", "fwd"):
            copies[name].wait()
        fwd_v[...] = jnp.concatenate(halves(fwd_f[...]), 1)
        taps = phi_v[...].astype(BF16).astype(F32).T.astype(BF16)
        coeff_high, coeff_low = halves(coeff_v[...])
        kernel_taps = dot(taps, coeff_high) + dot(taps, coeff_low)
        both = jnp.concatenate([kernel_taps[:LEAF], kernel_taps[LEAF:]], 1)
        high, low = halves(both)
        hat = dot(fwd_v[...], jnp.concatenate([high, high], 0)) + dot(fwd_v[:, :LEAF], low)
        a_re, a_im = hat[:LEAF, :WIDTH], hat[LEAF:, :WIDTH]
        b_re, b_im = hat[:LEAF, WIDTH:], hat[LEAF:, WIDTH:]
        row = lax.broadcasted_iota(jnp.int32, (LEAF, WIDTH), 0)
        sign = (1 - 2 * lax.rem(row, 2)).astype(F32)
        khat[0] = a_re
        khat[1] = a_im
        khat[2] = b_re - sign * a_im
        khat[3] = b_im + sign * a_re

    def tables_moments():
        copies["up"].wait()
        copies["lift"].wait()
        base = up_v[...]
        first = [fine_dot(lift_v[0, k], base) for k in range(2)]
        for leaf in range(LEAVES):
            second = fine_dot(lift_v[1, leaf // 2], first[leaf % 2])
            high, low = halves(jnp.concatenate([base, first[leaf % 2], second], 0))
            mom_m[leaf] = jnp.concatenate([high, low], 1)

    def tables_lift():
        def pair(level):
            return place_dot(lift_v[level, 0], selector(128, 32, 0, 128)) + place_dot(
                lift_v[level, 1], selector(128, 32, 16, 128)
            )

        def blocks(level, copies_of):
            rows = jnp.concatenate([pair(level)] * copies_of, 0)
            row = lax.broadcasted_iota(jnp.int32, rows.shape, 0)
            lane = lax.broadcasted_iota(jnp.int32, rows.shape, 1)
            return jnp.where(lax.div(row, RANK) == lax.div(lane, 2 * RANK), rows, 0.0)

        three = blocks(2, 8)
        four = fine_dot(blocks(3, 2), three)
        five = fine_dot(blocks(4, 1), jnp.concatenate([four, jnp.zeros((96, 128), F32)], 0))
        whole = jnp.concatenate([four, three[32:64], five, three[:32]], 0)
        high, low = halves(whole)
        lift_m[...] = jnp.concatenate([high, low], 1)
        six = place_dot(lift_v[5, 0], selector(128, 32, 0, 64)) + place_dot(
            lift_v[5, 1], selector(128, 32, 16, 64)
        )
        high = six.astype(BF16).astype(F32)
        lane = lax.broadcasted_iota(jnp.int32, six.shape, 1)
        six_m[...] = jnp.where(lane < 32, high, six - high).astype(BF16)

    def tables_far():
        copies["spread"].wait()
        copies["down"].wait()
        row = lax.broadcasted_iota(jnp.int32, (RANK, LEAF), 0)
        lane = lax.broadcasted_iota(jnp.int32, (RANK, LEAF), 1)
        summing = (lax.div(lane, RANK) == row).astype(F32)
        chain = None
        for k in range(5):
            if k > 0:
                step = spread_v[1 + k, lax.rem(lax.div(t, 2 ** (k - 1)), 2)]
                chain = step if k == 1 else fine_dot(chain, step)
            high, low = halves(summing if k == 0 else place_dot(chain, summing))
            red_m[k] = jnp.concatenate([high, low], 0)
        turned = down_v[...].T
        for leaf in range(LEAVES):
            near_step = spread_v[0, leaf % 2]
            both_steps = fine_dot(near_step, spread_v[1, leaf // 2])
            mix = (
                selector(LEAF, 48, 0, 144)
                + place_dot(near_step, selector(LEAF, 48, 16, 144))
                + place_dot(both_steps, selector(LEAF, 48, 32, 144))
            )
            whole = fine_dot(turned, mix)
            high = whole.astype(BF16).astype(F32)
            lane_at = lax.broadcasted_iota(jnp.int32, whole.shape, 1)
            far_m[leaf] = jnp.where(lane_at < 96, high, whole - high).astype(BF16)

    def pair_rows(first):
        return pl.ds(first * LEAF, 2 * LEAF)

    def scaled_rows(first, slots):
        rows = pair_rows(first)
        squares = jnp.zeros((2 * LEAF, WIDTH), F32)
        columns = []
        for slot in slots:
            tokens = g[slot, rows, :].astype(F32)
            squares = squares + tokens * tokens
            scale = gain_v[:, pl.ds(pl.multiple_of(owners[slot] * WIDTH, WIDTH), WIDTH)]
            columns.append((tokens * scale).astype(BF16))
        return jnp.concatenate(columns, 1), squares

    def gather_pair(first):
        scaled, squares = scaled_rows(first, (0, 1, 2))
        parts[pair_rows(first), :] = dot(scaled, w[:3].reshape(3 * WIDTH, 2 * WIDTH))
        part_squares[pair_rows(first), :] = squares[:, : WIDTH // 2] + squares[:, WIDTH // 2 :]

    def values_of(first):
        rows = pair_rows(first)
        scaled, squares = scaled_rows(first, (3,))
        squares = squares[:, : WIDTH // 2] + squares[:, WIDTH // 2 :] + part_squares[rows, :]
        inverse = lax.rsqrt(jnp.sum(squares, axis=1, keepdims=True) / 1024 + 1e-06)
        part_squares[rows, :] = jnp.broadcast_to(inverse, squares.shape)
        value = ((parts[rows, :WIDTH] + dot(scaled, w[3, :, :WIDTH])) * inverse).astype(BF16)
        vals[rows, :] = value
        for k in range(2):
            leaf_value = value[k * LEAF : (k + 1) * LEAF]
            moms[first + k] = dot(mom_m[first + k], jnp.concatenate([leaf_value, leaf_value], 0))

    def gates_of(first):
        rows = pair_rows(first)
        scaled, _ = scaled_rows(first, (3,))
        half = 0.5 * part_squares[rows, :]
        sums = parts[rows, WIDTH:] + dot(scaled, w[3, :, WIDTH:])
        gate[rows, :] = 0.5 * jnp.tanh(sums * jnp.concatenate([half, half], 1)) + 0.5

    def spectra(first):
        both = jnp.concatenate([vals[leaf_rows(first), :], vals[leaf_rows(first + 1), :]], 1)
        result = dot(fwd_v[...], jnp.concatenate([both, both], 0))
        spec[first] = result[:, :WIDTH]
        spec[first + 1] = result[:, WIDTH:]

    def near_rows(leaves):
        columns = []
        for leaf in leaves:
            before = leaf - 1 if leaf > 0 else LEAVES
            a_re, a_im = spec[leaf, :LEAF, :], spec[leaf, LEAF:, :]
            b_re, b_im = spec[before, :LEAF, :], spec[before, LEAF:, :]
            out_re = khat[0] * a_re - khat[1] * a_im + khat[2] * b_re - khat[3] * b_im
            out_im = khat[0] * a_im + khat[1] * a_re + khat[2] * b_im + khat[3] * b_re
            columns.append(jnp.concatenate([out_re, out_im], 0).astype(BF16))
        total = dot(inv_v[...], jnp.concatenate(columns, 1))
        for k, leaf in enumerate(leaves):
            rows = leaf_rows(leaf)
            direct_term = skip_v[...] * vals[rows, :].astype(F32)
            near[rows, :] = total[:, k * WIDTH : (k + 1) * WIDTH] + direct_term

    def coupled(level, source_two, source_three):
        product = coup_v[level, 0] * source_two[None]
        if source_three is not None:
            product = product + coup_v[level, 1] * source_three[None]
        return product.reshape(RANK * RANK, WIDTH).astype(BF16)

    send_direct(0)

    copies = {}

    def local(name, source, target):
        copies[name] = pltpu.make_async_copy(source, target, local_sem.at[len(copies)])
        copies[name].start()

    local("tok", tok, g.at[0])
    for slot in range(4):
        rows = pl.ds(pl.multiple_of(owners[slot] * WIDTH, WIDTH), WIDTH)
        local(("v", slot), w_value.at[rows], w.at[slot, :, pl.ds(0, WIDTH)])
        local(("g", slot), w_gate.at[rows], w.at[slot, :, pl.ds(WIDTH, WIDTH)])
    for name, source, target in (
        ("gain", gain, gain_v),
        ("phi", phi, phi_v),
        ("coeff", coeff, coeff_v),
        ("fwd", fwd, fwd_f),
        ("skip", skip, skip_v),
        ("up", up, up_v),
        ("down", down, down_v),
        ("lift", lift, lift_v),
        ("spread", spread, spread_v),
        ("inv", inv, inv_f),
        ("coup", coup, coup_v),
    ):
        local(name, source, target)

    @pl.when(z > 0)
    def _():
        signal(ready_next, t - PLANE, x)

    for k in range(1, PLANE):

        @pl.when(rank >= k)
        def _():
            signal(ready_plane, at_rank(rank - k), x)

    def chain(place):
        @pl.when(z == PLANES - 1 - place)
        def _():
            if not isinstance(place, int) or place > 0:
                pl.semaphore_wait(ready_later, 1)
            if not isinstance(place, int) or place < PLANES - 1:
                signal(ready_later, t - PLANE, x)

    chain(0)
    tables_near()
    send_direct(1)
    chain(1)
    tables_moments()
    chain(2)
    tables_lift()
    chain(3)
    for slot in range(4):
        copies["v", slot].wait()
        copies["g", slot].wait()
    for name in ("tok", "gain", "skip", "coup", "inv"):
        copies[name].wait()
    pass_on(0)
    chain(4)

    @pl.when(rank < PLANE - 1)
    def _():
        pl.semaphore_wait(ready_plane, PLANE - 1 - rank)

    @pl.when(z < PLANES - 1)
    def _():
        pl.semaphore_wait(ready_next, 1)

        @pl.when(y == 0)
        def _():
            signal(ready_edge, z * PLANE + 6, x)
            signal(ready_edge, z * PLANE + 7, x)

    gather_pair(2)
    chain(5)
    tables_far()
    inv_v[...] = inv_f[...].astype(BF16)
    chain(6)
    pass_on(1)
    gather_pair(0)

    @pl.when((y == 3) & (z < PLANES - 1))
    def _():
        pl.semaphore_wait(ready_edge, 2)

    halo_copy = pltpu.make_async_remote_copy(
        src_ref=vals.at[pl.ds(3 * LEAF, LEAF)],
        dst_ref=halo,
        send_sem=hsem.at[0],
        recv_sem=hsem.at[1],
        device_id=(t + 1, x),
        device_id_type=MESH,
    )

    def ctx_copy(part):
        rows = pl.ds(0, 48) if part == 0 else pl.ds(48, 16)
        return pltpu.make_async_remote_copy(
            src_ref=ctx_out.at[rows],
            dst_ref=ctx_in.at[rows],
            send_sem=csem.at[0, part],
            recv_sem=csem.at[1, part],
            device_id=(t + 1, x),
            device_id_type=MESH,
        )

    summing = red_m[0, :RANK, :]

    def gathered(level, source_two, source_three=None):
        return dot(summing, coupled(level, source_two, source_three))

    wait_relayed(0)
    values_of(2)
    ctx_out[:48] = jnp.concatenate(
        [moms[2, 0:16, :], moms[3, 0:16, :], moms[2, 16:32, :] + moms[3, 16:32, :]], 0
    ).astype(BF16)

    @pl.when(t < PLANES * PLANE - 1)
    def _():
        halo_copy.start()
        ctx_copy(0).start()

    spectra(2)
    gates_of(2)
    near_rows((3,))

    wait_relayed(1)
    values_of(0)

    total = moms[0, 32:48, :] + moms[1, 32:48, :] + moms[2, 32:48, :] + moms[3, 32:48, :]
    m2[own] = total.astype(BF16)

    def plane_copy(k):
        return pltpu.make_async_remote_copy(
            src_ref=m2.at[own],
            dst_ref=m2.at[own],
            send_sem=s1,
            recv_sem=r1,
            device_id=(z * PLANE + lax.rem(own + k, PLANE), x),
            device_id_type=MESH,
        )

    plane_all = pltpu.make_async_remote_copy(
        src_ref=m2.at[pl.ds(0, PLANE - 1)],
        dst_ref=m2.at[pl.ds(0, PLANE - 1)],
        send_sem=s1,
        recv_sem=r1,
        device_id=(t, right),
        device_id_type=MESH,
    )

    for k in range(1, PLANE):
        plane_copy(k).start()

    def next_plane_copy(target, source):
        return pltpu.make_async_remote_copy(
            src_ref=m2.at[own],
            dst_ref=m2_prev.at[source],
            send_sem=s1p.at[target],
            recv_sem=r1p.at[source],
            device_id=((z + 1) * PLANE + target, x),
            device_id_type=MESH,
        )

    @pl.when((y == 3) & (z < PLANES - 1))
    def _():
        for target in range(2):
            next_plane_copy(target, core).start()

    ctx_out[48:] = (moms[0, 16:32, :] + moms[1, 16:32, :]).astype(BF16)

    @pl.when(t < PLANES * PLANE - 1)
    def _():
        ctx_copy(1).start()

    gates_of(0)
    spectra(0)
    near_rows((1, 2))

    plane_all.wait_recv()
    stack = m2[...].reshape(PLANE * RANK, WIDTH)
    lifted = dot(lift_m[...], jnp.concatenate([stack, stack], 0))
    pack_out[...] = lifted[:80].astype(BF16)


    def pack_copy(rows):
        return pltpu.make_async_remote_copy(
            src_ref=pack_out.at[pl.ds(0, rows)],
            dst_ref=pack_in.at[pl.ds(0, rows)],
            send_sem=s2,
            recv_sem=r2,
            device_id=(t + PLANE, x),
            device_id_type=MESH,
        )

    def five_copy(k):
        return pltpu.make_async_remote_copy(
            src_ref=pack_out.at[pl.ds(64, RANK)],
            dst_ref=m5_in.at[k],
            send_sem=s5.at[k],
            recv_sem=r5.at[k],
            device_id=(t + k * PLANE, x),
            device_id_type=MESH,
        )

    chain(7)

    for k in range(PLANES - 1, 1, -1):

        @pl.when(z + k < PLANES)
        def _():
            five_copy(k).start()

    @pl.when((z < PLANES - 1) & (y == 0))
    def _():
        pack_copy(48).start()

    @pl.when((z < PLANES - 1) & (y == 1))
    def _():
        pack_copy(64).start()

    @pl.when((z < PLANES - 1) & (y >= 2))
    def _():
        pack_copy(32).start()

    @pl.when(t > 0)
    def _():
        halo_copy.wait_recv()

    spec[LEAVES] = dot(fwd_v[...], jnp.concatenate([halo[...], halo[...]], 0))
    near_rows((0,))

    @pl.when(t > 0)
    def _():
        ctx_copy(0).wait_recv()
        ctx_copy(1).wait_recv()

    prev = ctx_in[...].astype(F32)
    far0[0] = gathered(0, prev[0:16])
    far0[1] = gathered(0, prev[16:32], prev[0:16])
    far0[2] = gathered(0, moms[0, 0:16, :])
    far0[3] = gathered(0, moms[1, 0:16, :], moms[0, 0:16, :])
    far1[0] = gathered(1, prev[48:64])
    far1[1] = gathered(1, prev[32:48], prev[48:64])

    gather_sent = g.at[pl.ds(0, 3)]
    pltpu.make_async_remote_copy(
        src_ref=gather_sent,
        dst_ref=gather_sent,
        send_sem=gsend,
        recv_sem=drecv.at[0, 0],
        device_id=(t, right),
        device_id_type=MESH,
    ).wait_send()

    plane_all.wait_send()

    @pl.when(t < PLANES * PLANE - 1)
    def _():
        halo_copy.wait_send()
        ctx_copy(0).wait_send()
        ctx_copy(1).wait_send()

    @pl.when((y == 3) & (z < PLANES - 1))
    def _():
        for target in range(2):
            next_plane_copy(target, core).wait_send()

    @pl.when((y == 0) & (z > 0))
    def _():
        for source in range(2):
            next_plane_copy(source, source).wait_recv()

    def reduced(k, source_two, source_three):
        return dot(red_m[k], coupled(2 + k, source_two, source_three))

    at = 2 * jnp.maximum(y - 1, 0)
    inside = y > 0
    two = jnp.where(inside, m2[at + core], m2_prev[core]).astype(F32)
    three = jnp.where(inside, m2[at], m2_prev[0]).astype(F32) * core.astype(F32)
    expansion = reduced(0, two, three)

    @pl.when((z > 0) & (y == 0))
    def _():
        pack_copy(48).wait_recv()

    @pl.when((z > 0) & (y == 1))
    def _():
        pack_copy(64).wait_recv()

    @pl.when((z > 0) & (y >= 2))
    def _():
        pack_copy(32).wait_recv()

    odd = lax.rem(y, 2)
    lower = y < 2
    here = jnp.where(odd == 1, lifted[96:112], lifted[80:96])
    coming = pack_in[pl.ds(pl.multiple_of(32 + odd * RANK, RANK), RANK), :].astype(F32)
    two = jnp.where(lower, coming, here)
    three = jnp.where(lower, pack_in[32:48, :].astype(F32), lifted[80:96]) * odd.astype(F32)
    expansion = expansion + reduced(1, two, three)
    odd = lax.div(y, 2)
    two = pack_in[pl.ds(pl.multiple_of(odd * RANK, RANK), RANK), :].astype(F32)
    three = pack_in[0:16, :].astype(F32) * odd.astype(F32)
    expansion = expansion + reduced(2, two, three)

    for k in range(2, PLANES):

        @pl.when(z >= k)
        def _():
            five_copy(k).wait_recv()

    odd = lax.rem(z, 2)
    expansion = expansion + reduced(
        3, m5_in[2].astype(F32), m5_in[3].astype(F32) * odd.astype(F32)
    )
    pad = jnp.zeros((64, WIDTH), BF16)

    def sixth(base):
        pair = [m5_in[base], m5_in[base - 1]]
        return dot(six_m[...], jnp.concatenate(pair + pair + [pad], 0))

    odd_six = lax.rem(lax.div(z, 2), 2)
    expansion = expansion + reduced(
        4, sixth(4 + odd), sixth(6 + odd) * odd_six.astype(F32)
    )

    expansion = expansion[:RANK] + expansion[RANK:]

    def out_copy(leaf):
        rows = leaf_rows(leaf)
        return pltpu.make_async_copy(out_v.at[rows], out.at[rows], osem.at[leaf])

    for leaf in range(LEAVES):
        rows = leaf_rows(leaf)
        high, low = halves(jnp.concatenate([far0[leaf], far1[leaf // 2], expansion], 0))
        whole = jnp.concatenate([high, low, high, jnp.zeros((112, WIDTH), BF16)], 0)
        combined = near[rows, :] + dot(far_m[leaf], whole)
        out_v[rows, :] = (gate[rows, :] * combined).astype(BF16)
        out_copy(leaf).start()

    @pl.when((z < PLANES - 1) & (y == 0))
    def _():
        pack_copy(48).wait_send()

    @pl.when((z < PLANES - 1) & (y == 1))
    def _():
        pack_copy(64).wait_send()

    @pl.when((z < PLANES - 1) & (y >= 2))
    def _():
        pack_copy(32).wait_send()

    for k in range(2, PLANES):

        @pl.when(z + k < PLANES)
        def _():
            five_copy(k).wait_send()

    for leaf in range(LEAVES):
        out_copy(leaf).wait()


def per_device(
    tokens,
    norm_gain,
    w_value,
    w_gate,
    phi_taps,
    tap_coeff,
    skip_gain,
    basis_up,
    basis_down,
    lift_maps,
    spread_maps,
    couplings,
):
    forward, inverse = transform_tables()
    in_hbm = pl.BlockSpec(memory_space=pltpu.HBM)
    frames = LEAF * LEAVES
    vmem = pltpu.VMEM
    dma = pltpu.SemaphoreType.DMA
    scratch = [
        vmem((4, frames, WIDTH), BF16),
        vmem((4, WIDTH, 2 * WIDTH), BF16),
        vmem((1, 4 * WIDTH), F32),
        vmem(phi_taps.shape, F32),
        vmem(tap_coeff.shape, F32),
        vmem((1, WIDTH), F32),
        vmem(basis_up.shape, F32),
        vmem(basis_down.shape, F32),
        vmem(lift_maps.shape, F32),
        vmem(spread_maps.shape, F32),
        vmem(couplings.shape, F32),
        vmem(forward.shape, F32),
        vmem(inverse.shape, F32),
        vmem((2 * LEAF, 2 * LEAF), BF16),
        vmem((LEAF, 2 * LEAF), BF16),
        vmem((frames, WIDTH), BF16),
        vmem((LEAF, WIDTH), BF16),
        vmem((frames, WIDTH), F32),
        vmem((frames, WIDTH), F32),
        vmem((LEAVES + 1, 2 * LEAF, WIDTH), F32),
        vmem((4, LEAF, WIDTH), F32),
        vmem((LEAVES, 48, 2 * LEAF), BF16),
        vmem((112, 256), BF16),
        vmem((RANK, 128), BF16),
        vmem((LEAVES, LEAF, LEAF), BF16),
        vmem((5, 2 * RANK, LEAF), BF16),
        vmem((LEAVES, 48, WIDTH), F32),
        vmem((PLANE, RANK, WIDTH), BF16),
        vmem((2, RANK, WIDTH), BF16),
        vmem((64, WIDTH), BF16),
        vmem((64, WIDTH), BF16),
        vmem((80, WIDTH), BF16),
        vmem((64, WIDTH), BF16),
        vmem((PLANES, RANK, WIDTH), BF16),
        vmem((LEAVES, RANK, WIDTH), F32),
        vmem((2, RANK, WIDTH), F32),
        vmem((frames, WIDTH), BF16),
        vmem((frames, 2 * WIDTH), F32),
        vmem((frames, WIDTH // 2), F32),
        dma((20,)),
        dma(()),
        dma((2, 2)),
        dma((2, 2)),
        dma((2,)),
        dma((2, 2)),
        dma(()),
        dma(()),
        dma((2,)),
        dma((2,)),
        dma(()),
        dma(()),
        dma((PLANES,)),
        dma((PLANES,)),
        pltpu.SemaphoreType.REGULAR,
        pltpu.SemaphoreType.REGULAR,
        pltpu.SemaphoreType.REGULAR,
        pltpu.SemaphoreType.REGULAR,
        dma((LEAVES,)),
    ]
    return pl.pallas_call(
        body,
        out_shape=jax.ShapeDtypeStruct(tokens.shape, BF16),
        in_specs=[in_hbm] * 14,
        out_specs=in_hbm,
        scratch_shapes=scratch,
        compiler_params=pltpu.CompilerParams(
            collective_id=0, has_side_effects=True, vmem_limit_bytes=60 * 1024 * 1024
        ),
        cost_estimate=pl.CostEstimate(flops=4 * 10**9, bytes_accessed=8 * 10**6, transcendentals=10**6),
    )(
        tokens,
        norm_gain.reshape(1, -1),
        w_value,
        w_gate,
        phi_taps,
        tap_coeff,
        skip_gain.reshape(1, -1),
        basis_up,
        basis_down,
        lift_maps,
        spread_maps,
        couplings,
        jnp.asarray(forward),
        jnp.asarray(inverse),
    )


def solution(mesh):
    placed = (
        P("tm", "chan"),
        P(),
        P(None, "chan"),
        P(None, "chan"),
        P(),
        P(None, "chan"),
        P("chan"),
        P(),
        P(),
        P(),
        P(),
        P(None, None, None, None, "chan"),
    )
    return jax.shard_map(
        per_device, mesh=mesh, in_specs=placed, out_specs=P("tm", "chan"), check_vma=False
    )
```

```python
import jax
import jax.numpy as jnp
import numpy as np
from jax import lax
from jax.experimental import pallas as pl
from jax.experimental.pallas import tpu as pltpu
from jax.sharding import PartitionSpec as P

MESH = pl.DeviceIdType.MESH
F32 = jnp.float32
BF16 = jnp.bfloat16

LEAF = 256
LEAVES = 4
WIDTH = 256
RANK = 16
PLANES = 8
PLANE = 8


def transform_tables():
    odd = np.arange(LEAF)[:, None] + 0.5
    angle = 2 * np.pi * odd * np.arange(LEAF)[None, :] / (2 * LEAF)
    forward = np.concatenate([np.cos(angle), -np.sin(angle)], 0)
    return forward.astype(np.float32), (forward.T / LEAF).astype(np.float32)


def dot(left, right):
    return jnp.dot(left, right, preferred_element_type=F32)


def halves(value):
    high = value.astype(BF16)
    return high, (value - high.astype(F32)).astype(BF16)


def fine_dot(left, right):
    left_high, left_low = halves(left)
    right_high, right_low = halves(right)
    return dot(left_high, right_high) + dot(left_high, right_low) + dot(left_low, right_high)


def place_dot(left, right):
    left_high, left_low = halves(left)
    ones = right.astype(BF16)
    return dot(left_high, ones) + dot(left_low, ones)


def selector(lanes, period, shift, limit):
    row = lax.broadcasted_iota(jnp.int32, (RANK, lanes), 0)
    lane = lax.broadcasted_iota(jnp.int32, (RANK, lanes), 1)
    return ((lax.rem(lane, period) == row + shift) & (lane < limit)).astype(F32)


def body(
    tok, gain, w_value, w_gate, phi, coeff, skip, up, down, lift, spread, coup, fwd, inv,
    out,
    g, w, gain_v, phi_v, coeff_v, skip_v, up_v, down_v, lift_v, spread_v, coup_v, fwd_f, inv_f, fwd_v, inv_v,
    vals, halo, gate, near, spec, khat, mom_m, lift_m, six_m, far_m, red_m, moms,
    m2, m2_prev, ctx_out, ctx_in, pack_out, pack_in, m5_in, far0, far1, out_v, parts, part_squares,
    local_sem, gsend, drecv, rrecv, hsem, csem, s1, r1, s1p, r1p, s2, r2, s5, r5, ready_plane, ready_next, ready_edge, ready_later, osem,
):
    t = lax.axis_index("tm")
    x = lax.axis_index("chan")
    core = lax.rem(t, 2)
    y = lax.rem(lax.div(t, 2), 4)
    z = lax.div(t, PLANE)
    own = lax.rem(t, PLANE)
    rank = 2 * y + 1 - core
    right, left = lax.rem(x + 1, 4), lax.rem(x + 3, 4)

    barrier = pltpu.get_barrier_semaphore()

    def signal(semaphore, frames, chans):
        pl.semaphore_signal(semaphore, inc=1, device_id=(frames, chans), device_id_type=MESH)

    signal(barrier, t, right)
    signal(barrier, t, left)

    @pl.when(z < PLANES - 1)
    def _():
        signal(barrier, t + PLANE, x)

    m2_prev[...] = jnp.zeros_like(m2_prev)
    ctx_in[...] = jnp.zeros_like(ctx_in)
    pack_in[...] = jnp.zeros_like(pack_in)
    m5_in[...] = jnp.zeros_like(m5_in)
    halo[...] = jnp.zeros_like(halo)

    def at_rank(other):
        return z * PLANE + 2 * lax.div(other, 2) + 1 - lax.rem(other, 2)

    for k in range(1, PLANE):

        @pl.when(rank + k < PLANE)
        def _():
            signal(barrier, at_rank(rank + k), x)

    pl.semaphore_wait(barrier, 2 + rank + jnp.where(z > 0, 1, 0))

    owners = [x, left, right, lax.rem(x + 2, 4)]

    def leaf_rows(leaf):
        return pl.ds(leaf * LEAF if isinstance(leaf, int) else pl.multiple_of(leaf * LEAF, LEAF), LEAF)

    def direct(group, way):
        rows = pl.ds((1 - group) * 2 * LEAF, 2 * LEAF)
        return pltpu.make_async_remote_copy(
            src_ref=tok.at[rows],
            dst_ref=g.at[1 + way, rows],
            send_sem=gsend,
            recv_sem=drecv.at[way, group],
            device_id=(t, left if way else right),
            device_id_type=MESH,
        )

    def relay(group, way):
        rows = leaf_rows((1 - group) * 2 + way)
        return pltpu.make_async_remote_copy(
            src_ref=g.at[1 + way, rows],
            dst_ref=g.at[3, rows],
            send_sem=gsend,
            recv_sem=rrecv.at[way, group],
            device_id=(t, left if way else right),
            device_id_type=MESH,
        )

    def send_direct(group):
        for way in range(2):
            direct(group, way).start()

    def pass_on(group):
        for way in range(2):
            direct(group, way).wait_recv()
            relay(group, way).start()

    def wait_relayed(group):
        for way in range(2):
            relay(group, way).wait_recv()

    def tables_near():
        for name in ("phi", "coeff", "fwd"):
            copies[name].wait()
        fwd_v[...] = jnp.concatenate(halves(fwd_f[...]), 1)
        taps = phi_v[...].astype(BF16).astype(F32).T.astype(BF16)
        coeff_high, coeff_low = halves(coeff_v[...])
        kernel_taps = dot(taps, coeff_high) + dot(taps, coeff_low)
        both = jnp.concatenate([kernel_taps[:LEAF], kernel_taps[LEAF:]], 1)
        high, low = halves(both)
        hat = dot(fwd_v[...], jnp.concatenate([high, high], 0)) + dot(fwd_v[:, :LEAF], low)
        a_re, a_im = hat[:LEAF, :WIDTH], hat[LEAF:, :WIDTH]
        b_re, b_im = hat[:LEAF, WIDTH:], hat[LEAF:, WIDTH:]
        row = lax.broadcasted_iota(jnp.int32, (LEAF, WIDTH), 0)
        sign = (1 - 2 * lax.rem(row, 2)).astype(F32)
        khat[0] = a_re
        khat[1] = a_im
        khat[2] = b_re - sign * a_im
        khat[3] = b_im + sign * a_re

    def tables_moments():
        copies["up"].wait()
        copies["lift"].wait()
        base = up_v[...]
        first = [fine_dot(lift_v[0, k], base) for k in range(2)]
        for leaf in range(LEAVES):
            second = fine_dot(lift_v[1, leaf // 2], first[leaf % 2])
            high, low = halves(jnp.concatenate([base, first[leaf % 2], second], 0))
            mom_m[leaf] = jnp.concatenate([high, low], 1)

    def tables_lift():
        def pair(level):
            return place_dot(lift_v[level, 0], selector(128, 32, 0, 128)) + place_dot(
                lift_v[level, 1], selector(128, 32, 16, 128)
            )

        def blocks(level, copies_of):
            rows = jnp.concatenate([pair(level)] * copies_of, 0)
            row = lax.broadcasted_iota(jnp.int32, rows.shape, 0)
            lane = lax.broadcasted_iota(jnp.int32, rows.shape, 1)
            return jnp.where(lax.div(row, RANK) == lax.div(lane, 2 * RANK), rows, 0.0)

        three = blocks(2, 8)
        four = fine_dot(blocks(3, 2), three)
        five = fine_dot(blocks(4, 1), jnp.concatenate([four, jnp.zeros((96, 128), F32)], 0))
        whole = jnp.concatenate([four, three[32:64], five, three[:32]], 0)
        high, low = halves(whole)
        lift_m[...] = jnp.concatenate([high, low], 1)
        six = place_dot(lift_v[5, 0], selector(128, 32, 0, 64)) + place_dot(
            lift_v[5, 1], selector(128, 32, 16, 64)
        )
        high = six.astype(BF16).astype(F32)
        lane = lax.broadcasted_iota(jnp.int32, six.shape, 1)
        six_m[...] = jnp.where(lane < 32, high, six - high).astype(BF16)

    def tables_far():
        copies["spread"].wait()
        copies["down"].wait()
        row = lax.broadcasted_iota(jnp.int32, (RANK, LEAF), 0)
        lane = lax.broadcasted_iota(jnp.int32, (RANK, LEAF), 1)
        summing = (lax.div(lane, RANK) == row).astype(F32)
        chain = None
        for k in range(5):
            if k > 0:
                step = spread_v[1 + k, lax.rem(lax.div(t, 2 ** (k - 1)), 2)]
                chain = step if k == 1 else fine_dot(chain, step)
            high, low = halves(summing if k == 0 else place_dot(chain, summing))
            red_m[k] = jnp.concatenate([high, low], 0)
        turned = down_v[...].T
        for leaf in range(LEAVES):
            near_step = spread_v[0, leaf % 2]
            both_steps = fine_dot(near_step, spread_v[1, leaf // 2])
            mix = (
                selector(LEAF, 48, 0, 144)
                + place_dot(near_step, selector(LEAF, 48, 16, 144))
                + place_dot(both_steps, selector(LEAF, 48, 32, 144))
            )
            whole = fine_dot(turned, mix)
            high = whole.astype(BF16).astype(F32)
            lane_at = lax.broadcasted_iota(jnp.int32, whole.shape, 1)
            far_m[leaf] = jnp.where(lane_at < 96, high, whole - high).astype(BF16)

    def pair_rows(first):
        return pl.ds(first * LEAF, 2 * LEAF)

    def scaled_rows(first, slots):
        rows = pair_rows(first)
        squares = jnp.zeros((2 * LEAF, WIDTH), F32)
        columns = []
        for slot in slots:
            tokens = g[slot, rows, :].astype(F32)
            squares = squares + tokens * tokens
            scale = gain_v[:, pl.ds(pl.multiple_of(owners[slot] * WIDTH, WIDTH), WIDTH)]
            columns.append((tokens * scale).astype(BF16))
        return jnp.concatenate(columns, 1), squares

    def gather_pair(first):
        scaled, squares = scaled_rows(first, (0, 1, 2))
        parts[pair_rows(first), :] = dot(scaled, w[:3].reshape(3 * WIDTH, 2 * WIDTH))
        part_squares[pair_rows(first), :] = squares[:, : WIDTH // 2] + squares[:, WIDTH // 2 :]

    def values_of(first):
        rows = pair_rows(first)
        scaled, squares = scaled_rows(first, (3,))
        squares = squares[:, : WIDTH // 2] + squares[:, WIDTH // 2 :] + part_squares[rows, :]
        inverse = lax.rsqrt(jnp.sum(squares, axis=1, keepdims=True) / 1024 + 1e-06)
        part_squares[rows, :] = jnp.broadcast_to(inverse, squares.shape)
        value = ((parts[rows, :WIDTH] + dot(scaled, w[3, :, :WIDTH])) * inverse).astype(BF16)
        vals[rows, :] = value
        for k in range(2):
            leaf_value = value[k * LEAF : (k + 1) * LEAF]
            moms[first + k] = dot(mom_m[first + k], jnp.concatenate([leaf_value, leaf_value], 0))

    def gates_of(first):
        rows = pair_rows(first)
        scaled, _ = scaled_rows(first, (3,))
        half = 0.5 * part_squares[rows, :]
        sums = parts[rows, WIDTH:] + dot(scaled, w[3, :, WIDTH:])
        gate[rows, :] = 0.5 * jnp.tanh(sums * jnp.concatenate([half, half], 1)) + 0.5

    def spectra(first):
        both = jnp.concatenate([vals[leaf_rows(first), :], vals[leaf_rows(first + 1), :]], 1)
        result = dot(fwd_v[...], jnp.concatenate([both, both], 0))
        spec[first] = result[:, :WIDTH]
        spec[first + 1] = result[:, WIDTH:]

    def near_rows(leaves):
        columns = []
        for leaf in leaves:
            before = leaf - 1 if leaf > 0 else LEAVES
            a_re, a_im = spec[leaf, :LEAF, :], spec[leaf, LEAF:, :]
            b_re, b_im = spec[before, :LEAF, :], spec[before, LEAF:, :]
            out_re = khat[0] * a_re - khat[1] * a_im + khat[2] * b_re - khat[3] * b_im
            out_im = khat[0] * a_im + khat[1] * a_re + khat[2] * b_im + khat[3] * b_re
            columns.append(jnp.concatenate([out_re, out_im], 0).astype(BF16))
        total = dot(inv_v[...], jnp.concatenate(columns, 1))
        for k, leaf in enumerate(leaves):
            rows = leaf_rows(leaf)
            direct_term = skip_v[...] * vals[rows, :].astype(F32)
            near[rows, :] = total[:, k * WIDTH : (k + 1) * WIDTH] + direct_term

    def coupled(level, source_two, source_three):
        product = coup_v[level, 0] * source_two[None]
        if source_three is not None:
            product = product + coup_v[level, 1] * source_three[None]
        return product.reshape(RANK * RANK, WIDTH).astype(BF16)

    send_direct(0)

    copies = {}

    def local(name, source, target):
        copies[name] = pltpu.make_async_copy(source, target, local_sem.at[len(copies)])
        copies[name].start()

    local("tok", tok, g.at[0])
    for slot in range(4):
        rows = pl.ds(pl.multiple_of(owners[slot] * WIDTH, WIDTH), WIDTH)
        local(("v", slot), w_value.at[rows], w.at[slot, :, pl.ds(0, WIDTH)])
        local(("g", slot), w_gate.at[rows], w.at[slot, :, pl.ds(WIDTH, WIDTH)])
    for name, source, target in (
        ("gain", gain, gain_v),
        ("phi", phi, phi_v),
        ("coeff", coeff, coeff_v),
        ("fwd", fwd, fwd_f),
        ("skip", skip, skip_v),
        ("up", up, up_v),
        ("down", down, down_v),
        ("lift", lift, lift_v),
        ("spread", spread, spread_v),
        ("inv", inv, inv_f),
        ("coup", coup, coup_v),
    ):
        local(name, source, target)

    @pl.when(z > 0)
    def _():
        signal(ready_next, t - PLANE, x)

    for k in range(1, PLANE):

        @pl.when(rank >= k)
        def _():
            signal(ready_plane, at_rank(rank - k), x)

    def chain(place):
        @pl.when(z == PLANES - 1 - place)
        def _():
            if not isinstance(place, int) or place > 0:
                pl.semaphore_wait(ready_later, 1)
            if not isinstance(place, int) or place < PLANES - 1:
                signal(ready_later, t - PLANE, x)

    chain(0)
    tables_near()
    send_direct(1)
    chain(1)
    tables_moments()
    chain(2)
    tables_lift()
    chain(3)
    for slot in range(4):
        copies["v", slot].wait()
        copies["g", slot].wait()
    for name in ("tok", "gain", "skip", "coup", "inv"):
        copies[name].wait()
    pass_on(0)
    chain(4)

    @pl.when(rank < PLANE - 1)
    def _():
        pl.semaphore_wait(ready_plane, PLANE - 1 - rank)

    @pl.when(z < PLANES - 1)
    def _():
        pl.semaphore_wait(ready_next, 1)

        @pl.when(y == 0)
        def _():
            signal(ready_edge, z * PLANE + 6, x)
            signal(ready_edge, z * PLANE + 7, x)

    gather_pair(2)
    chain(5)
    tables_far()
    inv_v[...] = inv_f[...].astype(BF16)
    chain(6)
    pass_on(1)
    gather_pair(0)

    @pl.when((y == 3) & (z < PLANES - 1))
    def _():
        pl.semaphore_wait(ready_edge, 2)

    halo_copy = pltpu.make_async_remote_copy(
        src_ref=vals.at[pl.ds(3 * LEAF, LEAF)],
        dst_ref=halo,
        send_sem=hsem.at[0],
        recv_sem=hsem.at[1],
        device_id=(t + 1, x),
        device_id_type=MESH,
    )

    def ctx_copy(part):
        rows = pl.ds(0, 48) if part == 0 else pl.ds(48, 16)
        return pltpu.make_async_remote_copy(
            src_ref=ctx_out.at[rows],
            dst_ref=ctx_in.at[rows],
            send_sem=csem.at[0, part],
            recv_sem=csem.at[1, part],
            device_id=(t + 1, x),
            device_id_type=MESH,
        )

    summing = red_m[0, :RANK, :]

    def gathered(level, source_two, source_three=None):
        return dot(summing, coupled(level, source_two, source_three))

    wait_relayed(0)
    values_of(2)
    ctx_out[:48] = jnp.concatenate(
        [moms[2, 0:16, :], moms[3, 0:16, :], moms[2, 16:32, :] + moms[3, 16:32, :]], 0
    ).astype(BF16)

    @pl.when(t < PLANES * PLANE - 1)
    def _():
        halo_copy.start()
        ctx_copy(0).start()

    spectra(2)
    gates_of(2)
    near_rows((3,))

    wait_relayed(1)
    values_of(0)

    total = moms[0, 32:48, :] + moms[1, 32:48, :] + moms[2, 32:48, :] + moms[3, 32:48, :]
    m2[own] = total.astype(BF16)

    def plane_copy(k):
        return pltpu.make_async_remote_copy(
            src_ref=m2.at[own],
            dst_ref=m2.at[own],
            send_sem=s1,
            recv_sem=r1,
            device_id=(z * PLANE + lax.rem(own + k, PLANE), x),
            device_id_type=MESH,
        )

    plane_all = pltpu.make_async_remote_copy(
        src_ref=m2.at[pl.ds(0, PLANE - 1)],
        dst_ref=m2.at[pl.ds(0, PLANE - 1)],
        send_sem=s1,
        recv_sem=r1,
        device_id=(t, right),
        device_id_type=MESH,
    )

    for k in range(1, PLANE):
        plane_copy(k).start()

    def next_plane_copy(target, source):
        return pltpu.make_async_remote_copy(
            src_ref=m2.at[own],
            dst_ref=m2_prev.at[source],
            send_sem=s1p.at[target],
            recv_sem=r1p.at[source],
            device_id=((z + 1) * PLANE + target, x),
            device_id_type=MESH,
        )

    @pl.when((y == 3) & (z < PLANES - 1))
    def _():
        for target in range(2):
            next_plane_copy(target, core).start()

    ctx_out[48:] = (moms[0, 16:32, :] + moms[1, 16:32, :]).astype(BF16)

    @pl.when(t < PLANES * PLANE - 1)
    def _():
        ctx_copy(1).start()

    gates_of(0)
    spectra(0)
    near_rows((1, 2))

    plane_all.wait_recv()
    stack = m2[...].reshape(PLANE * RANK, WIDTH)
    lifted = dot(lift_m[...], jnp.concatenate([stack, stack], 0))
    pack_out[...] = lifted[:80].astype(BF16)


    def pack_copy(rows):
        return pltpu.make_async_remote_copy(
            src_ref=pack_out.at[pl.ds(0, rows)],
            dst_ref=pack_in.at[pl.ds(0, rows)],
            send_sem=s2,
            recv_sem=r2,
            device_id=(t + PLANE, x),
            device_id_type=MESH,
        )

    def five_copy(k):
        return pltpu.make_async_remote_copy(
            src_ref=pack_out.at[pl.ds(64, RANK)],
            dst_ref=m5_in.at[k],
            send_sem=s5.at[k],
            recv_sem=r5.at[k],
            device_id=(t + k * PLANE, x),
            device_id_type=MESH,
        )

    chain(7)

    for k in range(PLANES - 1, 1, -1):

        @pl.when(z + k < PLANES)
        def _():
            five_copy(k).start()

    @pl.when((z < PLANES - 1) & (y == 0))
    def _():
        pack_copy(48).start()

    @pl.when((z < PLANES - 1) & (y == 1))
    def _():
        pack_copy(64).start()

    @pl.when((z < PLANES - 1) & (y >= 2))
    def _():
        pack_copy(32).start()

    @pl.when(t > 0)
    def _():
        halo_copy.wait_recv()

    spec[LEAVES] = dot(fwd_v[...], jnp.concatenate([halo[...], halo[...]], 0))
    near_rows((0,))

    @pl.when(t > 0)
    def _():
        ctx_copy(0).wait_recv()
        ctx_copy(1).wait_recv()

    prev = ctx_in[...].astype(F32)
    far0[0] = gathered(0, prev[0:16])
    far0[1] = gathered(0, prev[16:32], prev[0:16])
    far0[2] = gathered(0, moms[0, 0:16, :])
    far0[3] = gathered(0, moms[1, 0:16, :], moms[0, 0:16, :])
    far1[0] = gathered(1, prev[48:64])
    far1[1] = gathered(1, prev[32:48], prev[48:64])

    gather_sent = g.at[pl.ds(0, 3)]
    pltpu.make_async_remote_copy(
        src_ref=gather_sent,
        dst_ref=gather_sent,
        send_sem=gsend,
        recv_sem=drecv.at[0, 0],
        device_id=(t, right),
        device_id_type=MESH,
    ).wait_send()

    plane_all.wait_send()

    @pl.when(t < PLANES * PLANE - 1)
    def _():
        halo_copy.wait_send()
        ctx_copy(0).wait_send()
        ctx_copy(1).wait_send()

    @pl.when((y == 3) & (z < PLANES - 1))
    def _():
        for target in range(2):
            next_plane_copy(target, core).wait_send()

    @pl.when((y == 0) & (z > 0))
    def _():
        for source in range(2):
            next_plane_copy(source, source).wait_recv()

    def reduced(k, source_two, source_three):
        return dot(red_m[k], coupled(2 + k, source_two, source_three))

    at = 2 * jnp.maximum(y - 1, 0)
    inside = y > 0
    two = jnp.where(inside, m2[at + core], m2_prev[core]).astype(F32)
    three = jnp.where(inside, m2[at], m2_prev[0]).astype(F32) * core.astype(F32)
    expansion = reduced(0, two, three)

    for k in range(2, PLANES):

        @pl.when(z >= k)
        def _():
            five_copy(k).wait_recv()

    odd = lax.rem(z, 2)
    expansion = expansion + reduced(
        3, m5_in[2].astype(F32), m5_in[3].astype(F32) * odd.astype(F32)
    )
    pad = jnp.zeros((64, WIDTH), BF16)

    def sixth(base):
        pair = [m5_in[base], m5_in[base - 1]]
        return dot(six_m[...], jnp.concatenate(pair + pair + [pad], 0))

    odd_six = lax.rem(lax.div(z, 2), 2)
    expansion = expansion + reduced(
        4, sixth(4 + odd), sixth(6 + odd) * odd_six.astype(F32)
    )

    @pl.when((z > 0) & (y == 0))
    def _():
        pack_copy(48).wait_recv()

    @pl.when((z > 0) & (y == 1))
    def _():
        pack_copy(64).wait_recv()

    @pl.when((z > 0) & (y >= 2))
    def _():
        pack_copy(32).wait_recv()

    odd = lax.rem(y, 2)
    lower = y < 2
    here = jnp.where(odd == 1, lifted[96:112], lifted[80:96])
    coming = pack_in[pl.ds(pl.multiple_of(32 + odd * RANK, RANK), RANK), :].astype(F32)
    two = jnp.where(lower, coming, here)
    three = jnp.where(lower, pack_in[32:48, :].astype(F32), lifted[80:96]) * odd.astype(F32)
    expansion = expansion + reduced(1, two, three)
    odd = lax.div(y, 2)
    two = pack_in[pl.ds(pl.multiple_of(odd * RANK, RANK), RANK), :].astype(F32)
    three = pack_in[0:16, :].astype(F32) * odd.astype(F32)
    expansion = expansion + reduced(2, two, three)

    expansion = expansion[:RANK] + expansion[RANK:]

    def out_copy(leaf):
        rows = leaf_rows(leaf)
        return pltpu.make_async_copy(out_v.at[rows], out.at[rows], osem.at[leaf])

    for leaf in range(LEAVES):
        rows = leaf_rows(leaf)
        high, low = halves(jnp.concatenate([far0[leaf], far1[leaf // 2], expansion], 0))
        whole = jnp.concatenate([high, low, high, jnp.zeros((112, WIDTH), BF16)], 0)
        combined = near[rows, :] + dot(far_m[leaf], whole)
        out_v[rows, :] = (gate[rows, :] * combined).astype(BF16)
        out_copy(leaf).start()

    @pl.when((z < PLANES - 1) & (y == 0))
    def _():
        pack_copy(48).wait_send()

    @pl.when((z < PLANES - 1) & (y == 1))
    def _():
        pack_copy(64).wait_send()

    @pl.when((z < PLANES - 1) & (y >= 2))
    def _():
        pack_copy(32).wait_send()

    for k in range(2, PLANES):

        @pl.when(z + k < PLANES)
        def _():
            five_copy(k).wait_send()

    for leaf in range(LEAVES):
        out_copy(leaf).wait()


def per_device(
    tokens,
    norm_gain,
    w_value,
    w_gate,
    phi_taps,
    tap_coeff,
    skip_gain,
    basis_up,
    basis_down,
    lift_maps,
    spread_maps,
    couplings,
):
    forward, inverse = transform_tables()
    in_hbm = pl.BlockSpec(memory_space=pltpu.HBM)
    frames = LEAF * LEAVES
    vmem = pltpu.VMEM
    dma = pltpu.SemaphoreType.DMA
    scratch = [
        vmem((4, frames, WIDTH), BF16),
        vmem((4, WIDTH, 2 * WIDTH), BF16),
        vmem((1, 4 * WIDTH), F32),
        vmem(phi_taps.shape, F32),
        vmem(tap_coeff.shape, F32),
        vmem((1, WIDTH), F32),
        vmem(basis_up.shape, F32),
        vmem(basis_down.shape, F32),
        vmem(lift_maps.shape, F32),
        vmem(spread_maps.shape, F32),
        vmem(couplings.shape, F32),
        vmem(forward.shape, F32),
        vmem(inverse.shape, F32),
        vmem((2 * LEAF, 2 * LEAF), BF16),
        vmem((LEAF, 2 * LEAF), BF16),
        vmem((frames, WIDTH), BF16),
        vmem((LEAF, WIDTH), BF16),
        vmem((frames, WIDTH), F32),
        vmem((frames, WIDTH), F32),
        vmem((LEAVES + 1, 2 * LEAF, WIDTH), F32),
        vmem((4, LEAF, WIDTH), F32),
        vmem((LEAVES, 48, 2 * LEAF), BF16),
        vmem((112, 256), BF16),
        vmem((RANK, 128), BF16),
        vmem((LEAVES, LEAF, LEAF), BF16),
        vmem((5, 2 * RANK, LEAF), BF16),
        vmem((LEAVES, 48, WIDTH), F32),
        vmem((PLANE, RANK, WIDTH), BF16),
        vmem((2, RANK, WIDTH), BF16),
        vmem((64, WIDTH), BF16),
        vmem((64, WIDTH), BF16),
        vmem((80, WIDTH), BF16),
        vmem((64, WIDTH), BF16),
        vmem((PLANES, RANK, WIDTH), BF16),
        vmem((LEAVES, RANK, WIDTH), F32),
        vmem((2, RANK, WIDTH), F32),
        vmem((frames, WIDTH), BF16),
        vmem((frames, 2 * WIDTH), F32),
        vmem((frames, WIDTH // 2), F32),
        dma((20,)),
        dma(()),
        dma((2, 2)),
        dma((2, 2)),
        dma((2,)),
        dma((2, 2)),
        dma(()),
        dma(()),
        dma((2,)),
        dma((2,)),
        dma(()),
        dma(()),
        dma((PLANES,)),
        dma((PLANES,)),
        pltpu.SemaphoreType.REGULAR,
        pltpu.SemaphoreType.REGULAR,
        pltpu.SemaphoreType.REGULAR,
        pltpu.SemaphoreType.REGULAR,
        dma((LEAVES,)),
    ]
    return pl.pallas_call(
        body,
        out_shape=jax.ShapeDtypeStruct(tokens.shape, BF16),
        in_specs=[in_hbm] * 14,
        out_specs=in_hbm,
        scratch_shapes=scratch,
        compiler_params=pltpu.CompilerParams(
            collective_id=0, has_side_effects=True, vmem_limit_bytes=60 * 1024 * 1024
        ),
        cost_estimate=pl.CostEstimate(flops=4 * 10**9, bytes_accessed=8 * 10**6, transcendentals=10**6),
    )(
        tokens,
        norm_gain.reshape(1, -1),
        w_value,
        w_gate,
        phi_taps,
        tap_coeff,
        skip_gain.reshape(1, -1),
        basis_up,
        basis_down,
        lift_maps,
        spread_maps,
        couplings,
        jnp.asarray(forward),
        jnp.asarray(inverse),
    )


def solution(mesh):
    placed = (
        P("tm", "chan"),
        P(),
        P(None, "chan"),
        P(None, "chan"),
        P(),
        P(None, "chan"),
        P("chan"),
        P(),
        P(),
        P(),
        P(),
        P(None, None, None, None, "chan"),
    )
    return jax.shard_map(
        per_device, mesh=mesh, in_specs=placed, out_specs=P("tm", "chan"), check_vma=False
    )
```

```python
import jax
import jax.numpy as jnp
import numpy as np
from jax import lax
from jax.experimental import pallas as pl
from jax.experimental.pallas import tpu as pltpu
from jax.sharding import PartitionSpec as P

MESH = pl.DeviceIdType.MESH
F32 = jnp.float32
BF16 = jnp.bfloat16

LEAF = 256
LEAVES = 4
WIDTH = 256
RANK = 16
PLANES = 8
PLANE = 8


def transform_tables():
    odd = np.arange(LEAF)[:, None] + 0.5
    angle = 2 * np.pi * odd * np.arange(LEAF)[None, :] / (2 * LEAF)
    forward = np.concatenate([np.cos(angle), -np.sin(angle)], 0)
    return forward.astype(np.float32), (forward.T / LEAF).astype(np.float32)


def dot(left, right):
    return jnp.dot(left, right, preferred_element_type=F32)


def halves(value):
    high = value.astype(BF16)
    return high, (value - high.astype(F32)).astype(BF16)


def fine_dot(left, right):
    left_high, left_low = halves(left)
    right_high, right_low = halves(right)
    return dot(left_high, right_high) + dot(left_high, right_low) + dot(left_low, right_high)


def place_dot(left, right):
    left_high, left_low = halves(left)
    ones = right.astype(BF16)
    return dot(left_high, ones) + dot(left_low, ones)


def selector(lanes, period, shift, limit):
    row = lax.broadcasted_iota(jnp.int32, (RANK, lanes), 0)
    lane = lax.broadcasted_iota(jnp.int32, (RANK, lanes), 1)
    return ((lax.rem(lane, period) == row + shift) & (lane < limit)).astype(F32)


def body(
    tok, gain, w_value, w_gate, phi, coeff, skip, up, down, lift, spread, coup, fwd, inv,
    out,
    g, w, gain_v, phi_v, coeff_v, skip_v, up_v, down_v, lift_v, spread_v, coup_v, fwd_f, inv_f, fwd_v, inv_v,
    vals, halo, gate, near, spec, khat, mom_m, lift_m, six_m, far_m, red_m, moms,
    m2, m2_prev, ctx_out, ctx_in, pack_out, pack_in, m5_in, far0, far1, out_v, parts, part_squares,
    local_sem, gsend, drecv, rrecv, hsem, csem, s1, r1, s1p, r1p, s2, r2, s5, r5, ready_plane, ready_next, ready_edge, ready_later, osem,
):
    t = lax.axis_index("tm")
    x = lax.axis_index("chan")
    core = lax.rem(t, 2)
    y = lax.rem(lax.div(t, 2), 4)
    z = lax.div(t, PLANE)
    own = lax.rem(t, PLANE)
    rank = 2 * y + 1 - core
    right, left = lax.rem(x + 1, 4), lax.rem(x + 3, 4)

    def later(distance):
        return lax.rem(t + distance, PLANES * PLANE)

    barrier = pltpu.get_barrier_semaphore()

    def signal(semaphore, frames, chans):
        pl.semaphore_signal(semaphore, inc=1, device_id=(frames, chans), device_id_type=MESH)

    signal(barrier, t, right)
    signal(barrier, t, left)

    @pl.when(z < PLANES - 1)
    def _():
        signal(barrier, t + PLANE, x)

    m2_prev[...] = jnp.zeros_like(m2_prev)
    ctx_in[...] = jnp.zeros_like(ctx_in)
    pack_in[...] = jnp.zeros_like(pack_in)
    m5_in[...] = jnp.zeros_like(m5_in)
    halo[...] = jnp.zeros_like(halo)

    def at_rank(other):
        return z * PLANE + 2 * lax.div(other, 2) + 1 - lax.rem(other, 2)

    for k in range(1, PLANE):

        @pl.when(rank + k < PLANE)
        def _():
            signal(barrier, at_rank(rank + k), x)

    pl.semaphore_wait(barrier, 2 + rank + jnp.where(z > 0, 1, 0))

    owners = [x, left, right, lax.rem(x + 2, 4)]

    def leaf_rows(leaf):
        return pl.ds(leaf * LEAF if isinstance(leaf, int) else pl.multiple_of(leaf * LEAF, LEAF), LEAF)

    def direct(group, way):
        rows = pl.ds((1 - group) * 2 * LEAF, 2 * LEAF)
        return pltpu.make_async_remote_copy(
            src_ref=tok.at[rows],
            dst_ref=g.at[1 + way, rows],
            send_sem=gsend,
            recv_sem=drecv.at[way, group],
            device_id=(t, left if way else right),
            device_id_type=MESH,
        )

    def relay(group, way):
        rows = leaf_rows((1 - group) * 2 + way)
        return pltpu.make_async_remote_copy(
            src_ref=g.at[1 + way, rows],
            dst_ref=g.at[3, rows],
            send_sem=gsend,
            recv_sem=rrecv.at[way, group],
            device_id=(t, left if way else right),
            device_id_type=MESH,
        )

    def send_direct(group):
        for way in range(2):
            direct(group, way).start()

    def pass_on(group):
        for way in range(2):
            direct(group, way).wait_recv()
            relay(group, way).start()

    def wait_relayed(group):
        for way in range(2):
            relay(group, way).wait_recv()

    def tables_near():
        for name in ("phi", "coeff", "fwd"):
            copies[name].wait()
        fwd_v[...] = jnp.concatenate(halves(fwd_f[...]), 1)
        taps = phi_v[...].astype(BF16).astype(F32).T.astype(BF16)
        coeff_high, coeff_low = halves(coeff_v[...])
        kernel_taps = dot(taps, coeff_high) + dot(taps, coeff_low)
        both = jnp.concatenate([kernel_taps[:LEAF], kernel_taps[LEAF:]], 1)
        high, low = halves(both)
        hat = dot(fwd_v[...], jnp.concatenate([high, high], 0)) + dot(fwd_v[:, :LEAF], low)
        a_re, a_im = hat[:LEAF, :WIDTH], hat[LEAF:, :WIDTH]
        b_re, b_im = hat[:LEAF, WIDTH:], hat[LEAF:, WIDTH:]
        row = lax.broadcasted_iota(jnp.int32, (LEAF, WIDTH), 0)
        sign = (1 - 2 * lax.rem(row, 2)).astype(F32)
        khat[0] = a_re
        khat[1] = a_im
        khat[2] = b_re - sign * a_im
        khat[3] = b_im + sign * a_re

    def tables_moments():
        copies["up"].wait()
        copies["lift"].wait()
        base = up_v[...]
        first = [fine_dot(lift_v[0, k], base) for k in range(2)]
        for leaf in range(LEAVES):
            second = fine_dot(lift_v[1, leaf // 2], first[leaf % 2])
            high, low = halves(jnp.concatenate([base, first[leaf % 2], second], 0))
            mom_m[leaf] = jnp.concatenate([high, low], 1)

    def tables_lift():
        def pair(level):
            return place_dot(lift_v[level, 0], selector(128, 32, 0, 128)) + place_dot(
                lift_v[level, 1], selector(128, 32, 16, 128)
            )

        def blocks(level, copies_of):
            rows = jnp.concatenate([pair(level)] * copies_of, 0)
            row = lax.broadcasted_iota(jnp.int32, rows.shape, 0)
            lane = lax.broadcasted_iota(jnp.int32, rows.shape, 1)
            return jnp.where(lax.div(row, RANK) == lax.div(lane, 2 * RANK), rows, 0.0)

        three = blocks(2, 8)
        four = fine_dot(blocks(3, 2), three)
        five = fine_dot(blocks(4, 1), jnp.concatenate([four, jnp.zeros((96, 128), F32)], 0))
        whole = jnp.concatenate([four, three[32:64], five, three[:32]], 0)
        high, low = halves(whole)
        lift_m[...] = jnp.concatenate([high, low], 1)
        six = place_dot(lift_v[5, 0], selector(128, 32, 0, 64)) + place_dot(
            lift_v[5, 1], selector(128, 32, 16, 64)
        )
        high = six.astype(BF16).astype(F32)
        lane = lax.broadcasted_iota(jnp.int32, six.shape, 1)
        six_m[...] = jnp.where(lane < 32, high, six - high).astype(BF16)

    def tables_far():
        copies["spread"].wait()
        copies["down"].wait()
        row = lax.broadcasted_iota(jnp.int32, (RANK, LEAF), 0)
        lane = lax.broadcasted_iota(jnp.int32, (RANK, LEAF), 1)
        summing = (lax.div(lane, RANK) == row).astype(F32)
        chain = None
        for k in range(5):
            if k > 0:
                step = spread_v[1 + k, lax.rem(lax.div(t, 2 ** (k - 1)), 2)]
                chain = step if k == 1 else fine_dot(chain, step)
            high, low = halves(summing if k == 0 else place_dot(chain, summing))
            red_m[k] = jnp.concatenate([high, low], 0)
        turned = down_v[...].T
        for leaf in range(LEAVES):
            near_step = spread_v[0, leaf % 2]
            both_steps = fine_dot(near_step, spread_v[1, leaf // 2])
            mix = (
                selector(LEAF, 48, 0, 144)
                + place_dot(near_step, selector(LEAF, 48, 16, 144))
                + place_dot(both_steps, selector(LEAF, 48, 32, 144))
            )
            whole = fine_dot(turned, mix)
            high = whole.astype(BF16).astype(F32)
            lane_at = lax.broadcasted_iota(jnp.int32, whole.shape, 1)
            far_m[leaf] = jnp.where(lane_at < 96, high, whole - high).astype(BF16)

    def pair_rows(first):
        return pl.ds(first * LEAF, 2 * LEAF)

    def scaled_rows(first, slots):
        rows = pair_rows(first)
        squares = jnp.zeros((2 * LEAF, WIDTH), F32)
        columns = []
        for slot in slots:
            tokens = g[slot, rows, :].astype(F32)
            squares = squares + tokens * tokens
            scale = gain_v[:, pl.ds(pl.multiple_of(owners[slot] * WIDTH, WIDTH), WIDTH)]
            columns.append((tokens * scale).astype(BF16))
        return jnp.concatenate(columns, 1), squares

    def gather_pair(first):
        scaled, squares = scaled_rows(first, (0, 1, 2))
        parts[pair_rows(first), :] = dot(scaled, w[:3].reshape(3 * WIDTH, 2 * WIDTH))
        part_squares[pair_rows(first), :] = squares[:, : WIDTH // 2] + squares[:, WIDTH // 2 :]

    def values_of(first):
        rows = pair_rows(first)
        scaled, squares = scaled_rows(first, (3,))
        squares = squares[:, : WIDTH // 2] + squares[:, WIDTH // 2 :] + part_squares[rows, :]
        inverse = lax.rsqrt(jnp.sum(squares, axis=1, keepdims=True) / 1024 + 1e-06)
        part_squares[rows, :] = jnp.broadcast_to(inverse, squares.shape)
        value = ((parts[rows, :WIDTH] + dot(scaled, w[3, :, :WIDTH])) * inverse).astype(BF16)
        vals[rows, :] = value
        for k in range(2):
            leaf_value = value[k * LEAF : (k + 1) * LEAF]
            moms[first + k] = dot(mom_m[first + k], jnp.concatenate([leaf_value, leaf_value], 0))

    def gates_of(first):
        rows = pair_rows(first)
        scaled, _ = scaled_rows(first, (3,))
        half = 0.5 * part_squares[rows, :]
        sums = parts[rows, WIDTH:] + dot(scaled, w[3, :, WIDTH:])
        gate[rows, :] = 0.5 * jnp.tanh(sums * jnp.concatenate([half, half], 1)) + 0.5

    def spectra(first):
        both = jnp.concatenate([vals[leaf_rows(first), :], vals[leaf_rows(first + 1), :]], 1)
        result = dot(fwd_v[...], jnp.concatenate([both, both], 0))
        spec[first] = result[:, :WIDTH]
        spec[first + 1] = result[:, WIDTH:]

    def near_rows(leaves):
        columns = []
        for leaf in leaves:
            before = leaf - 1 if leaf > 0 else LEAVES
            a_re, a_im = spec[leaf, :LEAF, :], spec[leaf, LEAF:, :]
            b_re, b_im = spec[before, :LEAF, :], spec[before, LEAF:, :]
            out_re = khat[0] * a_re - khat[1] * a_im + khat[2] * b_re - khat[3] * b_im
            out_im = khat[0] * a_im + khat[1] * a_re + khat[2] * b_im + khat[3] * b_re
            columns.append(jnp.concatenate([out_re, out_im], 0).astype(BF16))
        total = dot(inv_v[...], jnp.concatenate(columns, 1))
        for k, leaf in enumerate(leaves):
            rows = leaf_rows(leaf)
            direct_term = skip_v[...] * vals[rows, :].astype(F32)
            near[rows, :] = total[:, k * WIDTH : (k + 1) * WIDTH] + direct_term

    def coupled(level, source_two, source_three):
        product = coup_v[level, 0] * source_two[None]
        if source_three is not None:
            product = product + coup_v[level, 1] * source_three[None]
        return product.reshape(RANK * RANK, WIDTH).astype(BF16)

    send_direct(0)

    copies = {}

    def local(name, source, target):
        copies[name] = pltpu.make_async_copy(source, target, local_sem.at[len(copies)])
        copies[name].start()

    local("tok", tok, g.at[0])
    for slot in range(4):
        rows = pl.ds(pl.multiple_of(owners[slot] * WIDTH, WIDTH), WIDTH)
        local(("v", slot), w_value.at[rows], w.at[slot, :, pl.ds(0, WIDTH)])
        local(("g", slot), w_gate.at[rows], w.at[slot, :, pl.ds(WIDTH, WIDTH)])
    for name, source, target in (
        ("gain", gain, gain_v),
        ("phi", phi, phi_v),
        ("coeff", coeff, coeff_v),
        ("fwd", fwd, fwd_f),
        ("skip", skip, skip_v),
        ("up", up, up_v),
        ("down", down, down_v),
        ("lift", lift, lift_v),
        ("spread", spread, spread_v),
        ("inv", inv, inv_f),
        ("coup", coup, coup_v),
    ):
        local(name, source, target)

    @pl.when(z > 0)
    def _():
        signal(ready_next, t - PLANE, x)

    for k in range(1, PLANE):

        @pl.when(rank >= k)
        def _():
            signal(ready_plane, at_rank(rank - k), x)

    def chain(place):
        @pl.when(z == PLANES - 1 - place)
        def _():
            if not isinstance(place, int) or place > 0:
                pl.semaphore_wait(ready_later, 1)
            if not isinstance(place, int) or place < PLANES - 1:
                signal(ready_later, t - PLANE, x)

    chain(0)
    tables_near()
    send_direct(1)
    chain(1)
    tables_moments()
    chain(2)
    tables_lift()
    chain(3)
    for slot in range(4):
        copies["v", slot].wait()
        copies["g", slot].wait()
    for name in ("tok", "gain", "skip", "coup", "inv"):
        copies[name].wait()
    pass_on(0)
    chain(4)

    @pl.when(rank < PLANE - 1)
    def _():
        pl.semaphore_wait(ready_plane, PLANE - 1 - rank)

    @pl.when(z < PLANES - 1)
    def _():
        pl.semaphore_wait(ready_next, 1)

        @pl.when(y == 0)
        def _():
            signal(ready_edge, z * PLANE + 6, x)
            signal(ready_edge, z * PLANE + 7, x)

    gather_pair(2)
    chain(5)
    tables_far()
    inv_v[...] = inv_f[...].astype(BF16)
    chain(6)
    pass_on(1)
    gather_pair(0)

    @pl.when((y == 3) & (z < PLANES - 1))
    def _():
        pl.semaphore_wait(ready_edge, 2)

    halo_copy = pltpu.make_async_remote_copy(
        src_ref=vals.at[pl.ds(3 * LEAF, LEAF)],
        dst_ref=halo,
        send_sem=hsem.at[0],
        recv_sem=hsem.at[1],
        device_id=(later(1), x),
        device_id_type=MESH,
    )

    def ctx_copy(part):
        rows = pl.ds(0, 48) if part == 0 else pl.ds(48, 16)
        return pltpu.make_async_remote_copy(
            src_ref=ctx_out.at[rows],
            dst_ref=ctx_in.at[rows],
            send_sem=csem.at[0, part],
            recv_sem=csem.at[1, part],
            device_id=(later(1), x),
            device_id_type=MESH,
        )

    summing = red_m[0, :RANK, :]

    def gathered(level, source_two, source_three=None):
        return dot(summing, coupled(level, source_two, source_three))

    wait_relayed(0)
    values_of(2)
    ctx_out[:48] = jnp.concatenate(
        [moms[2, 0:16, :], moms[3, 0:16, :], moms[2, 16:32, :] + moms[3, 16:32, :]], 0
    ).astype(BF16)

    @pl.when(t < PLANES * PLANE - 1)
    def _():
        halo_copy.start()
        ctx_copy(0).start()

    spectra(2)
    gates_of(2)
    near_rows((3,))

    wait_relayed(1)
    values_of(0)

    total = moms[0, 32:48, :] + moms[1, 32:48, :] + moms[2, 32:48, :] + moms[3, 32:48, :]
    m2[own] = total.astype(BF16)

    def plane_copy(k):
        return pltpu.make_async_remote_copy(
            src_ref=m2.at[own],
            dst_ref=m2.at[own],
            send_sem=s1,
            recv_sem=r1,
            device_id=(z * PLANE + lax.rem(own + k, PLANE), x),
            device_id_type=MESH,
        )

    plane_all = pltpu.make_async_remote_copy(
        src_ref=m2.at[pl.ds(0, PLANE - 1)],
        dst_ref=m2.at[pl.ds(0, PLANE - 1)],
        send_sem=s1,
        recv_sem=r1,
        device_id=(t, right),
        device_id_type=MESH,
    )

    for k in range(1, PLANE):
        plane_copy(k).start()

    def next_plane_copy(target, source):
        return pltpu.make_async_remote_copy(
            src_ref=m2.at[own],
            dst_ref=m2_prev.at[source],
            send_sem=s1p.at[target],
            recv_sem=r1p.at[source],
            device_id=(lax.rem(z + 1, PLANES) * PLANE + target, x),
            device_id_type=MESH,
        )

    @pl.when((y == 3) & (z < PLANES - 1))
    def _():
        for target in range(2):
            next_plane_copy(target, core).start()

    ctx_out[48:] = (moms[0, 16:32, :] + moms[1, 16:32, :]).astype(BF16)

    @pl.when(t < PLANES * PLANE - 1)
    def _():
        ctx_copy(1).start()

    gates_of(0)
    spectra(0)
    near_rows((1, 2))

    plane_all.wait_recv()
    stack = m2[...].reshape(PLANE * RANK, WIDTH)
    lifted = dot(lift_m[...], jnp.concatenate([stack, stack], 0))
    pack_out[...] = lifted[:80].astype(BF16)


    def pack_copy(rows):
        return pltpu.make_async_remote_copy(
            src_ref=pack_out.at[pl.ds(0, rows)],
            dst_ref=pack_in.at[pl.ds(0, rows)],
            send_sem=s2,
            recv_sem=r2,
            device_id=(later(PLANE), x),
            device_id_type=MESH,
        )

    def five_copy(k):
        return pltpu.make_async_remote_copy(
            src_ref=pack_out.at[pl.ds(64, RANK)],
            dst_ref=m5_in.at[k],
            send_sem=s5.at[k],
            recv_sem=r5.at[k],
            device_id=(later(k * PLANE), x),
            device_id_type=MESH,
        )

    chain(7)

    for k in range(PLANES - 1, 1, -1):

        @pl.when(z + k < PLANES)
        def _():
            five_copy(k).start()

    @pl.when((z < PLANES - 1) & (y == 0))
    def _():
        pack_copy(48).start()

    @pl.when((z < PLANES - 1) & (y == 1))
    def _():
        pack_copy(64).start()

    @pl.when((z < PLANES - 1) & (y >= 2))
    def _():
        pack_copy(32).start()

    @pl.when(t > 0)
    def _():
        halo_copy.wait_recv()

    spec[LEAVES] = dot(fwd_v[...], jnp.concatenate([halo[...], halo[...]], 0))
    near_rows((0,))

    @pl.when(t > 0)
    def _():
        ctx_copy(0).wait_recv()
        ctx_copy(1).wait_recv()

    prev = ctx_in[...].astype(F32)
    far0[0] = gathered(0, prev[0:16])
    far0[1] = gathered(0, prev[16:32], prev[0:16])
    far0[2] = gathered(0, moms[0, 0:16, :])
    far0[3] = gathered(0, moms[1, 0:16, :], moms[0, 0:16, :])
    far1[0] = gathered(1, prev[48:64])
    far1[1] = gathered(1, prev[32:48], prev[48:64])

    @pl.when((y == 0) & (z > 0))
    def _():
        for source in range(2):
            next_plane_copy(source, source).wait_recv()

    def reduced(k, source_two, source_three):
        return dot(red_m[k], coupled(2 + k, source_two, source_three))

    at = 2 * jnp.maximum(y - 1, 0)
    inside = y > 0
    two = jnp.where(inside, m2[at + core], m2_prev[core]).astype(F32)
    three = jnp.where(inside, m2[at], m2_prev[0]).astype(F32) * core.astype(F32)
    expansion = reduced(0, two, three)

    @pl.when((z > 0) & (y == 0))
    def _():
        pack_copy(48).wait_recv()

    @pl.when((z > 0) & (y == 1))
    def _():
        pack_copy(64).wait_recv()

    @pl.when((z > 0) & (y >= 2))
    def _():
        pack_copy(32).wait_recv()

    odd = lax.rem(y, 2)
    lower = y < 2
    here = jnp.where(odd == 1, lifted[96:112], lifted[80:96])
    coming = pack_in[pl.ds(pl.multiple_of(32 + odd * RANK, RANK), RANK), :].astype(F32)
    two = jnp.where(lower, coming, here)
    three = jnp.where(lower, pack_in[32:48, :].astype(F32), lifted[80:96]) * odd.astype(F32)
    expansion = expansion + reduced(1, two, three)
    odd = lax.div(y, 2)
    two = pack_in[pl.ds(pl.multiple_of(odd * RANK, RANK), RANK), :].astype(F32)
    three = pack_in[0:16, :].astype(F32) * odd.astype(F32)
    expansion = expansion + reduced(2, two, three)

    for k in range(2, PLANES):

        @pl.when(z >= k)
        def _():
            five_copy(k).wait_recv()

    odd = lax.rem(z, 2)
    expansion = expansion + reduced(
        3, m5_in[2].astype(F32), m5_in[3].astype(F32) * odd.astype(F32)
    )
    pad = jnp.zeros((64, WIDTH), BF16)

    def sixth(base):
        pair = [m5_in[base], m5_in[base - 1]]
        return dot(six_m[...], jnp.concatenate(pair + pair + [pad], 0))

    odd_six = lax.rem(lax.div(z, 2), 2)
    expansion = expansion + reduced(
        4, sixth(4 + odd), sixth(6 + odd) * odd_six.astype(F32)
    )

    expansion = expansion[:RANK] + expansion[RANK:]

    def out_copy(leaf):
        rows = leaf_rows(leaf)
        return pltpu.make_async_copy(out_v.at[rows], out.at[rows], osem.at[leaf])

    for leaf in range(LEAVES):
        rows = leaf_rows(leaf)
        high, low = halves(jnp.concatenate([far0[leaf], far1[leaf // 2], expansion], 0))
        whole = jnp.concatenate([high, low, high, jnp.zeros((112, WIDTH), BF16)], 0)
        combined = near[rows, :] + dot(far_m[leaf], whole)
        out_v[rows, :] = (gate[rows, :] * combined).astype(BF16)
        out_copy(leaf).start()

    gather_sent = g.at[pl.ds(0, 3)]
    pltpu.make_async_remote_copy(
        src_ref=gather_sent,
        dst_ref=gather_sent,
        send_sem=gsend,
        recv_sem=drecv.at[0, 0],
        device_id=(t, right),
        device_id_type=MESH,
    ).wait_send()

    plane_all.wait_send()

    @pl.when(t < PLANES * PLANE - 1)
    def _():
        halo_copy.wait_send()
        ctx_copy(0).wait_send()
        ctx_copy(1).wait_send()

    @pl.when((y == 3) & (z < PLANES - 1))
    def _():
        for target in range(2):
            next_plane_copy(target, core).wait_send()

    @pl.when((z < PLANES - 1) & (y == 0))
    def _():
        pack_copy(48).wait_send()

    @pl.when((z < PLANES - 1) & (y == 1))
    def _():
        pack_copy(64).wait_send()

    @pl.when((z < PLANES - 1) & (y >= 2))
    def _():
        pack_copy(32).wait_send()

    for k in range(2, PLANES):

        @pl.when(z + k < PLANES)
        def _():
            five_copy(k).wait_send()

    for leaf in range(LEAVES):
        out_copy(leaf).wait()


def per_device(
    tokens,
    norm_gain,
    w_value,
    w_gate,
    phi_taps,
    tap_coeff,
    skip_gain,
    basis_up,
    basis_down,
    lift_maps,
    spread_maps,
    couplings,
):
    forward, inverse = transform_tables()
    in_hbm = pl.BlockSpec(memory_space=pltpu.HBM)
    frames = LEAF * LEAVES
    vmem = pltpu.VMEM
    dma = pltpu.SemaphoreType.DMA
    scratch = [
        vmem((4, frames, WIDTH), BF16),
        vmem((4, WIDTH, 2 * WIDTH), BF16),
        vmem((1, 4 * WIDTH), F32),
        vmem(phi_taps.shape, F32),
        vmem(tap_coeff.shape, F32),
        vmem((1, WIDTH), F32),
        vmem(basis_up.shape, F32),
        vmem(basis_down.shape, F32),
        vmem(lift_maps.shape, F32),
        vmem(spread_maps.shape, F32),
        vmem(couplings.shape, F32),
        vmem(forward.shape, F32),
        vmem(inverse.shape, F32),
        vmem((2 * LEAF, 2 * LEAF), BF16),
        vmem((LEAF, 2 * LEAF), BF16),
        vmem((frames, WIDTH), BF16),
        vmem((LEAF, WIDTH), BF16),
        vmem((frames, WIDTH), F32),
        vmem((frames, WIDTH), F32),
        vmem((LEAVES + 1, 2 * LEAF, WIDTH), F32),
        vmem((4, LEAF, WIDTH), F32),
        vmem((LEAVES, 48, 2 * LEAF), BF16),
        vmem((112, 256), BF16),
        vmem((RANK, 128), BF16),
        vmem((LEAVES, LEAF, LEAF), BF16),
        vmem((5, 2 * RANK, LEAF), BF16),
        vmem((LEAVES, 48, WIDTH), F32),
        vmem((PLANE, RANK, WIDTH), BF16),
        vmem((2, RANK, WIDTH), BF16),
        vmem((64, WIDTH), BF16),
        vmem((64, WIDTH), BF16),
        vmem((80, WIDTH), BF16),
        vmem((64, WIDTH), BF16),
        vmem((PLANES, RANK, WIDTH), BF16),
        vmem((LEAVES, RANK, WIDTH), F32),
        vmem((2, RANK, WIDTH), F32),
        vmem((frames, WIDTH), BF16),
        vmem((frames, 2 * WIDTH), F32),
        vmem((frames, WIDTH // 2), F32),
        dma((20,)),
        dma(()),
        dma((2, 2)),
        dma((2, 2)),
        dma((2,)),
        dma((2, 2)),
        dma(()),
        dma(()),
        dma((2,)),
        dma((2,)),
        dma(()),
        dma(()),
        dma((PLANES,)),
        dma((PLANES,)),
        pltpu.SemaphoreType.REGULAR,
        pltpu.SemaphoreType.REGULAR,
        pltpu.SemaphoreType.REGULAR,
        pltpu.SemaphoreType.REGULAR,
        dma((LEAVES,)),
    ]
    return pl.pallas_call(
        body,
        out_shape=jax.ShapeDtypeStruct(tokens.shape, BF16),
        in_specs=[in_hbm] * 14,
        out_specs=in_hbm,
        scratch_shapes=scratch,
        compiler_params=pltpu.CompilerParams(
            collective_id=0, has_side_effects=True, vmem_limit_bytes=60 * 1024 * 1024
        ),
        cost_estimate=pl.CostEstimate(flops=4 * 10**9, bytes_accessed=8 * 10**6, transcendentals=10**6),
    )(
        tokens,
        norm_gain.reshape(1, -1),
        w_value,
        w_gate,
        phi_taps,
        tap_coeff,
        skip_gain.reshape(1, -1),
        basis_up,
        basis_down,
        lift_maps,
        spread_maps,
        couplings,
        jnp.asarray(forward),
        jnp.asarray(inverse),
    )


def solution(mesh):
    placed = (
        P("tm", "chan"),
        P(),
        P(None, "chan"),
        P(None, "chan"),
        P(),
        P(None, "chan"),
        P("chan"),
        P(),
        P(),
        P(),
        P(),
        P(None, None, None, None, "chan"),
    )
    return jax.shard_map(
        per_device, mesh=mesh, in_specs=placed, out_specs=P("tm", "chan"), check_vma=False
    )
```

```python
import jax
import jax.numpy as jnp
import numpy as np
from jax import lax
from jax.experimental import pallas as pl
from jax.experimental.pallas import tpu as pltpu
from jax.sharding import PartitionSpec as P

MESH = pl.DeviceIdType.MESH
F32 = jnp.float32
BF16 = jnp.bfloat16

LEAF = 256
LEAVES = 4
WIDTH = 256
RANK = 16
PLANES = 8
PLANE = 8


def transform_tables():
    odd = np.arange(LEAF)[:, None] + 0.5
    angle = 2 * np.pi * odd * np.arange(LEAF)[None, :] / (2 * LEAF)
    forward = np.concatenate([np.cos(angle), -np.sin(angle)], 0)
    return forward.astype(np.float32), (forward.T / LEAF).astype(np.float32)


def dot(left, right):
    return jnp.dot(left, right, preferred_element_type=F32)


def halves(value):
    high = value.astype(BF16)
    return high, (value - high.astype(F32)).astype(BF16)


def fine_dot(left, right):
    left_high, left_low = halves(left)
    right_high, right_low = halves(right)
    return dot(left_high, right_high) + dot(left_high, right_low) + dot(left_low, right_high)


def place_dot(left, right):
    left_high, left_low = halves(left)
    ones = right.astype(BF16)
    return dot(left_high, ones) + dot(left_low, ones)


def selector(lanes, period, shift, limit):
    row = lax.broadcasted_iota(jnp.int32, (RANK, lanes), 0)
    lane = lax.broadcasted_iota(jnp.int32, (RANK, lanes), 1)
    return ((lax.rem(lane, period) == row + shift) & (lane < limit)).astype(F32)


def body(
    tok, gain, w_value, w_gate, phi, coeff, skip, up, down, lift, spread, coup, fwd, inv,
    out,
    g, w, gain_v, phi_v, coeff_v, skip_v, up_v, down_v, lift_v, spread_v, coup_v, fwd_f, inv_f, fwd_v, inv_v,
    vals, halo, gate, near, spec, khat, mom_m, lift_m, six_m, far_m, red_m, moms,
    m2, m2_prev, ctx_out, ctx_in, pack_out, pack_in, m5_in, far0, far1, out_v, parts, part_squares,
    local_sem, gsend, drecv, rrecv, hsem, csem, s1, r1, s1p, r1p, s2, r2, s5, r5, ready_plane, ready_next, ready_edge, ready_later, osem,
):
    t = lax.axis_index("tm")
    x = lax.axis_index("chan")
    core = lax.rem(t, 2)
    y = lax.rem(lax.div(t, 2), 4)
    z = lax.div(t, PLANE)
    own = lax.rem(t, PLANE)
    rank = 2 * y + 1 - core
    right, left = lax.rem(x + 1, 4), lax.rem(x + 3, 4)

    def later(distance):
        return lax.rem(t + distance, PLANES * PLANE)

    barrier = pltpu.get_barrier_semaphore()

    def signal(semaphore, frames, chans):
        pl.semaphore_signal(semaphore, inc=1, device_id=(frames, chans), device_id_type=MESH)

    signal(barrier, t, right)
    signal(barrier, t, left)

    @pl.when(z < PLANES - 1)
    def _():
        signal(barrier, t + PLANE, x)

    m2_prev[...] = jnp.zeros_like(m2_prev)
    ctx_in[...] = jnp.zeros_like(ctx_in)
    pack_in[...] = jnp.zeros_like(pack_in)
    m5_in[...] = jnp.zeros_like(m5_in)
    halo[...] = jnp.zeros_like(halo)

    def at_rank(other):
        return z * PLANE + 2 * lax.div(other, 2) + 1 - lax.rem(other, 2)

    for k in range(1, PLANE):

        @pl.when(rank + k < PLANE)
        def _():
            signal(barrier, at_rank(rank + k), x)

    pl.semaphore_wait(barrier, 2 + rank + jnp.where(z > 0, 1, 0))

    owners = [x, left, right, lax.rem(x + 2, 4)]

    def leaf_rows(leaf):
        return pl.ds(leaf * LEAF if isinstance(leaf, int) else pl.multiple_of(leaf * LEAF, LEAF), LEAF)

    def direct(group, way):
        rows = pl.ds((1 - group) * 2 * LEAF, 2 * LEAF)
        return pltpu.make_async_remote_copy(
            src_ref=tok.at[rows],
            dst_ref=g.at[1 + way, rows],
            send_sem=gsend,
            recv_sem=drecv.at[way, group],
            device_id=(t, left if way else right),
            device_id_type=MESH,
        )

    def relay(group, way):
        rows = leaf_rows((1 - group) * 2 + way)
        return pltpu.make_async_remote_copy(
            src_ref=g.at[1 + way, rows],
            dst_ref=g.at[3, rows],
            send_sem=gsend,
            recv_sem=rrecv.at[way, group],
            device_id=(t, left if way else right),
            device_id_type=MESH,
        )

    def send_direct(group):
        for way in range(2):
            direct(group, way).start()

    def pass_on(group):
        for way in range(2):
            direct(group, way).wait_recv()
            relay(group, way).start()

    def wait_relayed(group):
        for way in range(2):
            relay(group, way).wait_recv()

    def tables_near():
        for name in ("phi", "coeff", "fwd"):
            copies[name].wait()
        fwd_v[...] = jnp.concatenate(halves(fwd_f[...]), 1)
        taps = phi_v[...].astype(BF16).astype(F32).T.astype(BF16)
        coeff_high, coeff_low = halves(coeff_v[...])
        kernel_taps = dot(taps, coeff_high) + dot(taps, coeff_low)
        both = jnp.concatenate([kernel_taps[:LEAF], kernel_taps[LEAF:]], 1)
        high, low = halves(both)
        hat = dot(fwd_v[...], jnp.concatenate([high, high], 0)) + dot(fwd_v[:, :LEAF], low)
        a_re, a_im = hat[:LEAF, :WIDTH], hat[LEAF:, :WIDTH]
        b_re, b_im = hat[:LEAF, WIDTH:], hat[LEAF:, WIDTH:]
        row = lax.broadcasted_iota(jnp.int32, (LEAF, WIDTH), 0)
        sign = (1 - 2 * lax.rem(row, 2)).astype(F32)
        khat[0] = a_re
        khat[1] = a_im
        khat[2] = b_re - sign * a_im
        khat[3] = b_im + sign * a_re

    def tables_moments():
        copies["up"].wait()
        copies["lift"].wait()
        base = up_v[...]
        first = [fine_dot(lift_v[0, k], base) for k in range(2)]
        for leaf in range(LEAVES):
            second = fine_dot(lift_v[1, leaf // 2], first[leaf % 2])
            high, low = halves(jnp.concatenate([base, first[leaf % 2], second], 0))
            mom_m[leaf] = jnp.concatenate([high, low], 1)

    def tables_lift():
        def pair(level):
            return place_dot(lift_v[level, 0], selector(128, 32, 0, 128)) + place_dot(
                lift_v[level, 1], selector(128, 32, 16, 128)
            )

        def blocks(level, copies_of):
            rows = jnp.concatenate([pair(level)] * copies_of, 0)
            row = lax.broadcasted_iota(jnp.int32, rows.shape, 0)
            lane = lax.broadcasted_iota(jnp.int32, rows.shape, 1)
            return jnp.where(lax.div(row, RANK) == lax.div(lane, 2 * RANK), rows, 0.0)

        three = blocks(2, 8)
        four = fine_dot(blocks(3, 2), three)
        five = fine_dot(blocks(4, 1), jnp.concatenate([four, jnp.zeros((96, 128), F32)], 0))
        whole = jnp.concatenate([four, three[32:64], five, three[:32]], 0)
        high, low = halves(whole)
        lift_m[...] = jnp.concatenate([high, low], 1)
        six = place_dot(lift_v[5, 0], selector(128, 32, 0, 64)) + place_dot(
            lift_v[5, 1], selector(128, 32, 16, 64)
        )
        high = six.astype(BF16).astype(F32)
        lane = lax.broadcasted_iota(jnp.int32, six.shape, 1)
        six_m[...] = jnp.where(lane < 32, high, six - high).astype(BF16)

    def tables_far():
        copies["spread"].wait()
        copies["down"].wait()
        row = lax.broadcasted_iota(jnp.int32, (RANK, LEAF), 0)
        lane = lax.broadcasted_iota(jnp.int32, (RANK, LEAF), 1)
        summing = (lax.div(lane, RANK) == row).astype(F32)
        chain = None
        for k in range(5):
            if k > 0:
                step = spread_v[1 + k, lax.rem(lax.div(t, 2 ** (k - 1)), 2)]
                chain = step if k == 1 else fine_dot(chain, step)
            high, low = halves(summing if k == 0 else place_dot(chain, summing))
            red_m[k] = jnp.concatenate([high, low], 0)
        turned = down_v[...].T
        for leaf in range(LEAVES):
            near_step = spread_v[0, leaf % 2]
            both_steps = fine_dot(near_step, spread_v[1, leaf // 2])
            mix = (
                selector(LEAF, 48, 0, 144)
                + place_dot(near_step, selector(LEAF, 48, 16, 144))
                + place_dot(both_steps, selector(LEAF, 48, 32, 144))
            )
            whole = fine_dot(turned, mix)
            high = whole.astype(BF16).astype(F32)
            lane_at = lax.broadcasted_iota(jnp.int32, whole.shape, 1)
            far_m[leaf] = jnp.where(lane_at < 96, high, whole - high).astype(BF16)

    def pair_rows(first):
        return pl.ds(first * LEAF, 2 * LEAF)

    def scaled_rows(first, slots):
        rows = pair_rows(first)
        squares = jnp.zeros((2 * LEAF, WIDTH), F32)
        columns = []
        for slot in slots:
            tokens = g[slot, rows, :].astype(F32)
            squares = squares + tokens * tokens
            scale = gain_v[:, pl.ds(pl.multiple_of(owners[slot] * WIDTH, WIDTH), WIDTH)]
            columns.append((tokens * scale).astype(BF16))
        return jnp.concatenate(columns, 1), squares

    def gather_pair(first):
        scaled, squares = scaled_rows(first, (0, 1, 2))
        parts[pair_rows(first), :] = dot(scaled, w[:3].reshape(3 * WIDTH, 2 * WIDTH))
        part_squares[pair_rows(first), :] = squares[:, : WIDTH // 2] + squares[:, WIDTH // 2 :]

    def values_of(first):
        rows = pair_rows(first)
        scaled, squares = scaled_rows(first, (3,))
        squares = squares[:, : WIDTH // 2] + squares[:, WIDTH // 2 :] + part_squares[rows, :]
        inverse = lax.rsqrt(jnp.sum(squares, axis=1, keepdims=True) / 1024 + 1e-06)
        part_squares[rows, :] = jnp.broadcast_to(inverse, squares.shape)
        value = ((parts[rows, :WIDTH] + dot(scaled, w[3, :, :WIDTH])) * inverse).astype(BF16)
        vals[rows, :] = value
        for k in range(2):
            leaf_value = value[k * LEAF : (k + 1) * LEAF]
            moms[first + k] = dot(mom_m[first + k], jnp.concatenate([leaf_value, leaf_value], 0))

    def gates_of(first):
        rows = pair_rows(first)
        scaled, _ = scaled_rows(first, (3,))
        half = 0.5 * part_squares[rows, :]
        sums = parts[rows, WIDTH:] + dot(scaled, w[3, :, WIDTH:])
        gate[rows, :] = 0.5 * jnp.tanh(sums * jnp.concatenate([half, half], 1)) + 0.5

    def spectra(first):
        both = jnp.concatenate([vals[leaf_rows(first), :], vals[leaf_rows(first + 1), :]], 1)
        result = dot(fwd_v[...], jnp.concatenate([both, both], 0))
        spec[first] = result[:, :WIDTH]
        spec[first + 1] = result[:, WIDTH:]

    def near_rows(leaves):
        columns = []
        for leaf in leaves:
            before = leaf - 1 if leaf > 0 else LEAVES
            a_re, a_im = spec[leaf, :LEAF, :], spec[leaf, LEAF:, :]
            b_re, b_im = spec[before, :LEAF, :], spec[before, LEAF:, :]
            out_re = khat[0] * a_re - khat[1] * a_im + khat[2] * b_re - khat[3] * b_im
            out_im = khat[0] * a_im + khat[1] * a_re + khat[2] * b_im + khat[3] * b_re
            columns.append(jnp.concatenate([out_re, out_im], 0).astype(BF16))
        total = dot(inv_v[...], jnp.concatenate(columns, 1))
        for k, leaf in enumerate(leaves):
            rows = leaf_rows(leaf)
            direct_term = skip_v[...] * vals[rows, :].astype(F32)
            near[rows, :] = total[:, k * WIDTH : (k + 1) * WIDTH] + direct_term

    def coupled(level, source_two, source_three):
        product = coup_v[level, 0] * source_two[None]
        if source_three is not None:
            product = product + coup_v[level, 1] * source_three[None]
        return product.reshape(RANK * RANK, WIDTH).astype(BF16)

    send_direct(0)

    copies = {}

    def local(name, source, target):
        copies[name] = pltpu.make_async_copy(source, target, local_sem.at[len(copies)])
        copies[name].start()

    local("tok", tok, g.at[0])
    for slot in range(4):
        rows = pl.ds(pl.multiple_of(owners[slot] * WIDTH, WIDTH), WIDTH)
        local(("v", slot), w_value.at[rows], w.at[slot, :, pl.ds(0, WIDTH)])
        local(("g", slot), w_gate.at[rows], w.at[slot, :, pl.ds(WIDTH, WIDTH)])
    for name, source, target in (
        ("gain", gain, gain_v),
        ("phi", phi, phi_v),
        ("coeff", coeff, coeff_v),
        ("fwd", fwd, fwd_f),
        ("skip", skip, skip_v),
        ("up", up, up_v),
        ("down", down, down_v),
        ("lift", lift, lift_v),
        ("spread", spread, spread_v),
        ("inv", inv, inv_f),
        ("coup", coup, coup_v),
    ):
        local(name, source, target)

    @pl.when(z > 0)
    def _():
        signal(ready_next, t - PLANE, x)

    for k in range(1, PLANE):

        @pl.when(rank >= k)
        def _():
            signal(ready_plane, at_rank(rank - k), x)

    def chain(place):
        @pl.when(z == PLANES - 1 - place)
        def _():
            if not isinstance(place, int) or place > 0:
                pl.semaphore_wait(ready_later, 1)
            if not isinstance(place, int) or place < PLANES - 1:
                signal(ready_later, t - PLANE, x)

    chain(0)
    tables_near()
    send_direct(1)
    chain(1)
    tables_moments()
    chain(2)
    tables_lift()
    chain(3)
    for slot in range(4):
        copies["v", slot].wait()
        copies["g", slot].wait()
    for name in ("tok", "gain", "skip", "coup", "inv"):
        copies[name].wait()
    pass_on(0)
    chain(4)

    @pl.when(rank < PLANE - 1)
    def _():
        pl.semaphore_wait(ready_plane, PLANE - 1 - rank)

    @pl.when(z < PLANES - 1)
    def _():
        pl.semaphore_wait(ready_next, 1)

        @pl.when(y == 0)
        def _():
            signal(ready_edge, z * PLANE + 6, x)
            signal(ready_edge, z * PLANE + 7, x)

    gather_pair(2)
    chain(5)
    tables_far()
    inv_v[...] = inv_f[...].astype(BF16)
    chain(6)
    pass_on(1)
    gather_pair(0)

    @pl.when((y == 3) & (z < PLANES - 1))
    def _():
        pl.semaphore_wait(ready_edge, 2)

    halo_copy = pltpu.make_async_remote_copy(
        src_ref=vals.at[pl.ds(3 * LEAF, LEAF)],
        dst_ref=halo,
        send_sem=hsem.at[0],
        recv_sem=hsem.at[1],
        device_id=(later(1), x),
        device_id_type=MESH,
    )

    def ctx_copy(part):
        rows = pl.ds(0, 48) if part == 0 else pl.ds(48, 16)
        return pltpu.make_async_remote_copy(
            src_ref=ctx_out.at[rows],
            dst_ref=ctx_in.at[rows],
            send_sem=csem.at[0, part],
            recv_sem=csem.at[1, part],
            device_id=(later(1), x),
            device_id_type=MESH,
        )

    summing = red_m[0, :RANK, :]

    def gathered(level, source_two, source_three=None):
        return dot(summing, coupled(level, source_two, source_three))

    wait_relayed(0)
    values_of(2)
    ctx_out[:48] = jnp.concatenate(
        [moms[2, 0:16, :], moms[3, 0:16, :], moms[2, 16:32, :] + moms[3, 16:32, :]], 0
    ).astype(BF16)

    @pl.when(t < PLANES * PLANE - 1)
    def _():
        halo_copy.start()
        ctx_copy(0).start()

    spectra(2)

    wait_relayed(1)
    values_of(0)

    total = moms[0, 32:48, :] + moms[1, 32:48, :] + moms[2, 32:48, :] + moms[3, 32:48, :]
    m2[own] = total.astype(BF16)

    def plane_copy(k):
        return pltpu.make_async_remote_copy(
            src_ref=m2.at[own],
            dst_ref=m2.at[own],
            send_sem=s1,
            recv_sem=r1,
            device_id=(z * PLANE + lax.rem(own + k, PLANE), x),
            device_id_type=MESH,
        )

    plane_all = pltpu.make_async_remote_copy(
        src_ref=m2.at[pl.ds(0, PLANE - 1)],
        dst_ref=m2.at[pl.ds(0, PLANE - 1)],
        send_sem=s1,
        recv_sem=r1,
        device_id=(t, right),
        device_id_type=MESH,
    )

    for k in range(1, PLANE):
        plane_copy(k).start()

    def next_plane_copy(target, source):
        return pltpu.make_async_remote_copy(
            src_ref=m2.at[own],
            dst_ref=m2_prev.at[source],
            send_sem=s1p.at[target],
            recv_sem=r1p.at[source],
            device_id=(lax.rem(z + 1, PLANES) * PLANE + target, x),
            device_id_type=MESH,
        )

    @pl.when((y == 3) & (z < PLANES - 1))
    def _():
        for target in range(2):
            next_plane_copy(target, core).start()

    ctx_out[48:] = (moms[0, 16:32, :] + moms[1, 16:32, :]).astype(BF16)

    @pl.when(t < PLANES * PLANE - 1)
    def _():
        ctx_copy(1).start()

    gates_of(0)
    spectra(0)
    near_rows((1, 2))

    plane_all.wait_recv()
    stack = m2[...].reshape(PLANE * RANK, WIDTH)
    lifted = dot(lift_m[...], jnp.concatenate([stack, stack], 0))
    pack_out[...] = lifted[:80].astype(BF16)


    def pack_copy(rows):
        return pltpu.make_async_remote_copy(
            src_ref=pack_out.at[pl.ds(0, rows)],
            dst_ref=pack_in.at[pl.ds(0, rows)],
            send_sem=s2,
            recv_sem=r2,
            device_id=(later(PLANE), x),
            device_id_type=MESH,
        )

    def five_copy(k):
        return pltpu.make_async_remote_copy(
            src_ref=pack_out.at[pl.ds(64, RANK)],
            dst_ref=m5_in.at[k],
            send_sem=s5.at[k],
            recv_sem=r5.at[k],
            device_id=(later(k * PLANE), x),
            device_id_type=MESH,
        )

    chain(7)

    for k in range(PLANES - 1, 1, -1):

        @pl.when(z + k < PLANES)
        def _():
            five_copy(k).start()

    @pl.when((z < PLANES - 1) & (y == 0))
    def _():
        pack_copy(48).start()

    @pl.when((z < PLANES - 1) & (y == 1))
    def _():
        pack_copy(64).start()

    @pl.when((z < PLANES - 1) & (y >= 2))
    def _():
        pack_copy(32).start()

    gates_of(2)
    near_rows((3,))

    @pl.when(t > 0)
    def _():
        halo_copy.wait_recv()

    spec[LEAVES] = dot(fwd_v[...], jnp.concatenate([halo[...], halo[...]], 0))
    near_rows((0,))

    @pl.when(t > 0)
    def _():
        ctx_copy(0).wait_recv()
        ctx_copy(1).wait_recv()

    prev = ctx_in[...].astype(F32)
    far0[0] = gathered(0, prev[0:16])
    far0[1] = gathered(0, prev[16:32], prev[0:16])
    far0[2] = gathered(0, moms[0, 0:16, :])
    far0[3] = gathered(0, moms[1, 0:16, :], moms[0, 0:16, :])
    far1[0] = gathered(1, prev[48:64])
    far1[1] = gathered(1, prev[32:48], prev[48:64])

    @pl.when((y == 0) & (z > 0))
    def _():
        for source in range(2):
            next_plane_copy(source, source).wait_recv()

    def reduced(k, source_two, source_three):
        return dot(red_m[k], coupled(2 + k, source_two, source_three))

    at = 2 * jnp.maximum(y - 1, 0)
    inside = y > 0
    two = jnp.where(inside, m2[at + core], m2_prev[core]).astype(F32)
    three = jnp.where(inside, m2[at], m2_prev[0]).astype(F32) * core.astype(F32)
    expansion = reduced(0, two, three)

    @pl.when((z > 0) & (y == 0))
    def _():
        pack_copy(48).wait_recv()

    @pl.when((z > 0) & (y == 1))
    def _():
        pack_copy(64).wait_recv()

    @pl.when((z > 0) & (y >= 2))
    def _():
        pack_copy(32).wait_recv()

    odd = lax.rem(y, 2)
    lower = y < 2
    here = jnp.where(odd == 1, lifted[96:112], lifted[80:96])
    coming = pack_in[pl.ds(pl.multiple_of(32 + odd * RANK, RANK), RANK), :].astype(F32)
    two = jnp.where(lower, coming, here)
    three = jnp.where(lower, pack_in[32:48, :].astype(F32), lifted[80:96]) * odd.astype(F32)
    expansion = expansion + reduced(1, two, three)
    odd = lax.div(y, 2)
    two = pack_in[pl.ds(pl.multiple_of(odd * RANK, RANK), RANK), :].astype(F32)
    three = pack_in[0:16, :].astype(F32) * odd.astype(F32)
    expansion = expansion + reduced(2, two, three)

    for k in range(2, PLANES):

        @pl.when(z >= k)
        def _():
            five_copy(k).wait_recv()

    odd = lax.rem(z, 2)
    expansion = expansion + reduced(
        3, m5_in[2].astype(F32), m5_in[3].astype(F32) * odd.astype(F32)
    )
    pad = jnp.zeros((64, WIDTH), BF16)

    def sixth(base):
        pair = [m5_in[base], m5_in[base - 1]]
        return dot(six_m[...], jnp.concatenate(pair + pair + [pad], 0))

    odd_six = lax.rem(lax.div(z, 2), 2)
    expansion = expansion + reduced(
        4, sixth(4 + odd), sixth(6 + odd) * odd_six.astype(F32)
    )

    expansion = expansion[:RANK] + expansion[RANK:]

    def out_copy(leaf):
        rows = leaf_rows(leaf)
        return pltpu.make_async_copy(out_v.at[rows], out.at[rows], osem.at[leaf])

    for leaf in range(LEAVES):
        rows = leaf_rows(leaf)
        high, low = halves(jnp.concatenate([far0[leaf], far1[leaf // 2], expansion], 0))
        whole = jnp.concatenate([high, low, high, jnp.zeros((112, WIDTH), BF16)], 0)
        combined = near[rows, :] + dot(far_m[leaf], whole)
        out_v[rows, :] = (gate[rows, :] * combined).astype(BF16)
        out_copy(leaf).start()

    gather_sent = g.at[pl.ds(0, 3)]
    pltpu.make_async_remote_copy(
        src_ref=gather_sent,
        dst_ref=gather_sent,
        send_sem=gsend,
        recv_sem=drecv.at[0, 0],
        device_id=(t, right),
        device_id_type=MESH,
    ).wait_send()

    plane_all.wait_send()

    @pl.when(t < PLANES * PLANE - 1)
    def _():
        halo_copy.wait_send()
        ctx_copy(0).wait_send()
        ctx_copy(1).wait_send()

    @pl.when((y == 3) & (z < PLANES - 1))
    def _():
        for target in range(2):
            next_plane_copy(target, core).wait_send()

    @pl.when((z < PLANES - 1) & (y == 0))
    def _():
        pack_copy(48).wait_send()

    @pl.when((z < PLANES - 1) & (y == 1))
    def _():
        pack_copy(64).wait_send()

    @pl.when((z < PLANES - 1) & (y >= 2))
    def _():
        pack_copy(32).wait_send()

    for k in range(2, PLANES):

        @pl.when(z + k < PLANES)
        def _():
            five_copy(k).wait_send()

    for leaf in range(LEAVES):
        out_copy(leaf).wait()


def per_device(
    tokens,
    norm_gain,
    w_value,
    w_gate,
    phi_taps,
    tap_coeff,
    skip_gain,
    basis_up,
    basis_down,
    lift_maps,
    spread_maps,
    couplings,
):
    forward, inverse = transform_tables()
    in_hbm = pl.BlockSpec(memory_space=pltpu.HBM)
    frames = LEAF * LEAVES
    vmem = pltpu.VMEM
    dma = pltpu.SemaphoreType.DMA
    scratch = [
        vmem((4, frames, WIDTH), BF16),
        vmem((4, WIDTH, 2 * WIDTH), BF16),
        vmem((1, 4 * WIDTH), F32),
        vmem(phi_taps.shape, F32),
        vmem(tap_coeff.shape, F32),
        vmem((1, WIDTH), F32),
        vmem(basis_up.shape, F32),
        vmem(basis_down.shape, F32),
        vmem(lift_maps.shape, F32),
        vmem(spread_maps.shape, F32),
        vmem(couplings.shape, F32),
        vmem(forward.shape, F32),
        vmem(inverse.shape, F32),
        vmem((2 * LEAF, 2 * LEAF), BF16),
        vmem((LEAF, 2 * LEAF), BF16),
        vmem((frames, WIDTH), BF16),
        vmem((LEAF, WIDTH), BF16),
        vmem((frames, WIDTH), F32),
        vmem((frames, WIDTH), F32),
        vmem((LEAVES + 1, 2 * LEAF, WIDTH), F32),
        vmem((4, LEAF, WIDTH), F32),
        vmem((LEAVES, 48, 2 * LEAF), BF16),
        vmem((112, 256), BF16),
        vmem((RANK, 128), BF16),
        vmem((LEAVES, LEAF, LEAF), BF16),
        vmem((5, 2 * RANK, LEAF), BF16),
        vmem((LEAVES, 48, WIDTH), F32),
        vmem((PLANE, RANK, WIDTH), BF16),
        vmem((2, RANK, WIDTH), BF16),
        vmem((64, WIDTH), BF16),
        vmem((64, WIDTH), BF16),
        vmem((80, WIDTH), BF16),
        vmem((64, WIDTH), BF16),
        vmem((PLANES, RANK, WIDTH), BF16),
        vmem((LEAVES, RANK, WIDTH), F32),
        vmem((2, RANK, WIDTH), F32),
        vmem((frames, WIDTH), BF16),
        vmem((frames, 2 * WIDTH), F32),
        vmem((frames, WIDTH // 2), F32),
        dma((20,)),
        dma(()),
        dma((2, 2)),
        dma((2, 2)),
        dma((2,)),
        dma((2, 2)),
        dma(()),
        dma(()),
        dma((2,)),
        dma((2,)),
        dma(()),
        dma(()),
        dma((PLANES,)),
        dma((PLANES,)),
        pltpu.SemaphoreType.REGULAR,
        pltpu.SemaphoreType.REGULAR,
        pltpu.SemaphoreType.REGULAR,
        pltpu.SemaphoreType.REGULAR,
        dma((LEAVES,)),
    ]
    return pl.pallas_call(
        body,
        out_shape=jax.ShapeDtypeStruct(tokens.shape, BF16),
        in_specs=[in_hbm] * 14,
        out_specs=in_hbm,
        scratch_shapes=scratch,
        compiler_params=pltpu.CompilerParams(
            collective_id=0, has_side_effects=True, vmem_limit_bytes=60 * 1024 * 1024
        ),
        cost_estimate=pl.CostEstimate(flops=4 * 10**9, bytes_accessed=8 * 10**6, transcendentals=10**6),
    )(
        tokens,
        norm_gain.reshape(1, -1),
        w_value,
        w_gate,
        phi_taps,
        tap_coeff,
        skip_gain.reshape(1, -1),
        basis_up,
        basis_down,
        lift_maps,
        spread_maps,
        couplings,
        jnp.asarray(forward),
        jnp.asarray(inverse),
    )


def solution(mesh):
    placed = (
        P("tm", "chan"),
        P(),
        P(None, "chan"),
        P(None, "chan"),
        P(),
        P(None, "chan"),
        P("chan"),
        P(),
        P(),
        P(),
        P(),
        P(None, None, None, None, "chan"),
    )
    return jax.shard_map(
        per_device, mesh=mesh, in_specs=placed, out_specs=P("tm", "chan"), check_vma=False
    )
```

```python
import jax
import jax.numpy as jnp
import numpy as np
from jax import lax
from jax.experimental import pallas as pl
from jax.experimental.pallas import tpu as pltpu
from jax.sharding import PartitionSpec as P

MESH = pl.DeviceIdType.MESH
F32 = jnp.float32
BF16 = jnp.bfloat16

LEAF = 256
LEAVES = 4
WIDTH = 256
RANK = 16
PLANES = 8
PLANE = 8


def transform_tables():
    odd = np.arange(LEAF)[:, None] + 0.5
    angle = 2 * np.pi * odd * np.arange(LEAF)[None, :] / (2 * LEAF)
    forward = np.concatenate([np.cos(angle), -np.sin(angle)], 0)
    return forward.astype(np.float32), (forward.T / LEAF).astype(np.float32)


def dot(left, right):
    return jnp.dot(left, right, preferred_element_type=F32)


def halves(value):
    high = value.astype(BF16)
    return high, (value - high.astype(F32)).astype(BF16)


def fine_dot(left, right):
    left_high, left_low = halves(left)
    right_high, right_low = halves(right)
    return dot(left_high, right_high) + dot(left_high, right_low) + dot(left_low, right_high)


def place_dot(left, right):
    left_high, left_low = halves(left)
    ones = right.astype(BF16)
    return dot(left_high, ones) + dot(left_low, ones)


def selector(lanes, period, shift, limit):
    row = lax.broadcasted_iota(jnp.int32, (RANK, lanes), 0)
    lane = lax.broadcasted_iota(jnp.int32, (RANK, lanes), 1)
    return ((lax.rem(lane, period) == row + shift) & (lane < limit)).astype(F32)


def body(
    tok, gain, w_value, w_gate, phi, coeff, skip, up, down, lift, spread, coup, fwd, inv,
    out,
    g, w, gain_v, phi_v, coeff_v, skip_v, up_v, down_v, lift_v, spread_v, coup_v, fwd_f, inv_f, fwd_v, inv_v,
    vals, halo, gate, near, spec, khat, mom_m, lift_m, six_m, far_m, red_m, moms,
    m2, m2_prev, ctx_out, ctx_in, pack_out, pack_in, m5_in, far0, far1, out_v, parts, part_squares,
    local_sem, gsend, drecv, rrecv, hsem, csem, s1, r1, s1p, r1p, s2, r2, s5, r5, ready_plane, ready_next, ready_edge, ready_later, osem,
):
    t = lax.axis_index("tm")
    x = lax.axis_index("chan")
    core = lax.rem(t, 2)
    y = lax.rem(lax.div(t, 2), 4)
    z = lax.div(t, PLANE)
    own = lax.rem(t, PLANE)
    rank = 2 * y + 1 - core
    right, left = lax.rem(x + 1, 4), lax.rem(x + 3, 4)

    def later(distance):
        return lax.rem(t + distance, PLANES * PLANE)

    barrier = pltpu.get_barrier_semaphore()

    def signal(semaphore, frames, chans):
        pl.semaphore_signal(semaphore, inc=1, device_id=(frames, chans), device_id_type=MESH)

    signal(barrier, t, right)
    signal(barrier, t, left)

    @pl.when(z < PLANES - 1)
    def _():
        signal(barrier, t + PLANE, x)

    m2_prev[...] = jnp.zeros_like(m2_prev)
    ctx_in[...] = jnp.zeros_like(ctx_in)
    pack_in[...] = jnp.zeros_like(pack_in)
    m5_in[...] = jnp.zeros_like(m5_in)
    halo[...] = jnp.zeros_like(halo)

    def at_rank(other):
        return z * PLANE + 2 * lax.div(other, 2) + 1 - lax.rem(other, 2)

    for k in range(1, PLANE):

        @pl.when(rank + k < PLANE)
        def _():
            signal(barrier, at_rank(rank + k), x)

    pl.semaphore_wait(barrier, 2 + rank + jnp.where(z > 0, 1, 0))

    owners = [x, left, right, lax.rem(x + 2, 4)]

    def leaf_rows(leaf):
        return pl.ds(leaf * LEAF if isinstance(leaf, int) else pl.multiple_of(leaf * LEAF, LEAF), LEAF)

    def direct(group, way):
        rows = pl.ds((1 - group) * 2 * LEAF, 2 * LEAF)
        return pltpu.make_async_remote_copy(
            src_ref=tok.at[rows],
            dst_ref=g.at[1 + way, rows],
            send_sem=gsend,
            recv_sem=drecv.at[way, group],
            device_id=(t, left if way else right),
            device_id_type=MESH,
        )

    def relay(group, way):
        rows = leaf_rows((1 - group) * 2 + way)
        return pltpu.make_async_remote_copy(
            src_ref=g.at[1 + way, rows],
            dst_ref=g.at[3, rows],
            send_sem=gsend,
            recv_sem=rrecv.at[way, group],
            device_id=(t, left if way else right),
            device_id_type=MESH,
        )

    def send_direct(group):
        for way in range(2):
            direct(group, way).start()

    def pass_on(group):
        for way in range(2):
            direct(group, way).wait_recv()
            relay(group, way).start()

    def wait_relayed(group):
        for way in range(2):
            relay(group, way).wait_recv()

    def tables_near():
        for name in ("phi", "coeff", "fwd"):
            copies[name].wait()
        fwd_v[...] = jnp.concatenate(halves(fwd_f[...]), 1)
        taps = phi_v[...].astype(BF16).astype(F32).T.astype(BF16)
        coeff_high, coeff_low = halves(coeff_v[...])
        kernel_taps = dot(taps, coeff_high) + dot(taps, coeff_low)
        both = jnp.concatenate([kernel_taps[:LEAF], kernel_taps[LEAF:]], 1)
        high, low = halves(both)
        hat = dot(fwd_v[...], jnp.concatenate([high, high], 0)) + dot(fwd_v[:, :LEAF], low)
        a_re, a_im = hat[:LEAF, :WIDTH], hat[LEAF:, :WIDTH]
        b_re, b_im = hat[:LEAF, WIDTH:], hat[LEAF:, WIDTH:]
        row = lax.broadcasted_iota(jnp.int32, (LEAF, WIDTH), 0)
        sign = (1 - 2 * lax.rem(row, 2)).astype(F32)
        khat[0] = a_re
        khat[1] = a_im
        khat[2] = b_re - sign * a_im
        khat[3] = b_im + sign * a_re

    def tables_moments():
        copies["up"].wait()
        copies["lift"].wait()
        base = up_v[...]
        first = [fine_dot(lift_v[0, k], base) for k in range(2)]
        for leaf in range(LEAVES):
            second = fine_dot(lift_v[1, leaf // 2], first[leaf % 2])
            high, low = halves(jnp.concatenate([base, first[leaf % 2], second], 0))
            mom_m[leaf] = jnp.concatenate([high, low], 1)

    def tables_lift():
        def pair(level):
            return place_dot(lift_v[level, 0], selector(128, 32, 0, 128)) + place_dot(
                lift_v[level, 1], selector(128, 32, 16, 128)
            )

        def blocks(level, copies_of):
            rows = jnp.concatenate([pair(level)] * copies_of, 0)
            row = lax.broadcasted_iota(jnp.int32, rows.shape, 0)
            lane = lax.broadcasted_iota(jnp.int32, rows.shape, 1)
            return jnp.where(lax.div(row, RANK) == lax.div(lane, 2 * RANK), rows, 0.0)

        three = blocks(2, 8)
        four = fine_dot(blocks(3, 2), three)
        five = fine_dot(blocks(4, 1), jnp.concatenate([four, jnp.zeros((96, 128), F32)], 0))
        whole = jnp.concatenate([four, three[32:64], five, three[:32]], 0)
        high, low = halves(whole)
        lift_m[...] = jnp.concatenate([high, low], 1)
        six = place_dot(lift_v[5, 0], selector(128, 32, 0, 64)) + place_dot(
            lift_v[5, 1], selector(128, 32, 16, 64)
        )
        high = six.astype(BF16).astype(F32)
        lane = lax.broadcasted_iota(jnp.int32, six.shape, 1)
        six_m[...] = jnp.where(lane < 32, high, six - high).astype(BF16)

    def tables_far():
        copies["spread"].wait()
        copies["down"].wait()
        row = lax.broadcasted_iota(jnp.int32, (RANK, LEAF), 0)
        lane = lax.broadcasted_iota(jnp.int32, (RANK, LEAF), 1)
        summing = (lax.div(lane, RANK) == row).astype(F32)
        chain = None
        for k in range(5):
            if k > 0:
                step = spread_v[1 + k, lax.rem(lax.div(t, 2 ** (k - 1)), 2)]
                chain = step if k == 1 else fine_dot(chain, step)
            high, low = halves(summing if k == 0 else place_dot(chain, summing))
            red_m[k] = jnp.concatenate([high, low], 0)
        turned = down_v[...].T
        for leaf in range(LEAVES):
            near_step = spread_v[0, leaf % 2]
            both_steps = fine_dot(near_step, spread_v[1, leaf // 2])
            mix = (
                selector(LEAF, 48, 0, 144)
                + place_dot(near_step, selector(LEAF, 48, 16, 144))
                + place_dot(both_steps, selector(LEAF, 48, 32, 144))
            )
            whole = fine_dot(turned, mix)
            high = whole.astype(BF16).astype(F32)
            lane_at = lax.broadcasted_iota(jnp.int32, whole.shape, 1)
            far_m[leaf] = jnp.where(lane_at < 96, high, whole - high).astype(BF16)

    def pair_rows(first):
        return pl.ds(first * LEAF, 2 * LEAF)

    def scaled_rows(first, slots):
        rows = pair_rows(first)
        squares = jnp.zeros((2 * LEAF, WIDTH), F32)
        columns = []
        for slot in slots:
            tokens = g[slot, rows, :].astype(F32)
            squares = squares + tokens * tokens
            scale = gain_v[:, pl.ds(pl.multiple_of(owners[slot] * WIDTH, WIDTH), WIDTH)]
            columns.append((tokens * scale).astype(BF16))
        return jnp.concatenate(columns, 1), squares

    def gather_pair(first):
        scaled, squares = scaled_rows(first, (0, 1, 2))
        parts[pair_rows(first), :] = dot(scaled, w[:3].reshape(3 * WIDTH, 2 * WIDTH))
        part_squares[pair_rows(first), :] = squares[:, : WIDTH // 2] + squares[:, WIDTH // 2 :]

    def values_of(first):
        rows = pair_rows(first)
        scaled, squares = scaled_rows(first, (3,))
        squares = squares[:, : WIDTH // 2] + squares[:, WIDTH // 2 :] + part_squares[rows, :]
        inverse = lax.rsqrt(jnp.sum(squares, axis=1, keepdims=True) / 1024 + 1e-06)
        part_squares[rows, :] = jnp.broadcast_to(inverse, squares.shape)
        value = ((parts[rows, :WIDTH] + dot(scaled, w[3, :, :WIDTH])) * inverse).astype(BF16)
        vals[rows, :] = value
        for k in range(2):
            leaf_value = value[k * LEAF : (k + 1) * LEAF]
            moms[first + k] = dot(mom_m[first + k], jnp.concatenate([leaf_value, leaf_value], 0))

    def gates_of(first):
        rows = pair_rows(first)
        scaled, _ = scaled_rows(first, (3,))
        half = 0.5 * part_squares[rows, :]
        sums = parts[rows, WIDTH:] + dot(scaled, w[3, :, WIDTH:])
        gate[rows, :] = 0.5 * jnp.tanh(sums * jnp.concatenate([half, half], 1)) + 0.5

    def spectra(first):
        both = jnp.concatenate([vals[leaf_rows(first), :], vals[leaf_rows(first + 1), :]], 1)
        result = dot(fwd_v[...], jnp.concatenate([both, both], 0))
        spec[first] = result[:, :WIDTH]
        spec[first + 1] = result[:, WIDTH:]

    def near_rows(leaves):
        columns = []
        for leaf in leaves:
            before = leaf - 1 if leaf > 0 else LEAVES
            a_re, a_im = spec[leaf, :LEAF, :], spec[leaf, LEAF:, :]
            b_re, b_im = spec[before, :LEAF, :], spec[before, LEAF:, :]
            out_re = khat[0] * a_re - khat[1] * a_im + khat[2] * b_re - khat[3] * b_im
            out_im = khat[0] * a_im + khat[1] * a_re + khat[2] * b_im + khat[3] * b_re
            columns.append(jnp.concatenate([out_re, out_im], 0).astype(BF16))
        total = dot(inv_v[...], jnp.concatenate(columns, 1))
        for k, leaf in enumerate(leaves):
            rows = leaf_rows(leaf)
            direct_term = skip_v[...] * vals[rows, :].astype(F32)
            near[rows, :] = total[:, k * WIDTH : (k + 1) * WIDTH] + direct_term

    def coupled(level, source_two, source_three):
        product = coup_v[level, 0] * source_two[None]
        if source_three is not None:
            product = product + coup_v[level, 1] * source_three[None]
        return product.reshape(RANK * RANK, WIDTH).astype(BF16)

    send_direct(0)

    copies = {}

    def local(name, source, target):
        copies[name] = pltpu.make_async_copy(source, target, local_sem.at[len(copies)])
        copies[name].start()

    local("tok", tok, g.at[0])
    for slot in range(4):
        rows = pl.ds(pl.multiple_of(owners[slot] * WIDTH, WIDTH), WIDTH)
        local(("v", slot), w_value.at[rows], w.at[slot, :, pl.ds(0, WIDTH)])
        local(("g", slot), w_gate.at[rows], w.at[slot, :, pl.ds(WIDTH, WIDTH)])
    for name, source, target in (
        ("gain", gain, gain_v),
        ("phi", phi, phi_v),
        ("coeff", coeff, coeff_v),
        ("fwd", fwd, fwd_f),
        ("skip", skip, skip_v),
        ("up", up, up_v),
        ("down", down, down_v),
        ("lift", lift, lift_v),
        ("spread", spread, spread_v),
        ("inv", inv, inv_f),
        ("coup", coup, coup_v),
    ):
        local(name, source, target)

    @pl.when(z > 0)
    def _():
        signal(ready_next, t - PLANE, x)

    for k in range(1, PLANE):

        @pl.when(rank >= k)
        def _():
            signal(ready_plane, at_rank(rank - k), x)

    def chain(place):
        @pl.when(z == PLANES - 1 - place)
        def _():
            if not isinstance(place, int) or place > 0:
                pl.semaphore_wait(ready_later, 1)
            if not isinstance(place, int) or place < PLANES - 1:
                signal(ready_later, t - PLANE, x)

    chain(0)
    send_direct(1)
    tables_near()
    chain(1)
    tables_moments()
    chain(2)
    tables_lift()
    chain(3)
    for slot in range(4):
        copies["v", slot].wait()
        copies["g", slot].wait()
    for name in ("tok", "gain", "skip", "coup", "inv"):
        copies[name].wait()
    pass_on(0)
    chain(4)

    @pl.when(rank < PLANE - 1)
    def _():
        pl.semaphore_wait(ready_plane, PLANE - 1 - rank)

    @pl.when(z < PLANES - 1)
    def _():
        pl.semaphore_wait(ready_next, 1)

        @pl.when(y == 0)
        def _():
            signal(ready_edge, z * PLANE + 6, x)
            signal(ready_edge, z * PLANE + 7, x)

    gather_pair(2)
    chain(5)
    tables_far()
    inv_v[...] = inv_f[...].astype(BF16)
    chain(6)
    pass_on(1)
    gather_pair(0)

    @pl.when((y == 3) & (z < PLANES - 1))
    def _():
        pl.semaphore_wait(ready_edge, 2)

    halo_copy = pltpu.make_async_remote_copy(
        src_ref=vals.at[pl.ds(3 * LEAF, LEAF)],
        dst_ref=halo,
        send_sem=hsem.at[0],
        recv_sem=hsem.at[1],
        device_id=(later(1), x),
        device_id_type=MESH,
    )

    def ctx_copy(part):
        rows = pl.ds(0, 48) if part == 0 else pl.ds(48, 16)
        return pltpu.make_async_remote_copy(
            src_ref=ctx_out.at[rows],
            dst_ref=ctx_in.at[rows],
            send_sem=csem.at[0, part],
            recv_sem=csem.at[1, part],
            device_id=(later(1), x),
            device_id_type=MESH,
        )

    summing = red_m[0, :RANK, :]

    def gathered(level, source_two, source_three=None):
        return dot(summing, coupled(level, source_two, source_three))

    wait_relayed(0)
    values_of(2)
    ctx_out[:48] = jnp.concatenate(
        [moms[2, 0:16, :], moms[3, 0:16, :], moms[2, 16:32, :] + moms[3, 16:32, :]], 0
    ).astype(BF16)

    @pl.when(t < PLANES * PLANE - 1)
    def _():
        halo_copy.start()
        ctx_copy(0).start()

    spectra(2)
    gates_of(2)
    near_rows((3,))

    wait_relayed(1)
    values_of(0)

    total = moms[0, 32:48, :] + moms[1, 32:48, :] + moms[2, 32:48, :] + moms[3, 32:48, :]
    m2[own] = total.astype(BF16)

    def plane_copy(k):
        return pltpu.make_async_remote_copy(
            src_ref=m2.at[own],
            dst_ref=m2.at[own],
            send_sem=s1,
            recv_sem=r1,
            device_id=(z * PLANE + lax.rem(own + k, PLANE), x),
            device_id_type=MESH,
        )

    plane_all = pltpu.make_async_remote_copy(
        src_ref=m2.at[pl.ds(0, PLANE - 1)],
        dst_ref=m2.at[pl.ds(0, PLANE - 1)],
        send_sem=s1,
        recv_sem=r1,
        device_id=(t, right),
        device_id_type=MESH,
    )

    for k in range(1, PLANE):
        plane_copy(k).start()

    def next_plane_copy(target, source):
        return pltpu.make_async_remote_copy(
            src_ref=m2.at[own],
            dst_ref=m2_prev.at[source],
            send_sem=s1p.at[target],
            recv_sem=r1p.at[source],
            device_id=(lax.rem(z + 1, PLANES) * PLANE + target, x),
            device_id_type=MESH,
        )

    @pl.when((y == 3) & (z < PLANES - 1))
    def _():
        for target in range(2):
            next_plane_copy(target, core).start()

    ctx_out[48:] = (moms[0, 16:32, :] + moms[1, 16:32, :]).astype(BF16)

    @pl.when(t < PLANES * PLANE - 1)
    def _():
        ctx_copy(1).start()

    gates_of(0)
    spectra(0)
    near_rows((1, 2))

    plane_all.wait_recv()
    stack = m2[...].reshape(PLANE * RANK, WIDTH)
    lifted = dot(lift_m[...], jnp.concatenate([stack, stack], 0))
    pack_out[...] = lifted[:80].astype(BF16)


    def pack_copy(rows):
        return pltpu.make_async_remote_copy(
            src_ref=pack_out.at[pl.ds(0, rows)],
            dst_ref=pack_in.at[pl.ds(0, rows)],
            send_sem=s2,
            recv_sem=r2,
            device_id=(later(PLANE), x),
            device_id_type=MESH,
        )

    def five_copy(k):
        return pltpu.make_async_remote_copy(
            src_ref=pack_out.at[pl.ds(64, RANK)],
            dst_ref=m5_in.at[k],
            send_sem=s5.at[k],
            recv_sem=r5.at[k],
            device_id=(later(k * PLANE), x),
            device_id_type=MESH,
        )

    chain(7)

    for k in range(PLANES - 1, 1, -1):

        @pl.when(z + k < PLANES)
        def _():
            five_copy(k).start()

    @pl.when((z < PLANES - 1) & (y == 0))
    def _():
        pack_copy(48).start()

    @pl.when((z < PLANES - 1) & (y == 1))
    def _():
        pack_copy(64).start()

    @pl.when((z < PLANES - 1) & (y >= 2))
    def _():
        pack_copy(32).start()

    @pl.when(t > 0)
    def _():
        halo_copy.wait_recv()

    spec[LEAVES] = dot(fwd_v[...], jnp.concatenate([halo[...], halo[...]], 0))
    near_rows((0,))

    @pl.when(t > 0)
    def _():
        ctx_copy(0).wait_recv()
        ctx_copy(1).wait_recv()

    prev = ctx_in[...].astype(F32)
    far0[0] = gathered(0, prev[0:16])
    far0[1] = gathered(0, prev[16:32], prev[0:16])
    far0[2] = gathered(0, moms[0, 0:16, :])
    far0[3] = gathered(0, moms[1, 0:16, :], moms[0, 0:16, :])
    far1[0] = gathered(1, prev[48:64])
    far1[1] = gathered(1, prev[32:48], prev[48:64])

    @pl.when((y == 0) & (z > 0))
    def _():
        for source in range(2):
            next_plane_copy(source, source).wait_recv()

    def reduced(k, source_two, source_three):
        return dot(red_m[k], coupled(2 + k, source_two, source_three))

    at = 2 * jnp.maximum(y - 1, 0)
    inside = y > 0
    two = jnp.where(inside, m2[at + core], m2_prev[core]).astype(F32)
    three = jnp.where(inside, m2[at], m2_prev[0]).astype(F32) * core.astype(F32)
    expansion = reduced(0, two, three)

    @pl.when((z > 0) & (y == 0))
    def _():
        pack_copy(48).wait_recv()

    @pl.when((z > 0) & (y == 1))
    def _():
        pack_copy(64).wait_recv()

    @pl.when((z > 0) & (y >= 2))
    def _():
        pack_copy(32).wait_recv()

    odd = lax.rem(y, 2)
    lower = y < 2
    here = jnp.where(odd == 1, lifted[96:112], lifted[80:96])
    coming = pack_in[pl.ds(pl.multiple_of(32 + odd * RANK, RANK), RANK), :].astype(F32)
    two = jnp.where(lower, coming, here)
    three = jnp.where(lower, pack_in[32:48, :].astype(F32), lifted[80:96]) * odd.astype(F32)
    expansion = expansion + reduced(1, two, three)
    odd = lax.div(y, 2)
    two = pack_in[pl.ds(pl.multiple_of(odd * RANK, RANK), RANK), :].astype(F32)
    three = pack_in[0:16, :].astype(F32) * odd.astype(F32)
    expansion = expansion + reduced(2, two, three)

    for k in range(2, PLANES):

        @pl.when(z >= k)
        def _():
            five_copy(k).wait_recv()

    odd = lax.rem(z, 2)
    expansion = expansion + reduced(
        3, m5_in[2].astype(F32), m5_in[3].astype(F32) * odd.astype(F32)
    )
    pad = jnp.zeros((64, WIDTH), BF16)

    def sixth(base):
        pair = [m5_in[base], m5_in[base - 1]]
        return dot(six_m[...], jnp.concatenate(pair + pair + [pad], 0))

    odd_six = lax.rem(lax.div(z, 2), 2)
    expansion = expansion + reduced(
        4, sixth(4 + odd), sixth(6 + odd) * odd_six.astype(F32)
    )

    expansion = expansion[:RANK] + expansion[RANK:]

    def out_copy(leaf):
        rows = leaf_rows(leaf)
        return pltpu.make_async_copy(out_v.at[rows], out.at[rows], osem.at[leaf])

    for leaf in range(LEAVES):
        rows = leaf_rows(leaf)
        high, low = halves(jnp.concatenate([far0[leaf], far1[leaf // 2], expansion], 0))
        whole = jnp.concatenate([high, low, high, jnp.zeros((112, WIDTH), BF16)], 0)
        combined = near[rows, :] + dot(far_m[leaf], whole)
        out_v[rows, :] = (gate[rows, :] * combined).astype(BF16)
        out_copy(leaf).start()

    gather_sent = g.at[pl.ds(0, 3)]
    pltpu.make_async_remote_copy(
        src_ref=gather_sent,
        dst_ref=gather_sent,
        send_sem=gsend,
        recv_sem=drecv.at[0, 0],
        device_id=(t, right),
        device_id_type=MESH,
    ).wait_send()

    plane_all.wait_send()

    @pl.when(t < PLANES * PLANE - 1)
    def _():
        halo_copy.wait_send()
        ctx_copy(0).wait_send()
        ctx_copy(1).wait_send()

    @pl.when((y == 3) & (z < PLANES - 1))
    def _():
        for target in range(2):
            next_plane_copy(target, core).wait_send()

    @pl.when((z < PLANES - 1) & (y == 0))
    def _():
        pack_copy(48).wait_send()

    @pl.when((z < PLANES - 1) & (y == 1))
    def _():
        pack_copy(64).wait_send()

    @pl.when((z < PLANES - 1) & (y >= 2))
    def _():
        pack_copy(32).wait_send()

    for k in range(2, PLANES):

        @pl.when(z + k < PLANES)
        def _():
            five_copy(k).wait_send()

    for leaf in range(LEAVES):
        out_copy(leaf).wait()


def per_device(
    tokens,
    norm_gain,
    w_value,
    w_gate,
    phi_taps,
    tap_coeff,
    skip_gain,
    basis_up,
    basis_down,
    lift_maps,
    spread_maps,
    couplings,
):
    forward, inverse = transform_tables()
    in_hbm = pl.BlockSpec(memory_space=pltpu.HBM)
    frames = LEAF * LEAVES
    vmem = pltpu.VMEM
    dma = pltpu.SemaphoreType.DMA
    scratch = [
        vmem((4, frames, WIDTH), BF16),
        vmem((4, WIDTH, 2 * WIDTH), BF16),
        vmem((1, 4 * WIDTH), F32),
        vmem(phi_taps.shape, F32),
        vmem(tap_coeff.shape, F32),
        vmem((1, WIDTH), F32),
        vmem(basis_up.shape, F32),
        vmem(basis_down.shape, F32),
        vmem(lift_maps.shape, F32),
        vmem(spread_maps.shape, F32),
        vmem(couplings.shape, F32),
        vmem(forward.shape, F32),
        vmem(inverse.shape, F32),
        vmem((2 * LEAF, 2 * LEAF), BF16),
        vmem((LEAF, 2 * LEAF), BF16),
        vmem((frames, WIDTH), BF16),
        vmem((LEAF, WIDTH), BF16),
        vmem((frames, WIDTH), F32),
        vmem((frames, WIDTH), F32),
        vmem((LEAVES + 1, 2 * LEAF, WIDTH), F32),
        vmem((4, LEAF, WIDTH), F32),
        vmem((LEAVES, 48, 2 * LEAF), BF16),
        vmem((112, 256), BF16),
        vmem((RANK, 128), BF16),
        vmem((LEAVES, LEAF, LEAF), BF16),
        vmem((5, 2 * RANK, LEAF), BF16),
        vmem((LEAVES, 48, WIDTH), F32),
        vmem((PLANE, RANK, WIDTH), BF16),
        vmem((2, RANK, WIDTH), BF16),
        vmem((64, WIDTH), BF16),
        vmem((64, WIDTH), BF16),
        vmem((80, WIDTH), BF16),
        vmem((64, WIDTH), BF16),
        vmem((PLANES, RANK, WIDTH), BF16),
        vmem((LEAVES, RANK, WIDTH), F32),
        vmem((2, RANK, WIDTH), F32),
        vmem((frames, WIDTH), BF16),
        vmem((frames, 2 * WIDTH), F32),
        vmem((frames, WIDTH // 2), F32),
        dma((20,)),
        dma(()),
        dma((2, 2)),
        dma((2, 2)),
        dma((2,)),
        dma((2, 2)),
        dma(()),
        dma(()),
        dma((2,)),
        dma((2,)),
        dma(()),
        dma(()),
        dma((PLANES,)),
        dma((PLANES,)),
        pltpu.SemaphoreType.REGULAR,
        pltpu.SemaphoreType.REGULAR,
        pltpu.SemaphoreType.REGULAR,
        pltpu.SemaphoreType.REGULAR,
        dma((LEAVES,)),
    ]
    return pl.pallas_call(
        body,
        out_shape=jax.ShapeDtypeStruct(tokens.shape, BF16),
        in_specs=[in_hbm] * 14,
        out_specs=in_hbm,
        scratch_shapes=scratch,
        compiler_params=pltpu.CompilerParams(
            collective_id=0, has_side_effects=True, vmem_limit_bytes=60 * 1024 * 1024
        ),
        cost_estimate=pl.CostEstimate(flops=4 * 10**9, bytes_accessed=8 * 10**6, transcendentals=10**6),
    )(
        tokens,
        norm_gain.reshape(1, -1),
        w_value,
        w_gate,
        phi_taps,
        tap_coeff,
        skip_gain.reshape(1, -1),
        basis_up,
        basis_down,
        lift_maps,
        spread_maps,
        couplings,
        jnp.asarray(forward),
        jnp.asarray(inverse),
    )


def solution(mesh):
    placed = (
        P("tm", "chan"),
        P(),
        P(None, "chan"),
        P(None, "chan"),
        P(),
        P(None, "chan"),
        P("chan"),
        P(),
        P(),
        P(),
        P(),
        P(None, None, None, None, "chan"),
    )
    return jax.shard_map(
        per_device, mesh=mesh, in_specs=placed, out_specs=P("tm", "chan"), check_vma=False
    )
```
